32 devices in a mesh: dp: 8 (over y, x, core), tensor: 4 (over z).
Axes of the slice: x: 2, y: 2, z: 4, core: 2. Of those that a mesh axis runs over, the one named last changes fastest.
Arguments:
- context: bfloat16 [512, 180, 768], P(('dp', 'tensor')), may hold values from -6 to 6
- stream: bfloat16 [512, 180, 768], P(('dp', 'tensor')), may hold values from -6 to 6
- out_weight: bfloat16 [768, 768], replicated, may hold values from -0.21875 to 0.21875
- gain: float32 [768], replicated, may hold values from 0.5 to 1.5
- bias: float32 [768], replicated, may hold values from -3 to 3
- proj_weight: bfloat16 [768, 128], replicated, may hold values from -0.21875 to 0.21875
- query_states: bfloat16 [8, 32, 768], P('dp'), may hold values from -6 to 6
- passage_len: int32 [512], P(('dp', 'tensor')), may hold values from 45 to 180, as said below
- passage_dest: int32 [512], P(('dp', 'tensor')), may hold values from 0 to 511, as said below
- teacher_states: bfloat16 [512, 212, 1024], P(('dp', 'tensor')), may hold values from -6 to 6
- teacher_query: bfloat16 [1024, 1024], P(None, 'tensor'), may hold values from -0.1875 to 0.1875
- teacher_key: bfloat16 [1024, 1024], P(None, 'tensor'), may hold values from -0.1875 to 0.1875
Outputs:
- loss: float32 [], replicated
- grad_out: float32 [768, 768], replicated
- grad_proj: float32 [768, 128], replicated
- grad_gain: float32 [768], replicated
- grad_bias: float32 [768], replicated
- grad_context: bfloat16 [512, 180, 768], P(('dp', 'tensor'))
The draws below stay inside these ranges and needn't reach their ends.
Inputs may be any that keep to these rules, and one draw needn't show every extreme that they name: `passage_dest`: A permutation of the pair positions. Passage rows form runs of 16 (run a = i * 4 + t), and so do pair positions; run a sends exactly 16 / 8 of its rows into each pair run j * 4 + t, for every j. `passage_len`: every run of 16 passage rows holds one passage of full length.
All inputs are finite; a program needn't handle non-finite values.
Results may differ from the reference program's by a relative error of at most 0.011.
Values may be sent and summed in bfloat16 or wider, within the bound.
No kernel may reach another device: no remote copies, remote signals or barrier semaphores. Data moves between devices by JAX's collectives and lax.ppermute only.
A program may use at most 192 MiB of HBM per device.

```python
import math
import jax
import jax.numpy as jnp
from jax import lax

D = 768
EMB = 128
SEARCH_WORD_SIZE = 32
LP = 180
NPQ = 64
PAIR_DEV = 16
TD = 1024
PAIRS = 512
PASSAGES = 512
QUERIES = 8
N_DP = 8
N_TENSOR = 4


def draw_passage_len(key, part):
    key_lengths, key_slots = jax.random.split(jax.random.fold_in(key, 11))
    lengths = jax.random.randint(key_lengths, (PASSAGES // PAIR_DEV, PAIR_DEV), LP // 4, LP + 1)
    full_slot = jax.random.randint(key_slots, (PASSAGES // PAIR_DEV,), 0, PAIR_DEV)
    row_index = jnp.arange(PAIR_DEV, dtype=jnp.int32)[None, :]
    return jnp.where(row_index == full_slot[:, None], LP, lengths).reshape(-1).astype(jnp.int32)


def draw_passage_dest(key, part):
    key_slots, key_rows = jax.random.split(jax.random.fold_in(key, 23))
    per_dest = PAIR_DEV // N_DP
    groups = N_DP * N_TENSOR
    slot_perms = jax.vmap(lambda inner: jax.random.permutation(inner, PAIR_DEV))(jax.random.split(key_slots, groups)).reshape(N_DP, N_TENSOR, PAIR_DEV)
    row_perms = jax.vmap(lambda inner: jax.random.permutation(inner, PAIR_DEV))(jax.random.split(key_rows, groups)).reshape(N_DP, N_TENSOR, PAIR_DEV)
    sender = slot_perms // per_dest
    within = slot_perms % per_dest
    target = jnp.arange(N_DP, dtype=jnp.int32)[:, None, None]
    member = jnp.arange(N_TENSOR, dtype=jnp.int32)[None, :, None]
    position = jnp.arange(PAIR_DEV, dtype=jnp.int32)[None, None, :]
    local_slot = target * per_dest + within
    member_full = jnp.broadcast_to(member, sender.shape)
    local_row = row_perms[sender, member_full, local_slot]
    source_pos = (sender * N_TENSOR + member_full) * PAIR_DEV + local_row
    pair_pos = (target * N_TENSOR + member) * PAIR_DEV + position
    result = jnp.zeros((PAIRS,), jnp.int32).at[source_pos.reshape(-1)].set(jnp.broadcast_to(pair_pos, source_pos.shape).reshape(-1).astype(jnp.int32))
    return result


def steps_of(stream_key, shape, cuts, smallest, high):
    level, own = 1.0, jax.random.fold_in(stream_key, 6)
    for dim, parts in cuts:
        heights = jnp.exp(jax.random.uniform(jax.random.fold_in(own, dim), (parts,), jnp.float32, smallest / len(cuts), high / len(cuts)))
        level = level * jnp.repeat(heights, shape[dim] // parts).reshape([-1 if axis == dim else 1 for axis in range(len(shape))])
    return level


def gaussian(rng, extent, scale, reach, pieces=(), held_as=jnp.bfloat16):
    factor_of = steps_of(rng, extent, pieces, -0.22, 0.18) if pieces else 1.0
    values = jax.random.normal(rng, extent, jnp.float32) * scale * factor_of
    return jnp.minimum(jnp.maximum(values, -reach), reach).astype(held_as)


def setup_inputs(seed: int = 0) -> dict:
    arg_keys = jax.random.split(jax.random.key(seed), 13)
    context = gaussian(arg_keys[0], (PASSAGES, LP, D), 1.0, 6.0, ((0, 32),))
    stream = gaussian(arg_keys[1], (PASSAGES, LP, D), 1.0, 6.0, ((0, 32),))
    out_weight = gaussian(arg_keys[2], (D, D), D ** -0.5, 0.21875)
    gain = jnp.clip(1.0 + 0.1 * jax.random.normal(arg_keys[3], (D,), jnp.float32), 0.5, 1.5)
    bias = gaussian(arg_keys[4], (D,), 0.5, 3.0, (), jnp.float32)
    proj_weight = gaussian(arg_keys[5], (D, EMB), D ** -0.5, 0.21875)
    query_states = gaussian(arg_keys[6], (QUERIES, SEARCH_WORD_SIZE, D), 1.0, 6.0, ((0, 8),))
    passage_len = draw_passage_len(jax.random.fold_in(arg_keys[12], 71), 0)
    passage_dest = draw_passage_dest(jax.random.fold_in(arg_keys[12], 71), 0)
    teacher_states = gaussian(arg_keys[9], (PAIRS, SEARCH_WORD_SIZE + LP, TD), 1.0, 6.0, ((0, 32),))
    teacher_query = gaussian(arg_keys[10], (TD, TD), TD ** -0.5, 0.1875, ((1, 4),))
    teacher_key = gaussian(arg_keys[11], (TD, TD), TD ** -0.5, 0.1875, ((1, 4),))
    return {"context": context, "stream": stream, "out_weight": out_weight, "gain": gain, "bias": bias, "proj_weight": proj_weight, "query_states": query_states, "passage_len": passage_len, "passage_dest": passage_dest, "teacher_states": teacher_states, "teacher_query": teacher_query, "teacher_key": teacher_key}


sharpness_divisor = 0.05
softcap = 10.0
epsilon = 1e-06

def student_forward(context_rows, stream_rows, out_weight, gain, bias, proj_weight):
    summed = stream_rows.astype(jnp.float32) + jnp.einsum('ptd,de->pte', context_rows.astype(jnp.float32), out_weight.astype(jnp.float32))
    centred = summed - lax.optimization_barrier(jnp.mean(summed, axis=-1, keepdims=True))
    inverse = lax.rsqrt(lax.optimization_barrier(jnp.mean(centred * centred, axis=-1, keepdims=True)) + epsilon)
    normed = centred * inverse
    hidden = (normed * gain + bias).astype(jnp.bfloat16)
    embeds = jnp.einsum('ptd,de->pte', hidden.astype(jnp.float32), proj_weight.astype(jnp.float32))
    length = jnp.sqrt(lax.optimization_barrier(jnp.sum(embeds * embeds, axis=-1, keepdims=True)) + epsilon)
    return (hidden, normed, inverse, embeds, length)

def teacher_map(states, teacher_query, teacher_key):
    query_side = jnp.einsum('pqd,de->pqe', states[:, :SEARCH_WORD_SIZE].astype(jnp.float32), teacher_query.astype(jnp.float32)).astype(jnp.bfloat16)
    key_side = jnp.einsum('pkd,de->pke', states[:, SEARCH_WORD_SIZE:].astype(jnp.float32), teacher_key.astype(jnp.float32)).astype(jnp.bfloat16)
    raw_map = jnp.einsum('pqe,pke->pqk', query_side.astype(jnp.float32), key_side.astype(jnp.float32)) / math.sqrt(TD)
    return softcap * jnp.tanh(raw_map / softcap)

def reference(context, stream, out_weight, gain, bias, proj_weight, query_states, passage_len, passage_dest, teacher_states, teacher_query, teacher_key):
    blocks = PASSAGES // PAIR_DEV
    context_blocks = context.reshape(blocks, PAIR_DEV, LP, D)
    stream_blocks = stream.reshape(blocks, PAIR_DEV, LP, D)

    def forward_block(inputs):
        hidden, normed, inverse, embeds, length = student_forward(inputs[0], inputs[1], out_weight, gain, bias, proj_weight)
        return (embeds / length).astype(jnp.bfloat16)
    unit_vecs = lax.map(forward_block, (context_blocks, stream_blocks)).reshape(PASSAGES, LP, EMB)
    source = jnp.zeros((PAIRS,), jnp.int32).at[passage_dest].set(jnp.arange(PASSAGES, dtype=jnp.int32))
    matched_direction_arrays = unit_vecs[source]
    pair_len = passage_len[source]
    teacher = lax.map(lambda states: teacher_map(states, teacher_query, teacher_key), teacher_states.reshape(blocks, PAIR_DEV, SEARCH_WORD_SIZE + LP, TD)).reshape(PAIRS, SEARCH_WORD_SIZE, LP)
    query_embeds = jnp.einsum('nqd,de->nqe', query_states.astype(jnp.float32), proj_weight.astype(jnp.float32))
    query_length = jnp.sqrt(lax.optimization_barrier(jnp.sum(query_embeds * query_embeds, axis=-1, keepdims=True)) + epsilon)
    query_dir = query_embeds / query_length
    query_unit = query_dir.astype(jnp.bfloat16)
    matched_search_rescaled = query_unit[jnp.arange(PAIRS, dtype=jnp.int32) // NPQ]
    learner_raw_ratings = jnp.einsum('hsn,hfn->hsf', matched_search_rescaled.astype(jnp.float32), matched_direction_arrays.astype(jnp.float32)) / sharpness_divisor
    valid = jnp.arange(LP, dtype=jnp.int32)[None, None, :] < pair_len[:, None, None]
    student_exp = jnp.where(valid, jnp.exp(learner_raw_ratings), 0.0)
    student_total = lax.optimization_barrier(jnp.sum(student_exp, axis=-1, keepdims=True))
    learner_likelihood = student_exp / student_total
    student_log = learner_raw_ratings - jnp.log(student_total)
    teacher_exp = jnp.where(valid, jnp.exp(teacher), 0.0)
    teacher_total = lax.optimization_barrier(jnp.sum(teacher_exp, axis=-1, keepdims=True))
    mentor_likelihood = teacher_exp / teacher_total
    teacher_log = teacher - jnp.log(teacher_total)
    diverge = lax.optimization_barrier(jnp.sum(jnp.where(valid, mentor_likelihood * (teacher_log - student_log), 0.0), axis=-1))
    loss = jnp.sum(diverge) / (PAIRS * SEARCH_WORD_SIZE)
    angle_similarity_slope = ((learner_likelihood - mentor_likelihood) / (SEARCH_WORD_SIZE * sharpness_divisor)).astype(jnp.bfloat16)
    unit_grad = jnp.einsum('pqk,pqc->pkc', angle_similarity_slope.astype(jnp.float32), matched_search_rescaled.astype(jnp.float32)).astype(jnp.bfloat16)
    pair_qgrad = jnp.einsum('pqk,pkc->pqc', angle_similarity_slope.astype(jnp.float32), matched_direction_arrays.astype(jnp.float32))
    query_grad = lax.optimization_barrier(jnp.sum(pair_qgrad.reshape(QUERIES, NPQ, SEARCH_WORD_SIZE, EMB), axis=1))
    query_embed_grad = (query_grad - query_dir * lax.optimization_barrier(jnp.sum(query_dir * query_grad, axis=-1, keepdims=True))) / query_length
    proj_query = jnp.einsum('nqd,nqe->de', query_states.astype(jnp.float32), query_embed_grad, precision=lax.Precision.HIGHEST)
    passage_grad = unit_grad[passage_dest].reshape(blocks, PAIR_DEV, LP, EMB)

    def backward_block(carry, inputs):
        wo_grad, proj_grad, gain_grad, bias_grad = carry
        context_rows, stream_rows, unit_rows = inputs
        hidden, normed, inverse, embeds, length = student_forward(context_rows, stream_rows, out_weight, gain, bias, proj_weight)
        direction = embeds / length
        upstream = unit_rows.astype(jnp.float32)
        embed_grad = ((upstream - direction * lax.optimization_barrier(jnp.sum(direction * upstream, axis=-1, keepdims=True))) / length).astype(jnp.bfloat16)
        proj_grad = proj_grad + jnp.einsum('ptd,pte->de', hidden.astype(jnp.float32), embed_grad.astype(jnp.float32))
        hidden_grad = jnp.einsum('pte,de->ptd', embed_grad.astype(jnp.float32), proj_weight.astype(jnp.float32))
        gain_grad = gain_grad + lax.optimization_barrier(jnp.sum(hidden_grad * normed, axis=(0, 1)))
        bias_grad = bias_grad + lax.optimization_barrier(jnp.sum(hidden_grad, axis=(0, 1)))
        scaled = hidden_grad * gain
        summed_grad = (inverse * (scaled - lax.optimization_barrier(jnp.mean(scaled, axis=-1, keepdims=True)) - normed * lax.optimization_barrier(jnp.mean(scaled * normed, axis=-1, keepdims=True)))).astype(jnp.bfloat16)
        wo_grad = wo_grad + jnp.einsum('ptd,pte->de', context_rows.astype(jnp.float32), summed_grad.astype(jnp.float32))
        context_grad = jnp.einsum('pte,de->ptd', summed_grad.astype(jnp.float32), out_weight.astype(jnp.float32)).astype(jnp.bfloat16)
        return ((wo_grad, proj_grad, gain_grad, bias_grad), context_grad)
    start = (jnp.zeros((D, D), jnp.float32), jnp.zeros((D, EMB), jnp.float32), jnp.zeros((D,), jnp.float32), jnp.zeros((D,), jnp.float32))
    totals, context_grads = lax.scan(backward_block, start, (context_blocks, stream_blocks, passage_grad))
    return (loss, totals[0], totals[1] + proj_query, totals[2], totals[3], context_grads.reshape(PASSAGES, LP, D))
```

```python
import functools
import math

import jax
import jax.numpy as jnp
from jax import lax
from jax.experimental import pallas as pl
from jax.experimental.pallas import tpu as pltpu
from jax.sharding import PartitionSpec as P

sharpness = 0.05
softcap = 10.0
epsilon = 1e-06
CORES = 2
VMEM_LIMIT = 56 * 1024 * 1024

F32 = jnp.float32
BF16 = jnp.bfloat16
VMEM = pl.BlockSpec(memory_space=pltpu.VMEM)
SMEM = pl.BlockSpec(memory_space=pltpu.SMEM)
ANY = pl.BlockSpec(memory_space=pl.ANY)


def up(n, m):
    return -(-n // m) * m


def dot(a, b, ca, cb):
    return lax.dot_general(a, b, (((ca,), (cb,)), ((), ())), preferred_element_type=F32)


def params(**kw):
    return pltpu.CompilerParams(vmem_limit_bytes=VMEM_LIMIT, **kw)


def cost(flops, nbytes):
    return pl.CostEstimate(flops=int(flops), bytes_accessed=int(nbytes), transcendentals=0)


def forward_kernel(ctx_ref, str_ref, wo_ref, gain_ref, bias_ref, wp_ref, normed_ref, emb_ref, inv_ref, x_s):
    group, seq, width = ctx_ref.shape
    pad = x_s.shape[0] // group
    for p in range(group):
        x_s[p * pad : p * pad + seq] = ctx_ref[p]
    product = dot(x_s[...], wo_ref[...], 1, 0)
    hidden = []
    for p in range(group):
        summed = product[p * pad : p * pad + seq] + str_ref[p].astype(F32)
        centred = summed - jnp.mean(summed, axis=-1, keepdims=True)
        inverse = lax.rsqrt(jnp.mean(centred * centred, axis=-1, keepdims=True) + epsilon)
        normed = centred * inverse
        normed_ref[p] = normed.astype(BF16)
        inv_ref[p] = jnp.broadcast_to(inverse, inv_ref.shape[1:])
        x_s[p * pad : p * pad + seq] = (normed * gain_ref[...] + bias_ref[...]).astype(BF16)
    embeds = dot(x_s[...], wp_ref[...], 1, 0)
    for p in range(group):
        emb_ref[p] = embeds[p * pad : p * pad + seq]


def student_forward(context, stream, out_weight, gain, bias, proj_weight, group):
    count, seq, width = context.shape
    emb = proj_weight.shape[1]
    pad = up(seq, 16)
    block = lambda last: pl.BlockSpec((group, seq, last), lambda s: (s, 0, 0))
    whole = lambda a: pl.BlockSpec(a.shape, lambda s: (0,) * a.ndim)
    return pl.pallas_call(
        forward_kernel,
        grid=(count // group,),
        in_specs=[block(width), block(width), whole(out_weight), whole(gain), whole(bias), whole(proj_weight)],
        out_specs=[block(width), block(emb), block(128)],
        out_shape=[
            jax.ShapeDtypeStruct((count, seq, width), BF16),
            jax.ShapeDtypeStruct((count, seq, emb), F32),
            jax.ShapeDtypeStruct((count, seq, 128), F32),
        ],
        scratch_shapes=[pltpu.VMEM((group * pad, width), BF16)],
        compiler_params=params(),
        cost_estimate=cost(2 * count * seq * width * (width + emb), 8 * count * seq * width),
        name="student_forward",
    )(context, stream, out_weight, gain, bias, proj_weight)


def teacher_kernel(parts, dests, per, tokens, order_ref, rows_ref, states_ref, wq_ref, wk_ref, *rest):
    pieces, outs = rest[:parts], rest[parts : parts + dests]
    w_s, own_s, q_s, slab_s, q_sem, slab_sem, w_sem, own_sem = rest[parts + dests :]
    pairs, total, depth = slab_s.shape
    slices = w_s.shape[0] // 2
    part_rows = pieces[0].shape[1]
    started = []
    own = [
        pltpu.make_async_copy(wq_ref, own_s.at[0], own_sem.at[0]),
        pltpu.make_async_copy(wk_ref, own_s.at[1], own_sem.at[1]),
    ]
    queries = [
        pltpu.make_async_copy(
            states_ref.at[order_ref[n], pl.ds(0, tokens)], q_s.at[pl.ds(n * tokens, tokens)], q_sem.at[n]
        )
        for n in range(pairs)
    ]
    gathered = [
        pltpu.make_async_copy(
            pieces[a],
            w_s.at[:, pl.ds(pl.multiple_of(rows_ref[a] * part_rows, part_rows), part_rows), :],
            w_sem.at[a],
        )
        for a in range(parts)
    ]
    slabs = [
        pltpu.make_async_copy(states_ref.at[order_ref[n]], slab_s.at[n], slab_sem.at[n]) for n in range(pairs)
    ]
    for copy in own + queries + gathered + slabs:
        copy.start()
    for copy in own + queries:
        copy.wait()
    q = q_s[...]
    mixed = dot(dot(q, own_s[0], 1, 0).astype(BF16), own_s[1], 1, 1)
    for copy in gathered:
        copy.wait()
    for k in range(slices):
        mixed = mixed + dot(dot(q, w_s[2 * k], 1, 0).astype(BF16), w_s[2 * k + 1], 1, 1)
    mixed = mixed.astype(BF16)
    scale = 1.0 / (math.sqrt(depth) * softcap)
    for n in range(pairs):
        slabs[n].wait()
        raw = dot(mixed[n * tokens : (n + 1) * tokens], slab_s[n, tokens:], 1, 1)
        outs[n // per][n % per] = jnp.exp(softcap * jnp.tanh(raw * scale)).astype(BF16)


def teacher_maps(order, rows, states, wq, wk, pieces, dests, tokens):
    pairs, total, depth = states.shape
    heads = wq.shape[1]
    per = pairs // dests
    parts = len(pieces)
    slices = pieces[0].shape[0]
    return pl.pallas_call(
        functools.partial(teacher_kernel, parts, dests, per, tokens),
        in_specs=[SMEM, SMEM] + [ANY] * (3 + parts),
        out_specs=[VMEM] * dests,
        out_shape=[jax.ShapeDtypeStruct((per, tokens, total - tokens), BF16)] * dests,
        scratch_shapes=[
            pltpu.VMEM((slices, depth, heads), BF16),
            pltpu.VMEM((2, depth, heads), BF16),
            pltpu.VMEM((pairs * tokens, depth), BF16),
            pltpu.VMEM((pairs, total, depth), BF16),
            pltpu.SemaphoreType.DMA((pairs,)),
            pltpu.SemaphoreType.DMA((pairs,)),
            pltpu.SemaphoreType.DMA((parts,)),
            pltpu.SemaphoreType.DMA((2,)),
        ],
        compiler_params=params(),
        cost_estimate=cost(4 * pairs * tokens * depth * depth, 2 * states.size + 4 * depth * depth),
        name="teacher_maps",
    )(order, rows, states, wq, wk, *pieces)


def backward_kernel(
    dests, per, tokens, group_queries,
    qidx_ref, midx_ref, len_ref, core_ref, *rest,
):
    maps, payloads = rest[:dests], rest[dests : 2 * dests]
    (ctx_ref, normed_ref, emb_ref, inv_ref, gain_ref, bias_ref, wp_ref, wpt_ref,
     sg_ref, send_ref, keep_ref,
     maps_s, qs_s, qunit_s, qdir_s, qlen_s, qg_s, wo_s, nt_s, s_s, l_s, right_s,
     x_s, n_s, i_s, eg_s) = rest[2 * dests :]
    step = pl.program_id(0)
    group, seq, width = ctx_ref.shape
    pad = x_s.shape[0] // group
    emb = wp_ref.shape[1]

    @pl.when(step == 0)
    def _():
        for k in range(dests):
            maps_s[k * per : (k + 1) * per] = maps[k][...]
            qs_s[k * group_queries * tokens : (k + 1) * group_queries * tokens] = payloads[k][
                : group_queries * tokens
            ]
        qe = dot(qs_s[...], wp_ref[...], 1, 0)
        length = jnp.sqrt(jnp.sum(qe * qe, axis=-1, keepdims=True) + epsilon)
        qdir = qe / length
        qdir_s[...] = qdir
        qlen_s[...] = jnp.broadcast_to(length, qlen_s.shape)
        qunit_s[...] = qdir.astype(BF16).reshape(qunit_s.shape)
        qg_s[...] = jnp.zeros_like(qg_s)
        wo_s[...] = jnp.zeros_like(wo_s)
        nt_s[...] = jnp.zeros_like(nt_s)
        s_s[...] = jnp.zeros_like(s_s)
        l_s[...] = jnp.zeros_like(l_s)
        x_s[...] = jnp.zeros_like(x_s)
        n_s[...] = jnp.zeros_like(n_s)
        i_s[...] = jnp.zeros_like(i_s)
        eg_s[...] = jnp.zeros_like(eg_s)

    for p in range(group):
        row = step * group + p
        e = emb_ref[p]
        length = jnp.sqrt(jnp.sum(e * e, axis=-1, keepdims=True) + epsilon)
        direction = e / length
        units = direction.astype(BF16)
        q = qunit_s[qidx_ref[row]]
        logits = dot(q, units, 1, 1) / sharpness
        valid = lax.broadcasted_iota(jnp.int32, logits.shape, 1) < len_ref[row]
        student = jnp.where(valid, jnp.exp(logits), 0.0)
        student_total = jnp.sum(student, axis=-1, keepdims=True)
        teacher = maps_s[midx_ref[row]].astype(F32)
        teacher_log = jnp.log(teacher)
        teacher = jnp.where(valid, teacher, 0.0)
        teacher_total = jnp.sum(teacher, axis=-1, keepdims=True)
        student_prob = student / student_total
        teacher_prob = teacher / teacher_total
        gap = (teacher_log - jnp.log(teacher_total)) - (logits - jnp.log(student_total))
        diverge = jnp.sum(jnp.where(valid, teacher_prob * gap, 0.0), axis=-1, keepdims=True)
        l_s[...] += jnp.broadcast_to(diverge, l_s.shape)
        slope = ((student_prob - teacher_prob) / (tokens * sharpness)).astype(BF16)
        upstream = dot(slope, q, 0, 0).astype(BF16).astype(F32)
        qg_s[qidx_ref[row]] += dot(slope, units, 1, 0)
        eg = (upstream - direction * jnp.sum(direction * upstream, axis=-1, keepdims=True)) / length
        eg_s[p * pad : p * pad + seq] = eg.astype(BF16)
        x_s[p * pad : p * pad + seq] = ctx_ref[p]
        n_s[p * pad : p * pad + seq] = normed_ref[p]
        i_s[p * pad : p * pad + seq] = inv_ref[p]

    eg = eg_s[...]
    normed16 = n_s[...]
    normed = normed16.astype(F32)
    scaled = dot(eg, wp_ref[...], 1, 1) * gain_ref[...]
    mean = jnp.mean(scaled, axis=-1, keepdims=True)
    along = jnp.mean(scaled * normed, axis=-1, keepdims=True)
    sg = (i_s[:, :1] * (scaled - mean - normed * along)).astype(BF16)
    for p in range(group):
        sg_ref[p] = sg[p * pad : p * pad + seq]
    wo_s[...] += dot(x_s[...], sg, 0, 0)
    nt_s[...] += dot(eg, normed16, 0, 0)
    s_s[...] += dot(eg, jnp.ones((eg.shape[0], 128), BF16), 0, 0)

    @pl.when(step == pl.num_programs(0) - 1)
    def _():
        qg = qg_s[...].reshape(qdir_s.shape)
        qdir = qdir_s[...]
        qeg = (qg - qdir * jnp.sum(qdir * qg, axis=-1, keepdims=True)) / qlen_s[:, :1]
        high = qeg.astype(BF16)
        low = (qeg - high.astype(F32)).astype(BF16)
        qs = qs_s[...]
        proj_query = dot(high, qs, 0, 0) + dot(low, qs, 0, 0)
        nt = nt_s[...]
        s = s_s[:, :1]
        wpt = wpt_ref[...].astype(F32)
        proj = nt * gain_ref[...] + s * bias_ref[...] + proj_query
        gain_row = jnp.sum(wpt * nt, axis=0, keepdims=True)
        bias_row = jnp.sum(wpt * s, axis=0, keepdims=True)
        index = lax.broadcasted_iota(jnp.int32, (tokens, width), 0)
        top = jnp.where(index == 0, gain_row, jnp.where(index == 1, bias_row, 0.0))
        spread = jnp.broadcast_to(l_s[:, :1], (tokens, width))
        rest_rows = jnp.zeros((128 - 2 * tokens, width), F32)
        right_s[...] = jnp.concatenate([proj, top, spread, rest_rows], axis=0).T
        half = width // CORES
        chunk = send_ref.shape[1]
        for ref, which in ((send_ref, 1 - core_ref[0]), (keep_ref, core_ref[0])):
            start = pl.multiple_of(which * half, half)
            left = wo_s[pl.ds(start, half)].astype(BF16)
            right = right_s[pl.ds(start, half)].astype(BF16)
            for c in range(half // chunk):
                ref[c, :, :width] = left[c * chunk : (c + 1) * chunk]
                ref[c, :, width:] = right[c * chunk : (c + 1) * chunk]


def student_backward(
    qidx, midx, lens, core, maps, payloads, context, normed, embeds, inverse, gain, bias, wp, wpt,
    group, tokens, group_queries, chunk,
):
    count, seq, width = context.shape
    emb = wp.shape[1]
    pad = up(seq, 16)
    dests = len(maps)
    per = count // dests
    chunks = width // CORES // chunk
    block = lambda last: pl.BlockSpec((group, seq, last), lambda s, *_: (s, 0, 0))
    whole = lambda a: pl.BlockSpec(a.shape, lambda s, *_: (0,) * a.ndim)
    full = pl.BlockSpec((chunks, chunk, width + emb + 128), lambda s, *_: (0, 0, 0))
    queries = dests * group_queries
    return pl.pallas_call(
        functools.partial(backward_kernel, dests, per, tokens, group_queries),
        grid_spec=pltpu.PrefetchScalarGridSpec(
            num_scalar_prefetch=4,
            grid=(count // group,),
            in_specs=[whole(a) for a in maps]
            + [whole(a) for a in payloads]
            + [block(width), block(width), block(emb), block(128)]
            + [whole(a) for a in (gain, bias, wp, wpt)],
            out_specs=[block(width), full, full],
            scratch_shapes=[
                pltpu.VMEM((count, tokens, seq), BF16),
                pltpu.VMEM((queries * tokens, width), BF16),
                pltpu.VMEM((queries, tokens, emb), BF16),
                pltpu.VMEM((queries * tokens, emb), F32),
                pltpu.VMEM((queries * tokens, 128), F32),
                pltpu.VMEM((queries, tokens, emb), F32),
                pltpu.VMEM((width, width), F32),
                pltpu.VMEM((emb, width), F32),
                pltpu.VMEM((emb, 128), F32),
                pltpu.VMEM((tokens, 128), F32),
                pltpu.VMEM((width, emb + 128), F32),
                pltpu.VMEM((group * pad, width), BF16),
                pltpu.VMEM((group * pad, width), BF16),
                pltpu.VMEM((group * pad, 128), F32),
                pltpu.VMEM((group * pad, emb), BF16),
            ],
        ),
        out_shape=[
            jax.ShapeDtypeStruct((count, seq, width), BF16),
            jax.ShapeDtypeStruct((chunks, chunk, width + emb + 128), BF16),
            jax.ShapeDtypeStruct((chunks, chunk, width + emb + 128), BF16),
        ],
        compiler_params=params(),
        cost_estimate=cost(2 * count * seq * width * (width + 2 * emb), 8 * count * seq * width),
        name="student_backward",
    )(qidx, midx, lens, core, *maps, *payloads, context, normed, embeds, inverse, gain, bias, wp, wpt)


def context_kernel(sg_ref, wo_ref, out_ref, x_s):
    group, seq, width = sg_ref.shape
    pad = x_s.shape[0] // group
    for p in range(group):
        x_s[p * pad : p * pad + seq] = sg_ref[p]
    product = dot(x_s[...], wo_ref[...], 1, 1).astype(BF16)
    for p in range(group):
        out_ref[p] = product[p * pad : p * pad + seq]


def context_grad(sg, out_weight, group):
    count, seq, width = sg.shape
    block = pl.BlockSpec((group, seq, width), lambda s: (s, 0, 0))
    return pl.pallas_call(
        context_kernel,
        grid=(count // group,),
        in_specs=[block, pl.BlockSpec(out_weight.shape, lambda s: (0, 0))],
        out_specs=block,
        out_shape=jax.ShapeDtypeStruct(sg.shape, BF16),
        scratch_shapes=[pltpu.VMEM((group * up(seq, 16), width), BF16)],
        compiler_params=params(),
        cost_estimate=cost(2 * count * seq * width * width, 4 * count * seq * width),
        name="context_grad",
    )(sg, out_weight)


def split_sum_kernel(inputs, outputs, index_ref, *rest):
    ins, outs, total_s = rest[:inputs], rest[inputs : inputs + outputs], rest[-1]
    total = ins[0][...].astype(F32)
    for ref in ins[1:]:
        total = total + ref[...].astype(F32)
    total_s[...] = total.astype(BF16).reshape(total_s.shape)
    for k in range(outputs):
        outs[k][...] = total_s[index_ref[k]].reshape(outs[k].shape)


def split_sum(arrays, index, name):
    outputs = index.shape[0]
    shape = arrays[0].shape
    lead = shape[0] // outputs
    out = shape[1:] if lead == 1 else (lead,) + shape[1:]
    return pl.pallas_call(
        functools.partial(split_sum_kernel, len(arrays), outputs),
        in_specs=[SMEM] + [VMEM] * len(arrays),
        out_specs=[VMEM] * outputs,
        out_shape=[jax.ShapeDtypeStruct(out, BF16)] * outputs,
        scratch_shapes=[pltpu.VMEM((outputs, lead) + shape[1:], BF16)],
        compiler_params=params(),
        name=name,
    )(index, *arrays)


def sum_kernel(*refs):
    total = refs[0][...].astype(F32)
    for ref in refs[1:-1]:
        total = total + ref[...].astype(F32)
    refs[-1][...] = total.astype(BF16)


def plain_sum(arrays, name):
    return pl.pallas_call(
        sum_kernel,
        in_specs=[VMEM] * len(arrays),
        out_specs=VMEM,
        out_shape=jax.ShapeDtypeStruct(arrays[0].shape, BF16),
        compiler_params=params(),
        name=name,
    )(*arrays)


def unpack_kernel(parts, width, emb, index_ref, *rest):
    ins = rest[:parts]
    wo_ref, proj_ref, small_ref = rest[parts:]
    per = ins[0].shape[0]
    for a in range(parts):
        for k in range(per):
            c = index_ref[a * per + k]
            value = ins[a][k].astype(F32)
            wo_ref[c] = value[:, :width]
            proj_ref[c] = value[:, width : width + emb]
            small_ref[c] = value[:, width + emb :]


def unpack(arrays, index, width, emb):
    parts = len(arrays)
    per, chunk, _ = arrays[0].shape
    chunks = parts * per
    return pl.pallas_call(
        functools.partial(unpack_kernel, parts, width, emb),
        in_specs=[SMEM] + [VMEM] * parts,
        out_specs=[VMEM] * 3,
        out_shape=[jax.ShapeDtypeStruct((chunks, chunk, n), F32) for n in (width, emb, 128)],
        compiler_params=params(),
        name="unpack",
    )(index, *arrays)


def local(
    context,
    stream,
    out_weight,
    gain,
    bias,
    proj_weight,
    query_states,
    passage_len,
    passage_dest,
    teacher_states,
    teacher_query,
    teacher_key,
):
    dp = lax.axis_size("dp")
    nt = lax.axis_size("tensor")
    chips = dp // CORES
    me = lax.axis_index("dp")
    chip, core = me // CORES, me % CORES
    mt = lax.axis_index("tensor")
    count, seq, width = context.shape
    emb = proj_weight.shape[1]
    group_queries, tokens, _ = query_states.shape
    depth, heads = teacher_query.shape
    per = count // dp
    per_query = count * nt // group_queries
    group = 4 if count % 4 == 0 else 1

    def shift_dp(x, k):
        return lax.ppermute(x, "dp", [(d, (d + k) % dp) for d in range(dp)])

    def shift_chip(x, k):
        return lax.ppermute(
            x, "dp", [(c * CORES + o, (c + k) % chips * CORES + o) for c in range(chips) for o in range(CORES)]
        )

    def swap_core(x):
        return lax.ppermute(x, "dp", [(d, d ^ 1) for d in range(dp)])

    def shift_t(x, k):
        return lax.ppermute(x, "tensor", [(t, (t + k) % nt) for t in range(nt)])

    part = depth // dp
    mine = jnp.stack(
        [lax.dynamic_slice_in_dim(w, me * part, part, 0) for w in (teacher_query, teacher_key)]
    )
    along = jnp.concatenate([shift_t(mine, k) for k in range(1, nt)], axis=0)
    plane = [along] + [shift_chip(along, k) for k in range(1, chips)]
    pieces = plane + [swap_core(x) for x in plane]
    shifts = jnp.arange(chips, dtype=jnp.int32)
    behind = (chip - shifts) % chips
    piece_rows = jnp.concatenate([behind * CORES + core, behind * CORES + 1 - core]).astype(jnp.int32)

    dest_group = passage_dest // (count * nt)
    rows = jnp.arange(count, dtype=jnp.int32)
    rank = jnp.sum(
        (dest_group[:, None] == dest_group[None, :]) & (rows[None, :] < rows[:, None]), axis=1, dtype=jnp.int32
    )
    place = dest_group * per + rank
    positions = jnp.sum(
        jnp.where(place[:, None] == rows[None, :], (passage_dest % count)[:, None], 0), axis=0
    )
    queries = query_states.reshape(group_queries * tokens, width)
    extra = jnp.pad(positions.astype(BF16)[None, :], ((0, 15), (0, width - count)))
    payload = jnp.concatenate([queries, extra], axis=0)
    payloads = [payload] + [shift_dp(payload, k) for k in range(1, dp)]
    told = jnp.stack([payloads[(dp - k) % dp][group_queries * tokens, :count] for k in range(dp)])
    order = lax.dynamic_slice_in_dim(told.astype(jnp.int32), me * per, per, 1).reshape(-1)
    from_shift = (me - dest_group) % dp
    midx = (from_shift * per + rank).astype(jnp.int32)
    qidx = (from_shift * group_queries + passage_dest // per_query - dest_group * group_queries).astype(jnp.int32)

    gain2, bias2 = gain.reshape(1, width), bias.reshape(1, width)
    normed, embeds, inverse = student_forward(context, stream, out_weight, gain2, bias2, proj_weight, group)
    maps = teacher_maps(order, piece_rows, teacher_states, teacher_query, teacher_key, pieces, dp, tokens)
    maps = [maps[0]] + [shift_dp(maps[k], k) for k in range(1, dp)]
    chunk = width // (CORES * chips * nt)
    sg, send, keep = student_backward(
        qidx, midx, passage_len, core.astype(jnp.int32).reshape(1), maps, payloads,
        context, normed, embeds, inverse, gain2, bias2, proj_weight, proj_weight.T,
        group, tokens, group_queries, chunk,
    )
    grad_context = context_grad(sg, out_weight, group)

    ahead = ((chip + shifts) % chips).astype(jnp.int32)
    t_shifts = jnp.arange(nt, dtype=jnp.int32)
    t_ahead = ((mt + t_shifts) % nt).astype(jnp.int32)
    parts = split_sum([keep, swap_core(send)], ahead, "sum_cores")
    parts = [parts[0]] + [shift_chip(parts[k], k) for k in range(1, chips)]
    parts = split_sum(parts, t_ahead, "sum_plane")
    parts = [parts[0]] + [shift_t(parts[k], k) for k in range(1, nt)]
    total = plain_sum(parts, "sum_tensor")
    line = jnp.stack([total] + [shift_t(total, k) for k in range(1, nt)])
    plane = [line] + [shift_chip(line, k) for k in range(1, chips)]
    arrays = plane + [swap_core(x) for x in plane]
    t_behind = (mt - t_shifts) % nt
    base = jnp.concatenate([core * chips + behind, (1 - core) * chips + behind]) * nt
    index = (base[:, None] + t_behind[None, :]).reshape(-1).astype(jnp.int32)
    grad_out, grad_proj, small = unpack(arrays, index, width, emb)
    small = small.reshape(width, 128)
    loss = jnp.sum(small[0, tokens : 2 * tokens]) / (count * dp * nt * tokens)
    return (
        loss,
        grad_out.reshape(width, width),
        grad_proj.reshape(width, emb),
        small[:, 0],
        small[:, 1],
        grad_context,
    )


def solution(mesh):
    return jax.shard_map(
        local,
        mesh=mesh,
        in_specs=(
            P(("dp", "tensor"), None, None),
            P(("dp", "tensor"), None, None),
            P(),
            P(),
            P(),
            P(),
            P("dp", None, None),
            P(("dp", "tensor")),
            P(("dp", "tensor")),
            P(("dp", "tensor"), None, None),
            P(None, "tensor"),
            P(None, "tensor"),
        ),
        out_specs=(P(), P(), P(), P(), P(), P(("dp", "tensor"), None, None)),
        check_vma=False,
    )
```

```python
import functools
import math

import jax
import jax.numpy as jnp
from jax import lax
from jax.experimental import pallas as pl
from jax.experimental.pallas import tpu as pltpu
from jax.sharding import PartitionSpec as P

sharpness = 0.05
softcap = 10.0
epsilon = 1e-06
CORES = 2
VMEM_LIMIT = 56 * 1024 * 1024

F32 = jnp.float32
BF16 = jnp.bfloat16
VMEM = pl.BlockSpec(memory_space=pltpu.VMEM)
SMEM = pl.BlockSpec(memory_space=pltpu.SMEM)
ANY = pl.BlockSpec(memory_space=pl.ANY)


def up(n, m):
    return -(-n // m) * m


def dot(a, b, ca, cb):
    return lax.dot_general(a, b, (((ca,), (cb,)), ((), ())), preferred_element_type=F32)


def split_rows(rows, most):
    return max(n for n in range(16, most + 1, 16) if rows % n == 0)


def params(**kw):
    return pltpu.CompilerParams(vmem_limit_bytes=VMEM_LIMIT, **kw)


def cost(flops, nbytes):
    return pl.CostEstimate(flops=int(flops), bytes_accessed=int(nbytes), transcendentals=0)


def forward_kernel(x_ref, str_ref, wo_ref, gain_ref, bias_ref, wp_ref, after_ref, normed_ref, emb_ref, inv_ref, prod_s, hid_s):
    rows, width = x_ref.shape
    sub = split_rows(rows, 256)
    gain, bias = gain_ref[...], bias_ref[...]
    for b in range(0, rows, sub):
        prod_s[b : b + sub] = dot(x_ref[b : b + sub], wo_ref[...], 1, 0)
        for c in range(b, b + sub, 16):
            summed = prod_s[c : c + 16] + str_ref[c : c + 16].astype(F32)
            centred = summed - jnp.mean(summed, axis=-1, keepdims=True)
            inverse = lax.rsqrt(jnp.mean(centred * centred, axis=-1, keepdims=True) + epsilon)
            normed = centred * inverse
            normed_ref[c : c + 16] = normed.astype(BF16)
            inv_ref[c : c + 16] = jnp.broadcast_to(inverse, (16, inv_ref.shape[1]))
            hid_s[c : c + 16] = (normed * gain + bias).astype(BF16)
        emb_ref[b : b + sub] = dot(hid_s[b : b + sub], wp_ref[...], 1, 0)


def student_forward(x, stream, out_weight, gain, bias, proj_weight, after):
    total, width = x.shape
    emb = proj_weight.shape[1]
    rows = split_rows(total, 720)
    block = lambda last: pl.BlockSpec((rows, last), lambda s: (s, 0))
    whole = lambda a: pl.BlockSpec(a.shape, lambda s: (0,) * a.ndim)
    return pl.pallas_call(
        forward_kernel,
        grid=(total // rows,),
        in_specs=[block(width), block(width)] + [whole(a) for a in (out_weight, gain, bias, proj_weight)] + [ANY],
        out_specs=[block(width), block(emb), block(128)],
        out_shape=[
            jax.ShapeDtypeStruct((total, width), BF16),
            jax.ShapeDtypeStruct((total, emb), F32),
            jax.ShapeDtypeStruct((total, 128), F32),
        ],
        scratch_shapes=[pltpu.VMEM((rows, width), F32), pltpu.VMEM((rows, width), BF16)],
        compiler_params=params(),
        cost_estimate=cost(2 * total * width * (width + emb), 8 * total * width),
        name="student_forward",
    )(x, stream, out_weight, gain, bias, proj_weight, after)


def teacher_kernel(parts, count, tokens, order_ref, rows_ref, states_ref, wq_ref, wk_ref, after_ref, *rest):
    pieces, out_ref = rest[:parts], rest[parts]
    w_s, own_s, q_s, g_s, key_s, e_s, map_s, q_sem, key_sem, w_sem, own_sem = rest[parts + 1 :]
    depth = q_s.shape[1]
    slices = w_s.shape[0] // 2
    part_rows = pieces[0].shape[1]
    total = key_s.shape[0]
    seq = total // count
    blocks = key_sem.shape[0]
    rows = total // blocks
    first = count * tokens
    own = [
        pltpu.make_async_copy(wq_ref, own_s.at[0], own_sem.at[0]),
        pltpu.make_async_copy(wk_ref, own_s.at[1], own_sem.at[1]),
    ]
    queries = pltpu.make_async_copy(states_ref.at[pl.ds(0, first)], q_s, q_sem)
    gathered = [
        pltpu.make_async_copy(
            pieces[a],
            w_s.at[:, pl.ds(pl.multiple_of(rows_ref[a] * part_rows, part_rows), part_rows), :],
            w_sem.at[a],
        )
        for a in range(parts)
    ]
    keys = [
        pltpu.make_async_copy(
            states_ref.at[pl.ds(first + b * rows, rows)], key_s.at[pl.ds(b * rows, rows)], key_sem.at[b]
        )
        for b in range(blocks)
    ]
    queries.start()
    for copy in own + gathered + keys:
        copy.start()
    queries.wait()
    for copy in own:
        copy.wait()
    q = q_s[...]
    mixed = dot(dot(q, own_s[0], 1, 0).astype(BF16), own_s[1], 1, 1)
    for copy in gathered:
        copy.wait()
    for k in range(slices):
        mixed = mixed + dot(dot(q, w_s[2 * k], 1, 0).astype(BF16), w_s[2 * k + 1], 1, 1)
    for v in range(depth // 128):
        g_s[v] = mixed[:, v * 128 : (v + 1) * 128]
        for p in range(count):
            q_s[p * tokens : (p + 1) * tokens, v * 128 : (v + 1) * 128] = g_s[
                v, pl.ds(p, tokens, stride=count), :
            ].astype(BF16)
    mixed = q_s[...]
    scale = 1.0 / (math.sqrt(depth) * softcap)
    side = 128 // tokens
    pair = lax.broadcasted_iota(jnp.int32, (rows, 128), 0) % count
    for b in range(blocks):
        keys[b].wait()
        raw = dot(key_s[b * rows : (b + 1) * rows], mixed, 1, 1)
        mine = raw[:, :128]
        for v in range(1, count // side):
            mine = jnp.where(pair >= v * side, raw[:, v * 128 : (v + 1) * 128], mine)
        e_s[b * rows : (b + 1) * rows] = jnp.exp(softcap * jnp.tanh(mine * scale))
    lane = lax.broadcasted_iota(jnp.int32, (seq, 128), 1) // tokens
    filler = jnp.zeros((up(seq, 128) - seq, 128), F32)
    for g in range(count // side):
        both = e_s[pl.ds(g * side, seq, stride=count), :]
        for v in range(1, side):
            both = jnp.where(lane == v, e_s[pl.ds(g * side + v, seq, stride=count), :], both)
        turned = jnp.concatenate([both, filler], axis=0).T
        for v in range(side):
            map_s[g * side + v] = turned[v * tokens : (v + 1) * tokens, :seq].astype(BF16)
    for n in range(count):
        out_ref[n] = map_s[order_ref[n]]


def teacher_maps(order, rows, states, wq, wk, after, pieces, count, tokens):
    total, depth = states.shape
    keys = total - count * tokens
    heads = wq.shape[1]
    parts = len(pieces)
    slices = pieces[0].shape[0]
    blocks = keys // split_rows(keys, 720)
    return pl.pallas_call(
        functools.partial(teacher_kernel, parts, count, tokens),
        in_specs=[SMEM, SMEM] + [ANY] * (4 + parts),
        out_specs=VMEM,
        out_shape=jax.ShapeDtypeStruct((count, tokens, keys // count), BF16),
        scratch_shapes=[
            pltpu.VMEM((slices, depth, heads), BF16),
            pltpu.VMEM((2, depth, heads), BF16),
            pltpu.VMEM((count * tokens, depth), BF16),
            pltpu.VMEM((depth // 128, count * tokens, 128), F32),
            pltpu.VMEM((keys, depth), BF16),
            pltpu.VMEM((keys, 128), F32),
            pltpu.VMEM((count, tokens, keys // count), BF16),
            pltpu.SemaphoreType.DMA,
            pltpu.SemaphoreType.DMA((blocks,)),
            pltpu.SemaphoreType.DMA((parts,)),
            pltpu.SemaphoreType.DMA((2,)),
        ],
        compiler_params=params(),
        cost_estimate=cost(8 * count * tokens * depth * depth, 2 * states.size + 4 * depth * depth),
        name="teacher_maps",
    )(order, rows, states, wq, wk, after, *pieces)


def score_rows(tokens, count, per, group_queries, qidx_ref, midx_ref, len_ref, maps_ref, payload_ref, emb_ref, wp_ref,
               qs_s, qunit_s, qdir_s, qlen_s, qg_s, dir_s, un_s, up_s, eg_s, l_s):
    total, emb = emb_ref.shape
    seq = total // count
    sub = split_rows(total, 128)
    each = group_queries * tokens
    for k in range(payload_ref.shape[0]):
        qs_s[k * each : (k + 1) * each] = payload_ref[k, :each]
    qe = dot(qs_s[...], wp_ref[...], 1, 0)
    length = jnp.sqrt(jnp.sum(qe * qe, axis=-1, keepdims=True) + epsilon)
    qdir = qe / length
    qdir_s[...] = qdir
    qlen_s[...] = jnp.broadcast_to(length, qlen_s.shape)
    qunit_s[...] = qdir.astype(BF16).reshape(qunit_s.shape)
    qg_s[...] = jnp.zeros_like(qg_s)
    for b in range(0, total, sub):
        e = emb_ref[b : b + sub]
        dir_s[b : b + sub] = e / jnp.sqrt(jnp.sum(e * e, axis=-1, keepdims=True) + epsilon)
    spread = jnp.zeros((tokens, 1), F32)
    sums = []
    for r in range(count):
        units = dir_s[pl.ds(r, seq, stride=count), :].astype(BF16)
        q = qunit_s[qidx_ref[r]]
        logits = dot(q, units, 1, 1) / sharpness
        valid = lax.broadcasted_iota(jnp.int32, logits.shape, 1) < len_ref[r]
        student = jnp.where(valid, jnp.exp(logits), 0.0)
        student_total = jnp.sum(student, axis=-1, keepdims=True)
        teacher = maps_ref[midx_ref[r]].astype(F32)
        teacher_log = jnp.log(teacher)
        teacher = jnp.where(valid, teacher, 0.0)
        teacher_total = jnp.sum(teacher, axis=-1, keepdims=True)
        student_prob = student / student_total
        teacher_prob = teacher / teacher_total
        gap = (teacher_log - jnp.log(teacher_total)) - (logits - jnp.log(student_total))
        spread += jnp.sum(jnp.where(valid, teacher_prob * gap, 0.0), axis=-1, keepdims=True)
        slope = ((student_prob - teacher_prob) / (tokens * sharpness)).astype(BF16)
        up_s[pl.ds(r, seq, stride=count), :] = dot(slope, q, 0, 0).astype(BF16).astype(F32)
        un_s[r] = dot(slope, units, 1, 0)
    for r in range(count):
        qg_s[qidx_ref[r]] += un_s[r]
    l_s[...] = jnp.broadcast_to(spread, l_s.shape)
    for b in range(0, total, sub):
        e = emb_ref[b : b + sub]
        upstream = up_s[b : b + sub]
        length = jnp.sqrt(jnp.sum(e * e, axis=-1, keepdims=True) + epsilon)
        direction = dir_s[b : b + sub]
        eg = (upstream - direction * jnp.sum(direction * upstream, axis=-1, keepdims=True)) / length
        eg_s[b : b + sub] = eg.astype(BF16)


def backward_kernel(
    tokens, count, per, group_queries,
    qidx_ref, midx_ref, len_ref, core_ref,
    maps_ref, payload_ref, emb_ref, x_ref, normed_ref, inv_ref, gain_ref, bias_ref, wp_ref, wpt_ref,
    sg_ref, send_ref, keep_ref,
    qs_s, qunit_s, qdir_s, qlen_s, qg_s, dir_s, un_s, up_s, eg_s, l_s,
    hg_s, wo_s, nt_s, s_s, right_s,
):
    step = pl.program_id(0)
    rows, width = x_ref.shape
    sub = split_rows(rows, 256)
    gain = gain_ref[...]

    @pl.when(step == 0)
    def _():
        score_rows(tokens, count, per, group_queries, qidx_ref, midx_ref, len_ref, maps_ref, payload_ref, emb_ref,
                   wp_ref, qs_s, qunit_s, qdir_s, qlen_s, qg_s, dir_s, un_s, up_s, eg_s, l_s)
        wo_s[...] = jnp.zeros_like(wo_s)
        nt_s[...] = jnp.zeros_like(nt_s)
        s_s[...] = jnp.zeros_like(s_s)

    base = pl.multiple_of(step * rows, 16)
    for b in range(0, rows, sub):
        hg_s[b : b + sub] = dot(eg_s[pl.ds(base + b, sub)], wp_ref[...], 1, 1)
        for c in range(b, b + sub, 16):
            scaled = hg_s[c : c + 16] * gain
            normed = normed_ref[c : c + 16].astype(F32)
            mean = jnp.mean(scaled, axis=-1, keepdims=True)
            along = jnp.mean(scaled * normed, axis=-1, keepdims=True)
            sg_ref[c : c + 16] = (inv_ref[c : c + 16, :1] * (scaled - mean - normed * along)).astype(BF16)
    eg = eg_s[pl.ds(base, rows)]
    wo_s[...] += dot(x_ref[...], sg_ref[...], 0, 0)
    nt_s[...] += dot(eg, normed_ref[...], 0, 0)
    s_s[...] += dot(eg, jnp.ones((rows, 128), BF16), 0, 0)

    @pl.when(step == pl.num_programs(0) - 1)
    def _():
        qg = qg_s[...].reshape(qdir_s.shape)
        qdir = qdir_s[...]
        qeg = (qg - qdir * jnp.sum(qdir * qg, axis=-1, keepdims=True)) / qlen_s[:, :1]
        high = qeg.astype(BF16)
        low = (qeg - high.astype(F32)).astype(BF16)
        qs = qs_s[...]
        proj_query = dot(high, qs, 0, 0) + dot(low, qs, 0, 0)
        nt = nt_s[...]
        s = s_s[:, :1]
        wpt = wpt_ref[...].astype(F32)
        proj = nt * gain + s * bias_ref[...] + proj_query
        gain_row = jnp.sum(wpt * nt, axis=0, keepdims=True)
        bias_row = jnp.sum(wpt * s, axis=0, keepdims=True)
        index = lax.broadcasted_iota(jnp.int32, (tokens, width), 0)
        top = jnp.where(index == 0, gain_row, jnp.where(index == 1, bias_row, 0.0))
        spread = jnp.broadcast_to(l_s[:, :1], (tokens, width))
        rest_rows = jnp.zeros((128 - 2 * tokens, width), F32)
        right_s[...] = jnp.concatenate([proj, top, spread, rest_rows], axis=0).T
        half = width // CORES
        chunk = send_ref.shape[1]
        for ref, which in ((send_ref, 1 - core_ref[0]), (keep_ref, core_ref[0])):
            start = pl.multiple_of(which * half, half)
            left = wo_s[pl.ds(start, half)].astype(BF16)
            right = right_s[pl.ds(start, half)].astype(BF16)
            for c in range(half // chunk):
                ref[c, :, :width] = left[c * chunk : (c + 1) * chunk]
                ref[c, :, width:] = right[c * chunk : (c + 1) * chunk]


def student_backward(
    qidx, midx, lens, core, maps, payload, embeds, x, normed, inverse, gain, bias, wp, wpt,
    count, tokens, group_queries, chunk,
):
    total, width = x.shape
    emb = wp.shape[1]
    rows = split_rows(total, 720)
    dests = payload.shape[0]
    per = count // dests
    chunks = width // CORES // chunk
    block = lambda last: pl.BlockSpec((rows, last), lambda s, *_: (s, 0))
    whole = lambda a: pl.BlockSpec(a.shape, lambda s, *_: (0,) * a.ndim)
    full = pl.BlockSpec((chunks, chunk, width + emb + 128), lambda s, *_: (0, 0, 0))
    queries = dests * group_queries
    return pl.pallas_call(
        functools.partial(backward_kernel, tokens, count, per, group_queries),
        grid_spec=pltpu.PrefetchScalarGridSpec(
            num_scalar_prefetch=4,
            grid=(total // rows,),
            in_specs=[whole(maps), whole(payload), whole(embeds), block(width), block(width), block(128)]
            + [whole(a) for a in (gain, bias, wp, wpt)],
            out_specs=[block(width), full, full],
            scratch_shapes=[
                pltpu.VMEM((queries * tokens, width), BF16),
                pltpu.VMEM((queries, tokens, emb), BF16),
                pltpu.VMEM((queries * tokens, emb), F32),
                pltpu.VMEM((queries * tokens, 128), F32),
                pltpu.VMEM((queries, tokens, emb), F32),
                pltpu.VMEM((total, emb), F32),
                pltpu.VMEM((count, tokens, emb), F32),
                pltpu.VMEM((total, emb), F32),
                pltpu.VMEM((total, emb), BF16),
                pltpu.VMEM((tokens, 128), F32),
                pltpu.VMEM((rows, width), F32),
                pltpu.VMEM((width, width), F32),
                pltpu.VMEM((emb, width), F32),
                pltpu.VMEM((emb, 128), F32),
                pltpu.VMEM((width, emb + 128), F32),
            ],
        ),
        out_shape=[
            jax.ShapeDtypeStruct((total, width), BF16),
            jax.ShapeDtypeStruct((chunks, chunk, width + emb + 128), BF16),
            jax.ShapeDtypeStruct((chunks, chunk, width + emb + 128), BF16),
        ],
        compiler_params=params(),
        cost_estimate=cost(2 * total * width * (width + 2 * emb), 8 * total * width),
        name="student_backward",
    )(qidx, midx, lens, core, maps, payload, embeds, x, normed, inverse, gain, bias, wp, wpt)


def context_kernel(sg_ref, wo_ref, after_ref, out_ref):
    out_ref[...] = dot(sg_ref[...], wo_ref[...], 1, 1).astype(BF16)


def context_grad(sg, out_weight, after):
    total, width = sg.shape
    rows = split_rows(total, 720)
    block = pl.BlockSpec((rows, width), lambda s: (s, 0))
    return pl.pallas_call(
        context_kernel,
        grid=(total // rows,),
        in_specs=[block, pl.BlockSpec(out_weight.shape, lambda s: (0, 0)), ANY],
        out_specs=block,
        out_shape=jax.ShapeDtypeStruct(sg.shape, BF16),
        compiler_params=params(),
        cost_estimate=cost(2 * total * width * width, 4 * total * width),
        name="context_grad",
    )(sg, out_weight, after)


def split_sum_kernel(inputs, outputs, after, index_ref, *rest):
    ins, outs, total_s = rest[:inputs], rest[inputs + after : inputs + after + outputs], rest[-1]
    total = ins[0][...].astype(F32)
    for ref in ins[1:]:
        total = total + ref[...].astype(F32)
    total_s[...] = total.astype(BF16).reshape(total_s.shape)
    for k in range(outputs):
        outs[k][...] = total_s[index_ref[k]].reshape(outs[k].shape)


def split_sum(arrays, index, name, after=()):
    outputs = index.shape[0]
    shape = arrays[0].shape
    lead = shape[0] // outputs
    out = shape[1:] if lead == 1 else (lead,) + shape[1:]
    return pl.pallas_call(
        functools.partial(split_sum_kernel, len(arrays), outputs, len(after)),
        in_specs=[SMEM] + [VMEM] * len(arrays) + [ANY] * len(after),
        out_specs=[VMEM] * outputs,
        out_shape=[jax.ShapeDtypeStruct(out, BF16)] * outputs,
        scratch_shapes=[pltpu.VMEM((outputs, lead) + shape[1:], BF16)],
        compiler_params=params(),
        name=name,
    )(index, *arrays, *after)


def sum_kernel(*refs):
    total = refs[0][...].astype(F32)
    for ref in refs[1:-1]:
        total = total + ref[...].astype(F32)
    refs[-1][...] = total.astype(BF16)


def plain_sum(arrays, name):
    return pl.pallas_call(
        sum_kernel,
        in_specs=[VMEM] * len(arrays),
        out_specs=VMEM,
        out_shape=jax.ShapeDtypeStruct(arrays[0].shape, BF16),
        compiler_params=params(),
        name=name,
    )(*arrays)


def unpack_kernel(parts, width, emb, tokens, scale, index_ref, *rest):
    ins = rest[:parts]
    wo_ref, proj_ref, gain_ref, bias_ref, loss_ref, small_s = rest[parts:]
    per = ins[0].shape[0]
    for a in range(parts):
        for k in range(per):
            c = index_ref[a * per + k]
            value = ins[a][k].astype(F32)
            wo_ref[c] = value[:, :width]
            proj_ref[c] = value[:, width : width + emb]
            small_s[c] = value[:, width + emb :]
    turned = small_s[...].reshape(width, 128).T
    gain_ref[...] = turned[0:1]
    bias_ref[...] = turned[1:2]
    loss_ref[0] = jnp.sum(turned[tokens : 2 * tokens, 0:1]) * scale


def unpack(arrays, index, width, emb, tokens, scale):
    parts = len(arrays)
    per, chunk, _ = arrays[0].shape
    chunks = parts * per
    return pl.pallas_call(
        functools.partial(unpack_kernel, parts, width, emb, tokens, scale),
        in_specs=[SMEM] + [VMEM] * parts,
        out_specs=[VMEM] * 4 + [SMEM],
        out_shape=[jax.ShapeDtypeStruct((chunks, chunk, n), F32) for n in (width, emb)]
        + [jax.ShapeDtypeStruct((1, width), F32)] * 2
        + [jax.ShapeDtypeStruct((1,), F32)],
        scratch_shapes=[pltpu.VMEM((chunks, chunk, 128), F32)],
        compiler_params=params(),
        name="unpack",
    )(index, *arrays)


def local(
    context,
    stream,
    out_weight,
    gain,
    bias,
    proj_weight,
    query_states,
    passage_len,
    passage_dest,
    teacher_states,
    teacher_query,
    teacher_key,
):
    dp = lax.axis_size("dp")
    nt = lax.axis_size("tensor")
    chips = dp // CORES
    me = lax.axis_index("dp")
    chip, core = me // CORES, me % CORES
    mt = lax.axis_index("tensor")
    count, seq, width = context.shape
    emb = proj_weight.shape[1]
    group_queries, tokens, _ = query_states.shape
    depth, heads = teacher_query.shape
    per = count // dp
    per_query = count * nt // group_queries

    def flat(a):
        return a.transpose(1, 0, 2).reshape(-1, a.shape[2])

    def shift_chip(x, k):
        return lax.ppermute(
            x, "dp", [(c * CORES + o, (c + k) % chips * CORES + o) for c in range(chips) for o in range(CORES)]
        )

    def swap_core(x):
        return lax.ppermute(x, "dp", [(d, d ^ 1) for d in range(dp)])

    def shift_t(x, k):
        return lax.ppermute(x, "tensor", [(t, (t + k) % nt) for t in range(nt)])

    part = depth // dp
    mine = jnp.stack(
        [lax.dynamic_slice_in_dim(w, me * part, part, 0) for w in (teacher_query, teacher_key)]
    )
    along = jnp.concatenate([shift_t(mine, k) for k in range(1, nt)], axis=0)
    plane = [along] + [shift_chip(along, k) for k in range(1, chips)]
    pieces = plane + [swap_core(x) for x in plane]
    shifts = jnp.arange(chips, dtype=jnp.int32)
    behind = (chip - shifts) % chips
    piece_rows = jnp.concatenate([behind * CORES + core, behind * CORES + 1 - core]).astype(jnp.int32)

    dest_group = passage_dest // (count * nt)
    rows = jnp.arange(count, dtype=jnp.int32)
    rank = jnp.sum(
        (dest_group[:, None] == dest_group[None, :]) & (rows[None, :] < rows[:, None]), axis=1, dtype=jnp.int32
    )
    place = dest_group * per + rank
    positions = jnp.sum(
        jnp.where(place[:, None] == rows[None, :], (passage_dest % count)[:, None], 0), axis=0
    )
    queries = query_states.reshape(group_queries * tokens, width)
    extra = jnp.pad(positions.astype(BF16)[None, :], ((0, 15), (0, width - count)))
    payload = jnp.concatenate([queries, extra], axis=0)
    payload = lax.all_to_all(
        jnp.broadcast_to(payload[None], (dp,) + payload.shape), "dp", split_axis=0, concat_axis=0, tiled=True
    )
    told = payload[:, group_queries * tokens, :count].astype(jnp.int32)
    order = lax.dynamic_slice_in_dim(told, me * per, per, 1).reshape(-1)
    midx = place.astype(jnp.int32)
    qidx = (passage_dest // per_query).astype(jnp.int32)

    gain2, bias2 = gain.reshape(1, width), bias.reshape(1, width)
    x = flat(context)
    normed, embeds, inverse = student_forward(x, flat(stream), out_weight, gain2, bias2, proj_weight, along)
    maps = teacher_maps(
        order, piece_rows, flat(teacher_states), teacher_query, teacher_key, inverse, pieces, count, tokens
    )
    maps = lax.all_to_all(maps, "dp", split_axis=0, concat_axis=0, tiled=True)
    chunk = width // (CORES * chips * nt)
    sg, send, keep = student_backward(
        qidx, midx, passage_len, core.astype(jnp.int32).reshape(1), maps, payload,
        embeds, x, normed, inverse, gain2, bias2, proj_weight, proj_weight.T,
        count, tokens, group_queries, chunk,
    )

    ahead = ((chip + shifts) % chips).astype(jnp.int32)
    t_shifts = jnp.arange(nt, dtype=jnp.int32)
    t_ahead = ((mt + t_shifts) % nt).astype(jnp.int32)
    parts = split_sum([keep, swap_core(send)], ahead, "sum_cores")
    grad_context = context_grad(sg, out_weight, parts[0])
    parts = [parts[0]] + [shift_chip(parts[k], k) for k in range(1, chips)]
    parts = split_sum(parts, t_ahead, "sum_plane", (grad_context,))
    parts = [parts[0]] + [shift_t(parts[k], k) for k in range(1, nt)]
    total = plain_sum(parts, "sum_tensor")
    line = jnp.stack([total] + [shift_t(total, k) for k in range(1, nt)])
    plane = [line] + [shift_chip(line, k) for k in range(1, chips)]
    arrays = plane + [swap_core(x) for x in plane]
    t_behind = (mt - t_shifts) % nt
    base = jnp.concatenate([core * chips + behind, (1 - core) * chips + behind]) * nt
    index = (base[:, None] + t_behind[None, :]).reshape(-1).astype(jnp.int32)
    grad_out, grad_proj, grad_gain, grad_bias, loss = unpack(
        arrays, index, width, emb, tokens, 1.0 / (count * dp * nt * tokens)
    )
    return (
        loss.reshape(()),
        grad_out.reshape(width, width),
        grad_proj.reshape(width, emb),
        grad_gain.reshape(width),
        grad_bias.reshape(width),
        grad_context.reshape(seq, count, width).transpose(1, 0, 2),
    )


def solution(mesh):
    return jax.shard_map(
        local,
        mesh=mesh,
        in_specs=(
            P(("dp", "tensor"), None, None),
            P(("dp", "tensor"), None, None),
            P(),
            P(),
            P(),
            P(),
            P("dp", None, None),
            P(("dp", "tensor")),
            P(("dp", "tensor")),
            P(("dp", "tensor"), None, None),
            P(None, "tensor"),
            P(None, "tensor"),
        ),
        out_specs=(P(), P(), P(), P(), P(), P(("dp", "tensor"), None, None)),
        check_vma=False,
    )
```

```python
import functools
import math

import jax
import jax.numpy as jnp
from jax import lax
from jax.experimental import pallas as pl
from jax.experimental.pallas import tpu as pltpu
from jax.sharding import PartitionSpec as P

sharpness = 0.05
softcap = 10.0
epsilon = 1e-06
CORES = 2
VMEM_LIMIT = 56 * 1024 * 1024
SMALL_LIMIT = 14 * 1024 * 1024

F32 = jnp.float32
BF16 = jnp.bfloat16
VMEM = pl.BlockSpec(memory_space=pltpu.VMEM)
SMEM = pl.BlockSpec(memory_space=pltpu.SMEM)
ANY = pl.BlockSpec(memory_space=pl.ANY)
TOKEN = jax.ShapeDtypeStruct((8, 128), F32)


def up(n, m):
    return -(-n // m) * m


def dot(a, b, ca, cb):
    return lax.dot_general(a, b, (((ca,), (cb,)), ((), ())), preferred_element_type=F32)


def split_rows(rows, most):
    return max(n for n in range(16, most + 1, 16) if rows % n == 0)


def params(**kw):
    return pltpu.CompilerParams(vmem_limit_bytes=VMEM_LIMIT, **kw)


def cost(flops, nbytes):
    return pl.CostEstimate(flops=int(flops), bytes_accessed=int(nbytes), transcendentals=0)


def forward_kernel(x_ref, str_ref, wo_ref, gain_ref, bias_ref, wp_ref, normed_ref, emb_ref, inv_ref, prod_s, hid_s):
    rows, width = x_ref.shape
    sub = split_rows(rows, 256)
    gain, bias = gain_ref[...], bias_ref[...]
    for b in range(0, rows, sub):
        prod_s[b : b + sub] = dot(x_ref[b : b + sub], wo_ref[...], 1, 0)
        for c in range(b, b + sub, 16):
            summed = prod_s[c : c + 16] + str_ref[c : c + 16].astype(F32)
            centred = summed - jnp.mean(summed, axis=-1, keepdims=True)
            inverse = lax.rsqrt(jnp.mean(centred * centred, axis=-1, keepdims=True) + epsilon)
            normed = centred * inverse
            normed_ref[c : c + 16] = normed.astype(BF16)
            inv_ref[c : c + 16] = jnp.broadcast_to(inverse, (16, inv_ref.shape[1]))
            hid_s[c : c + 16] = (normed * gain + bias).astype(BF16)
        emb_ref[b : b + sub] = dot(hid_s[b : b + sub], wp_ref[...], 1, 0)


def student_forward(x, stream, out_weight, gain, bias, proj_weight):
    total, width = x.shape
    emb = proj_weight.shape[1]
    rows = split_rows(total, 720)
    block = lambda last: pl.BlockSpec((rows, last), lambda s: (s, 0))
    whole = lambda a: pl.BlockSpec(a.shape, lambda s: (0,) * a.ndim)
    return pl.pallas_call(
        forward_kernel,
        grid=(total // rows,),
        in_specs=[block(width), block(width)] + [whole(a) for a in (out_weight, gain, bias, proj_weight)],
        out_specs=[block(width), block(emb), block(128)],
        out_shape=[
            jax.ShapeDtypeStruct((total, width), BF16),
            jax.ShapeDtypeStruct((total, emb), F32),
            jax.ShapeDtypeStruct((total, 128), F32),
        ],
        scratch_shapes=[pltpu.VMEM((rows, width), F32), pltpu.VMEM((rows, width), BF16)],
        compiler_params=params(),
        cost_estimate=cost(2 * total * width * (width + emb), 8 * total * width),
        name="student_forward",
    )(x, stream, out_weight, gain, bias, proj_weight)


def teacher_kernel(parts, count, tokens, order_ref, rows_ref, states_ref, wq_ref, wk_ref, *rest):
    pieces, out_ref, token_ref = rest[:parts], rest[parts], rest[parts + 1]
    w_s, own_s, q_s, g_s, key_s, e_s, map_s, q_sem, key_sem, w_sem, own_sem = rest[parts + 2 :]
    depth = q_s.shape[1]
    slices = w_s.shape[1]
    part_rows = pieces[0].shape[2]
    total = key_s.shape[0]
    seq = total // count
    blocks = key_sem.shape[0]
    rows = total // blocks
    first = count * tokens
    own = [
        pltpu.make_async_copy(wq_ref, own_s.at[0], own_sem.at[0]),
        pltpu.make_async_copy(wk_ref, own_s.at[1], own_sem.at[1]),
    ]
    queries = pltpu.make_async_copy(states_ref.at[pl.ds(0, first)], q_s, q_sem)
    gathered = []
    chips = pieces[0].shape[0]
    for a in range(parts):
        for c in range(chips):
            start = pl.multiple_of(rows_ref[a // 2 * chips + c] * part_rows, part_rows)
            gathered.append(
                pltpu.make_async_copy(
                    pieces[a].at[c], w_s.at[a % 2, :, pl.ds(start, part_rows), :], w_sem.at[a * chips + c]
                )
            )
    keys = [
        pltpu.make_async_copy(
            states_ref.at[pl.ds(first + b * rows, rows)], key_s.at[pl.ds(b * rows, rows)], key_sem.at[b]
        )
        for b in range(blocks)
    ]
    queries.start()
    for copy in own + gathered + keys:
        copy.start()
    queries.wait()
    for copy in own:
        copy.wait()
    q = q_s[...]
    mixed = dot(dot(q, own_s[0], 1, 0).astype(BF16), own_s[1], 1, 1)
    for copy in gathered:
        copy.wait()
    for k in range(slices):
        mixed = mixed + dot(dot(q, w_s[0, k], 1, 0).astype(BF16), w_s[1, k], 1, 1)
    for v in range(depth // 128):
        g_s[v] = mixed[:, v * 128 : (v + 1) * 128]
        for p in range(count):
            q_s[p * tokens : (p + 1) * tokens, v * 128 : (v + 1) * 128] = g_s[
                v, pl.ds(p, tokens, stride=count), :
            ].astype(BF16)
    mixed = q_s[...]
    scale = 1.0 / (math.sqrt(depth) * softcap)
    side = 128 // tokens
    pair = lax.broadcasted_iota(jnp.int32, (rows, 128), 0) % count
    for b in range(blocks):
        keys[b].wait()
        raw = dot(key_s[b * rows : (b + 1) * rows], mixed, 1, 1)
        mine = raw[:, :128]
        for v in range(1, count // side):
            mine = jnp.where(pair >= v * side, raw[:, v * 128 : (v + 1) * 128], mine)
        e_s[b * rows : (b + 1) * rows] = jnp.exp(softcap * jnp.tanh(mine * scale))
    lane = lax.broadcasted_iota(jnp.int32, (seq, 128), 1) // tokens
    filler = jnp.zeros((up(seq, 128) - seq, 128), F32)
    for g in range(count // side):
        both = e_s[pl.ds(g * side, seq, stride=count), :]
        for v in range(1, side):
            both = jnp.where(lane == v, e_s[pl.ds(g * side + v, seq, stride=count), :], both)
        turned = jnp.concatenate([both, filler], axis=0).T
        for v in range(side):
            map_s[g * side + v] = turned[v * tokens : (v + 1) * tokens, :seq].astype(BF16)
    for n in range(count):
        out_ref[n] = map_s[order_ref[n]]
    token_ref[...] = jnp.zeros_like(token_ref)


def teacher_maps(order, rows, states, wq, wk, pieces, count, tokens):
    total, depth = states.shape
    keys = total - count * tokens
    heads = wq.shape[1]
    parts = len(pieces)
    chips, slices = pieces[0].shape[:2]
    blocks = keys // split_rows(keys, 720)
    return pl.pallas_call(
        functools.partial(teacher_kernel, parts, count, tokens),
        in_specs=[SMEM, SMEM] + [ANY] * (3 + parts),
        out_specs=[VMEM, VMEM],
        out_shape=[jax.ShapeDtypeStruct((count, tokens, keys // count), BF16), TOKEN],
        scratch_shapes=[
            pltpu.VMEM((2, slices, depth, heads), BF16),
            pltpu.VMEM((2, depth, heads), BF16),
            pltpu.VMEM((count * tokens, depth), BF16),
            pltpu.VMEM((depth // 128, count * tokens, 128), F32),
            pltpu.VMEM((keys, depth), BF16),
            pltpu.VMEM((keys, 128), F32),
            pltpu.VMEM((count, tokens, keys // count), BF16),
            pltpu.SemaphoreType.DMA,
            pltpu.SemaphoreType.DMA((blocks,)),
            pltpu.SemaphoreType.DMA((parts * chips,)),
            pltpu.SemaphoreType.DMA((2,)),
        ],
        compiler_params=params(),
        cost_estimate=cost(8 * count * tokens * depth * depth, 2 * states.size + 4 * depth * depth),
        name="teacher_maps",
    )(order, rows, states, wq, wk, *pieces)


def scores_kernel(tokens, count, group_queries, qidx_ref, len_ref, payload_ref, emb_ref, wp_ref, after_ref,
                  prob_ref, log_ref, units_ref, qunit_ref, qdir_ref, qlen_ref, qs_s, dir_s):
    total, emb = emb_ref.shape
    seq = total // count
    sub = split_rows(total, 128)
    each = group_queries * tokens
    for k in range(payload_ref.shape[0]):
        qs_s[k * each : (k + 1) * each] = payload_ref[k, :each]
    qe = dot(qs_s[...], wp_ref[...], 1, 0)
    length = jnp.sqrt(jnp.sum(qe * qe, axis=-1, keepdims=True) + epsilon)
    qdir = qe / length
    qdir_ref[...] = qdir
    qlen_ref[...] = jnp.broadcast_to(length, qlen_ref.shape)
    qunit_ref[...] = qdir.astype(BF16).reshape(qunit_ref.shape)
    for b in range(0, total, sub):
        e = emb_ref[b : b + sub]
        dir_s[b : b + sub] = e / jnp.sqrt(jnp.sum(e * e, axis=-1, keepdims=True) + epsilon)
    for r in range(count):
        units = dir_s[pl.ds(r, seq, stride=count), :].astype(BF16)
        units_ref[r] = units
        logits = dot(qunit_ref[qidx_ref[r]], units, 1, 1) / sharpness
        valid = lax.broadcasted_iota(jnp.int32, logits.shape, 1) < len_ref[r]
        student = jnp.where(valid, jnp.exp(logits), 0.0)
        student_total = jnp.sum(student, axis=-1, keepdims=True)
        prob_ref[r] = student / student_total
        log_ref[r] = logits - jnp.log(student_total)


def student_scores(qidx, lens, payload, embeds, wp, after, count, tokens, group_queries):
    total, emb = embeds.shape
    seq = total // count
    queries = payload.shape[0] * group_queries
    return pl.pallas_call(
        functools.partial(scores_kernel, tokens, count, group_queries),
        in_specs=[SMEM, SMEM, VMEM, VMEM, VMEM, ANY],
        out_specs=[VMEM] * 6,
        out_shape=[
            jax.ShapeDtypeStruct((count, tokens, seq), F32),
            jax.ShapeDtypeStruct((count, tokens, seq), F32),
            jax.ShapeDtypeStruct((count, seq, emb), BF16),
            jax.ShapeDtypeStruct((queries, tokens, emb), BF16),
            jax.ShapeDtypeStruct((queries * tokens, emb), F32),
            jax.ShapeDtypeStruct((queries * tokens, 128), F32),
        ],
        scratch_shapes=[pltpu.VMEM((queries * tokens, payload.shape[2]), BF16), pltpu.VMEM((total, emb), F32)],
        compiler_params=params(),
        cost_estimate=cost(1e9, 4 * total * emb),
        name="student_scores",
    )(qidx, lens, payload, embeds, wp, after)


def two_parts(a, b):
    high = a.astype(BF16)
    low = (a - high.astype(F32)).astype(BF16)
    return dot(high, b, 1, 0) + dot(low, b, 1, 0)


def backward_kernel(
    tokens, count, blocks, group_queries,
    qidx_ref, midx_ref, len_ref, core_ref,
    maps_in, prob_in, log_in, units_in, qunit_in, emb_in, x_in, normed_in, inv_in, payload_in,
    qdir_ref, qlen_ref, gain_ref, bias_ref, wp_ref, wpt_ref,
    sg_out, send_ref, keep_ref,
    maps_s, prob_s, log_s, units_s, qunit_s, emb_s, x_s, normed_s, inv_s, payload_s,
    up_s, eg_s, mean_s, along_s, un_s, qg_s, hg_s, sg_s, wo_s, nt_s, right_s,
    first_sem, block_sem, out_sem, last_sem,
):
    total, width = x_s.shape
    emb = emb_s.shape[1]
    seq = total // count
    rows = total // blocks
    sub = split_rows(rows, 256)
    thin = split_rows(total, 128)
    step = split_rows(sub, 48)
    first = [
        pltpu.make_async_copy(src, dst, first_sem.at[n])
        for n, (src, dst) in enumerate(
            (
                (qunit_in, qunit_s), (maps_in, maps_s), (prob_in, prob_s), (log_in, log_s), (units_in, units_s),
                (emb_in, emb_s), (inv_in, inv_s),
            )
        )
    ]
    loads = [
        [
            pltpu.make_async_copy(src.at[pl.ds(b * rows, rows)], dst.at[pl.ds(b * rows, rows)], block_sem.at[2 * b + n])
            for n, (src, dst) in enumerate(((normed_in, normed_s), (x_in, x_s)))
        ]
        for b in range(blocks)
    ]
    last = pltpu.make_async_copy(payload_in, payload_s, last_sem)
    for copy in first:
        copy.start()
    for pair in loads:
        for copy in pair:
            copy.start()
    last.start()
    gain, bias = gain_ref[...], bias_ref[...]
    gain_w = two_parts(gain, wp_ref[...])
    bias_w = two_parts(bias, wp_ref[...])
    qg_s[...] = jnp.zeros_like(qg_s)
    for copy in first:
        copy.wait()

    spread = jnp.zeros((tokens, 1), F32)
    for r in range(count):
        teacher = maps_s[midx_ref[r]].astype(F32)
        valid = lax.broadcasted_iota(jnp.int32, teacher.shape, 1) < len_ref[r]
        teacher_log = jnp.log(teacher)
        teacher = jnp.where(valid, teacher, 0.0)
        teacher_total = jnp.sum(teacher, axis=-1, keepdims=True)
        teacher_prob = teacher / teacher_total
        gap = (teacher_log - jnp.log(teacher_total)) - log_s[r]
        spread += jnp.sum(jnp.where(valid, teacher_prob * gap, 0.0), axis=-1, keepdims=True)
        slope = ((prob_s[r] - teacher_prob) / (tokens * sharpness)).astype(BF16)
        up_s[pl.ds(r, seq, stride=count), :] = dot(slope, qunit_s[qidx_ref[r]], 0, 0).astype(BF16).astype(F32)
        un_s[r] = dot(slope, units_s[r], 1, 0)
    for r in range(count):
        qg_s[qidx_ref[r]] += un_s[r]
    total_eg = jnp.zeros((1, emb), F32)
    for b in range(0, total, thin):
        e = emb_s[b : b + thin]
        upstream = up_s[b : b + thin]
        length = jnp.sqrt(jnp.sum(e * e, axis=-1, keepdims=True) + epsilon)
        direction = e / length
        eg = (upstream - direction * jnp.sum(direction * upstream, axis=-1, keepdims=True)) / length
        eg = eg.astype(BF16)
        eg_s[b : b + thin] = eg
        eg = eg.astype(F32)
        total_eg += jnp.sum(eg, axis=0, keepdims=True)
        inverse = inv_s[b : b + thin]
        mean_s[b : b + thin] = inverse * (jnp.sum(eg * gain_w, axis=-1, keepdims=True) / width)
        along_s[b : b + thin] = inverse * (jnp.sum(eg * (e - bias_w), axis=-1, keepdims=True) / width)

    def wide(b):
        hg_s[...] = dot(eg_s[b : b + sub], wp_ref[...], 1, 1)
        for c in range(b, b + sub, step):
            inverse, mean, along = inv_s[c : c + step], mean_s[c : c + step], along_s[c : c + step]
            for v in range(0, width, 128):
                scaled = hg_s[c - b : c - b + step, v : v + 128] * gain[:, v : v + 128]
                normed = normed_s[c : c + step, v : v + 128].astype(F32)
                sg_s[c : c + step, v : v + 128] = (inverse * scaled - mean - normed * along).astype(BF16)

    def products(b, part, parts):
        span = width // parts
        x = x_s[b * rows : (b + 1) * rows, part * span : (part + 1) * span]
        value = dot(x, sg_s[b * rows : (b + 1) * rows], 0, 0)
        if b == 0:
            wo_s[part * span : (part + 1) * span] = value
        else:
            wo_s[part * span : (part + 1) * span] += value

    parts = rows // sub if width % (rows // sub * 128) == 0 else 1
    stores = []
    for b in range(blocks):
        for copy in loads[b]:
            copy.wait()
        for n in range(rows // sub):
            wide(b * rows + n * sub)
            if b > 0 and n < parts:
                products(b - 1, n, parts)
        stores.append(
            pltpu.make_async_copy(
                sg_s.at[pl.ds(b * rows, rows)], sg_out.at[pl.ds(b * rows, rows)], out_sem.at[b]
            )
        )
        stores[-1].start()
        value = dot(eg_s[b * rows : (b + 1) * rows], normed_s[b * rows : (b + 1) * rows], 0, 0)
        if b == 0:
            nt_s[...] = value
        else:
            nt_s[...] += value
    for n in range(parts):
        products(blocks - 1, n, parts)

    last.wait()
    qg = qg_s[...].reshape(qdir_ref.shape)
    qdir = qdir_ref[...]
    qeg = (qg - qdir * jnp.sum(qdir * qg, axis=-1, keepdims=True)) / qlen_ref[:, :1]
    high = qeg.astype(BF16)
    low = (qeg - high.astype(F32)).astype(BF16)
    each = group_queries * tokens
    proj_query = jnp.zeros((emb, width), F32)
    for k in range(payload_s.shape[0]):
        qs = payload_s[k, :each]
        part = slice(k * each, (k + 1) * each)
        proj_query = proj_query + (dot(high[part], qs, 0, 0) + dot(low[part], qs, 0, 0))
    nt = nt_s[...]
    s = jnp.broadcast_to(total_eg, (emb, emb)).T[:, :1]
    wpt = wpt_ref[...].astype(F32)
    proj = nt * gain + s * bias + proj_query
    gain_row = jnp.sum(wpt * nt, axis=0, keepdims=True)
    bias_row = jnp.sum(wpt * s, axis=0, keepdims=True)
    index = lax.broadcasted_iota(jnp.int32, (tokens, width), 0)
    top = jnp.where(index == 0, gain_row, jnp.where(index == 1, bias_row, 0.0))
    rest_rows = jnp.zeros((128 - 2 * tokens, width), F32)
    right_s[...] = jnp.concatenate([proj, top, jnp.broadcast_to(spread, (tokens, width)), rest_rows], axis=0).T
    half = width // CORES
    chunk = send_ref.shape[1]
    for ref, which in ((send_ref, 1 - core_ref[0]), (keep_ref, core_ref[0])):
        start = pl.multiple_of(which * half, half)
        left = wo_s[pl.ds(start, half)].astype(BF16)
        right = right_s[pl.ds(start, half)].astype(BF16)
        for c in range(half // chunk):
            ref[c, :, :width] = left[c * chunk : (c + 1) * chunk]
            ref[c, :, width:] = right[c * chunk : (c + 1) * chunk]
    for copy in stores:
        copy.wait()


def student_backward(
    qidx, midx, lens, core, maps, scores, payload, embeds, x, normed, inverse, gain, bias, wp, wpt,
    count, tokens, group_queries, chunk,
):
    total, width = x.shape
    emb = wp.shape[1]
    blocks = total // split_rows(total, 720)
    sub = split_rows(total // blocks, 256)
    chunks = width // CORES // chunk
    prob, log, units, qunit, qdir, qlen = scores
    manual = [maps, prob, log, units, qunit, embeds, x, normed, inverse, payload]
    packed = jax.ShapeDtypeStruct((chunks, chunk, width + emb + 128), BF16)
    return pl.pallas_call(
        functools.partial(backward_kernel, tokens, count, blocks, group_queries),
        in_specs=[SMEM] * 4 + [ANY] * len(manual) + [VMEM] * 6,
        out_specs=[ANY, VMEM, VMEM],
        scratch_shapes=[pltpu.VMEM(a.shape, a.dtype) for a in manual]
        + [
            pltpu.VMEM((total, emb), F32),
            pltpu.VMEM((total, emb), BF16),
            pltpu.VMEM((total, 128), F32),
            pltpu.VMEM((total, 128), F32),
            pltpu.VMEM((count, tokens, emb), F32),
            pltpu.VMEM(qunit.shape, F32),
            pltpu.VMEM((sub, width), F32),
            pltpu.VMEM((total, width), BF16),
            pltpu.VMEM((width, width), F32),
            pltpu.VMEM((emb, width), F32),
            pltpu.VMEM((width, emb + 128), F32),
            pltpu.SemaphoreType.DMA((7,)),
            pltpu.SemaphoreType.DMA((2 * blocks,)),
            pltpu.SemaphoreType.DMA((blocks,)),
            pltpu.SemaphoreType.DMA,
        ],
        out_shape=[jax.ShapeDtypeStruct((total, width), BF16), packed, packed],
        compiler_params=params(),
        cost_estimate=cost(2 * total * width * (width + 2 * emb), 8 * total * width),
        name="student_backward",
    )(qidx, midx, lens, core, *manual, qdir, qlen, gain, bias, wp, wpt)


def context_kernel(sg_ref, wo_ref, after_ref, out_ref, token_ref):
    token_ref[...] = jnp.zeros_like(token_ref)
    out_ref[...] = dot(sg_ref[...], wo_ref[...], 1, 1).astype(BF16)


def context_grad(sg, out_weight, after):
    total, width = sg.shape
    rows = split_rows(total, 720)
    block = pl.BlockSpec((rows, width), lambda s: (s, 0))
    return pl.pallas_call(
        context_kernel,
        grid=(total // rows,),
        in_specs=[block, pl.BlockSpec(out_weight.shape, lambda s: (0, 0)), ANY],
        out_specs=[block, pl.BlockSpec(TOKEN.shape, lambda s: (0, 0))],
        out_shape=[jax.ShapeDtypeStruct(sg.shape, BF16), TOKEN],
        compiler_params=params(),
        cost_estimate=cost(2 * total * width * width, 4 * total * width),
        name="context_grad",
    )(sg, out_weight, after)


def sum_kernel(inputs, lead, *refs):
    total = None
    for ref in refs[:inputs]:
        for value in [ref[n] for n in range(ref.shape[0])] if lead else [ref[...]]:
            total = value.astype(F32) if total is None else total + value.astype(F32)
    total = total.astype(BF16)
    out = refs[-2]
    refs[-1][...] = jnp.zeros_like(refs[-1])
    if len(out.shape) > len(total.shape):
        for n in range(out.shape[0]):
            out[n] = total
    else:
        out[...] = total


def summed(arrays, name, lead=False, copies=0, after=()):
    shape = arrays[0].shape[1:] if lead else arrays[0].shape
    return pl.pallas_call(
        functools.partial(sum_kernel, len(arrays), lead),
        in_specs=[VMEM] * len(arrays) + [ANY] * len(after),
        out_specs=[VMEM, VMEM],
        out_shape=[jax.ShapeDtypeStruct(((copies,) if copies else ()) + shape, BF16), TOKEN],
        compiler_params=pltpu.CompilerParams(vmem_limit_bytes=SMALL_LIMIT),
        name=name,
    )(*arrays, *after)


def unpack_kernel(parts, width, emb, tokens, scale, index_ref, *rest):
    ins = rest[:parts]
    wo_ref, proj_ref, gain_ref, bias_ref, loss_ref, small_s = rest[parts:]
    per = ins[0].shape[0]
    for a in range(parts):
        for k in range(per):
            c = index_ref[a * per + k]
            value = ins[a][k].astype(F32)
            wo_ref[c] = value[:, :width]
            proj_ref[c] = value[:, width : width + emb]
            small_s[c] = value[:, width + emb :]
    turned = small_s[...].reshape(width, 128).T
    for v in range(width // 128):
        gain_ref[v : v + 1] = turned[0:1, v * 128 : (v + 1) * 128]
        bias_ref[v : v + 1] = turned[1:2, v * 128 : (v + 1) * 128]
    loss_ref[0] = jnp.sum(turned[tokens : 2 * tokens, 0:1]) * scale


def unpack(arrays, index, width, emb, tokens, scale):
    parts = len(arrays)
    per, chunk, _ = arrays[0].shape
    chunks = parts * per
    return pl.pallas_call(
        functools.partial(unpack_kernel, parts, width, emb, tokens, scale),
        in_specs=[SMEM] + [VMEM] * parts,
        out_specs=[VMEM] * 4 + [SMEM],
        out_shape=[jax.ShapeDtypeStruct((chunks, chunk, n), F32) for n in (width, emb)]
        + [jax.ShapeDtypeStruct((width // 128, 128), F32)] * 2
        + [jax.ShapeDtypeStruct((1,), F32)],
        scratch_shapes=[pltpu.VMEM((chunks, chunk, 128), F32)],
        compiler_params=pltpu.CompilerParams(vmem_limit_bytes=SMALL_LIMIT),
        name="unpack",
    )(index, *arrays)


def local(
    context,
    stream,
    out_weight,
    gain,
    bias,
    proj_weight,
    query_states,
    passage_len,
    passage_dest,
    teacher_states,
    teacher_query,
    teacher_key,
):
    dp = lax.axis_size("dp")
    nt = lax.axis_size("tensor")
    chips = dp // CORES
    me = lax.axis_index("dp")
    chip, core = me // CORES, me % CORES
    mt = lax.axis_index("tensor")
    count, seq, width = context.shape
    emb = proj_weight.shape[1]
    group_queries, tokens, _ = query_states.shape
    depth, heads = teacher_query.shape
    per = count // dp
    per_query = count * nt // group_queries

    def flat(a):
        return a.transpose(1, 0, 2).reshape(-1, a.shape[2])

    def shift_chip(x, k):
        return lax.ppermute(
            x, "dp", [(c * CORES + o, (c + k) % chips * CORES + o) for c in range(chips) for o in range(CORES)]
        )

    def swap_core(x):
        return lax.ppermute(x, "dp", [(d, d ^ 1) for d in range(dp)])

    def shift_t(x, k):
        return lax.ppermute(x, "tensor", [(t, (t + k) % nt) for t in range(nt)])

    chip_groups = [[c * CORES + o for c in range(chips)] for o in range(CORES)]

    def exchange_chips(x):
        return lax.all_to_all(x, "dp", split_axis=0, concat_axis=0, tiled=True, axis_index_groups=chip_groups)

    def exchange_t(x):
        return lax.all_to_all(x, "tensor", split_axis=0, concat_axis=0, tiled=True)

    part = depth // dp
    plane = []
    for w in (teacher_query, teacher_key):
        mine = lax.dynamic_slice_in_dim(w, me * part, part, 0)
        along = jnp.stack([shift_t(mine, k) for k in range(1, nt)])
        plane.append(exchange_chips(jnp.broadcast_to(along[None], (chips,) + along.shape)))
    shifts = jnp.arange(chips, dtype=jnp.int32)
    piece_rows = jnp.concatenate([shifts * CORES + core, shifts * CORES + 1 - core]).astype(jnp.int32)

    dest_group = passage_dest // (count * nt)
    rows = jnp.arange(count, dtype=jnp.int32)
    rank = jnp.sum(
        (dest_group[:, None] == dest_group[None, :]) & (rows[None, :] < rows[:, None]), axis=1, dtype=jnp.int32
    )
    place = dest_group * per + rank
    positions = jnp.sum(
        jnp.where(place[:, None] == rows[None, :], (passage_dest % count)[:, None], 0), axis=0
    )
    queries = query_states.reshape(group_queries * tokens, width)
    extra = jnp.pad(positions.astype(BF16)[None, :], ((0, 15), (0, width - count)))
    payload = jnp.concatenate([queries, extra], axis=0)
    payload = lax.all_to_all(
        jnp.broadcast_to(payload[None], (dp,) + payload.shape), "dp", split_axis=0, concat_axis=0, tiled=True
    )
    told = payload[:, group_queries * tokens, :count].astype(jnp.int32)
    order = lax.dynamic_slice_in_dim(told, me * per, per, 1).reshape(-1)
    midx = place.astype(jnp.int32)
    qidx = (passage_dest // per_query).astype(jnp.int32)

    gain2, bias2 = gain.reshape(1, width), bias.reshape(1, width)
    x = flat(context)
    normed, embeds, inverse = student_forward(x, flat(stream), out_weight, gain2, bias2, proj_weight)
    plane[0], plane[1], normed, embeds, inverse = lax.optimization_barrier(
        (plane[0], plane[1], normed, embeds, inverse)
    )
    pieces = plane + [swap_core(a) for a in plane]
    maps, token = teacher_maps(
        order, piece_rows, flat(teacher_states), teacher_query, teacher_key, pieces, count, tokens
    )
    maps = lax.all_to_all(maps, "dp", split_axis=0, concat_axis=0, tiled=True)
    scores = student_scores(qidx, passage_len, payload, embeds, proj_weight, token, count, tokens, group_queries)
    chunk = width // (CORES * chips * nt)
    sg, send, keep = student_backward(
        qidx, midx, passage_len, core.astype(jnp.int32).reshape(1), maps, scores, payload,
        embeds, x, normed, inverse, gain2, bias2, proj_weight, proj_weight.T,
        count, tokens, group_queries, chunk,
    )

    parts, token = summed([keep, swap_core(send)], "sum_cores")
    grad_context, token = context_grad(sg, out_weight, token)
    parts = exchange_chips(parts.reshape(chips, nt, chunk, -1))
    parts, _ = summed([parts], "sum_plane", lead=True, after=(token,))
    parts, _ = summed([exchange_t(parts)], "sum_tensor", lead=True, copies=nt)
    line = exchange_t(parts)
    plane = [line] + [shift_chip(line, k) for k in range(1, chips)]
    arrays = plane + [swap_core(a) for a in plane]
    behind = (chip - shifts) % chips
    base = jnp.concatenate([core * chips + behind, (1 - core) * chips + behind]) * nt
    index = (base[:, None] + jnp.arange(nt)[None, :]).reshape(-1).astype(jnp.int32)
    grad_out, grad_proj, grad_gain, grad_bias, loss = unpack(
        arrays, index, width, emb, tokens, 1.0 / (count * dp * nt * tokens)
    )
    return (
        loss.reshape(()),
        grad_out.reshape(width, width),
        grad_proj.reshape(width, emb),
        grad_gain.reshape(width),
        grad_bias.reshape(width),
        grad_context.reshape(seq, count, width).transpose(1, 0, 2),
    )


def solution(mesh):
    return jax.shard_map(
        local,
        mesh=mesh,
        in_specs=(
            P(("dp", "tensor"), None, None),
            P(("dp", "tensor"), None, None),
            P(),
            P(),
            P(),
            P(),
            P("dp", None, None),
            P(("dp", "tensor")),
            P(("dp", "tensor")),
            P(("dp", "tensor"), None, None),
            P(None, "tensor"),
            P(None, "tensor"),
        ),
        out_specs=(P(), P(), P(), P(), P(), P(("dp", "tensor"), None, None)),
        check_vma=False,
    )
```

```python
import functools
import math

import jax
import jax.numpy as jnp
from jax import lax
from jax.experimental import pallas as pl
from jax.experimental.pallas import tpu as pltpu
from jax.sharding import PartitionSpec as P

sharpness = 0.05
softcap = 10.0
epsilon = 1e-06
CORES = 2
VMEM_LIMIT = 56 * 1024 * 1024
SMALL_LIMIT = 14 * 1024 * 1024

F32 = jnp.float32
BF16 = jnp.bfloat16
VMEM = pl.BlockSpec(memory_space=pltpu.VMEM)
SMEM = pl.BlockSpec(memory_space=pltpu.SMEM)
ANY = pl.BlockSpec(memory_space=pl.ANY)
TOKEN = jax.ShapeDtypeStruct((8, 128), F32)


def up(n, m):
    return -(-n // m) * m


def dot(a, b, ca, cb):
    return lax.dot_general(a, b, (((ca,), (cb,)), ((), ())), preferred_element_type=F32)


def split_rows(rows, most):
    return max(n for n in range(16, most + 1, 16) if rows % n == 0)


def params(**kw):
    return pltpu.CompilerParams(vmem_limit_bytes=VMEM_LIMIT, **kw)


def cost(flops, nbytes):
    return pl.CostEstimate(flops=int(flops), bytes_accessed=int(nbytes), transcendentals=0)


def forward_kernel(x_ref, str_ref, wo_ref, gain_ref, bias_ref, wp_ref, normed_ref, emb_ref, inv_ref, turned_ref, prod_s, hid_s):
    rows, width = x_ref.shape
    sub = split_rows(rows, 256)
    gain, bias = gain_ref[...], bias_ref[...]
    for b in range(0, rows, sub):
        prod_s[b : b + sub] = dot(x_ref[b : b + sub], wo_ref[...], 1, 0)
        for c in range(b, b + sub, 16):
            summed = prod_s[c : c + 16] + str_ref[c : c + 16].astype(F32)
            centred = summed - jnp.mean(summed, axis=-1, keepdims=True)
            inverse = lax.rsqrt(jnp.mean(centred * centred, axis=-1, keepdims=True) + epsilon)
            normed = centred * inverse
            normed_ref[c : c + 16] = normed.astype(BF16)
            inv_ref[c : c + 16] = jnp.broadcast_to(inverse, (16, inv_ref.shape[1]))
            hid_s[c : c + 16] = (normed * gain + bias).astype(BF16)
        emb_ref[b : b + sub] = dot(hid_s[b : b + sub], wp_ref[...], 1, 0)
    turned_ref[0] = x_ref[...].T


def student_forward(x, stream, out_weight, gain, bias, proj_weight):
    total, width = x.shape
    emb = proj_weight.shape[1]
    rows = split_rows(total, 720)
    block = lambda last: pl.BlockSpec((rows, last), lambda s: (s, 0))
    whole = lambda a: pl.BlockSpec(a.shape, lambda s: (0,) * a.ndim)
    return pl.pallas_call(
        forward_kernel,
        grid=(total // rows,),
        in_specs=[block(width), block(width)] + [whole(a) for a in (out_weight, gain, bias, proj_weight)],
        out_specs=[block(width), block(emb), block(128), pl.BlockSpec((1, width, rows), lambda s: (s, 0, 0))],
        out_shape=[
            jax.ShapeDtypeStruct((total, width), BF16),
            jax.ShapeDtypeStruct((total, emb), F32),
            jax.ShapeDtypeStruct((total, 128), F32),
            jax.ShapeDtypeStruct((total // rows, width, rows), BF16),
        ],
        scratch_shapes=[pltpu.VMEM((rows, width), F32), pltpu.VMEM((rows, width), BF16)],
        compiler_params=params(),
        cost_estimate=cost(2 * total * width * (width + emb), 8 * total * width),
        name="student_forward",
    )(x, stream, out_weight, gain, bias, proj_weight)


def teacher_kernel(parts, count, tokens, order_ref, rows_ref, states_ref, wq_ref, wk_ref, *rest):
    pieces, out_ref, token_ref = rest[:parts], rest[parts], rest[parts + 1]
    w_s, own_s, q_s, g_s, key_s, e_s, map_s, q_sem, key_sem, w_sem, own_sem = rest[parts + 2 :]
    depth = q_s.shape[1]
    slices = w_s.shape[0] // 2
    part_rows = pieces[0].shape[1]
    total = key_s.shape[0]
    seq = total // count
    blocks = key_sem.shape[0]
    rows = total // blocks
    first = count * tokens
    own = [
        pltpu.make_async_copy(wq_ref, own_s.at[0], own_sem.at[0]),
        pltpu.make_async_copy(wk_ref, own_s.at[1], own_sem.at[1]),
    ]
    queries = pltpu.make_async_copy(states_ref.at[pl.ds(0, first)], q_s, q_sem)
    gathered = [
        pltpu.make_async_copy(
            pieces[a],
            w_s.at[:, pl.ds(pl.multiple_of(rows_ref[a] * part_rows, part_rows), part_rows), :],
            w_sem.at[a],
        )
        for a in range(parts)
    ]
    keys = [
        pltpu.make_async_copy(
            states_ref.at[pl.ds(first + b * rows, rows)], key_s.at[pl.ds(b * rows, rows)], key_sem.at[b]
        )
        for b in range(blocks)
    ]
    queries.start()
    for copy in own + gathered:
        copy.start()
    queries.wait()
    for copy in own:
        copy.wait()
    for copy in keys:
        copy.start()
    q = q_s[...]
    mixed = dot(dot(q, own_s[0], 1, 0).astype(BF16), own_s[1], 1, 1)
    for copy in gathered:
        copy.wait()
    for k in range(slices):
        mixed = mixed + dot(dot(q, w_s[2 * k], 1, 0).astype(BF16), w_s[2 * k + 1], 1, 1)
    for v in range(depth // 128):
        g_s[v] = mixed[:, v * 128 : (v + 1) * 128]
        for p in range(count):
            q_s[p * tokens : (p + 1) * tokens, v * 128 : (v + 1) * 128] = g_s[
                v, pl.ds(p, tokens, stride=count), :
            ].astype(BF16)
    mixed = q_s[...]
    scale = 1.0 / (math.sqrt(depth) * softcap)
    side = 128 // tokens
    pair = lax.broadcasted_iota(jnp.int32, (rows, 128), 0) % count
    for b in range(blocks):
        keys[b].wait()
        raw = dot(key_s[b * rows : (b + 1) * rows], mixed, 1, 1)
        mine = raw[:, :128]
        for v in range(1, count // side):
            mine = jnp.where(pair >= v * side, raw[:, v * 128 : (v + 1) * 128], mine)
        e_s[b * rows : (b + 1) * rows] = jnp.exp(softcap * jnp.tanh(mine * scale))
    lane = lax.broadcasted_iota(jnp.int32, (seq, 128), 1) // tokens
    filler = jnp.zeros((up(seq, 128) - seq, 128), F32)
    for g in range(count // side):
        both = e_s[pl.ds(g * side, seq, stride=count), :]
        for v in range(1, side):
            both = jnp.where(lane == v, e_s[pl.ds(g * side + v, seq, stride=count), :], both)
        turned = jnp.concatenate([both, filler], axis=0).T
        for v in range(side):
            map_s[g * side + v] = turned[v * tokens : (v + 1) * tokens, :seq].astype(BF16)
    for n in range(count):
        out_ref[n] = map_s[order_ref[n]]
    token_ref[...] = jnp.zeros_like(token_ref)


def teacher_maps(order, rows, states, wq, wk, pieces, count, tokens):
    total, depth = states.shape
    keys = total - count * tokens
    heads = wq.shape[1]
    parts = len(pieces)
    slices = pieces[0].shape[0]
    blocks = keys // split_rows(keys, 720)
    return pl.pallas_call(
        functools.partial(teacher_kernel, parts, count, tokens),
        in_specs=[SMEM, SMEM] + [ANY] * (3 + parts),
        out_specs=[VMEM, VMEM],
        out_shape=[jax.ShapeDtypeStruct((count, tokens, keys // count), BF16), TOKEN],
        scratch_shapes=[
            pltpu.VMEM((slices, depth, heads), BF16),
            pltpu.VMEM((2, depth, heads), BF16),
            pltpu.VMEM((count * tokens, depth), BF16),
            pltpu.VMEM((depth // 128, count * tokens, 128), F32),
            pltpu.VMEM((keys, depth), BF16),
            pltpu.VMEM((keys, 128), F32),
            pltpu.VMEM((count, tokens, keys // count), BF16),
            pltpu.SemaphoreType.DMA,
            pltpu.SemaphoreType.DMA((blocks,)),
            pltpu.SemaphoreType.DMA((parts,)),
            pltpu.SemaphoreType.DMA((2,)),
        ],
        compiler_params=params(),
        cost_estimate=cost(8 * count * tokens * depth * depth, 2 * states.size + 4 * depth * depth),
        name="teacher_maps",
    )(order, rows, states, wq, wk, *pieces)


def scores_kernel(tokens, count, group_queries, qidx_ref, len_ref, payload_ref, emb_ref, wp_ref, after_ref,
                  prob_ref, log_ref, units_ref, qunit_ref, qdir_ref, qlen_ref, qs_s, dir_s):
    total, emb = emb_ref.shape
    seq = total // count
    sub = split_rows(total, 128)
    each = group_queries * tokens
    for k in range(payload_ref.shape[0]):
        qs_s[k * each : (k + 1) * each] = payload_ref[k, :each]
    qe = dot(qs_s[...], wp_ref[...], 1, 0)
    length = jnp.sqrt(jnp.sum(qe * qe, axis=-1, keepdims=True) + epsilon)
    qdir = qe / length
    qdir_ref[...] = qdir
    qlen_ref[...] = jnp.broadcast_to(length, qlen_ref.shape)
    qunit_ref[...] = qdir.astype(BF16).reshape(qunit_ref.shape)
    for b in range(0, total, sub):
        e = emb_ref[b : b + sub]
        dir_s[b : b + sub] = e / jnp.sqrt(jnp.sum(e * e, axis=-1, keepdims=True) + epsilon)
    for r in range(count):
        units = dir_s[pl.ds(r, seq, stride=count), :].astype(BF16)
        units_ref[r] = units
        logits = dot(qunit_ref[qidx_ref[r]], units, 1, 1) / sharpness
        valid = lax.broadcasted_iota(jnp.int32, logits.shape, 1) < len_ref[r]
        student = jnp.where(valid, jnp.exp(logits), 0.0)
        student_total = jnp.sum(student, axis=-1, keepdims=True)
        prob_ref[r] = student / student_total
        log_ref[r] = logits - jnp.log(student_total)


def student_scores(qidx, lens, payload, embeds, wp, after, count, tokens, group_queries):
    total, emb = embeds.shape
    seq = total // count
    queries = payload.shape[0] * group_queries
    return pl.pallas_call(
        functools.partial(scores_kernel, tokens, count, group_queries),
        in_specs=[SMEM, SMEM, VMEM, VMEM, VMEM, ANY],
        out_specs=[VMEM] * 6,
        out_shape=[
            jax.ShapeDtypeStruct((count, tokens, seq), F32),
            jax.ShapeDtypeStruct((count, tokens, seq), F32),
            jax.ShapeDtypeStruct((count, seq, emb), BF16),
            jax.ShapeDtypeStruct((queries, tokens, emb), BF16),
            jax.ShapeDtypeStruct((queries * tokens, emb), F32),
            jax.ShapeDtypeStruct((queries * tokens, 128), F32),
        ],
        scratch_shapes=[pltpu.VMEM((queries * tokens, payload.shape[2]), BF16), pltpu.VMEM((total, emb), F32)],
        compiler_params=params(),
        cost_estimate=cost(1e9, 4 * total * emb),
        name="student_scores",
    )(qidx, lens, payload, embeds, wp, after)


def two_parts(a, b):
    high = a.astype(BF16)
    low = (a - high.astype(F32)).astype(BF16)
    return dot(high, b, 1, 0) + dot(low, b, 1, 0)


def backward_kernel(
    tokens, count, blocks, group_queries,
    qidx_ref, midx_ref, len_ref, core_ref,
    maps_in, prob_in, log_in, units_in, qunit_in, emb_in, x_in, normed_in, inv_in, payload_in,
    qdir_ref, qlen_ref, gain_ref, bias_ref, wp_ref, wpt_ref,
    sg_out, send_ref, keep_ref,
    maps_s, prob_s, log_s, units_s, qunit_s, emb_s, x_s, normed_s, inv_s, payload_s,
    up_s, eg_s, mean_s, along_s, un_s, qg_s, hg_both, sg_s, wo_s, nt_s, right_s,
    first_sem, block_sem, out_sem, last_sem,
):
    total, width = normed_s.shape
    emb = emb_s.shape[1]
    seq = total // count
    rows = total // blocks
    sub = split_rows(rows, 256)
    thin = split_rows(total, 128)
    step = split_rows(sub, 48)
    first = [
        pltpu.make_async_copy(src, dst, first_sem.at[n])
        for n, (src, dst) in enumerate(
            (
                (qunit_in, qunit_s), (maps_in, maps_s), (prob_in, prob_s), (log_in, log_s), (units_in, units_s),
                (emb_in, emb_s), (inv_in, inv_s),
            )
        )
    ]
    loads = [
        [
            pltpu.make_async_copy(
                normed_in.at[pl.ds(b * rows, rows)], normed_s.at[pl.ds(b * rows, rows)], block_sem.at[2 * b]
            ),
            pltpu.make_async_copy(x_in.at[b], x_s.at[b], block_sem.at[2 * b + 1]),
        ]
        for b in range(blocks)
    ]
    last = pltpu.make_async_copy(payload_in, payload_s, last_sem)
    for copy in first:
        copy.start()
    gain, bias = gain_ref[...], bias_ref[...]
    gain_w = two_parts(gain, wp_ref[...])
    bias_w = two_parts(bias, wp_ref[...])
    qg_s[...] = jnp.zeros_like(qg_s)
    for copy in first:
        copy.wait()
    for pair in loads:
        for copy in pair:
            copy.start()
    last.start()

    spread = jnp.zeros((tokens, 1), F32)
    for r in range(count):
        teacher = maps_s[midx_ref[r]].astype(F32)
        valid = lax.broadcasted_iota(jnp.int32, teacher.shape, 1) < len_ref[r]
        teacher_log = jnp.log(teacher)
        teacher = jnp.where(valid, teacher, 0.0)
        teacher_total = jnp.sum(teacher, axis=-1, keepdims=True)
        teacher_prob = teacher / teacher_total
        gap = (teacher_log - jnp.log(teacher_total)) - log_s[r]
        spread += jnp.sum(jnp.where(valid, teacher_prob * gap, 0.0), axis=-1, keepdims=True)
        slope = ((prob_s[r] - teacher_prob) / (tokens * sharpness)).astype(BF16)
        up_s[pl.ds(r, seq, stride=count), :] = dot(slope, qunit_s[qidx_ref[r]], 0, 0).astype(BF16).astype(F32)
        un_s[r] = dot(slope, units_s[r], 1, 0)
    for r in range(count):
        qg_s[qidx_ref[r]] += un_s[r]
    total_eg = jnp.zeros((1, emb), F32)
    for b in range(0, total, thin):
        e = emb_s[b : b + thin]
        upstream = up_s[b : b + thin]
        length = jnp.sqrt(jnp.sum(e * e, axis=-1, keepdims=True) + epsilon)
        direction = e / length
        eg = (upstream - direction * jnp.sum(direction * upstream, axis=-1, keepdims=True)) / length
        eg = eg.astype(BF16)
        eg_s[b : b + thin] = eg
        eg = eg.astype(F32)
        total_eg += jnp.sum(eg, axis=0, keepdims=True)
        inverse = inv_s[b : b + thin]
        mean_s[b : b + thin] = inverse * (jnp.sum(eg * gain_w, axis=-1, keepdims=True) / width)
        along_s[b : b + thin] = inverse * (jnp.sum(eg * (e - bias_w), axis=-1, keepdims=True) / width)

    def wide(b):
        hg_s = hg_both.at[b // sub % 2]
        hg_s[...] = dot(eg_s[b : b + sub], wpt_ref[...], 1, 0)
        for c in range(b, b + sub, step):
            inverse, mean, along = inv_s[c : c + step], mean_s[c : c + step], along_s[c : c + step]
            for v in range(0, width, 128):
                scaled = hg_s[c - b : c - b + step, v : v + 128] * gain[:, v : v + 128]
                normed = normed_s[c : c + step, v : v + 128].astype(F32)
                sg_s[c : c + step, v : v + 128] = (inverse * scaled - mean - normed * along).astype(BF16)

    def products(b, part, parts):
        span = width // parts
        value = dot(x_s[b, part * span : (part + 1) * span], sg_s[b * rows : (b + 1) * rows], 1, 0)
        if b == 0:
            wo_s[part * span : (part + 1) * span] = value
        else:
            wo_s[part * span : (part + 1) * span] += value

    parts = rows // sub if width % (rows // sub * 128) == 0 else 1
    stores = []
    for b in range(blocks):
        for copy in loads[b]:
            copy.wait()
        for n in range(rows // sub):
            wide(b * rows + n * sub)
            if b > 0 and n < parts:
                products(b - 1, n, parts)
        stores.append(
            pltpu.make_async_copy(
                sg_s.at[pl.ds(b * rows, rows)], sg_out.at[pl.ds(b * rows, rows)], out_sem.at[b]
            )
        )
        stores[-1].start()
        value = dot(eg_s[b * rows : (b + 1) * rows], normed_s[b * rows : (b + 1) * rows], 0, 0)
        if b == 0:
            nt_s[...] = value
        else:
            nt_s[...] += value
    for n in range(parts):
        products(blocks - 1, n, parts)

    last.wait()
    qg = qg_s[...].reshape(qdir_ref.shape)
    qdir = qdir_ref[...]
    qeg = (qg - qdir * jnp.sum(qdir * qg, axis=-1, keepdims=True)) / qlen_ref[:, :1]
    high = qeg.astype(BF16)
    low = (qeg - high.astype(F32)).astype(BF16)
    each = group_queries * tokens
    proj_query = jnp.zeros((emb, width), F32)
    for k in range(payload_s.shape[0]):
        qs = payload_s[k, :each]
        part = slice(k * each, (k + 1) * each)
        proj_query = proj_query + (dot(high[part], qs, 0, 0) + dot(low[part], qs, 0, 0))
    nt = nt_s[...]
    s = jnp.broadcast_to(total_eg, (emb, emb)).T[:, :1]
    wpt = wpt_ref[...].astype(F32)
    proj = nt * gain + s * bias + proj_query
    gain_row = jnp.sum(wpt * nt, axis=0, keepdims=True)
    bias_row = jnp.sum(wpt * s, axis=0, keepdims=True)
    index = lax.broadcasted_iota(jnp.int32, (tokens, width), 0)
    top = jnp.where(index == 0, gain_row, jnp.where(index == 1, bias_row, 0.0))
    rest_rows = jnp.zeros((128 - 2 * tokens, width), F32)
    right_s[...] = jnp.concatenate([proj, top, jnp.broadcast_to(spread, (tokens, width)), rest_rows], axis=0).T
    half = width // CORES
    chunk = send_ref.shape[1]
    for ref, which in ((send_ref, 1 - core_ref[0]), (keep_ref, core_ref[0])):
        start = pl.multiple_of(which * half, half)
        left = wo_s[pl.ds(start, half)].astype(BF16)
        right = right_s[pl.ds(start, half)].astype(BF16)
        for c in range(half // chunk):
            ref[c, :, :width] = left[c * chunk : (c + 1) * chunk]
            ref[c, :, width:] = right[c * chunk : (c + 1) * chunk]
    for copy in stores:
        copy.wait()


def student_backward(
    qidx, midx, lens, core, maps, scores, payload, embeds, x, normed, inverse, gain, bias, wp, wpt,
    count, tokens, group_queries, chunk,
):
    total, width = normed.shape
    emb = wp.shape[1]
    blocks = x.shape[0]
    sub = split_rows(total // blocks, 256)
    chunks = width // CORES // chunk
    prob, log, units, qunit, qdir, qlen = scores
    manual = [maps, prob, log, units, qunit, embeds, x, normed, inverse, payload]
    packed = jax.ShapeDtypeStruct((chunks, chunk, width + emb + 128), BF16)
    return pl.pallas_call(
        functools.partial(backward_kernel, tokens, count, blocks, group_queries),
        in_specs=[SMEM] * 4 + [ANY] * len(manual) + [VMEM] * 6,
        out_specs=[ANY, VMEM, VMEM],
        scratch_shapes=[pltpu.VMEM(a.shape, a.dtype) for a in manual]
        + [
            pltpu.VMEM((total, emb), F32),
            pltpu.VMEM((total, emb), BF16),
            pltpu.VMEM((total, 128), F32),
            pltpu.VMEM((total, 128), F32),
            pltpu.VMEM((count, tokens, emb), F32),
            pltpu.VMEM(qunit.shape, F32),
            pltpu.VMEM((2, sub, width), F32),
            pltpu.VMEM((total, width), BF16),
            pltpu.VMEM((width, width), F32),
            pltpu.VMEM((emb, width), F32),
            pltpu.VMEM((width, emb + 128), F32),
            pltpu.SemaphoreType.DMA((7,)),
            pltpu.SemaphoreType.DMA((2 * blocks,)),
            pltpu.SemaphoreType.DMA((blocks,)),
            pltpu.SemaphoreType.DMA,
        ],
        out_shape=[jax.ShapeDtypeStruct((total, width), BF16), packed, packed],
        compiler_params=params(),
        cost_estimate=cost(2 * total * width * (width + 2 * emb), 8 * total * width),
        name="student_backward",
    )(qidx, midx, lens, core, *manual, qdir, qlen, gain, bias, wp, wpt)


def context_kernel(sg_ref, wo_ref, after_ref, out_ref, token_ref):
    token_ref[...] = jnp.zeros_like(token_ref)
    out_ref[...] = dot(sg_ref[...], wo_ref[...], 1, 1).astype(BF16)


def context_grad(sg, out_weight, after):
    total, width = sg.shape
    rows = split_rows(total, 720)
    block = pl.BlockSpec((rows, width), lambda s: (s, 0))
    return pl.pallas_call(
        context_kernel,
        grid=(total // rows,),
        in_specs=[block, pl.BlockSpec(out_weight.shape, lambda s: (0, 0)), ANY],
        out_specs=[block, pl.BlockSpec(TOKEN.shape, lambda s: (0, 0))],
        out_shape=[jax.ShapeDtypeStruct(sg.shape, BF16), TOKEN],
        compiler_params=params(),
        cost_estimate=cost(2 * total * width * width, 4 * total * width),
        name="context_grad",
    )(sg, out_weight, after)


def split_sum_kernel(inputs, outputs, after, index_ref, *rest):
    ins, outs = rest[:inputs], rest[inputs + after : inputs + after + outputs]
    token_ref, total_s = rest[-2:]
    total = ins[0][...].astype(F32)
    for ref in ins[1:]:
        total = total + ref[...].astype(F32)
    total_s[...] = total.astype(BF16).reshape(total_s.shape)
    for k in range(outputs):
        outs[k][...] = total_s[index_ref[k]].reshape(outs[k].shape)
    token_ref[...] = jnp.zeros_like(token_ref)


def split_sum(arrays, index, name, after=()):
    outputs = index.shape[0]
    shape = arrays[0].shape
    lead = shape[0] // outputs
    out = shape[1:] if lead == 1 else (lead,) + shape[1:]
    *parts, token = pl.pallas_call(
        functools.partial(split_sum_kernel, len(arrays), outputs, len(after)),
        in_specs=[SMEM] + [VMEM] * len(arrays) + [ANY] * len(after),
        out_specs=[VMEM] * (outputs + 1),
        out_shape=[jax.ShapeDtypeStruct(out, BF16)] * outputs + [TOKEN],
        scratch_shapes=[pltpu.VMEM((outputs, lead) + shape[1:], BF16)],
        compiler_params=pltpu.CompilerParams(vmem_limit_bytes=SMALL_LIMIT),
        name=name,
    )(index, *arrays, *after)
    return parts, token


def sum_kernel(*refs):
    total = refs[0][...].astype(F32)
    for ref in refs[1:-1]:
        total = total + ref[...].astype(F32)
    refs[-1][...] = total.astype(BF16)


def plain_sum(arrays, name):
    return pl.pallas_call(
        sum_kernel,
        in_specs=[VMEM] * len(arrays),
        out_specs=VMEM,
        out_shape=jax.ShapeDtypeStruct(arrays[0].shape, BF16),
        compiler_params=pltpu.CompilerParams(vmem_limit_bytes=SMALL_LIMIT),
        name=name,
    )(*arrays)


def unpack_kernel(parts, width, emb, tokens, scale, index_ref, *rest):
    ins = rest[:parts]
    wo_ref, proj_ref, gain_ref, bias_ref, loss_ref, small_s = rest[parts:]
    per = ins[0].shape[0]
    for a in range(parts):
        for k in range(per):
            c = index_ref[a * per + k]
            value = ins[a][k].astype(F32)
            wo_ref[c] = value[:, :width]
            proj_ref[c] = value[:, width : width + emb]
            small_s[c] = value[:, width + emb :]
    turned = small_s[...].reshape(width, 128).T
    for v in range(width // 128):
        gain_ref[v : v + 1] = turned[0:1, v * 128 : (v + 1) * 128]
        bias_ref[v : v + 1] = turned[1:2, v * 128 : (v + 1) * 128]
    loss_ref[0] = jnp.sum(turned[tokens : 2 * tokens, 0:1]) * scale


def unpack(arrays, index, width, emb, tokens, scale):
    parts = len(arrays)
    per, chunk, _ = arrays[0].shape
    chunks = parts * per
    return pl.pallas_call(
        functools.partial(unpack_kernel, parts, width, emb, tokens, scale),
        in_specs=[SMEM] + [VMEM] * parts,
        out_specs=[VMEM] * 4 + [SMEM],
        out_shape=[jax.ShapeDtypeStruct((chunks, chunk, n), F32) for n in (width, emb)]
        + [jax.ShapeDtypeStruct((width // 128, 128), F32)] * 2
        + [jax.ShapeDtypeStruct((1,), F32)],
        scratch_shapes=[pltpu.VMEM((chunks, chunk, 128), F32)],
        compiler_params=pltpu.CompilerParams(vmem_limit_bytes=SMALL_LIMIT),
        name="unpack",
    )(index, *arrays)


def local(
    context,
    stream,
    out_weight,
    gain,
    bias,
    proj_weight,
    query_states,
    passage_len,
    passage_dest,
    teacher_states,
    teacher_query,
    teacher_key,
):
    dp = lax.axis_size("dp")
    nt = lax.axis_size("tensor")
    chips = dp // CORES
    me = lax.axis_index("dp")
    chip, core = me // CORES, me % CORES
    mt = lax.axis_index("tensor")
    count, seq, width = context.shape
    emb = proj_weight.shape[1]
    group_queries, tokens, _ = query_states.shape
    depth, heads = teacher_query.shape
    per = count // dp
    per_query = count * nt // group_queries

    def flat(a):
        return a.transpose(1, 0, 2).reshape(-1, a.shape[2])

    def shift_chip(x, k):
        return lax.ppermute(
            x, "dp", [(c * CORES + o, (c + k) % chips * CORES + o) for c in range(chips) for o in range(CORES)]
        )

    def swap_core(x):
        return lax.ppermute(x, "dp", [(d, d ^ 1) for d in range(dp)])

    def shift_t(x, k):
        return lax.ppermute(x, "tensor", [(t, (t + k) % nt) for t in range(nt)])

    part = depth // dp
    mine = jnp.stack(
        [lax.dynamic_slice_in_dim(w, me * part, part, 0) for w in (teacher_query, teacher_key)]
    )
    along = jnp.concatenate([shift_t(mine, k) for k in range(1, nt)], axis=0)
    pieces = [along] + [shift_chip(along, k) for k in range(1, chips)]
    shifts = jnp.arange(chips, dtype=jnp.int32)
    behind = (chip - shifts) % chips
    piece_rows = jnp.concatenate([behind * CORES + core, behind * CORES + 1 - core]).astype(jnp.int32)

    dest_group = passage_dest // (count * nt)
    rows = jnp.arange(count, dtype=jnp.int32)
    rank = jnp.sum(
        (dest_group[:, None] == dest_group[None, :]) & (rows[None, :] < rows[:, None]), axis=1, dtype=jnp.int32
    )
    place = dest_group * per + rank
    positions = jnp.sum(
        jnp.where(place[:, None] == rows[None, :], (passage_dest % count)[:, None], 0), axis=0
    )
    queries = query_states.reshape(group_queries * tokens, width)
    extra = jnp.pad(positions.astype(BF16)[None, :], ((0, 15), (0, width - count)))
    payload = jnp.concatenate([queries, extra], axis=0)
    payload = lax.all_to_all(
        jnp.broadcast_to(payload[None], (dp,) + payload.shape), "dp", split_axis=0, concat_axis=0, tiled=True
    )
    midx = place.astype(jnp.int32)
    qidx = (passage_dest // per_query).astype(jnp.int32)

    gain2, bias2 = gain.reshape(1, width), bias.reshape(1, width)
    x = flat(context)
    normed, embeds, inverse, turned = student_forward(x, flat(stream), out_weight, gain2, bias2, proj_weight)
    pieces[1:], payload, normed, embeds, inverse, turned = lax.optimization_barrier(
        (pieces[1:], payload, normed, embeds, inverse, turned)
    )
    pieces = pieces + [swap_core(a) for a in pieces]
    told = payload[:, group_queries * tokens, :count].astype(jnp.int32)
    order = lax.dynamic_slice_in_dim(told, me * per, per, 1).reshape(-1)
    maps, token = teacher_maps(
        order, piece_rows, flat(teacher_states), teacher_query, teacher_key, pieces, count, tokens
    )
    maps = lax.all_to_all(maps, "dp", split_axis=0, concat_axis=0, tiled=True)
    scores = student_scores(qidx, passage_len, payload, embeds, proj_weight, token, count, tokens, group_queries)
    chunk = width // (CORES * chips * nt)
    sg, send, keep = student_backward(
        qidx, midx, passage_len, core.astype(jnp.int32).reshape(1), maps, scores, payload,
        embeds, turned, normed, inverse, gain2, bias2, proj_weight, proj_weight.T,
        count, tokens, group_queries, chunk,
    )

    ahead = ((chip + shifts) % chips).astype(jnp.int32)
    t_shifts = jnp.arange(nt, dtype=jnp.int32)
    t_ahead = ((mt + t_shifts) % nt).astype(jnp.int32)
    parts, token = split_sum([keep, swap_core(send)], ahead, "sum_cores")
    grad_context, token = context_grad(sg, out_weight, token)
    parts = [parts[0]] + [shift_chip(parts[k], k) for k in range(1, chips)]
    parts, _ = split_sum(parts, t_ahead, "sum_plane", (token,))
    parts = [parts[0]] + [shift_t(parts[k], k) for k in range(1, nt)]
    total = plain_sum(parts, "sum_tensor")
    line = jnp.stack([total] + [shift_t(total, k) for k in range(1, nt)])
    plane = [line] + [shift_chip(line, k) for k in range(1, chips)]
    arrays = plane + [swap_core(a) for a in plane]
    base = jnp.concatenate([core * chips + behind, (1 - core) * chips + behind]) * nt
    index = (base[:, None] + ((mt - t_shifts) % nt)[None, :]).reshape(-1).astype(jnp.int32)
    grad_out, grad_proj, grad_gain, grad_bias, loss = unpack(
        arrays, index, width, emb, tokens, 1.0 / (count * dp * nt * tokens)
    )
    return (
        loss.reshape(()),
        grad_out.reshape(width, width),
        grad_proj.reshape(width, emb),
        grad_gain.reshape(width),
        grad_bias.reshape(width),
        grad_context.reshape(seq, count, width).transpose(1, 0, 2),
    )


def solution(mesh):
    return jax.shard_map(
        local,
        mesh=mesh,
        in_specs=(
            P(("dp", "tensor"), None, None),
            P(("dp", "tensor"), None, None),
            P(),
            P(),
            P(),
            P(),
            P("dp", None, None),
            P(("dp", "tensor")),
            P(("dp", "tensor")),
            P(("dp", "tensor"), None, None),
            P(None, "tensor"),
            P(None, "tensor"),
        ),
        out_specs=(P(), P(), P(), P(), P(), P(("dp", "tensor"), None, None)),
        check_vma=False,
    )
```

```python
import functools
import math

import jax
import jax.numpy as jnp
from jax import lax
from jax.experimental import pallas as pl
from jax.experimental.pallas import tpu as pltpu
from jax.sharding import PartitionSpec as P

sharpness = 0.05
softcap = 10.0
epsilon = 1e-06
CORES = 2
VMEM_LIMIT = 56 * 1024 * 1024
SMALL_LIMIT = 14 * 1024 * 1024

F32 = jnp.float32
BF16 = jnp.bfloat16
VMEM = pl.BlockSpec(memory_space=pltpu.VMEM)
SMEM = pl.BlockSpec(memory_space=pltpu.SMEM)
ANY = pl.BlockSpec(memory_space=pl.ANY)
TOKEN = jax.ShapeDtypeStruct((8, 128), F32)


def up(n, m):
    return -(-n // m) * m


def dot(a, b, ca, cb):
    return lax.dot_general(a, b, (((ca,), (cb,)), ((), ())), preferred_element_type=F32)


def split_rows(rows, most):
    return max(n for n in range(16, most + 1, 16) if rows % n == 0)


def one_row(ref):
    return jnp.concatenate([ref[v : v + 1] for v in range(ref.shape[0])], axis=1)


def params(**kw):
    return pltpu.CompilerParams(vmem_limit_bytes=VMEM_LIMIT, **kw)


def cost(flops, nbytes):
    return pl.CostEstimate(flops=int(flops), bytes_accessed=int(nbytes), transcendentals=0)


def forward_kernel(x_ref, str_ref, wo_ref, gain_ref, bias_ref, wp_ref, normed_ref, emb_ref, inv_ref, turned_ref, prod_s, hid_s):
    rows, width = x_ref.shape
    sub = rows
    gain, bias = one_row(gain_ref), one_row(bias_ref)
    for b in range(0, rows, sub):
        prod_s[b : b + sub] = dot(x_ref[b : b + sub], wo_ref[...], 1, 0)
        for c in range(b, b + sub, 16):
            summed = prod_s[c : c + 16] + str_ref[c : c + 16].astype(F32)
            centred = summed - jnp.mean(summed, axis=-1, keepdims=True)
            inverse = lax.rsqrt(jnp.mean(centred * centred, axis=-1, keepdims=True) + epsilon)
            normed = centred * inverse
            normed_ref[c : c + 16] = normed.astype(BF16)
            inv_ref[c : c + 16] = jnp.broadcast_to(inverse, (16, inv_ref.shape[1]))
            hid_s[c : c + 16] = (normed * gain + bias).astype(BF16)
        emb_ref[b : b + sub] = dot(hid_s[b : b + sub], wp_ref[...], 1, 0)
    turned_ref[0] = x_ref[...].T


def student_forward(x, stream, out_weight, gain, bias, proj_weight):
    total, width = x.shape
    emb = proj_weight.shape[1]
    rows = split_rows(total, 720)
    block = lambda last: pl.BlockSpec((rows, last), lambda s: (s, 0))
    whole = lambda a: pl.BlockSpec(a.shape, lambda s: (0,) * a.ndim)
    return pl.pallas_call(
        forward_kernel,
        grid=(total // rows,),
        in_specs=[block(width), block(width)] + [whole(a) for a in (out_weight, gain, bias, proj_weight)],
        out_specs=[block(width), block(emb), block(128), pl.BlockSpec((1, width, rows), lambda s: (s, 0, 0))],
        out_shape=[
            jax.ShapeDtypeStruct((total, width), BF16),
            jax.ShapeDtypeStruct((total, emb), F32),
            jax.ShapeDtypeStruct((total, 128), F32),
            jax.ShapeDtypeStruct((total // rows, width, rows), BF16),
        ],
        scratch_shapes=[pltpu.VMEM((rows, width), F32), pltpu.VMEM((rows, width), BF16)],
        compiler_params=params(),
        cost_estimate=cost(2 * total * width * (width + emb), 8 * total * width),
        name="student_forward",
    )(x, stream, out_weight, gain, bias, proj_weight)


def teacher_kernel(parts, count, tokens, order_ref, rows_ref, states_ref, wq_ref, wk_ref, *rest):
    pieces, out_ref, token_ref = rest[:parts], rest[parts], rest[parts + 1]
    w_s, own_s, q_s, g_s, key_s, e_s, map_s, q_sem, key_sem, w_sem, own_sem = rest[parts + 2 :]
    depth = q_s.shape[1]
    slices = w_s.shape[0] // 2
    part_rows = pieces[0].shape[1]
    total = key_s.shape[0]
    seq = total // count
    blocks = key_sem.shape[0]
    rows = total // blocks
    first = count * tokens
    own = [
        pltpu.make_async_copy(wq_ref, own_s.at[0], own_sem.at[0]),
        pltpu.make_async_copy(wk_ref, own_s.at[1], own_sem.at[1]),
    ]
    queries = pltpu.make_async_copy(states_ref.at[pl.ds(0, first)], q_s, q_sem)
    gathered = [
        pltpu.make_async_copy(
            pieces[a],
            w_s.at[:, pl.ds(pl.multiple_of(rows_ref[a] * part_rows, part_rows), part_rows), :],
            w_sem.at[a],
        )
        for a in range(parts)
    ]
    keys = [
        pltpu.make_async_copy(
            states_ref.at[pl.ds(first + b * rows, rows)], key_s.at[pl.ds(b * rows, rows)], key_sem.at[b]
        )
        for b in range(blocks)
    ]
    queries.start()
    for copy in own + gathered:
        copy.start()
    queries.wait()
    for copy in own:
        copy.wait()
    for copy in keys:
        copy.start()
    q = q_s[...]
    mixed = dot(dot(q, own_s[0], 1, 0).astype(BF16), own_s[1], 1, 1)
    for copy in gathered:
        copy.wait()
    for k in range(slices):
        mixed = mixed + dot(dot(q, w_s[2 * k], 1, 0).astype(BF16), w_s[2 * k + 1], 1, 1)
    for v in range(depth // 128):
        g_s[v] = mixed[:, v * 128 : (v + 1) * 128]
        for p in range(count):
            q_s[p * tokens : (p + 1) * tokens, v * 128 : (v + 1) * 128] = g_s[
                v, pl.ds(p, tokens, stride=count), :
            ].astype(BF16)
    mixed = q_s[...].T
    scale = 1.0 / (math.sqrt(depth) * softcap)
    side = 128 // tokens
    pair = lax.broadcasted_iota(jnp.int32, (rows, 128), 0) % count
    for b in range(blocks):
        keys[b].wait()
        raw = dot(key_s[b * rows : (b + 1) * rows], mixed, 1, 0)
        mine = raw[:, :128]
        for v in range(1, count // side):
            mine = jnp.where(pair >= v * side, raw[:, v * 128 : (v + 1) * 128], mine)
        e_s[b * rows : (b + 1) * rows] = jnp.exp(softcap * jnp.tanh(mine * scale))
    lane = lax.broadcasted_iota(jnp.int32, (seq, 128), 1) // tokens
    filler = jnp.zeros((up(seq, 128) - seq, 128), F32)
    for g in range(count // side):
        both = e_s[pl.ds(g * side, seq, stride=count), :]
        for v in range(1, side):
            both = jnp.where(lane == v, e_s[pl.ds(g * side + v, seq, stride=count), :], both)
        turned = jnp.concatenate([both, filler], axis=0).T
        for v in range(side):
            map_s[g * side + v] = turned[v * tokens : (v + 1) * tokens, :seq].astype(BF16)
    for n in range(count):
        out_ref[n] = map_s[order_ref[n]]
    token_ref[...] = jnp.zeros_like(token_ref)


def teacher_maps(order, rows, states, wq, wk, pieces, count, tokens):
    total, depth = states.shape
    keys = total - count * tokens
    heads = wq.shape[1]
    parts = len(pieces)
    slices = pieces[0].shape[0]
    blocks = keys // split_rows(keys, 720)
    return pl.pallas_call(
        functools.partial(teacher_kernel, parts, count, tokens),
        in_specs=[SMEM, SMEM] + [ANY] * (3 + parts),
        out_specs=[VMEM, VMEM],
        out_shape=[jax.ShapeDtypeStruct((count, tokens, keys // count), BF16), TOKEN],
        scratch_shapes=[
            pltpu.VMEM((slices, depth, heads), BF16),
            pltpu.VMEM((2, depth, heads), BF16),
            pltpu.VMEM((count * tokens, depth), BF16),
            pltpu.VMEM((depth // 128, count * tokens, 128), F32),
            pltpu.VMEM((keys, depth), BF16),
            pltpu.VMEM((keys, 128), F32),
            pltpu.VMEM((count, tokens, keys // count), BF16),
            pltpu.SemaphoreType.DMA,
            pltpu.SemaphoreType.DMA((blocks,)),
            pltpu.SemaphoreType.DMA((parts,)),
            pltpu.SemaphoreType.DMA((2,)),
        ],
        compiler_params=params(),
        cost_estimate=cost(8 * count * tokens * depth * depth, 2 * states.size + 4 * depth * depth),
        name="teacher_maps",
    )(order, rows, states, wq, wk, *pieces)


def scores_kernel(tokens, count, group_queries, qidx_ref, len_ref, payload_ref, emb_ref, wp_ref, after_ref,
                  prob_ref, log_ref, units_ref, qunit_ref, qdir_ref, qlen_ref, qs_s, dir_s):
    total, emb = emb_ref.shape
    seq = total // count
    sub = split_rows(total, 128)
    each = group_queries * tokens
    for k in range(payload_ref.shape[0]):
        qs_s[k * each : (k + 1) * each] = payload_ref[k, :each]
    qe = dot(qs_s[...], wp_ref[...], 1, 0)
    length = jnp.sqrt(jnp.sum(qe * qe, axis=-1, keepdims=True) + epsilon)
    qdir = qe / length
    qdir_ref[...] = qdir
    qlen_ref[...] = jnp.broadcast_to(length, qlen_ref.shape)
    qunit_ref[...] = qdir.astype(BF16).reshape(qunit_ref.shape)
    for b in range(0, total, sub):
        e = emb_ref[b : b + sub]
        dir_s[b : b + sub] = e / jnp.sqrt(jnp.sum(e * e, axis=-1, keepdims=True) + epsilon)
    for r in range(count):
        units = dir_s[pl.ds(r, seq, stride=count), :].astype(BF16)
        units_ref[r] = units
        logits = dot(qunit_ref[qidx_ref[r]], units, 1, 1) / sharpness
        valid = lax.broadcasted_iota(jnp.int32, logits.shape, 1) < len_ref[r]
        student = jnp.where(valid, jnp.exp(logits), 0.0)
        student_total = jnp.sum(student, axis=-1, keepdims=True)
        prob_ref[r] = student / student_total
        log_ref[r] = logits - jnp.log(student_total)


def student_scores(qidx, lens, payload, embeds, wp, after, count, tokens, group_queries):
    total, emb = embeds.shape
    seq = total // count
    queries = payload.shape[0] * group_queries
    return pl.pallas_call(
        functools.partial(scores_kernel, tokens, count, group_queries),
        in_specs=[SMEM, SMEM, VMEM, VMEM, VMEM, ANY],
        out_specs=[VMEM] * 6,
        out_shape=[
            jax.ShapeDtypeStruct((count, tokens, seq), F32),
            jax.ShapeDtypeStruct((count, tokens, seq), F32),
            jax.ShapeDtypeStruct((count, seq, emb), BF16),
            jax.ShapeDtypeStruct((queries, tokens, emb), BF16),
            jax.ShapeDtypeStruct((queries * tokens, emb), F32),
            jax.ShapeDtypeStruct((queries * tokens, 128), F32),
        ],
        scratch_shapes=[pltpu.VMEM((queries * tokens, payload.shape[2]), BF16), pltpu.VMEM((total, emb), F32)],
        compiler_params=params(),
        cost_estimate=cost(1e9, 4 * total * emb),
        name="student_scores",
    )(qidx, lens, payload, embeds, wp, after)


def two_parts(a, b):
    high = a.astype(BF16)
    low = (a - high.astype(F32)).astype(BF16)
    return dot(high, b, 1, 0) + dot(low, b, 1, 0)


def backward_kernel(
    tokens, count, blocks, group_queries,
    qidx_ref, midx_ref, len_ref, core_ref,
    maps_in, prob_in, log_in, units_in, qunit_in, emb_in, x_in, normed_in, inv_in, payload_in,
    qdir_ref, qlen_ref, gain_ref, bias_ref, wp_ref, wpt_ref,
    sg_out, send_ref, keep_ref,
    maps_s, prob_s, log_s, units_s, qunit_s, emb_s, x_s, normed_s, inv_s, payload_s,
    up_s, eg_s, mean_s, along_s, un_s, qg_s, hg_both, sg_s, wo_s, nt_s, right_s,
    first_sem, block_sem, out_sem, last_sem,
):
    total, width = normed_s.shape
    emb = emb_s.shape[1]
    seq = total // count
    rows = total // blocks
    sub = rows
    thin = split_rows(total, 128)
    step = split_rows(sub, 48)
    first = [
        pltpu.make_async_copy(src, dst, first_sem.at[n])
        for n, (src, dst) in enumerate(
            (
                (qunit_in, qunit_s), (maps_in, maps_s), (prob_in, prob_s), (log_in, log_s), (units_in, units_s),
                (emb_in, emb_s), (inv_in, inv_s),
            )
        )
    ]
    first, second = first[:5], first[5:]
    loads = [
        [
            pltpu.make_async_copy(
                normed_in.at[pl.ds(b * rows, rows)], normed_s.at[pl.ds(b * rows, rows)], block_sem.at[2 * b]
            ),
            pltpu.make_async_copy(x_in.at[b], x_s.at[b], block_sem.at[2 * b + 1]),
        ]
        for b in range(blocks)
    ]
    last = pltpu.make_async_copy(payload_in, payload_s, last_sem)
    for copy in first:
        copy.start()
    gain, bias = one_row(gain_ref), one_row(bias_ref)
    gain_w = two_parts(gain, wp_ref[...])
    bias_w = two_parts(bias, wp_ref[...])
    qg_s[...] = jnp.zeros_like(qg_s)
    for copy in first:
        copy.wait()
    for copy in second:
        copy.start()
    for pair in loads:
        for copy in pair:
            copy.start()
    last.start()

    spread = jnp.zeros((tokens, 1), F32)
    for r in range(count):
        teacher = maps_s[midx_ref[r]].astype(F32)
        valid = lax.broadcasted_iota(jnp.int32, teacher.shape, 1) < len_ref[r]
        teacher_log = jnp.log(teacher)
        teacher = jnp.where(valid, teacher, 0.0)
        teacher_total = jnp.sum(teacher, axis=-1, keepdims=True)
        teacher_prob = teacher / teacher_total
        gap = (teacher_log - jnp.log(teacher_total)) - log_s[r]
        spread += jnp.sum(jnp.where(valid, teacher_prob * gap, 0.0), axis=-1, keepdims=True)
        slope = ((prob_s[r] - teacher_prob) / (tokens * sharpness)).astype(BF16)
        up_s[pl.ds(r, seq, stride=count), :] = dot(slope, qunit_s[qidx_ref[r]], 0, 0).astype(BF16).astype(F32)
        un_s[r] = dot(slope, units_s[r], 1, 0)
    for r in range(count):
        qg_s[qidx_ref[r]] += un_s[r]
    total_eg = jnp.zeros((1, emb), F32)
    for copy in second:
        copy.wait()
    for b in range(0, total, thin):
        e = emb_s[b : b + thin]
        upstream = up_s[b : b + thin]
        length = jnp.sqrt(jnp.sum(e * e, axis=-1, keepdims=True) + epsilon)
        direction = e / length
        eg = (upstream - direction * jnp.sum(direction * upstream, axis=-1, keepdims=True)) / length
        eg = eg.astype(BF16)
        eg_s[b : b + thin] = eg
        eg = eg.astype(F32)
        total_eg += jnp.sum(eg, axis=0, keepdims=True)
        inverse = inv_s[b : b + thin]
        mean_s[b : b + thin] = inverse * (jnp.sum(eg * gain_w, axis=-1, keepdims=True) / width)
        along_s[b : b + thin] = inverse * (jnp.sum(eg * (e - bias_w), axis=-1, keepdims=True) / width)

    def wide(b):
        hg_s = hg_both.at[b // sub % 2]
        hg_s[...] = dot(eg_s[b : b + sub], wpt_ref[...], 1, 0)
        for c in range(b, b + sub, step):
            inverse, mean, along = inv_s[c : c + step], mean_s[c : c + step], along_s[c : c + step]
            for v in range(0, width, 128):
                scaled = hg_s[c - b : c - b + step, v : v + 128] * gain[:, v : v + 128]
                normed = normed_s[c : c + step, v : v + 128].astype(F32)
                sg_s[c : c + step, v : v + 128] = (inverse * scaled - mean - normed * along).astype(BF16)

    def products(b, part, parts):
        span = width // parts
        value = dot(x_s[b, part * span : (part + 1) * span], sg_s[b * rows : (b + 1) * rows], 1, 0)
        if b == 0:
            wo_s[part * span : (part + 1) * span] = value
        else:
            wo_s[part * span : (part + 1) * span] += value

    parts = 1
    stores = []
    for b in range(blocks):
        for copy in loads[b]:
            copy.wait()
        for n in range(rows // sub):
            wide(b * rows + n * sub)
            if b > 0 and n < parts:
                products(b - 1, n, parts)
        stores.append(
            pltpu.make_async_copy(
                sg_s.at[pl.ds(b * rows, rows)], sg_out.at[pl.ds(b * rows, rows)], out_sem.at[b]
            )
        )
        stores[-1].start()
        value = dot(eg_s[b * rows : (b + 1) * rows], normed_s[b * rows : (b + 1) * rows], 0, 0)
        if b == 0:
            nt_s[...] = value
        else:
            nt_s[...] += value
    for n in range(parts):
        products(blocks - 1, n, parts)

    last.wait()
    qg = qg_s[...].reshape(qdir_ref.shape)
    qdir = qdir_ref[...]
    qeg = (qg - qdir * jnp.sum(qdir * qg, axis=-1, keepdims=True)) / qlen_ref[:, :1]
    high = qeg.astype(BF16)
    low = (qeg - high.astype(F32)).astype(BF16)
    each = group_queries * tokens
    proj_query = jnp.zeros((emb, width), F32)
    for k in range(payload_s.shape[0]):
        qs = payload_s[k, :each]
        part = slice(k * each, (k + 1) * each)
        proj_query = proj_query + (dot(high[part], qs, 0, 0) + dot(low[part], qs, 0, 0))
    nt = nt_s[...]
    s = jnp.broadcast_to(total_eg, (emb, emb)).T[:, :1]
    wpt = wpt_ref[...].astype(F32)
    proj = nt * gain + s * bias + proj_query
    gain_row = jnp.sum(wpt * nt, axis=0, keepdims=True)
    bias_row = jnp.sum(wpt * s, axis=0, keepdims=True)
    index = lax.broadcasted_iota(jnp.int32, (tokens, width), 0)
    top = jnp.where(index == 0, gain_row, jnp.where(index == 1, bias_row, 0.0))
    rest_rows = jnp.zeros((128 - 2 * tokens, width), F32)
    right_s[...] = jnp.concatenate([proj, top, jnp.broadcast_to(spread, (tokens, width)), rest_rows], axis=0).T
    half = width // CORES
    chunk = send_ref.shape[1]
    for ref, which in ((send_ref, 1 - core_ref[0]), (keep_ref, core_ref[0])):
        start = pl.multiple_of(which * half, half)
        left = wo_s[pl.ds(start, half)].astype(BF16)
        right = right_s[pl.ds(start, half)].astype(BF16)
        for c in range(half // chunk):
            ref[c, :, :width] = left[c * chunk : (c + 1) * chunk]
            ref[c, :, width:] = right[c * chunk : (c + 1) * chunk]
    for copy in stores:
        copy.wait()


def student_backward(
    qidx, midx, lens, core, maps, scores, payload, embeds, x, normed, inverse, gain, bias, wp, wpt,
    count, tokens, group_queries, chunk,
):
    total, width = normed.shape
    emb = wp.shape[1]
    blocks = x.shape[0]
    sub = total // blocks
    chunks = width // CORES // chunk
    prob, log, units, qunit, qdir, qlen = scores
    manual = [maps, prob, log, units, qunit, embeds, x, normed, inverse, payload]
    packed = jax.ShapeDtypeStruct((chunks, chunk, width + emb + 128), BF16)
    return pl.pallas_call(
        functools.partial(backward_kernel, tokens, count, blocks, group_queries),
        in_specs=[SMEM] * 4 + [ANY] * len(manual) + [VMEM] * 6,
        out_specs=[ANY, VMEM, VMEM],
        scratch_shapes=[pltpu.VMEM(a.shape, a.dtype) for a in manual]
        + [
            pltpu.VMEM((total, emb), F32),
            pltpu.VMEM((total, emb), BF16),
            pltpu.VMEM((total, 128), F32),
            pltpu.VMEM((total, 128), F32),
            pltpu.VMEM((count, tokens, emb), F32),
            pltpu.VMEM(qunit.shape, F32),
            pltpu.VMEM((2, sub, width), F32),
            pltpu.VMEM((total, width), BF16),
            pltpu.VMEM((width, width), F32),
            pltpu.VMEM((emb, width), F32),
            pltpu.VMEM((width, emb + 128), F32),
            pltpu.SemaphoreType.DMA((7,)),
            pltpu.SemaphoreType.DMA((2 * blocks,)),
            pltpu.SemaphoreType.DMA((blocks,)),
            pltpu.SemaphoreType.DMA,
        ],
        out_shape=[jax.ShapeDtypeStruct((total, width), BF16), packed, packed],
        compiler_params=params(),
        cost_estimate=cost(2 * total * width * (width + 2 * emb), 8 * total * width),
        name="student_backward",
    )(qidx, midx, lens, core, *manual, qdir, qlen, gain, bias, wp, wpt)


def context_kernel(sg_ref, wo_ref, after_ref, out_ref, token_ref):
    token_ref[...] = jnp.zeros_like(token_ref)
    out_ref[...] = dot(sg_ref[...], wo_ref[...], 1, 0).astype(BF16)


def context_grad(sg, weight_turned, after):
    total, width = sg.shape
    rows = split_rows(total, 720)
    block = pl.BlockSpec((rows, width), lambda s: (s, 0))
    return pl.pallas_call(
        context_kernel,
        grid=(total // rows,),
        in_specs=[block, pl.BlockSpec(weight_turned.shape, lambda s: (0, 0)), ANY],
        out_specs=[block, pl.BlockSpec(TOKEN.shape, lambda s: (0, 0))],
        out_shape=[jax.ShapeDtypeStruct(sg.shape, BF16), TOKEN],
        compiler_params=params(),
        cost_estimate=cost(2 * total * width * width, 4 * total * width),
        name="context_grad",
    )(sg, weight_turned, after)


def split_sum_kernel(inputs, outputs, after, index_ref, *rest):
    ins, outs = rest[:inputs], rest[inputs + after : inputs + after + outputs]
    token_ref, total_s = rest[-2:]
    total = ins[0][...].astype(F32)
    for ref in ins[1:]:
        total = total + ref[...].astype(F32)
    total_s[...] = total.astype(BF16).reshape(total_s.shape)
    for k in range(outputs):
        outs[k][...] = total_s[index_ref[k]].reshape(outs[k].shape)
    token_ref[...] = jnp.zeros_like(token_ref)


def split_sum(arrays, index, name, after=()):
    outputs = index.shape[0]
    shape = arrays[0].shape
    lead = shape[0] // outputs
    out = shape[1:] if lead == 1 else (lead,) + shape[1:]
    *parts, token = pl.pallas_call(
        functools.partial(split_sum_kernel, len(arrays), outputs, len(after)),
        in_specs=[SMEM] + [VMEM] * len(arrays) + [ANY] * len(after),
        out_specs=[VMEM] * (outputs + 1),
        out_shape=[jax.ShapeDtypeStruct(out, BF16)] * outputs + [TOKEN],
        scratch_shapes=[pltpu.VMEM((outputs, lead) + shape[1:], BF16)],
        compiler_params=pltpu.CompilerParams(vmem_limit_bytes=SMALL_LIMIT),
        name=name,
    )(index, *arrays, *after)
    return parts, token


def sum_kernel(*refs):
    total = refs[0][...].astype(F32)
    for ref in refs[1:-1]:
        total = total + ref[...].astype(F32)
    refs[-1][...] = total.astype(BF16)


def plain_sum(arrays, name):
    return pl.pallas_call(
        sum_kernel,
        in_specs=[VMEM] * len(arrays),
        out_specs=VMEM,
        out_shape=jax.ShapeDtypeStruct(arrays[0].shape, BF16),
        compiler_params=pltpu.CompilerParams(vmem_limit_bytes=SMALL_LIMIT),
        name=name,
    )(*arrays)


def unpack_kernel(parts, width, emb, tokens, scale, index_ref, *rest):
    ins = rest[:parts]
    wo_ref, proj_ref, gain_ref, bias_ref, loss_ref, small_s = rest[parts:]
    per = ins[0].shape[0]
    for a in range(parts):
        for k in range(per):
            c = index_ref[a * per + k]
            value = ins[a][k].astype(F32)
            wo_ref[c] = value[:, :width]
            proj_ref[c] = value[:, width : width + emb]
            small_s[c] = value[:, width + emb :]
    turned = small_s[...].reshape(width, 128).T
    for v in range(width // 128):
        gain_ref[v : v + 1] = turned[0:1, v * 128 : (v + 1) * 128]
        bias_ref[v : v + 1] = turned[1:2, v * 128 : (v + 1) * 128]
    loss_ref[0] = jnp.sum(turned[tokens : 2 * tokens, 0:1]) * scale


def unpack(arrays, index, width, emb, tokens, scale):
    parts = len(arrays)
    per, chunk, _ = arrays[0].shape
    chunks = parts * per
    return pl.pallas_call(
        functools.partial(unpack_kernel, parts, width, emb, tokens, scale),
        in_specs=[SMEM] + [VMEM] * parts,
        out_specs=[VMEM] * 4 + [SMEM],
        out_shape=[jax.ShapeDtypeStruct((chunks, chunk, n), F32) for n in (width, emb)]
        + [jax.ShapeDtypeStruct((width // 128, 128), F32)] * 2
        + [jax.ShapeDtypeStruct((1,), F32)],
        scratch_shapes=[pltpu.VMEM((chunks, chunk, 128), F32)],
        compiler_params=pltpu.CompilerParams(vmem_limit_bytes=SMALL_LIMIT),
        name="unpack",
    )(index, *arrays)


def local(
    context,
    stream,
    out_weight,
    gain,
    bias,
    proj_weight,
    query_states,
    passage_len,
    passage_dest,
    teacher_states,
    teacher_query,
    teacher_key,
):
    dp = lax.axis_size("dp")
    nt = lax.axis_size("tensor")
    chips = dp // CORES
    me = lax.axis_index("dp")
    chip, core = me // CORES, me % CORES
    mt = lax.axis_index("tensor")
    count, seq, width = context.shape
    emb = proj_weight.shape[1]
    group_queries, tokens, _ = query_states.shape
    depth, heads = teacher_query.shape
    per = count // dp
    per_query = count * nt // group_queries

    def flat(a):
        return a.transpose(1, 0, 2).reshape(-1, a.shape[2])

    def shift_chip(x, k):
        return lax.ppermute(
            x, "dp", [(c * CORES + o, (c + k) % chips * CORES + o) for c in range(chips) for o in range(CORES)]
        )

    def swap_core(x):
        return lax.ppermute(x, "dp", [(d, d ^ 1) for d in range(dp)])

    def shift_t(x, k):
        return lax.ppermute(x, "tensor", [(t, (t + k) % nt) for t in range(nt)])

    dest_group = passage_dest // (count * nt)
    rows = jnp.arange(count, dtype=jnp.int32)
    rank = jnp.sum(
        (dest_group[:, None] == dest_group[None, :]) & (rows[None, :] < rows[:, None]), axis=1, dtype=jnp.int32
    )
    place = dest_group * per + rank
    positions = jnp.sum(
        jnp.where(place[:, None] == rows[None, :], (passage_dest % count)[:, None], 0), axis=0
    )
    queries = query_states.reshape(group_queries * tokens, width)
    extra = jnp.pad(positions.astype(BF16)[None, :], ((0, 15), (0, width - count)))
    payload = jnp.concatenate([queries, extra], axis=0)
    part = depth // dp
    mine = jnp.stack(
        [lax.dynamic_slice_in_dim(w, me * part, part, 0) for w in (teacher_query, teacher_key)]
    )
    payload, mine = lax.optimization_barrier((jnp.broadcast_to(payload[None], (dp,) + payload.shape), mine))
    payload = lax.all_to_all(payload, "dp", split_axis=0, concat_axis=0, tiled=True)
    along = jnp.concatenate([shift_t(mine, k) for k in range(1, nt)], axis=0)
    along, payload = lax.optimization_barrier((along, payload))
    pieces = [along] + [shift_chip(along, k) for k in range(1, chips)]
    shifts = jnp.arange(chips, dtype=jnp.int32)
    behind = (chip - shifts) % chips
    piece_rows = jnp.concatenate([behind * CORES + core, behind * CORES + 1 - core]).astype(jnp.int32)
    midx = place.astype(jnp.int32)
    qidx = (passage_dest // per_query).astype(jnp.int32)

    gain2, bias2 = gain.reshape(-1, 128), bias.reshape(-1, 128)
    x = flat(context)
    normed, embeds, inverse, turned = student_forward(x, flat(stream), out_weight, gain2, bias2, proj_weight)
    pieces[1:], payload, normed, embeds, inverse, turned, weight_turned, proj_turned = lax.optimization_barrier(
        (pieces[1:], payload, normed, embeds, inverse, turned, out_weight.T, proj_weight.T)
    )
    pieces = pieces + [swap_core(a) for a in pieces]
    told = payload[:, group_queries * tokens, :count].astype(jnp.int32)
    order = lax.dynamic_slice_in_dim(told, me * per, per, 1).reshape(-1)
    maps, token = teacher_maps(
        order, piece_rows, flat(teacher_states), teacher_query, teacher_key, pieces, count, tokens
    )
    maps = lax.all_to_all(maps, "dp", split_axis=0, concat_axis=0, tiled=True)
    scores = student_scores(qidx, passage_len, payload, embeds, proj_weight, token, count, tokens, group_queries)
    chunk = width // (CORES * chips * nt)
    sg, send, keep = student_backward(
        qidx, midx, passage_len, core.astype(jnp.int32).reshape(1), maps, scores, payload,
        embeds, turned, normed, inverse, gain2, bias2, proj_weight, proj_turned,
        count, tokens, group_queries, chunk,
    )

    ahead = ((chip + shifts) % chips).astype(jnp.int32)
    t_shifts = jnp.arange(nt, dtype=jnp.int32)
    t_ahead = ((mt + t_shifts) % nt).astype(jnp.int32)
    parts, token = split_sum([keep, swap_core(send)], ahead, "sum_cores")
    grad_context, token = context_grad(sg, weight_turned, token)
    parts = [parts[0]] + [shift_chip(parts[k], k) for k in range(1, chips)]
    parts, _ = split_sum(parts, t_ahead, "sum_plane", (token,))
    parts = [parts[0]] + [shift_t(parts[k], k) for k in range(1, nt)]
    total = plain_sum(parts, "sum_tensor")
    line = jnp.stack([total] + [shift_t(total, k) for k in range(1, nt)])
    plane = [line] + [shift_chip(line, k) for k in range(1, chips)]
    arrays = plane + [swap_core(a) for a in plane]
    base = jnp.concatenate([core * chips + behind, (1 - core) * chips + behind]) * nt
    index = (base[:, None] + ((mt - t_shifts) % nt)[None, :]).reshape(-1).astype(jnp.int32)
    grad_out, grad_proj, grad_gain, grad_bias, loss = unpack(
        arrays, index, width, emb, tokens, 1.0 / (count * dp * nt * tokens)
    )
    return (
        loss.reshape(()),
        grad_out.reshape(width, width),
        grad_proj.reshape(width, emb),
        grad_gain.reshape(width),
        grad_bias.reshape(width),
        grad_context.reshape(seq, count, width).transpose(1, 0, 2),
    )


def solution(mesh):
    return jax.shard_map(
        local,
        mesh=mesh,
        in_specs=(
            P(("dp", "tensor"), None, None),
            P(("dp", "tensor"), None, None),
            P(),
            P(),
            P(),
            P(),
            P("dp", None, None),
            P(("dp", "tensor")),
            P(("dp", "tensor")),
            P(("dp", "tensor"), None, None),
            P(None, "tensor"),
            P(None, "tensor"),
        ),
        out_specs=(P(), P(), P(), P(), P(), P(("dp", "tensor"), None, None)),
        check_vma=False,
    )
```

```python
import functools
import math

import jax
import jax.numpy as jnp
from jax import lax
from jax.experimental import pallas as pl
from jax.experimental.pallas import tpu as pltpu
from jax.sharding import PartitionSpec as P

sharpness = 0.05
softcap = 10.0
epsilon = 1e-06
CORES = 2
VMEM_LIMIT = 56 * 1024 * 1024
SMALL_LIMIT = 14 * 1024 * 1024

F32 = jnp.float32
BF16 = jnp.bfloat16
VMEM = pl.BlockSpec(memory_space=pltpu.VMEM)
SMEM = pl.BlockSpec(memory_space=pltpu.SMEM)
ANY = pl.BlockSpec(memory_space=pl.ANY)
TOKEN = jax.ShapeDtypeStruct((8, 128), F32)


def up(n, m):
    return -(-n // m) * m


def dot(a, b, ca, cb):
    return lax.dot_general(a, b, (((ca,), (cb,)), ((), ())), preferred_element_type=F32)


def split_rows(rows, most):
    return max(n for n in range(16, most + 1, 16) if rows % n == 0)


def loop(count, body):
    lax.fori_loop(0, count, lambda n, _: (body(n), 0)[1], 0)


def one_row(ref):
    return jnp.concatenate([ref[v : v + 1] for v in range(ref.shape[0])], axis=1)


def params(**kw):
    return pltpu.CompilerParams(vmem_limit_bytes=VMEM_LIMIT, **kw)


def cost(flops, nbytes):
    return pl.CostEstimate(flops=int(flops), bytes_accessed=int(nbytes), transcendentals=0)


def forward_kernel(x_ref, str_ref, wo_ref, gain_ref, bias_ref, wp_ref, normed_ref, emb_ref, inv_ref, turned_ref, prod_s, hid_s):
    rows, width = x_ref.shape
    sub = split_rows(rows, 256)
    thin = split_rows(sub, 48)
    gain, bias = one_row(gain_ref), one_row(bias_ref)

    def block(n):
        first = pl.multiple_of(n * sub, sub)
        part = pl.ds(first, sub)
        prod_s[...] = dot(x_ref[part], wo_ref[...], 1, 0)

        def chunk(c):
            inner = pl.ds(pl.multiple_of(c * thin, thin), thin)
            outer = pl.ds(pl.multiple_of(first + c * thin, thin), thin)
            summed = prod_s[inner] + str_ref[outer].astype(F32)
            centred = summed - jnp.mean(summed, axis=-1, keepdims=True)
            inverse = lax.rsqrt(jnp.mean(centred * centred, axis=-1, keepdims=True) + epsilon)
            normed = centred * inverse
            normed_ref[outer] = normed.astype(BF16)
            inv_ref[outer] = jnp.broadcast_to(inverse, (thin, inv_ref.shape[1]))
            hid_s[inner] = (normed * gain + bias).astype(BF16)

        loop(sub // thin, chunk)
        emb_ref[part] = dot(hid_s[...], wp_ref[...], 1, 0)

    loop(rows // sub, block)
    turned_ref[0] = x_ref[...].T


def student_forward(x, stream, out_weight, gain, bias, proj_weight):
    total, width = x.shape
    emb = proj_weight.shape[1]
    rows = split_rows(total, 720)
    sub = split_rows(rows, 256)
    block = lambda last: pl.BlockSpec((rows, last), lambda s: (s, 0))
    whole = lambda a: pl.BlockSpec(a.shape, lambda s: (0,) * a.ndim)
    return pl.pallas_call(
        forward_kernel,
        grid=(total // rows,),
        in_specs=[block(width), block(width)] + [whole(a) for a in (out_weight, gain, bias, proj_weight)],
        out_specs=[block(width), block(emb), block(128), pl.BlockSpec((1, width, rows), lambda s: (s, 0, 0))],
        out_shape=[
            jax.ShapeDtypeStruct((total, width), BF16),
            jax.ShapeDtypeStruct((total, emb), F32),
            jax.ShapeDtypeStruct((total, 128), F32),
            jax.ShapeDtypeStruct((total // rows, width, rows), BF16),
        ],
        scratch_shapes=[pltpu.VMEM((sub, width), F32), pltpu.VMEM((sub, width), BF16)],
        compiler_params=params(),
        cost_estimate=cost(2 * total * width * (width + emb), 8 * total * width),
        name="student_forward",
    )(x, stream, out_weight, gain, bias, proj_weight)


def teacher_kernel(parts, count, tokens, order_ref, rows_ref, states_ref, wq_ref, wk_ref, *rest):
    pieces, out_ref, token_ref = rest[:parts], rest[parts], rest[parts + 1]
    w_s, q_s, g_s, m_s, key_s, e_s, map_s, turned_s, q_sem, key_sem, w_sem, own_sem = rest[parts + 2 :]
    depth = q_s.shape[1]
    slices = w_s.shape[0] // 2
    others = pieces[0].shape[0]
    part_rows = pieces[0].shape[1]
    total = key_s.shape[0]
    seq = total // count
    blocks = key_sem.shape[0]
    rows = total // blocks
    first = count * tokens
    own = [
        pltpu.make_async_copy(wq_ref, w_s.at[others], own_sem.at[0]),
        pltpu.make_async_copy(wk_ref, w_s.at[others + 1], own_sem.at[1]),
    ]
    queries = pltpu.make_async_copy(states_ref.at[pl.ds(0, first)], q_s, q_sem)
    gathered = [
        pltpu.make_async_copy(
            pieces[a],
            w_s.at[pl.ds(0, others), pl.ds(pl.multiple_of(rows_ref[a] * part_rows, part_rows), part_rows), :],
            w_sem.at[a],
        )
        for a in range(parts)
    ]
    keys = [
        pltpu.make_async_copy(
            states_ref.at[pl.ds(first + b * rows, rows)], key_s.at[pl.ds(b * rows, rows)], key_sem.at[b]
        )
        for b in range(blocks)
    ]
    queries.start()
    for copy in own + gathered:
        copy.start()
    queries.wait()
    for copy in own + gathered:
        copy.wait()
    for copy in keys:
        copy.start()
    q = q_s[...]
    m_s[...] = jnp.zeros_like(m_s)

    def mix(k):
        m_s[...] += dot(dot(q, w_s[2 * k], 1, 0).astype(BF16), w_s[2 * k + 1], 1, 1)

    loop(slices, mix)
    for v in range(depth // 128):
        g_s[v] = m_s[:, v * 128 : (v + 1) * 128]

    def reorder(p):
        for v in range(depth // 128):
            q_s[pl.ds(pl.multiple_of(p * tokens, tokens), tokens), v * 128 : (v + 1) * 128] = g_s[
                v, pl.ds(p, tokens, stride=count), :
            ].astype(BF16)

    loop(count, reorder)
    turned_s[...] = q_s[...].T
    scale = 1.0 / (math.sqrt(depth) * softcap)
    side = 128 // tokens
    sub = split_rows(rows, 256)
    pair = lax.broadcasted_iota(jnp.int32, (sub, 128), 0) % count
    for copy in keys:
        copy.wait()

    def score(n):
        part = pl.ds(pl.multiple_of(n * sub, sub), sub)
        raw = dot(key_s[part], turned_s[...], 1, 0)
        mine = raw[:, :128]
        for v in range(1, count // side):
            mine = jnp.where(pair >= v * side, raw[:, v * 128 : (v + 1) * 128], mine)
        e_s[part] = jnp.exp(softcap * jnp.tanh(mine * scale))

    loop(total // sub, score)
    lane = lax.broadcasted_iota(jnp.int32, (seq, 128), 1) // tokens
    filler = jnp.zeros((up(seq, 128) - seq, 128), F32)

    def split(g):
        both = e_s[pl.ds(g * side, seq, stride=count), :]
        for v in range(1, side):
            both = jnp.where(lane == v, e_s[pl.ds(g * side + v, seq, stride=count), :], both)
        turned = jnp.concatenate([both, filler], axis=0).T
        for v in range(side):
            map_s[g * side + v] = turned[v * tokens : (v + 1) * tokens, :seq].astype(BF16)

    loop(count // side, split)

    def place(n):
        out_ref[n] = map_s[order_ref[n]]

    loop(count, place)
    token_ref[...] = jnp.zeros_like(token_ref)


def teacher_maps(order, rows, states, wq, wk, pieces, count, tokens):
    total, depth = states.shape
    keys = total - count * tokens
    heads = wq.shape[1]
    parts = len(pieces)
    slices = pieces[0].shape[0]
    blocks = keys // split_rows(keys, 720)
    return pl.pallas_call(
        functools.partial(teacher_kernel, parts, count, tokens),
        in_specs=[SMEM, SMEM] + [ANY] * (3 + parts),
        out_specs=[VMEM, VMEM],
        out_shape=[jax.ShapeDtypeStruct((count, tokens, keys // count), BF16), TOKEN],
        scratch_shapes=[
            pltpu.VMEM((slices + 2, depth, heads), BF16),
            pltpu.VMEM((count * tokens, depth), BF16),
            pltpu.VMEM((depth // 128, count * tokens, 128), F32),
            pltpu.VMEM((count * tokens, depth), F32),
            pltpu.VMEM((keys, depth), BF16),
            pltpu.VMEM((keys, 128), F32),
            pltpu.VMEM((count, tokens, keys // count), BF16),
            pltpu.VMEM((depth, count * tokens), BF16),
            pltpu.SemaphoreType.DMA,
            pltpu.SemaphoreType.DMA((blocks,)),
            pltpu.SemaphoreType.DMA((parts,)),
            pltpu.SemaphoreType.DMA((2,)),
        ],
        compiler_params=params(),
        cost_estimate=cost(8 * count * tokens * depth * depth, 2 * states.size + 4 * depth * depth),
        name="teacher_maps",
    )(order, rows, states, wq, wk, *pieces)


def scores_kernel(tokens, count, group_queries, qidx_ref, len_ref, payload_ref, emb_ref, wp_ref, after_ref,
                  prob_ref, log_ref, units_ref, qunit_ref, qdir_ref, qlen_ref, dir_s):
    total, emb = emb_ref.shape
    seq = total // count
    sub = split_rows(total, 128)
    qe = dot(payload_ref[...].reshape(-1, payload_ref.shape[2]), wp_ref[...], 1, 0)
    length = jnp.sqrt(jnp.sum(qe * qe, axis=-1, keepdims=True) + epsilon)
    qdir = qe / length
    qdir_ref[...] = qdir
    qlen_ref[...] = jnp.broadcast_to(length, qlen_ref.shape)
    qunit_ref[...] = qdir.astype(BF16).reshape(qunit_ref.shape)

    def direct(n):
        part = pl.ds(pl.multiple_of(n * sub, sub), sub)
        e = emb_ref[part]
        dir_s[part] = e / jnp.sqrt(jnp.sum(e * e, axis=-1, keepdims=True) + epsilon)

    loop(total // sub, direct)
    side = 4 if count % 4 == 0 else 1

    def score(n):
        for v in range(side):
            r = n * side + v
            units = dir_s[pl.ds(r, seq, stride=count), :].astype(BF16)
            units_ref[r] = units
            logits = dot(qunit_ref[qidx_ref[r]], units, 1, 1) / sharpness
            valid = lax.broadcasted_iota(jnp.int32, logits.shape, 1) < len_ref[r]
            student = jnp.where(valid, jnp.exp(logits), 0.0)
            student_total = jnp.sum(student, axis=-1, keepdims=True)
            prob_ref[r] = student / student_total
            log_ref[r] = logits - jnp.log(student_total)

    loop(count // side, score)


def student_scores(qidx, lens, payload, embeds, wp, after, count, tokens, group_queries):
    total, emb = embeds.shape
    seq = total // count
    queries = payload.shape[0] * group_queries
    return pl.pallas_call(
        functools.partial(scores_kernel, tokens, count, group_queries),
        in_specs=[SMEM, SMEM, VMEM, VMEM, VMEM, ANY],
        out_specs=[VMEM] * 6,
        out_shape=[
            jax.ShapeDtypeStruct((count, tokens, seq), F32),
            jax.ShapeDtypeStruct((count, tokens, seq), F32),
            jax.ShapeDtypeStruct((count, seq, emb), BF16),
            jax.ShapeDtypeStruct((queries, tokens, emb), BF16),
            jax.ShapeDtypeStruct((queries * tokens, emb), F32),
            jax.ShapeDtypeStruct((queries * tokens, 128), F32),
        ],
        scratch_shapes=[pltpu.VMEM((total, emb), F32)],
        compiler_params=params(),
        cost_estimate=cost(1e9, 4 * total * emb),
        name="student_scores",
    )(qidx, lens, payload, embeds, wp, after)


def two_parts(a, b):
    high = a.astype(BF16)
    low = (a - high.astype(F32)).astype(BF16)
    return dot(high, b, 1, 0) + dot(low, b, 1, 0)


def backward_kernel(
    tokens, count, blocks, group_queries,
    qidx_ref, midx_ref, len_ref, core_ref,
    maps_in, prob_in, log_in, units_in, qunit_in, emb_in, x_in, normed_in, inv_in, payload_in,
    qdir_ref, qlen_ref, gain_ref, bias_ref, wp_ref, wpt_ref,
    sg_out, send_ref, keep_ref,
    maps_s, prob_s, log_s, units_s, qunit_s, emb_s, x_s, normed_s, inv_s, payload_s,
    up_s, eg_s, mean_s, along_s, un_s, qg_s, hg_s, sg_s, wo_s, nt_s, right_s,
    first_sem, block_sem, out_sem, last_sem,
):
    total, width = normed_s.shape
    emb = emb_s.shape[1]
    seq = total // count
    rows = total // blocks
    sub = split_rows(rows, 256)
    thin = split_rows(total, 128)
    step = split_rows(sub, 48)
    first = [
        pltpu.make_async_copy(src, dst, first_sem.at[n])
        for n, (src, dst) in enumerate(
            (
                (qunit_in, qunit_s), (maps_in, maps_s), (prob_in, prob_s), (log_in, log_s), (units_in, units_s),
                (emb_in, emb_s), (inv_in, inv_s),
            )
        )
    ]
    first, second = first[:5], first[5:]
    loads = [
        [
            pltpu.make_async_copy(
                normed_in.at[pl.ds(b * rows, rows)], normed_s.at[pl.ds(b * rows, rows)], block_sem.at[2 * b]
            ),
            pltpu.make_async_copy(x_in.at[b], x_s.at[b], block_sem.at[2 * b + 1]),
        ]
        for b in range(blocks)
    ]
    last = pltpu.make_async_copy(payload_in, payload_s, last_sem)
    for copy in first:
        copy.start()
    gain, bias = one_row(gain_ref), one_row(bias_ref)
    gain_w = two_parts(gain, wp_ref[...])
    bias_w = two_parts(bias, wp_ref[...])
    qg_s[...] = jnp.zeros_like(qg_s)
    for copy in first:
        copy.wait()
    for copy in second:
        copy.start()
    for pair in loads:
        for copy in pair:
            copy.start()
    last.start()

    side = 4 if count % 4 == 0 else 1

    def score(n, spread):
        for v in range(side):
            r = n * side + v
            teacher = maps_s[midx_ref[r]].astype(F32)
            valid = lax.broadcasted_iota(jnp.int32, teacher.shape, 1) < len_ref[r]
            teacher_log = jnp.log(teacher)
            teacher = jnp.where(valid, teacher, 0.0)
            teacher_total = jnp.sum(teacher, axis=-1, keepdims=True)
            teacher_prob = teacher / teacher_total
            gap = (teacher_log - jnp.log(teacher_total)) - log_s[r]
            spread += jnp.sum(jnp.where(valid, teacher_prob * gap, 0.0), axis=-1, keepdims=True)
            slope = ((prob_s[r] - teacher_prob) / (tokens * sharpness)).astype(BF16)
            up_s[pl.ds(r, seq, stride=count), :] = dot(slope, qunit_s[qidx_ref[r]], 0, 0).astype(BF16).astype(F32)
            un_s[r] = dot(slope, units_s[r], 1, 0)
        return spread

    spread = lax.fori_loop(0, count // side, score, jnp.zeros((tokens, 1), F32))

    def gather(r):
        qg_s[qidx_ref[r]] += un_s[r]

    loop(count, gather)
    for copy in second:
        copy.wait()

    def narrow(n, total_eg):
        part = pl.ds(pl.multiple_of(n * thin, thin), thin)
        e = emb_s[part]
        upstream = up_s[part]
        length = jnp.sqrt(jnp.sum(e * e, axis=-1, keepdims=True) + epsilon)
        direction = e / length
        eg = (upstream - direction * jnp.sum(direction * upstream, axis=-1, keepdims=True)) / length
        eg = eg.astype(BF16)
        eg_s[part] = eg
        eg = eg.astype(F32)
        inverse = inv_s[part]
        mean_s[part] = inverse * (jnp.sum(eg * gain_w, axis=-1, keepdims=True) / width)
        along_s[part] = inverse * (jnp.sum(eg * (e - bias_w), axis=-1, keepdims=True) / width)
        return total_eg + jnp.sum(eg, axis=0, keepdims=True)

    total_eg = lax.fori_loop(0, total // thin, narrow, jnp.zeros((1, emb), F32))
    wo_s[...] = jnp.zeros_like(wo_s)
    nt_s[...] = jnp.zeros_like(nt_s)

    def wide(b):
        base = pl.multiple_of(b * rows, rows)
        pltpu.make_async_copy(normed_in.at[pl.ds(base, rows)], normed_s.at[pl.ds(base, rows)], block_sem.at[2 * b]).wait()

        def piece(n):
            first = pl.multiple_of(base + n * sub, sub)
            hg_s[...] = dot(eg_s[pl.ds(first, sub)], wpt_ref[...], 1, 0)

            def chunk(c):
                inner = pl.ds(pl.multiple_of(c * step, step), step)
                outer = pl.ds(pl.multiple_of(first + c * step, step), step)
                inverse, mean, along = inv_s[outer], mean_s[outer], along_s[outer]
                for v in range(0, width, 128):
                    scaled = hg_s[inner, v : v + 128] * gain[:, v : v + 128]
                    normed = normed_s[outer, v : v + 128].astype(F32)
                    sg_s[outer, v : v + 128] = (inverse * scaled - mean - normed * along).astype(BF16)

            loop(sub // step, chunk)

        loop(rows // sub, piece)
        part = pl.ds(base, rows)
        pltpu.make_async_copy(sg_s.at[part], sg_out.at[part], out_sem.at[b]).start()
        pltpu.make_async_copy(x_in.at[b], x_s.at[b], block_sem.at[2 * b + 1]).wait()
        wo_s[...] += dot(x_s[b], sg_s[part], 1, 0)
        nt_s[...] += dot(eg_s[part], normed_s[part], 0, 0)

    loop(blocks, wide)

    last.wait()
    qg = qg_s[...].reshape(qdir_ref.shape)
    qdir = qdir_ref[...]
    qeg = (qg - qdir * jnp.sum(qdir * qg, axis=-1, keepdims=True)) / qlen_ref[:, :1]
    high = qeg.astype(BF16)
    low = (qeg - high.astype(F32)).astype(BF16)
    qs = payload_s[...].reshape(-1, width)
    proj_query = dot(high, qs, 0, 0) + dot(low, qs, 0, 0)
    nt = nt_s[...]
    s = jnp.broadcast_to(total_eg, (emb, emb)).T[:, :1]
    wpt = wpt_ref[...].astype(F32)
    proj = nt * gain + s * bias + proj_query
    gain_row = jnp.sum(wpt * nt, axis=0, keepdims=True)
    bias_row = jnp.sum(wpt * s, axis=0, keepdims=True)
    index = lax.broadcasted_iota(jnp.int32, (tokens, width), 0)
    top = jnp.where(index == 0, gain_row, jnp.where(index == 1, bias_row, 0.0))
    rest_rows = jnp.zeros((128 - 2 * tokens, width), F32)
    right_s[...] = jnp.concatenate([proj, top, jnp.broadcast_to(spread, (tokens, width)), rest_rows], axis=0).T
    half = width // CORES
    chunk = send_ref.shape[1]
    for ref, which in ((send_ref, 1 - core_ref[0]), (keep_ref, core_ref[0])):
        start = pl.multiple_of(which * half, half)
        left = wo_s[pl.ds(start, half)].astype(BF16)
        right = right_s[pl.ds(start, half)].astype(BF16)
        for c in range(half // chunk):
            ref[c, :, :width] = left[c * chunk : (c + 1) * chunk]
            ref[c, :, width:] = right[c * chunk : (c + 1) * chunk]
    for b in range(blocks):
        part = pl.ds(b * rows, rows)
        pltpu.make_async_copy(sg_s.at[part], sg_out.at[part], out_sem.at[b]).wait()


def student_backward(
    qidx, midx, lens, core, maps, scores, payload, embeds, x, normed, inverse, gain, bias, wp, wpt,
    count, tokens, group_queries, chunk,
):
    total, width = normed.shape
    emb = wp.shape[1]
    blocks = x.shape[0]
    sub = split_rows(total // blocks, 256)
    chunks = width // CORES // chunk
    prob, log, units, qunit, qdir, qlen = scores
    manual = [maps, prob, log, units, qunit, embeds, x, normed, inverse, payload]
    packed = jax.ShapeDtypeStruct((chunks, chunk, width + emb + 128), BF16)
    return pl.pallas_call(
        functools.partial(backward_kernel, tokens, count, blocks, group_queries),
        in_specs=[SMEM] * 4 + [ANY] * len(manual) + [VMEM] * 6,
        out_specs=[ANY, VMEM, VMEM],
        scratch_shapes=[pltpu.VMEM(a.shape, a.dtype) for a in manual]
        + [
            pltpu.VMEM((total, emb), F32),
            pltpu.VMEM((total, emb), BF16),
            pltpu.VMEM((total, 128), F32),
            pltpu.VMEM((total, 128), F32),
            pltpu.VMEM((count, tokens, emb), F32),
            pltpu.VMEM(qunit.shape, F32),
            pltpu.VMEM((sub, width), F32),
            pltpu.VMEM((total, width), BF16),
            pltpu.VMEM((width, width), F32),
            pltpu.VMEM((emb, width), F32),
            pltpu.VMEM((width, emb + 128), F32),
            pltpu.SemaphoreType.DMA((7,)),
            pltpu.SemaphoreType.DMA((2 * blocks,)),
            pltpu.SemaphoreType.DMA((blocks,)),
            pltpu.SemaphoreType.DMA,
        ],
        out_shape=[jax.ShapeDtypeStruct((total, width), BF16), packed, packed],
        compiler_params=params(),
        cost_estimate=cost(2 * total * width * (width + 2 * emb), 8 * total * width),
        name="student_backward",
    )(qidx, midx, lens, core, *manual, qdir, qlen, gain, bias, wp, wpt)


def context_kernel(sg_ref, wo_ref, after_ref, out_ref, token_ref):
    token_ref[...] = jnp.zeros_like(token_ref)
    sub = split_rows(sg_ref.shape[0], 256)

    def block(n):
        part = pl.ds(pl.multiple_of(n * sub, sub), sub)
        out_ref[part] = dot(sg_ref[part], wo_ref[...], 1, 0).astype(BF16)

    loop(sg_ref.shape[0] // sub, block)


def context_grad(sg, weight_turned, after):
    total, width = sg.shape
    rows = split_rows(total, 720)
    block = pl.BlockSpec((rows, width), lambda s: (s, 0))
    return pl.pallas_call(
        context_kernel,
        grid=(total // rows,),
        in_specs=[block, pl.BlockSpec(weight_turned.shape, lambda s: (0, 0)), ANY],
        out_specs=[block, pl.BlockSpec(TOKEN.shape, lambda s: (0, 0))],
        out_shape=[jax.ShapeDtypeStruct(sg.shape, BF16), TOKEN],
        compiler_params=params(),
        cost_estimate=cost(2 * total * width * width, 4 * total * width),
        name="context_grad",
    )(sg, weight_turned, after)


def split_sum_kernel(inputs, outputs, after, index_ref, *rest):
    ins, outs = rest[:inputs], rest[inputs + after : inputs + after + outputs]
    token_ref, total_s = rest[-2:]
    total = ins[0][...].astype(F32)
    for ref in ins[1:]:
        total = total + ref[...].astype(F32)
    total_s[...] = total.astype(BF16).reshape(total_s.shape)
    for k in range(outputs):
        outs[k][...] = total_s[index_ref[k]].reshape(outs[k].shape)
    token_ref[...] = jnp.zeros_like(token_ref)


def split_sum(arrays, index, name, after=()):
    outputs = index.shape[0]
    shape = arrays[0].shape
    lead = shape[0] // outputs
    out = shape[1:] if lead == 1 else (lead,) + shape[1:]
    *parts, token = pl.pallas_call(
        functools.partial(split_sum_kernel, len(arrays), outputs, len(after)),
        in_specs=[SMEM] + [VMEM] * len(arrays) + [ANY] * len(after),
        out_specs=[VMEM] * (outputs + 1),
        out_shape=[jax.ShapeDtypeStruct(out, BF16)] * outputs + [TOKEN],
        scratch_shapes=[pltpu.VMEM((outputs, lead) + shape[1:], BF16)],
        compiler_params=pltpu.CompilerParams(vmem_limit_bytes=SMALL_LIMIT),
        name=name,
    )(index, *arrays, *after)
    return parts, token


def sum_kernel(*refs):
    total = refs[0][...].astype(F32)
    for ref in refs[1:-1]:
        total = total + ref[...].astype(F32)
    refs[-1][...] = total.astype(BF16)


def plain_sum(arrays, name):
    return pl.pallas_call(
        sum_kernel,
        in_specs=[VMEM] * len(arrays),
        out_specs=VMEM,
        out_shape=jax.ShapeDtypeStruct(arrays[0].shape, BF16),
        compiler_params=pltpu.CompilerParams(vmem_limit_bytes=SMALL_LIMIT),
        name=name,
    )(*arrays)


def unpack_kernel(parts, width, emb, tokens, scale, index_ref, *rest):
    ins = rest[:parts]
    wo_ref, proj_ref, gain_ref, bias_ref, loss_ref, small_s = rest[parts:]
    per = ins[0].shape[0]
    for a in range(parts):
        for k in range(per):
            c = index_ref[a * per + k]
            value = ins[a][k].astype(F32)
            wo_ref[c] = value[:, :width]
            proj_ref[c] = value[:, width : width + emb]
            small_s[c] = value[:, width + emb :]
    turned = small_s[...].reshape(width, 128).T
    for v in range(width // 128):
        gain_ref[v : v + 1] = turned[0:1, v * 128 : (v + 1) * 128]
        bias_ref[v : v + 1] = turned[1:2, v * 128 : (v + 1) * 128]
    loss_ref[0] = jnp.sum(turned[tokens : 2 * tokens, 0:1]) * scale


def unpack(arrays, index, width, emb, tokens, scale):
    parts = len(arrays)
    per, chunk, _ = arrays[0].shape
    chunks = parts * per
    return pl.pallas_call(
        functools.partial(unpack_kernel, parts, width, emb, tokens, scale),
        in_specs=[SMEM] + [VMEM] * parts,
        out_specs=[VMEM] * 4 + [SMEM],
        out_shape=[jax.ShapeDtypeStruct((chunks, chunk, n), F32) for n in (width, emb)]
        + [jax.ShapeDtypeStruct((width // 128, 128), F32)] * 2
        + [jax.ShapeDtypeStruct((1,), F32)],
        scratch_shapes=[pltpu.VMEM((chunks, chunk, 128), F32)],
        compiler_params=pltpu.CompilerParams(vmem_limit_bytes=SMALL_LIMIT),
        name="unpack",
    )(index, *arrays)


def local(
    context,
    stream,
    out_weight,
    gain,
    bias,
    proj_weight,
    query_states,
    passage_len,
    passage_dest,
    teacher_states,
    teacher_query,
    teacher_key,
):
    dp = lax.axis_size("dp")
    nt = lax.axis_size("tensor")
    chips = dp // CORES
    me = lax.axis_index("dp")
    chip, core = me // CORES, me % CORES
    mt = lax.axis_index("tensor")
    count, seq, width = context.shape
    emb = proj_weight.shape[1]
    group_queries, tokens, _ = query_states.shape
    depth, heads = teacher_query.shape
    per = count // dp
    per_query = count * nt // group_queries

    def flat(a):
        return a.transpose(1, 0, 2).reshape(-1, a.shape[2])

    def shift_chip(x, k):
        return lax.ppermute(
            x, "dp", [(c * CORES + o, (c + k) % chips * CORES + o) for c in range(chips) for o in range(CORES)]
        )

    def swap_core(x):
        return lax.ppermute(x, "dp", [(d, d ^ 1) for d in range(dp)])

    def shift_t(x, k):
        return lax.ppermute(x, "tensor", [(t, (t + k) % nt) for t in range(nt)])

    dest_group = passage_dest // (count * nt)
    rows = jnp.arange(count, dtype=jnp.int32)
    rank = jnp.sum(
        (dest_group[:, None] == dest_group[None, :]) & (rows[None, :] < rows[:, None]), axis=1, dtype=jnp.int32
    )
    place = dest_group * per + rank
    positions = jnp.sum(
        jnp.where(place[:, None] == rows[None, :], (passage_dest % count)[:, None], 0), axis=0
    )
    positions = positions.astype(jnp.int32).reshape(dp, per)
    part = depth // dp
    mine = jnp.stack(
        [lax.dynamic_slice_in_dim(w, me * part, part, 0) for w in (teacher_query, teacher_key)]
    )
    along = jnp.concatenate([shift_t(mine, k) for k in range(1, nt)], axis=0)
    order = lax.all_to_all(positions, "dp", split_axis=0, concat_axis=0, tiled=True).reshape(-1)
    along, order = lax.optimization_barrier((along, order))
    pieces = [along] + [shift_chip(along, k) for k in range(1, chips)]
    shifts = jnp.arange(chips, dtype=jnp.int32)
    behind = (chip - shifts) % chips
    piece_rows = jnp.concatenate([behind * CORES + core, behind * CORES + 1 - core]).astype(jnp.int32)
    midx = place.astype(jnp.int32)
    qidx = (passage_dest // per_query).astype(jnp.int32)

    gain2, bias2 = gain.reshape(-1, 128), bias.reshape(-1, 128)
    x = flat(context)
    normed, embeds, inverse, turned = student_forward(x, flat(stream), out_weight, gain2, bias2, proj_weight)
    payload = jnp.broadcast_to(query_states.reshape(1, -1, width), (dp, group_queries * tokens, width))
    pieces[1:], payload, normed, embeds, inverse, turned, weight_turned, proj_turned = lax.optimization_barrier(
        (pieces[1:], payload, normed, embeds, inverse, turned, out_weight.T, proj_weight.T)
    )
    pieces = pieces + [swap_core(a) for a in pieces]
    payload = lax.all_to_all(payload, "dp", split_axis=0, concat_axis=0, tiled=True)
    maps, token = teacher_maps(
        order, piece_rows, flat(teacher_states), teacher_query, teacher_key, pieces, count, tokens
    )
    maps = lax.all_to_all(maps, "dp", split_axis=0, concat_axis=0, tiled=True)
    scores = student_scores(qidx, passage_len, payload, embeds, proj_weight, token, count, tokens, group_queries)
    chunk = width // (CORES * chips * nt)
    sg, send, keep = student_backward(
        qidx, midx, passage_len, core.astype(jnp.int32).reshape(1), maps, scores, payload,
        embeds, turned, normed, inverse, gain2, bias2, proj_weight, proj_turned,
        count, tokens, group_queries, chunk,
    )

    ahead = ((chip + shifts) % chips).astype(jnp.int32)
    t_shifts = jnp.arange(nt, dtype=jnp.int32)
    t_ahead = ((mt + t_shifts) % nt).astype(jnp.int32)
    parts, token = split_sum([keep, swap_core(send)], ahead, "sum_cores")
    grad_context, token = context_grad(sg, weight_turned, token)
    parts = [parts[0]] + [shift_chip(parts[k], k) for k in range(1, chips)]
    parts, _ = split_sum(parts, t_ahead, "sum_plane", (token,))
    parts = [parts[0]] + [shift_t(parts[k], k) for k in range(1, nt)]
    total = plain_sum(parts, "sum_tensor")
    line = jnp.stack([total] + [shift_t(total, k) for k in range(1, nt)])
    plane = [line] + [shift_chip(line, k) for k in range(1, chips)]
    arrays = plane + [swap_core(a) for a in plane]
    base = jnp.concatenate([core * chips + behind, (1 - core) * chips + behind]) * nt
    index = (base[:, None] + ((mt - t_shifts) % nt)[None, :]).reshape(-1).astype(jnp.int32)
    grad_out, grad_proj, grad_gain, grad_bias, loss = unpack(
        arrays, index, width, emb, tokens, 1.0 / (count * dp * nt * tokens)
    )
    return (
        loss.reshape(()),
        grad_out.reshape(width, width),
        grad_proj.reshape(width, emb),
        grad_gain.reshape(width),
        grad_bias.reshape(width),
        grad_context.reshape(seq, count, width).transpose(1, 0, 2),
    )


def solution(mesh):
    return jax.shard_map(
        local,
        mesh=mesh,
        in_specs=(
            P(("dp", "tensor"), None, None),
            P(("dp", "tensor"), None, None),
            P(),
            P(),
            P(),
            P(),
            P("dp", None, None),
            P(("dp", "tensor")),
            P(("dp", "tensor")),
            P(("dp", "tensor"), None, None),
            P(None, "tensor"),
            P(None, "tensor"),
        ),
        out_specs=(P(), P(), P(), P(), P(), P(("dp", "tensor"), None, None)),
        check_vma=False,
    )
```

```python
import functools
import math

import jax
import jax.numpy as jnp
from jax import lax
from jax.experimental import pallas as pl
from jax.experimental.pallas import tpu as pltpu
from jax.sharding import PartitionSpec as P

sharpness = 0.05
softcap = 10.0
epsilon = 1e-06
CORES = 2
VMEM_LIMIT = 56 * 1024 * 1024
SMALL_LIMIT = 14 * 1024 * 1024
BACKWARD_LIMIT = 46 * 1024 * 1024

F32 = jnp.float32
BF16 = jnp.bfloat16
VMEM = pl.BlockSpec(memory_space=pltpu.VMEM)
SMEM = pl.BlockSpec(memory_space=pltpu.SMEM)
ANY = pl.BlockSpec(memory_space=pl.ANY)
TOKEN = jax.ShapeDtypeStruct((8, 128), F32)


def up(n, m):
    return -(-n // m) * m


def dot(a, b, ca, cb):
    return lax.dot_general(a, b, (((ca,), (cb,)), ((), ())), preferred_element_type=F32)


def split_rows(rows, most):
    return max(n for n in range(16, most + 1, 16) if rows % n == 0)


def one_row(ref):
    return jnp.concatenate([ref[v : v + 1] for v in range(ref.shape[0])], axis=1)


def params(**kw):
    return pltpu.CompilerParams(vmem_limit_bytes=VMEM_LIMIT, **kw)


def cost(flops, nbytes):
    return pl.CostEstimate(flops=int(flops), bytes_accessed=int(nbytes), transcendentals=0)


def forward_kernel(x_ref, str_ref, wo_ref, gain_ref, bias_ref, wp_ref, normed_ref, emb_ref, inv_ref, turned_ref, prod_s, hid_s):
    rows, width = x_ref.shape
    sub = rows
    gain, bias = one_row(gain_ref), one_row(bias_ref)
    for b in range(0, rows, sub):
        prod_s[b : b + sub] = dot(x_ref[b : b + sub], wo_ref[...], 1, 0)
        for c in range(b, b + sub, 16):
            summed = prod_s[c : c + 16] + str_ref[c : c + 16].astype(F32)
            centred = summed - jnp.mean(summed, axis=-1, keepdims=True)
            inverse = lax.rsqrt(jnp.mean(centred * centred, axis=-1, keepdims=True) + epsilon)
            normed = centred * inverse
            normed_ref[c : c + 16] = normed.astype(BF16)
            inv_ref[c : c + 16] = jnp.broadcast_to(inverse, (16, inv_ref.shape[1]))
            hid_s[c : c + 16] = (normed * gain + bias).astype(BF16)
        emb_ref[b : b + sub] = dot(hid_s[b : b + sub], wp_ref[...], 1, 0)
    turned_ref[0] = x_ref[...].T


def student_forward(x, stream, out_weight, gain, bias, proj_weight):
    total, width = x.shape
    emb = proj_weight.shape[1]
    rows = split_rows(total, 720)
    block = lambda last: pl.BlockSpec((rows, last), lambda s: (s, 0))
    whole = lambda a: pl.BlockSpec(a.shape, lambda s: (0,) * a.ndim)
    return pl.pallas_call(
        forward_kernel,
        grid=(total // rows,),
        in_specs=[block(width), block(width)] + [whole(a) for a in (out_weight, gain, bias, proj_weight)],
        out_specs=[block(width), block(emb), block(128), pl.BlockSpec((1, width, rows), lambda s: (s, 0, 0))],
        out_shape=[
            jax.ShapeDtypeStruct((total, width), BF16),
            jax.ShapeDtypeStruct((total, emb), F32),
            jax.ShapeDtypeStruct((total, 128), F32),
            jax.ShapeDtypeStruct((total // rows, width, rows), BF16),
        ],
        scratch_shapes=[pltpu.VMEM((rows, width), F32), pltpu.VMEM((rows, width), BF16)],
        compiler_params=params(),
        cost_estimate=cost(2 * total * width * (width + emb), 8 * total * width),
        name="student_forward",
    )(x, stream, out_weight, gain, bias, proj_weight)


def teacher_kernel(parts, count, tokens, order_ref, from_ref, rows_ref, states_ref, wq_ref, wk_ref, *rest):
    pieces, out_ref, token_ref = rest[:parts], rest[parts], rest[parts + 1]
    w_s, own_s, q_s, g_s, key_s, e_s, map_s, q_sem, key_sem, w_sem, own_sem = rest[parts + 2 :]
    depth = q_s.shape[1]
    slices = w_s.shape[0] // 2
    part_rows = pieces[0].shape[1]
    total = key_s.shape[0]
    seq = total // count
    blocks = key_sem.shape[0]
    rows = total // blocks
    first = count * tokens
    own = [
        pltpu.make_async_copy(wq_ref, own_s.at[0], own_sem.at[0]),
        pltpu.make_async_copy(wk_ref, own_s.at[1], own_sem.at[1]),
    ]
    queries = pltpu.make_async_copy(states_ref.at[pl.ds(0, first)], q_s, q_sem)
    gathered = [
        pltpu.make_async_copy(
            pieces[a].at[pl.ds(0, w_s.shape[0])],
            w_s.at[:, pl.ds(pl.multiple_of(rows_ref[a] * part_rows, part_rows), part_rows), :],
            w_sem.at[a],
        )
        for a in range(parts)
    ]
    keys = [
        pltpu.make_async_copy(
            states_ref.at[pl.ds(first + b * rows, rows)], key_s.at[pl.ds(b * rows, rows)], key_sem.at[b]
        )
        for b in range(blocks)
    ]
    queries.start()
    for copy in own + gathered:
        copy.start()
    queries.wait()
    for copy in own:
        copy.wait()
    for copy in keys:
        copy.start()
    q = q_s[...]
    mixed = dot(dot(q, own_s[0], 1, 0).astype(BF16), own_s[1], 1, 1)
    for copy in gathered:
        copy.wait()
    for k in range(slices):
        mixed = mixed + dot(dot(q, w_s[2 * k], 1, 0).astype(BF16), w_s[2 * k + 1], 1, 1)
    for v in range(depth // 128):
        g_s[v] = mixed[:, v * 128 : (v + 1) * 128]
        for p in range(count):
            q_s[p * tokens : (p + 1) * tokens, v * 128 : (v + 1) * 128] = g_s[
                v, pl.ds(p, tokens, stride=count), :
            ].astype(BF16)
    mixed = q_s[...].T
    scale = 1.0 / (math.sqrt(depth) * softcap)
    side = 128 // tokens
    pair = lax.broadcasted_iota(jnp.int32, (rows, 128), 0) % count
    for b in range(blocks):
        keys[b].wait()
        raw = dot(key_s[b * rows : (b + 1) * rows], mixed, 1, 0)
        mine = raw[:, :128]
        for v in range(1, count // side):
            mine = jnp.where(pair >= v * side, raw[:, v * 128 : (v + 1) * 128], mine)
        e_s[b * rows : (b + 1) * rows] = jnp.exp(softcap * jnp.tanh(mine * scale))
    lane = lax.broadcasted_iota(jnp.int32, (seq, 128), 1) // tokens
    filler = jnp.zeros((up(seq, 128) - seq, 128), F32)
    for g in range(count // side):
        both = e_s[pl.ds(g * side, seq, stride=count), :]
        for v in range(1, side):
            both = jnp.where(lane == v, e_s[pl.ds(g * side + v, seq, stride=count), :], both)
        turned = jnp.concatenate([both, filler], axis=0).T
        for v in range(side):
            map_s[g * side + v] = turned[v * tokens : (v + 1) * tokens, :seq].astype(BF16)
    per = count // parts
    for n in range(count):
        out_ref[n] = map_s[order_ref[from_ref[n // per], n % per]]
    token_ref[...] = jnp.zeros_like(token_ref)


def teacher_maps(order, source, rows, slices, states, wq, wk, pieces, count, tokens):
    total, depth = states.shape
    keys = total - count * tokens
    heads = wq.shape[1]
    parts = len(pieces)
    blocks = keys // split_rows(keys, 720)
    return pl.pallas_call(
        functools.partial(teacher_kernel, parts, count, tokens),
        in_specs=[SMEM] * 3 + [ANY] * (3 + parts),
        out_specs=[VMEM, VMEM],
        out_shape=[jax.ShapeDtypeStruct((count, tokens, keys // count), BF16), TOKEN],
        scratch_shapes=[
            pltpu.VMEM((slices, depth, heads), BF16),
            pltpu.VMEM((2, depth, heads), BF16),
            pltpu.VMEM((count * tokens, depth), BF16),
            pltpu.VMEM((depth // 128, count * tokens, 128), F32),
            pltpu.VMEM((keys, depth), BF16),
            pltpu.VMEM((keys, 128), F32),
            pltpu.VMEM((count, tokens, keys // count), BF16),
            pltpu.SemaphoreType.DMA,
            pltpu.SemaphoreType.DMA((blocks,)),
            pltpu.SemaphoreType.DMA((parts,)),
            pltpu.SemaphoreType.DMA((2,)),
        ],
        compiler_params=params(),
        cost_estimate=cost(8 * count * tokens * depth * depth, 2 * states.size + 4 * depth * depth),
        name="teacher_maps",
    )(order, source, rows, states, wq, wk, *pieces)


def rider_copies(pieces, slices, held, sem):
    part = pieces[0].shape[1]
    return [
        pltpu.make_async_copy(
            pieces[a].at[slices + x], held.at[a, pl.ds(x * part, part)], sem.at[a * (pieces[0].shape[0] - slices) + x]
        )
        for a in range(len(pieces))
        for x in range(pieces[0].shape[0] - slices)
    ]


def rider_states(held, a, each, width):
    heads = held.shape[2]
    return jnp.concatenate([held[a, n * each : (n + 1) * each] for n in range(width // heads)], axis=1)


def scores_kernel(tokens, count, group_queries, slices, parts, qidx_ref, len_ref, emb_ref, wp_ref, after_ref, *rest):
    pieces = rest[:parts]
    (prob_ref, log_ref, units_ref, qunit_ref, qdir_ref, qlen_ref, qs_s, dir_s, held_s, sem) = rest[parts:]
    copies = rider_copies(pieces, slices, held_s, sem)
    for copy in copies:
        copy.start()
    total, emb = emb_ref.shape
    seq = total // count
    sub = split_rows(total, 128)
    each = group_queries * tokens
    for copy in copies:
        copy.wait()
    for a in range(parts):
        qs_s[a * each : (a + 1) * each] = rider_states(held_s, a, each, qs_s.shape[1])
    qe = dot(qs_s[...], wp_ref[...], 1, 0)
    length = jnp.sqrt(jnp.sum(qe * qe, axis=-1, keepdims=True) + epsilon)
    qdir = qe / length
    qdir_ref[...] = qdir
    qlen_ref[...] = jnp.broadcast_to(length, qlen_ref.shape)
    qunit_ref[...] = qdir.astype(BF16).reshape(qunit_ref.shape)
    for b in range(0, total, sub):
        e = emb_ref[b : b + sub]
        dir_s[b : b + sub] = e / jnp.sqrt(jnp.sum(e * e, axis=-1, keepdims=True) + epsilon)
    for r in range(count):
        units = dir_s[pl.ds(r, seq, stride=count), :].astype(BF16)
        units_ref[r] = units
        logits = dot(qunit_ref[qidx_ref[r]], units, 1, 1) / sharpness
        valid = lax.broadcasted_iota(jnp.int32, logits.shape, 1) < len_ref[r]
        student = jnp.where(valid, jnp.exp(logits), 0.0)
        student_total = jnp.sum(student, axis=-1, keepdims=True)
        prob_ref[r] = student / student_total
        log_ref[r] = logits - jnp.log(student_total)


def student_scores(qidx, lens, embeds, wp, after, pieces, slices, count, tokens, group_queries):
    total, emb = embeds.shape
    seq = total // count
    parts = len(pieces)
    queries = parts * group_queries
    riders, part, heads = pieces[0].shape
    riders -= slices
    return pl.pallas_call(
        functools.partial(scores_kernel, tokens, count, group_queries, slices, parts),
        in_specs=[SMEM, SMEM, VMEM, VMEM] + [ANY] * (1 + parts),
        out_specs=[VMEM] * 6,
        out_shape=[
            jax.ShapeDtypeStruct((count, tokens, seq), F32),
            jax.ShapeDtypeStruct((count, tokens, seq), F32),
            jax.ShapeDtypeStruct((count, seq, emb), BF16),
            jax.ShapeDtypeStruct((queries, tokens, emb), BF16),
            jax.ShapeDtypeStruct((queries * tokens, emb), F32),
            jax.ShapeDtypeStruct((queries * tokens, 128), F32),
        ],
        scratch_shapes=[
            pltpu.VMEM((queries * tokens, wp.shape[0]), BF16),
            pltpu.VMEM((total, emb), F32),
            pltpu.VMEM((parts, riders * part, heads), BF16),
            pltpu.SemaphoreType.DMA((parts * riders,)),
        ],
        compiler_params=params(),
        cost_estimate=cost(1e9, 4 * total * emb),
        name="student_scores",
    )(qidx, lens, embeds, wp, after, *pieces)


def two_parts(a, b):
    high = a.astype(BF16)
    low = (a - high.astype(F32)).astype(BF16)
    return dot(high, b, 1, 0) + dot(low, b, 1, 0)


def backward_kernel(
    tokens, count, blocks, group_queries, slices, parts,
    qidx_ref, midx_ref, len_ref, core_ref, *rest,
):
    pieces = rest[:parts]
    (maps_in, prob_in, log_in, units_in, qunit_in, emb_in, x_in, normed_in, inv_in,
    qdir_ref, qlen_ref, gain_ref, bias_ref, wp_ref, wpt_ref,
    sg_out, send_ref, keep_ref,
    maps_s, prob_s, log_s, units_s, qunit_s, emb_s, x_s, normed_s, inv_s, held_s,
    up_s, eg_s, mean_s, along_s, un_s, qg_s, hg_s, sg_s, wo_s, nt_s, right_s,
    first_sem, block_sem, out_sem, last_sem) = rest[parts:]
    total, width = normed_s.shape
    emb = emb_s.shape[1]
    seq = total // count
    rows = total // blocks
    sub = split_rows(rows, 256)
    thin = split_rows(total, 128)
    first = [
        pltpu.make_async_copy(src, dst, first_sem.at[n])
        for n, (src, dst) in enumerate(
            (
                (qunit_in, qunit_s), (maps_in, maps_s), (prob_in, prob_s), (log_in, log_s), (units_in, units_s),
                (emb_in, emb_s), (inv_in, inv_s),
            )
        )
    ]
    first, second = first[:5], first[5:]
    loads = [
        [
            pltpu.make_async_copy(
                normed_in.at[pl.ds(b * rows, rows)], normed_s.at[pl.ds(b * rows, rows)], block_sem.at[2 * b]
            ),
            pltpu.make_async_copy(x_in.at[b], x_s.at[b], block_sem.at[2 * b + 1]),
        ]
        for b in range(blocks)
    ]
    last = rider_copies(pieces, slices, held_s, last_sem)
    for copy in first:
        copy.start()
    gain, bias = one_row(gain_ref), one_row(bias_ref)
    gain_w = two_parts(gain, wp_ref[...])
    bias_w = two_parts(bias, wp_ref[...])
    qg_s[...] = jnp.zeros_like(qg_s)
    for copy in first:
        copy.wait()
    for copy in second:
        copy.start()
    for pair in loads:
        for copy in pair:
            copy.start()
    for copy in last:
        copy.start()

    spread = jnp.zeros((tokens, 1), F32)
    for r in range(count):
        teacher = maps_s[midx_ref[r]].astype(F32)
        valid = lax.broadcasted_iota(jnp.int32, teacher.shape, 1) < len_ref[r]
        teacher_log = jnp.log(teacher)
        teacher = jnp.where(valid, teacher, 0.0)
        teacher_total = jnp.sum(teacher, axis=-1, keepdims=True)
        teacher_prob = teacher / teacher_total
        gap = (teacher_log - jnp.log(teacher_total)) - log_s[r]
        spread += jnp.sum(jnp.where(valid, teacher_prob * gap, 0.0), axis=-1, keepdims=True)
        slope = ((prob_s[r] - teacher_prob) / (tokens * sharpness)).astype(BF16)
        up_s[pl.ds(r, seq, stride=count), :] = dot(slope, qunit_s[qidx_ref[r]], 0, 0).astype(BF16).astype(F32)
        un_s[r] = dot(slope, units_s[r], 1, 0)
    for r in range(count):
        qg_s[qidx_ref[r]] += un_s[r]
    total_eg = jnp.zeros((1, emb), F32)
    for copy in second:
        copy.wait()
    for b in range(0, total, thin):
        e = emb_s[b : b + thin]
        upstream = up_s[b : b + thin]
        length = jnp.sqrt(jnp.sum(e * e, axis=-1, keepdims=True) + epsilon)
        direction = e / length
        eg = (upstream - direction * jnp.sum(direction * upstream, axis=-1, keepdims=True)) / length
        eg = eg.astype(BF16)
        eg_s[b : b + thin] = eg
        eg = eg.astype(F32)
        total_eg += jnp.sum(eg, axis=0, keepdims=True)
        inverse = inv_s[b : b + thin]
        mean_s[b : b + thin] = inverse * (jnp.sum(eg * gain_w, axis=-1, keepdims=True) / width)
        along_s[b : b + thin] = inverse * (jnp.sum(eg * (e - bias_w), axis=-1, keepdims=True) / width)

    wo_s[...] = jnp.zeros_like(wo_s)
    nt_s[...] = jnp.zeros_like(nt_s)

    def wide(b, _):
        base = pl.multiple_of(b * rows, rows)
        part = pl.ds(base, rows)
        pltpu.make_async_copy(normed_in.at[part], normed_s.at[part], block_sem.at[2 * b]).wait()
        for n in range(0, rows, sub):
            hg_s[n : n + sub] = dot(eg_s[pl.ds(base + n, sub)], wpt_ref[...], 1, 0)
            for c in range(n, n + sub, 16):
                here = pl.ds(base + c, 16)
                inverse, mean, along = inv_s[here], mean_s[here], along_s[here]
                for v in range(0, width, 128):
                    scaled = hg_s[c : c + 16, v : v + 128] * gain[:, v : v + 128]
                    normed = normed_s[here, v : v + 128].astype(F32)
                    sg_s[here, v : v + 128] = (inverse * scaled - mean - normed * along).astype(BF16)
        pltpu.make_async_copy(sg_s.at[part], sg_out.at[part], out_sem.at[b]).start()
        pltpu.make_async_copy(x_in.at[b], x_s.at[b], block_sem.at[2 * b + 1]).wait()
        wo_s[...] += dot(x_s[b], sg_s[part], 1, 0)
        nt_s[...] += dot(eg_s[part], normed_s[part], 0, 0)
        return 0

    lax.fori_loop(0, blocks, wide, 0)

    for copy in last:
        copy.wait()
    qg = qg_s[...].reshape(qdir_ref.shape)
    qdir = qdir_ref[...]
    qeg = (qg - qdir * jnp.sum(qdir * qg, axis=-1, keepdims=True)) / qlen_ref[:, :1]
    high = qeg.astype(BF16)
    low = (qeg - high.astype(F32)).astype(BF16)
    each = group_queries * tokens
    proj_query = jnp.zeros((emb, width), F32)
    for k in range(parts):
        qs = rider_states(held_s, k, each, width)
        part = slice(k * each, (k + 1) * each)
        proj_query = proj_query + (dot(high[part], qs, 0, 0) + dot(low[part], qs, 0, 0))
    nt = nt_s[...]
    s = jnp.broadcast_to(total_eg, (emb, emb)).T[:, :1]
    wpt = wpt_ref[...].astype(F32)
    proj = nt * gain + s * bias + proj_query
    gain_row = jnp.sum(wpt * nt, axis=0, keepdims=True)
    bias_row = jnp.sum(wpt * s, axis=0, keepdims=True)
    index = lax.broadcasted_iota(jnp.int32, (tokens, width), 0)
    top = jnp.where(index == 0, gain_row, jnp.where(index == 1, bias_row, 0.0))
    rest_rows = jnp.zeros((128 - 2 * tokens, width), F32)
    right_s[...] = jnp.concatenate([proj, top, jnp.broadcast_to(spread, (tokens, width)), rest_rows], axis=0).T
    half = width // CORES
    chunk = send_ref.shape[1]
    for ref, which in ((send_ref, 1 - core_ref[0]), (keep_ref, core_ref[0])):
        start = pl.multiple_of(which * half, half)
        left = wo_s[pl.ds(start, half)].astype(BF16)
        right = right_s[pl.ds(start, half)].astype(BF16)
        for c in range(half // chunk):
            ref[c, :, :width] = left[c * chunk : (c + 1) * chunk]
            ref[c, :, width:] = right[c * chunk : (c + 1) * chunk]
    for b in range(blocks):
        part = pl.ds(b * rows, rows)
        pltpu.make_async_copy(sg_s.at[part], sg_out.at[part], out_sem.at[b]).wait()


def student_backward(
    qidx, midx, lens, core, maps, scores, pieces, slices, embeds, x, normed, inverse, gain, bias, wp, wpt,
    count, tokens, group_queries, chunk,
):
    total, width = normed.shape
    emb = wp.shape[1]
    blocks = x.shape[0]
    chunks = width // CORES // chunk
    prob, log, units, qunit, qdir, qlen = scores
    manual = [maps, prob, log, units, qunit, embeds, x, normed, inverse]
    parts = len(pieces)
    riders, part, heads = pieces[0].shape
    riders -= slices
    packed = jax.ShapeDtypeStruct((chunks, chunk, width + emb + 128), BF16)
    return pl.pallas_call(
        functools.partial(backward_kernel, tokens, count, blocks, group_queries, slices, parts),
        in_specs=[SMEM] * 4 + [ANY] * (parts + len(manual)) + [VMEM] * 6,
        out_specs=[ANY, VMEM, VMEM],
        scratch_shapes=[pltpu.VMEM(a.shape, a.dtype) for a in manual]
        + [
            pltpu.VMEM((parts, riders * part, heads), BF16),
            pltpu.VMEM((total, emb), F32),
            pltpu.VMEM((total, emb), BF16),
            pltpu.VMEM((total, 128), F32),
            pltpu.VMEM((total, 128), F32),
            pltpu.VMEM((count, tokens, emb), F32),
            pltpu.VMEM(qunit.shape, F32),
            pltpu.VMEM((total // blocks, width), F32),
            pltpu.VMEM((total, width), BF16),
            pltpu.VMEM((width, width), F32),
            pltpu.VMEM((emb, width), F32),
            pltpu.VMEM((width, emb + 128), F32),
            pltpu.SemaphoreType.DMA((7,)),
            pltpu.SemaphoreType.DMA((2 * blocks,)),
            pltpu.SemaphoreType.DMA((blocks,)),
            pltpu.SemaphoreType.DMA((parts * riders,)),
        ],
        out_shape=[jax.ShapeDtypeStruct((total, width), BF16), packed, packed],
        compiler_params=pltpu.CompilerParams(vmem_limit_bytes=BACKWARD_LIMIT),
        cost_estimate=cost(2 * total * width * (width + 2 * emb), 8 * total * width),
        name="student_backward",
    )(qidx, midx, lens, core, *pieces, *manual, qdir, qlen, gain, bias, wp, wpt)


def context_kernel(sg_ref, wo_ref, after_ref, out_ref, token_ref):
    token_ref[...] = jnp.zeros_like(token_ref)
    out_ref[...] = dot(sg_ref[...], wo_ref[...], 1, 1).astype(BF16)


def context_grad(sg, out_weight, after):
    total, width = sg.shape
    rows = split_rows(total, 720)
    block = pl.BlockSpec((rows, width), lambda s: (s, 0))
    return pl.pallas_call(
        context_kernel,
        grid=(total // rows,),
        in_specs=[block, pl.BlockSpec(out_weight.shape, lambda s: (0, 0)), ANY],
        out_specs=[block, pl.BlockSpec(TOKEN.shape, lambda s: (0, 0))],
        out_shape=[jax.ShapeDtypeStruct(sg.shape, BF16), TOKEN],
        compiler_params=params(),
        cost_estimate=cost(2 * total * width * width, 4 * total * width),
        name="context_grad",
    )(sg, out_weight, after)


def split_sum_kernel(inputs, outputs, after, index_ref, *rest):
    ins, outs = rest[:inputs], rest[inputs + after : inputs + after + outputs]
    token_ref, total_s = rest[-2:]
    total = ins[0][...].astype(F32)
    for ref in ins[1:]:
        total = total + ref[...].astype(F32)
    total_s[...] = total.astype(BF16).reshape(total_s.shape)
    for k in range(outputs):
        outs[k][...] = total_s[index_ref[k]].reshape(outs[k].shape)
    token_ref[...] = jnp.zeros_like(token_ref)


def split_sum(arrays, index, name, after=()):
    outputs = index.shape[0]
    shape = arrays[0].shape
    lead = shape[0] // outputs
    out = shape[1:] if lead == 1 else (lead,) + shape[1:]
    *parts, token = pl.pallas_call(
        functools.partial(split_sum_kernel, len(arrays), outputs, len(after)),
        in_specs=[SMEM] + [VMEM] * len(arrays) + [ANY] * len(after),
        out_specs=[VMEM] * (outputs + 1),
        out_shape=[jax.ShapeDtypeStruct(out, BF16)] * outputs + [TOKEN],
        scratch_shapes=[pltpu.VMEM((outputs, lead) + shape[1:], BF16)],
        compiler_params=pltpu.CompilerParams(vmem_limit_bytes=SMALL_LIMIT),
        name=name,
    )(index, *arrays, *after)
    return parts, token


def sum_kernel(*refs):
    total = refs[0][...].astype(F32)
    for ref in refs[1:-1]:
        total = total + ref[...].astype(F32)
    refs[-1][...] = total.astype(BF16)


def plain_sum(arrays, name):
    return pl.pallas_call(
        sum_kernel,
        in_specs=[VMEM] * len(arrays),
        out_specs=VMEM,
        out_shape=jax.ShapeDtypeStruct(arrays[0].shape, BF16),
        compiler_params=pltpu.CompilerParams(vmem_limit_bytes=SMALL_LIMIT),
        name=name,
    )(*arrays)


def unpack_kernel(parts, width, emb, tokens, scale, index_ref, *rest):
    ins = rest[:parts]
    wo_ref, proj_ref, gain_ref, bias_ref, loss_ref, small_s = rest[parts:]
    per = ins[0].shape[0]
    for a in range(parts):
        for k in range(per):
            c = index_ref[a * per + k]
            value = ins[a][k].astype(F32)
            wo_ref[c] = value[:, :width]
            proj_ref[c] = value[:, width : width + emb]
            small_s[c] = value[:, width + emb :]
    turned = small_s[...].reshape(width, 128).T
    for v in range(width // 128):
        gain_ref[v : v + 1] = turned[0:1, v * 128 : (v + 1) * 128]
        bias_ref[v : v + 1] = turned[1:2, v * 128 : (v + 1) * 128]
    loss_ref[0] = jnp.sum(turned[tokens : 2 * tokens, 0:1]) * scale


def unpack(arrays, index, width, emb, tokens, scale):
    parts = len(arrays)
    per, chunk, _ = arrays[0].shape
    chunks = parts * per
    return pl.pallas_call(
        functools.partial(unpack_kernel, parts, width, emb, tokens, scale),
        in_specs=[SMEM] + [VMEM] * parts,
        out_specs=[VMEM] * 4 + [SMEM],
        out_shape=[jax.ShapeDtypeStruct((chunks, chunk, n), F32) for n in (width, emb)]
        + [jax.ShapeDtypeStruct((width // 128, 128), F32)] * 2
        + [jax.ShapeDtypeStruct((1,), F32)],
        scratch_shapes=[pltpu.VMEM((chunks, chunk, 128), F32)],
        compiler_params=pltpu.CompilerParams(vmem_limit_bytes=SMALL_LIMIT),
        name="unpack",
    )(index, *arrays)


def local(
    context,
    stream,
    out_weight,
    gain,
    bias,
    proj_weight,
    query_states,
    passage_len,
    passage_dest,
    teacher_states,
    teacher_query,
    teacher_key,
):
    dp = lax.axis_size("dp")
    nt = lax.axis_size("tensor")
    chips = dp // CORES
    me = lax.axis_index("dp")
    chip, core = me // CORES, me % CORES
    mt = lax.axis_index("tensor")
    count, seq, width = context.shape
    emb = proj_weight.shape[1]
    group_queries, tokens, _ = query_states.shape
    depth, heads = teacher_query.shape
    per = count // dp
    per_query = count * nt // group_queries

    def flat(a):
        return a.transpose(1, 0, 2).reshape(-1, a.shape[2])

    def shift_chip(x, k):
        return lax.ppermute(
            x, "dp", [(c * CORES + o, (c + k) % chips * CORES + o) for c in range(chips) for o in range(CORES)]
        )

    def swap_core(x):
        return lax.ppermute(x, "dp", [(d, d ^ 1) for d in range(dp)])

    def shift_t(x, k):
        return lax.ppermute(x, "tensor", [(t, (t + k) % nt) for t in range(nt)])

    dest_group = passage_dest // (count * nt)
    rows = jnp.arange(count, dtype=jnp.int32)
    rank = jnp.sum(
        (dest_group[:, None] == dest_group[None, :]) & (rows[None, :] < rows[:, None]), axis=1, dtype=jnp.int32
    )
    place = dest_group * per + rank
    positions = jnp.sum(
        jnp.where(place[:, None] == rows[None, :], (passage_dest % count)[:, None], 0), axis=0
    )
    each = group_queries * tokens
    states = query_states.reshape(each, width)
    column_blocks = [states[:, n * heads : (n + 1) * heads] for n in range(width // heads)]
    extra = jnp.pad(positions.astype(BF16)[None, :], ((0, 15), (0, heads - count)))
    rider = jnp.concatenate(column_blocks + [extra], axis=0)

    part = depth // dp
    mine = jnp.stack(
        [lax.dynamic_slice_in_dim(w, me * part, part, 0) for w in (teacher_query, teacher_key)]
    )
    rider = jnp.pad(rider, ((0, -rider.shape[0] % part), (0, 0))).reshape(-1, part, heads)
    slices = 2 * (nt - 1)
    along = jnp.concatenate([shift_t(mine, k) for k in range(1, nt)] + [rider], axis=0)
    pieces = [along] + [shift_chip(along, k) for k in range(1, chips)]
    shifts = jnp.arange(chips, dtype=jnp.int32)
    behind = (chip - shifts) % chips
    piece_rows = jnp.concatenate([behind * CORES + core, behind * CORES + 1 - core]).astype(jnp.int32)
    midx = place.astype(jnp.int32)
    def piece_of(group):
        return (chip - group // CORES) % chips + jnp.where(group % CORES == core, 0, chips)

    qidx = passage_dest // per_query - dest_group * group_queries + piece_of(dest_group) * group_queries
    qidx = qidx.astype(jnp.int32)
    source = piece_of(jnp.arange(dp, dtype=jnp.int32)).astype(jnp.int32)

    gain2, bias2 = gain.reshape(-1, 128), bias.reshape(-1, 128)
    x = flat(context)
    normed, embeds, inverse, turned = student_forward(x, flat(stream), out_weight, gain2, bias2, proj_weight)
    pieces[1:], normed, embeds, inverse, turned, proj_turned = lax.optimization_barrier(
        (pieces[1:], normed, embeds, inverse, turned, proj_weight.T)
    )
    pieces = pieces + [swap_core(a) for a in pieces]
    told = [a[slices:].reshape(-1, heads)[width // heads * each, :count] for a in pieces]
    order = lax.dynamic_slice_in_dim(jnp.stack(told), me * per, per, 1).astype(jnp.int32)
    maps, token = teacher_maps(
        order, source, piece_rows, slices, flat(teacher_states), teacher_query, teacher_key, pieces, count, tokens
    )
    maps = lax.all_to_all(maps, "dp", split_axis=0, concat_axis=0, tiled=True)
    scores = student_scores(
        qidx, passage_len, embeds, proj_weight, token, pieces, slices, count, tokens, group_queries
    )
    chunk = width // (CORES * chips * nt)
    sg, send, keep = student_backward(
        qidx, midx, passage_len, core.astype(jnp.int32).reshape(1), maps, scores, pieces, slices,
        embeds, turned, normed, inverse, gain2, bias2, proj_weight, proj_turned,
        count, tokens, group_queries, chunk,
    )

    ahead = ((chip + shifts) % chips).astype(jnp.int32)
    t_shifts = jnp.arange(nt, dtype=jnp.int32)
    t_ahead = ((mt + t_shifts) % nt).astype(jnp.int32)
    parts, token = split_sum([keep, swap_core(send)], ahead, "sum_cores")
    grad_context, token = context_grad(sg, out_weight, token)
    parts = [parts[0]] + [shift_chip(parts[k], k) for k in range(1, chips)]
    parts, _ = split_sum(parts, t_ahead, "sum_plane", (token,))
    parts = [parts[0]] + [shift_t(parts[k], k) for k in range(1, nt)]
    total = plain_sum(parts, "sum_tensor")
    line = jnp.stack([total] + [shift_t(total, k) for k in range(1, nt)])
    plane = [line] + [shift_chip(line, k) for k in range(1, chips)]
    arrays = plane + [swap_core(a) for a in plane]
    base = jnp.concatenate([core * chips + behind, (1 - core) * chips + behind]) * nt
    index = (base[:, None] + ((mt - t_shifts) % nt)[None, :]).reshape(-1).astype(jnp.int32)
    grad_out, grad_proj, grad_gain, grad_bias, loss = unpack(
        arrays, index, width, emb, tokens, 1.0 / (count * dp * nt * tokens)
    )
    return (
        loss.reshape(()),
        grad_out.reshape(width, width),
        grad_proj.reshape(width, emb),
        grad_gain.reshape(width),
        grad_bias.reshape(width),
        grad_context.reshape(seq, count, width).transpose(1, 0, 2),
    )


def solution(mesh):
    return jax.shard_map(
        local,
        mesh=mesh,
        in_specs=(
            P(("dp", "tensor"), None, None),
            P(("dp", "tensor"), None, None),
            P(),
            P(),
            P(),
            P(),
            P("dp", None, None),
            P(("dp", "tensor")),
            P(("dp", "tensor")),
            P(("dp", "tensor"), None, None),
            P(None, "tensor"),
            P(None, "tensor"),
        ),
        out_specs=(P(), P(), P(), P(), P(), P(("dp", "tensor"), None, None)),
        check_vma=False,
    )
```

```python
import functools
import math

import jax
import jax.numpy as jnp
from jax import lax
from jax.experimental import pallas as pl
from jax.experimental.pallas import tpu as pltpu
from jax.sharding import PartitionSpec as P

sharpness = 0.05
softcap = 10.0
epsilon = 1e-06
CORES = 2
VMEM_LIMIT = 56 * 1024 * 1024
SMALL_LIMIT = 14 * 1024 * 1024

F32 = jnp.float32
BF16 = jnp.bfloat16
VMEM = pl.BlockSpec(memory_space=pltpu.VMEM)
SMEM = pl.BlockSpec(memory_space=pltpu.SMEM)
ANY = pl.BlockSpec(memory_space=pl.ANY)


def up(n, m):
    return -(-n // m) * m


def dot(a, b, ca, cb):
    return lax.dot_general(a, b, (((ca,), (cb,)), ((), ())), preferred_element_type=F32)


def split_rows(rows, most):
    return max(n for n in range(16, most + 1, 16) if rows % n == 0)


def one_row(ref):
    return jnp.concatenate([ref[v : v + 1] for v in range(ref.shape[0])], axis=1)


def params(**kw):
    return pltpu.CompilerParams(vmem_limit_bytes=VMEM_LIMIT, **kw)


def cost(flops, nbytes):
    return pl.CostEstimate(flops=int(flops), bytes_accessed=int(nbytes), transcendentals=0)


def forward_kernel(x_ref, str_ref, wo_ref, gain_ref, bias_ref, wp_ref, normed_ref, emb_ref, inv_ref, turned_ref, prod_s, hid_s):
    rows, width = x_ref.shape
    sub = rows
    gain, bias = one_row(gain_ref), one_row(bias_ref)
    for b in range(0, rows, sub):
        prod_s[b : b + sub] = dot(x_ref[b : b + sub], wo_ref[...], 1, 0)
        for c in range(b, b + sub, 16):
            summed = prod_s[c : c + 16] + str_ref[c : c + 16].astype(F32)
            centred = summed - jnp.mean(summed, axis=-1, keepdims=True)
            inverse = lax.rsqrt(jnp.mean(centred * centred, axis=-1, keepdims=True) + epsilon)
            normed = centred * inverse
            normed_ref[c : c + 16] = normed.astype(BF16)
            inv_ref[c : c + 16] = jnp.broadcast_to(inverse, (16, inv_ref.shape[1]))
            hid_s[c : c + 16] = (normed * gain + bias).astype(BF16)
        emb_ref[b : b + sub] = dot(hid_s[b : b + sub], wp_ref[...], 1, 0)
    turned_ref[0] = x_ref[...].T


def student_forward(x, stream, out_weight, gain, bias, proj_weight):
    total, width = x.shape
    emb = proj_weight.shape[1]
    rows = split_rows(total, 720)
    block = lambda last: pl.BlockSpec((rows, last), lambda s: (s, 0))
    whole = lambda a: pl.BlockSpec(a.shape, lambda s: (0,) * a.ndim)
    return pl.pallas_call(
        forward_kernel,
        grid=(total // rows,),
        in_specs=[block(width), block(width)] + [whole(a) for a in (out_weight, gain, bias, proj_weight)],
        out_specs=[block(width), block(emb), block(128), pl.BlockSpec((1, width, rows), lambda s: (s, 0, 0))],
        out_shape=[
            jax.ShapeDtypeStruct((total, width), BF16),
            jax.ShapeDtypeStruct((total, emb), F32),
            jax.ShapeDtypeStruct((total, 128), F32),
            jax.ShapeDtypeStruct((total // rows, width, rows), BF16),
        ],
        scratch_shapes=[pltpu.VMEM((rows, width), F32), pltpu.VMEM((rows, width), BF16)],
        compiler_params=params(),
        cost_estimate=cost(2 * total * width * (width + emb), 8 * total * width),
        name="student_forward",
    )(x, stream, out_weight, gain, bias, proj_weight)


def pair_keys_kernel(count, tokens, states_ref, out_ref, wide_s):
    total = wide_s.shape[0]
    first = count * tokens
    sub = split_rows(total, 256)
    for b in range(0, total, sub):
        wide_s[b : b + sub] = states_ref[first + b : first + b + sub].astype(F32)
    for p in range(count):
        out_ref[p] = wide_s[pl.ds(p, total // count, stride=count), :].astype(BF16)


def pair_keys(states, count, tokens):
    total, depth = states.shape
    keys = total - count * tokens
    return pl.pallas_call(
        functools.partial(pair_keys_kernel, count, tokens),
        grid=(depth // 128,),
        in_specs=[pl.BlockSpec((total, 128), lambda s: (0, s))],
        out_specs=pl.BlockSpec((count, keys // count, 128), lambda s: (0, 0, s)),
        out_shape=jax.ShapeDtypeStruct((count, keys // count, depth), BF16),
        scratch_shapes=[pltpu.VMEM((keys, 128), F32)],
        compiler_params=params(),
        cost_estimate=cost(1e9, 4 * states.size),
        name="pair_keys",
    )(states)


def teacher_kernel(parts, count, tokens, order_ref, from_ref, rows_ref, states_ref, keys_ref, wq_ref, wk_ref, *rest):
    pieces, out_ref = rest[:parts], rest[parts]
    w_s, own_s, q_s, g_s, key_s, map_s, q_sem, key_sem, w_sem, own_sem = rest[parts + 1 :]
    depth = q_s.shape[1]
    slices = w_s.shape[0] // 2
    part_rows = pieces[0].shape[1]
    seq = key_s.shape[1]
    first = count * tokens
    own = [
        pltpu.make_async_copy(wq_ref, own_s.at[0], own_sem.at[0]),
        pltpu.make_async_copy(wk_ref, own_s.at[1], own_sem.at[1]),
    ]
    queries = pltpu.make_async_copy(states_ref.at[pl.ds(0, first)], q_s, q_sem)
    gathered = [
        pltpu.make_async_copy(
            pieces[a].at[pl.ds(0, w_s.shape[0])],
            w_s.at[:, pl.ds(pl.multiple_of(rows_ref[a] * part_rows, part_rows), part_rows), :],
            w_sem.at[a],
        )
        for a in range(parts)
    ]
    keys = [pltpu.make_async_copy(keys_ref.at[p], key_s.at[p], key_sem.at[p]) for p in range(count)]
    queries.start()
    for copy in own + gathered:
        copy.start()
    queries.wait()
    for copy in own:
        copy.wait()
    for copy in keys:
        copy.start()
    q = q_s[...]
    mixed = dot(dot(q, own_s[0], 1, 0).astype(BF16), own_s[1], 1, 1)
    for copy in gathered:
        copy.wait()
    for k in range(slices):
        mixed = mixed + dot(dot(q, w_s[2 * k], 1, 0).astype(BF16), w_s[2 * k + 1], 1, 1)
    for v in range(depth // 128):
        g_s[v] = mixed[:, v * 128 : (v + 1) * 128]
        for p in range(count):
            q_s[p * tokens : (p + 1) * tokens, v * 128 : (v + 1) * 128] = g_s[
                v, pl.ds(p, tokens, stride=count), :
            ].astype(BF16)
    mixed = q_s[...].T
    scale = 1.0 / (math.sqrt(depth) * softcap)
    side = 128 // tokens
    lane = lax.broadcasted_iota(jnp.int32, (seq, 128), 1) // tokens
    filler = jnp.zeros((up(seq, 128) - seq, 128), F32)
    for g in range(count // side):
        both = None
        for v in range(side):
            keys[g * side + v].wait()
            raw = dot(key_s[g * side + v], mixed[:, g * 128 : (g + 1) * 128], 1, 0)
            both = raw if both is None else jnp.where(lane == v, raw, both)
        both = jnp.exp(softcap * jnp.tanh(both * scale))
        turned = jnp.concatenate([both, filler], axis=0).T
        for v in range(side):
            map_s[g * side + v] = turned[v * tokens : (v + 1) * tokens, :seq].astype(BF16)
    per = count // parts
    for n in range(count):
        out_ref[n] = map_s[order_ref[from_ref[n // per], n % per]]


def teacher_maps(order, source, rows, slices, states, keys, wq, wk, pieces, count, tokens):
    depth = states.shape[1]
    seq = keys.shape[1]
    heads = wq.shape[1]
    parts = len(pieces)
    return pl.pallas_call(
        functools.partial(teacher_kernel, parts, count, tokens),
        in_specs=[SMEM] * 3 + [ANY] * (4 + parts),
        out_specs=VMEM,
        out_shape=jax.ShapeDtypeStruct((count, tokens, seq), BF16),
        scratch_shapes=[
            pltpu.VMEM((slices, depth, heads), BF16),
            pltpu.VMEM((2, depth, heads), BF16),
            pltpu.VMEM((count * tokens, depth), BF16),
            pltpu.VMEM((depth // 128, count * tokens, 128), F32),
            pltpu.VMEM((count, seq, depth), BF16),
            pltpu.VMEM((count, tokens, seq), BF16),
            pltpu.SemaphoreType.DMA,
            pltpu.SemaphoreType.DMA((count,)),
            pltpu.SemaphoreType.DMA((parts,)),
            pltpu.SemaphoreType.DMA((2,)),
        ],
        compiler_params=params(),
        cost_estimate=cost(8 * count * tokens * depth * depth, 2 * states.size + 4 * depth * depth),
        name="teacher_maps",
    )(order, source, rows, states, keys, wq, wk, *pieces)


def rider_copies(pieces, slices, held, sem):
    part = pieces[0].shape[1]
    return [
        pltpu.make_async_copy(
            pieces[a].at[slices + x], held.at[a, pl.ds(x * part, part)], sem.at[a * (pieces[0].shape[0] - slices) + x]
        )
        for a in range(len(pieces))
        for x in range(pieces[0].shape[0] - slices)
    ]


def rider_states(held, a, each, width):
    heads = held.shape[2]
    return jnp.concatenate([held[a, n * each : (n + 1) * each] for n in range(width // heads)], axis=1)


def scores_kernel(tokens, count, group_queries, slices, parts, qidx_ref, len_ref, emb_ref, wp_ref, *rest):
    pieces = rest[:parts]
    (prob_ref, log_ref, units_ref, qunit_ref, qdir_ref, qlen_ref, qs_s, dir_s, held_s, sem) = rest[parts:]
    copies = rider_copies(pieces, slices, held_s, sem)
    for copy in copies:
        copy.start()
    total, emb = emb_ref.shape
    seq = total // count
    sub = split_rows(total, 128)
    each = group_queries * tokens
    for b in range(0, total, sub):
        e = emb_ref[b : b + sub]
        dir_s[b : b + sub] = e / jnp.sqrt(jnp.sum(e * e, axis=-1, keepdims=True) + epsilon)
    for copy in copies:
        copy.wait()
    for a in range(parts):
        qs_s[a * each : (a + 1) * each] = rider_states(held_s, a, each, qs_s.shape[1])
    qe = dot(qs_s[...], wp_ref[...], 1, 0)
    length = jnp.sqrt(jnp.sum(qe * qe, axis=-1, keepdims=True) + epsilon)
    qdir = qe / length
    qdir_ref[...] = qdir
    qlen_ref[...] = jnp.broadcast_to(length, qlen_ref.shape)
    qunit_ref[...] = qdir.astype(BF16).reshape(qunit_ref.shape)
    for r in range(count):
        units = dir_s[pl.ds(r, seq, stride=count), :].astype(BF16)
        units_ref[r] = units
        logits = dot(qunit_ref[qidx_ref[r]], units, 1, 1) / sharpness
        valid = lax.broadcasted_iota(jnp.int32, logits.shape, 1) < len_ref[r]
        student = jnp.where(valid, jnp.exp(logits), 0.0)
        student_total = jnp.sum(student, axis=-1, keepdims=True)
        prob_ref[r] = student / student_total
        log_ref[r] = logits - jnp.log(student_total)


def student_scores(qidx, lens, embeds, wp, pieces, slices, count, tokens, group_queries):
    total, emb = embeds.shape
    seq = total // count
    parts = len(pieces)
    queries = parts * group_queries
    riders, part, heads = pieces[0].shape
    riders -= slices
    return pl.pallas_call(
        functools.partial(scores_kernel, tokens, count, group_queries, slices, parts),
        in_specs=[SMEM, SMEM, VMEM, VMEM] + [ANY] * parts,
        out_specs=[VMEM] * 6,
        out_shape=[
            jax.ShapeDtypeStruct((count, tokens, seq), F32),
            jax.ShapeDtypeStruct((count, tokens, seq), F32),
            jax.ShapeDtypeStruct((count, seq, emb), BF16),
            jax.ShapeDtypeStruct((queries, tokens, emb), BF16),
            jax.ShapeDtypeStruct((queries * tokens, emb), F32),
            jax.ShapeDtypeStruct((queries * tokens, 128), F32),
        ],
        scratch_shapes=[
            pltpu.VMEM((queries * tokens, wp.shape[0]), BF16),
            pltpu.VMEM((total, emb), F32),
            pltpu.VMEM((parts, riders * part, heads), BF16),
            pltpu.SemaphoreType.DMA((parts * riders,)),
        ],
        compiler_params=params(),
        cost_estimate=cost(1e9, 4 * total * emb),
        name="student_scores",
    )(qidx, lens, embeds, wp, *pieces)


def two_parts(a, b):
    high = a.astype(BF16)
    low = (a - high.astype(F32)).astype(BF16)
    return dot(high, b, 1, 0) + dot(low, b, 1, 0)


def backward_kernel(
    tokens, count, blocks, group_queries, slices, parts,
    qidx_ref, midx_ref, len_ref, core_ref, *rest,
):
    pieces = rest[:parts]
    (maps_in, prob_in, log_in, units_in, qunit_in, emb_in, x_in, normed_in, inv_in,
    qdir_ref, qlen_ref, gain_ref, bias_ref, wp_ref, wpt_ref,
    sg_out, send_ref, keep_ref,
    maps_s, prob_s, log_s, units_s, qunit_s, emb_s, x_s, normed_s, inv_s, held_s,
    up_s, eg_s, mean_s, along_s, un_s, qg_s, hg_s, sg_s, wo_s, nt_s, right_s,
    first_sem, block_sem, out_sem, last_sem) = rest[parts:]
    total, width = normed_s.shape
    emb = emb_s.shape[1]
    seq = total // count
    rows = total // blocks
    sub = split_rows(rows, 256)
    thin = split_rows(total, 128)
    first = [
        pltpu.make_async_copy(src, dst, first_sem.at[n])
        for n, (src, dst) in enumerate(
            (
                (qunit_in, qunit_s), (maps_in, maps_s), (prob_in, prob_s), (log_in, log_s), (units_in, units_s),
                (emb_in, emb_s), (inv_in, inv_s),
            )
        )
    ]
    first, second = first[:5], first[5:]
    loads = [
        [
            pltpu.make_async_copy(
                normed_in.at[pl.ds(b * rows, rows)], normed_s.at[pl.ds(b * rows, rows)], block_sem.at[2 * b]
            ),
            pltpu.make_async_copy(x_in.at[b], x_s.at[b], block_sem.at[2 * b + 1]),
        ]
        for b in range(blocks)
    ]
    last = rider_copies(pieces, slices, held_s, last_sem)
    for copy in first:
        copy.start()
    gain, bias = one_row(gain_ref), one_row(bias_ref)
    gain_w = two_parts(gain, wp_ref[...])
    bias_w = two_parts(bias, wp_ref[...])
    qg_s[...] = jnp.zeros_like(qg_s)
    for copy in first:
        copy.wait()
    for copy in second:
        copy.start()
    for pair in loads:
        for copy in pair:
            copy.start()
    for copy in last:
        copy.start()

    spread = jnp.zeros((tokens, 1), F32)
    for r in range(count):
        teacher = maps_s[midx_ref[r]].astype(F32)
        valid = lax.broadcasted_iota(jnp.int32, teacher.shape, 1) < len_ref[r]
        teacher_log = jnp.log(teacher)
        teacher = jnp.where(valid, teacher, 0.0)
        teacher_total = jnp.sum(teacher, axis=-1, keepdims=True)
        teacher_prob = teacher / teacher_total
        gap = (teacher_log - jnp.log(teacher_total)) - log_s[r]
        spread += jnp.sum(jnp.where(valid, teacher_prob * gap, 0.0), axis=-1, keepdims=True)
        slope = ((prob_s[r] - teacher_prob) / (tokens * sharpness)).astype(BF16)
        up_s[pl.ds(r, seq, stride=count), :] = dot(slope, qunit_s[qidx_ref[r]], 0, 0).astype(BF16).astype(F32)
        un_s[r] = dot(slope, units_s[r], 1, 0)
    for r in range(count):
        qg_s[qidx_ref[r]] += un_s[r]
    total_eg = jnp.zeros((1, emb), F32)
    for copy in second:
        copy.wait()
    for b in range(0, total, thin):
        e = emb_s[b : b + thin]
        upstream = up_s[b : b + thin]
        length = jnp.sqrt(jnp.sum(e * e, axis=-1, keepdims=True) + epsilon)
        direction = e / length
        eg = (upstream - direction * jnp.sum(direction * upstream, axis=-1, keepdims=True)) / length
        eg = eg.astype(BF16)
        eg_s[b : b + thin] = eg
        eg = eg.astype(F32)
        total_eg += jnp.sum(eg, axis=0, keepdims=True)
        inverse = inv_s[b : b + thin]
        mean_s[b : b + thin] = inverse * (jnp.sum(eg * gain_w, axis=-1, keepdims=True) / width)
        along_s[b : b + thin] = inverse * (jnp.sum(eg * (e - bias_w), axis=-1, keepdims=True) / width)

    wo_s[...] = jnp.zeros_like(wo_s)
    nt_s[...] = jnp.zeros_like(nt_s)

    def wide(b, _):
        base = pl.multiple_of(b * rows, rows)
        part = pl.ds(base, rows)
        pltpu.make_async_copy(normed_in.at[part], normed_s.at[part], block_sem.at[2 * b]).wait()
        for n in range(0, rows, sub):
            hg_s[n : n + sub] = dot(eg_s[pl.ds(base + n, sub)], wpt_ref[...], 1, 0)
            for c in range(n, n + sub, 16):
                here = pl.ds(base + c, 16)
                inverse, mean, along = inv_s[here], mean_s[here], along_s[here]
                for v in range(0, width, 128):
                    scaled = hg_s[c : c + 16, v : v + 128] * gain[:, v : v + 128]
                    normed = normed_s[here, v : v + 128].astype(F32)
                    sg_s[here, v : v + 128] = (inverse * scaled - mean - normed * along).astype(BF16)
        pltpu.make_async_copy(sg_s.at[part], sg_out.at[part], out_sem.at[b]).start()
        pltpu.make_async_copy(x_in.at[b], x_s.at[b], block_sem.at[2 * b + 1]).wait()
        wo_s[...] += dot(x_s[b], sg_s[part], 1, 0)
        nt_s[...] += dot(eg_s[part], normed_s[part], 0, 0)
        return 0

    lax.fori_loop(0, blocks, wide, 0)

    for copy in last:
        copy.wait()
    qg = qg_s[...].reshape(qdir_ref.shape)
    qdir = qdir_ref[...]
    qeg = (qg - qdir * jnp.sum(qdir * qg, axis=-1, keepdims=True)) / qlen_ref[:, :1]
    high = qeg.astype(BF16)
    low = (qeg - high.astype(F32)).astype(BF16)
    each = group_queries * tokens
    proj_query = jnp.zeros((emb, width), F32)
    for k in range(parts):
        qs = rider_states(held_s, k, each, width)
        part = slice(k * each, (k + 1) * each)
        proj_query = proj_query + (dot(high[part], qs, 0, 0) + dot(low[part], qs, 0, 0))
    nt = nt_s[...]
    s = jnp.broadcast_to(total_eg, (emb, emb)).T[:, :1]
    wpt = wpt_ref[...].astype(F32)
    proj = nt * gain + s * bias + proj_query
    gain_row = jnp.sum(wpt * nt, axis=0, keepdims=True)
    bias_row = jnp.sum(wpt * s, axis=0, keepdims=True)
    index = lax.broadcasted_iota(jnp.int32, (tokens, width), 0)
    top = jnp.where(index == 0, gain_row, jnp.where(index == 1, bias_row, 0.0))
    rest_rows = jnp.zeros((128 - 2 * tokens, width), F32)
    right_s[...] = jnp.concatenate([proj, top, jnp.broadcast_to(spread, (tokens, width)), rest_rows], axis=0).T
    half = width // CORES
    chunk = send_ref.shape[1]
    for ref, which in ((send_ref, 1 - core_ref[0]), (keep_ref, core_ref[0])):
        start = pl.multiple_of(which * half, half)
        left = wo_s[pl.ds(start, half)].astype(BF16)
        right = right_s[pl.ds(start, half)].astype(BF16)
        for c in range(half // chunk):
            ref[c, :, :width] = left[c * chunk : (c + 1) * chunk]
            ref[c, :, width:] = right[c * chunk : (c + 1) * chunk]
    for b in range(blocks):
        part = pl.ds(b * rows, rows)
        pltpu.make_async_copy(sg_s.at[part], sg_out.at[part], out_sem.at[b]).wait()


def student_backward(
    qidx, midx, lens, core, maps, scores, pieces, slices, embeds, x, normed, inverse, gain, bias, wp, wpt,
    count, tokens, group_queries, chunk,
):
    total, width = normed.shape
    emb = wp.shape[1]
    blocks = x.shape[0]
    chunks = width // CORES // chunk
    prob, log, units, qunit, qdir, qlen = scores
    manual = [maps, prob, log, units, qunit, embeds, x, normed, inverse]
    parts = len(pieces)
    riders, part, heads = pieces[0].shape
    riders -= slices
    packed = jax.ShapeDtypeStruct((chunks, chunk, width + emb + 128), BF16)
    return pl.pallas_call(
        functools.partial(backward_kernel, tokens, count, blocks, group_queries, slices, parts),
        in_specs=[SMEM] * 4 + [ANY] * (parts + len(manual)) + [VMEM] * 6,
        out_specs=[ANY, VMEM, VMEM],
        scratch_shapes=[pltpu.VMEM(a.shape, a.dtype) for a in manual]
        + [
            pltpu.VMEM((parts, riders * part, heads), BF16),
            pltpu.VMEM((total, emb), F32),
            pltpu.VMEM((total, emb), BF16),
            pltpu.VMEM((total, 128), F32),
            pltpu.VMEM((total, 128), F32),
            pltpu.VMEM((count, tokens, emb), F32),
            pltpu.VMEM(qunit.shape, F32),
            pltpu.VMEM((total // blocks, width), F32),
            pltpu.VMEM((total, width), BF16),
            pltpu.VMEM((width, width), F32),
            pltpu.VMEM((emb, width), F32),
            pltpu.VMEM((width, emb + 128), F32),
            pltpu.SemaphoreType.DMA((7,)),
            pltpu.SemaphoreType.DMA((2 * blocks,)),
            pltpu.SemaphoreType.DMA((blocks,)),
            pltpu.SemaphoreType.DMA((parts * riders,)),
        ],
        out_shape=[jax.ShapeDtypeStruct((total, width), BF16), packed, packed],
        compiler_params=params(),
        cost_estimate=cost(2 * total * width * (width + 2 * emb), 8 * total * width),
        name="student_backward",
    )(qidx, midx, lens, core, *pieces, *manual, qdir, qlen, gain, bias, wp, wpt)


def context_kernel(sg_ref, wo_ref, out_ref):
    out_ref[...] = dot(sg_ref[...], wo_ref[...], 1, 1).astype(BF16)


def context_grad(sg, out_weight):
    total, width = sg.shape
    rows = split_rows(total, 720)
    block = pl.BlockSpec((rows, width), lambda s: (s, 0))
    return pl.pallas_call(
        context_kernel,
        grid=(total // rows,),
        in_specs=[block, pl.BlockSpec(out_weight.shape, lambda s: (0, 0))],
        out_specs=block,
        out_shape=jax.ShapeDtypeStruct(sg.shape, BF16),
        compiler_params=params(),
        cost_estimate=cost(2 * total * width * width, 4 * total * width),
        name="context_grad",
    )(sg, out_weight)


def split_sum_kernel(inputs, outputs, index_ref, *rest):
    ins, outs, total_s = rest[:inputs], rest[inputs : inputs + outputs], rest[-1]
    total = ins[0][...].astype(F32)
    for ref in ins[1:]:
        total = total + ref[...].astype(F32)
    total_s[...] = total.astype(BF16).reshape(total_s.shape)
    for k in range(outputs):
        outs[k][...] = total_s[index_ref[k]].reshape(outs[k].shape)


def split_sum(arrays, index, name):
    outputs = index.shape[0]
    shape = arrays[0].shape
    lead = shape[0] // outputs
    out = shape[1:] if lead == 1 else (lead,) + shape[1:]
    return pl.pallas_call(
        functools.partial(split_sum_kernel, len(arrays), outputs),
        in_specs=[SMEM] + [VMEM] * len(arrays),
        out_specs=[VMEM] * outputs,
        out_shape=[jax.ShapeDtypeStruct(out, BF16)] * outputs,
        scratch_shapes=[pltpu.VMEM((outputs, lead) + shape[1:], BF16)],
        compiler_params=pltpu.CompilerParams(vmem_limit_bytes=SMALL_LIMIT),
        name=name,
    )(index, *arrays)


def sum_kernel(*refs):
    total = refs[0][...].astype(F32)
    for ref in refs[1:-1]:
        total = total + ref[...].astype(F32)
    refs[-1][...] = total.astype(BF16)


def plain_sum(arrays, name):
    return pl.pallas_call(
        sum_kernel,
        in_specs=[VMEM] * len(arrays),
        out_specs=VMEM,
        out_shape=jax.ShapeDtypeStruct(arrays[0].shape, BF16),
        compiler_params=pltpu.CompilerParams(vmem_limit_bytes=SMALL_LIMIT),
        name=name,
    )(*arrays)


def unpack_kernel(parts, width, emb, tokens, scale, index_ref, *rest):
    ins = rest[:parts]
    wo_out, proj_out, gain_ref, bias_ref, loss_ref, wo_s, proj_s, small_s, wo_sem, proj_sem = rest[parts:]
    per = ins[0].shape[0]
    copies = []
    for a in range(parts):
        for k in range(per):
            n = a * per + k
            c = index_ref[n]
            value = ins[a][k].astype(F32)
            wo_s[n] = value[:, :width]
            proj_s[n] = value[:, width : width + emb]
            small_s[c] = value[:, width + emb :]
            copies.append(pltpu.make_async_copy(wo_s.at[n], wo_out.at[c], wo_sem.at[n]))
            copies.append(pltpu.make_async_copy(proj_s.at[n], proj_out.at[c], proj_sem.at[n]))
            copies[-2].start()
            copies[-1].start()
    turned = small_s[...].reshape(width, 128).T
    for v in range(width // 128):
        gain_ref[v : v + 1] = turned[0:1, v * 128 : (v + 1) * 128]
        bias_ref[v : v + 1] = turned[1:2, v * 128 : (v + 1) * 128]
    loss_ref[0] = jnp.sum(turned[tokens : 2 * tokens, 0:1]) * scale
    for copy in copies:
        copy.wait()


def unpack(arrays, index, width, emb, tokens, scale):
    parts = len(arrays)
    per, chunk, _ = arrays[0].shape
    chunks = parts * per
    return pl.pallas_call(
        functools.partial(unpack_kernel, parts, width, emb, tokens, scale),
        in_specs=[SMEM] + [VMEM] * parts,
        out_specs=[ANY] * 2 + [VMEM] * 2 + [SMEM],
        out_shape=[jax.ShapeDtypeStruct((chunks, chunk, n), F32) for n in (width, emb)]
        + [jax.ShapeDtypeStruct((width // 128, 128), F32)] * 2
        + [jax.ShapeDtypeStruct((1,), F32)],
        scratch_shapes=[pltpu.VMEM((chunks, chunk, n), F32) for n in (width, emb, 128)]
        + [pltpu.SemaphoreType.DMA((chunks,))] * 2,
        compiler_params=pltpu.CompilerParams(vmem_limit_bytes=SMALL_LIMIT),
        name="unpack",
    )(index, *arrays)


def local(
    context,
    stream,
    out_weight,
    gain,
    bias,
    proj_weight,
    query_states,
    passage_len,
    passage_dest,
    teacher_states,
    teacher_query,
    teacher_key,
):
    dp = lax.axis_size("dp")
    nt = lax.axis_size("tensor")
    chips = dp // CORES
    me = lax.axis_index("dp")
    chip, core = me // CORES, me % CORES
    mt = lax.axis_index("tensor")
    count, seq, width = context.shape
    emb = proj_weight.shape[1]
    group_queries, tokens, _ = query_states.shape
    depth, heads = teacher_query.shape
    per = count // dp
    per_query = count * nt // group_queries

    def flat(a):
        return a.transpose(1, 0, 2).reshape(-1, a.shape[2])

    def shift_chip(x, k):
        return lax.ppermute(
            x, "dp", [(c * CORES + o, (c + k) % chips * CORES + o) for c in range(chips) for o in range(CORES)]
        )

    def swap_core(x):
        return lax.ppermute(x, "dp", [(d, d ^ 1) for d in range(dp)])

    def shift_t(x, k):
        return lax.ppermute(x, "tensor", [(t, (t + k) % nt) for t in range(nt)])

    dest_group = passage_dest // (count * nt)
    rows = jnp.arange(count, dtype=jnp.int32)
    rank = jnp.sum(
        (dest_group[:, None] == dest_group[None, :]) & (rows[None, :] < rows[:, None]), axis=1, dtype=jnp.int32
    )
    place = dest_group * per + rank
    positions = jnp.sum(
        jnp.where(place[:, None] == rows[None, :], (passage_dest % count)[:, None], 0), axis=0
    )
    each = group_queries * tokens
    states = query_states.reshape(each, width)
    column_blocks = [states[:, n * heads : (n + 1) * heads] for n in range(width // heads)]
    extra = jnp.pad(positions.astype(BF16)[None, :], ((0, 15), (0, heads - count)))
    rider = jnp.concatenate(column_blocks + [extra], axis=0)

    part = depth // dp
    mine = jnp.stack(
        [lax.dynamic_slice_in_dim(w, me * part, part, 0) for w in (teacher_query, teacher_key)]
    )
    rider = jnp.pad(rider, ((0, -rider.shape[0] % part), (0, 0))).reshape(-1, part, heads)
    slices = 2 * (nt - 1)
    along = jnp.concatenate([shift_t(mine, k) for k in range(1, nt)] + [rider], axis=0)
    pieces = [along] + [shift_chip(along, k) for k in range(1, chips)]
    shifts = jnp.arange(chips, dtype=jnp.int32)
    behind = (chip - shifts) % chips
    piece_rows = jnp.concatenate([behind * CORES + core, behind * CORES + 1 - core]).astype(jnp.int32)
    midx = place.astype(jnp.int32)
    def piece_of(group):
        return (chip - group // CORES) % chips + jnp.where(group % CORES == core, 0, chips)

    qidx = passage_dest // per_query - dest_group * group_queries + piece_of(dest_group) * group_queries
    qidx = qidx.astype(jnp.int32)
    source = piece_of(jnp.arange(dp, dtype=jnp.int32)).astype(jnp.int32)

    gain2, bias2 = gain.reshape(-1, 128), bias.reshape(-1, 128)
    x = flat(context)
    normed, embeds, inverse, turned = student_forward(x, flat(stream), out_weight, gain2, bias2, proj_weight)
    keys = pair_keys(flat(teacher_states), count, tokens)
    pieces[1:], normed, embeds, inverse, turned, keys, proj_turned = lax.optimization_barrier(
        (pieces[1:], normed, embeds, inverse, turned, keys, proj_weight.T)
    )
    pieces = pieces + [swap_core(a) for a in pieces]
    told = [a[slices:].reshape(-1, heads)[width // heads * each, :count] for a in pieces]
    order = lax.dynamic_slice_in_dim(jnp.stack(told), me * per, per, 1).astype(jnp.int32)
    maps = teacher_maps(
        order, source, piece_rows, slices, flat(teacher_states), keys, teacher_query, teacher_key, pieces, count, tokens
    )
    maps, embeds = lax.optimization_barrier((maps, embeds))
    maps = lax.all_to_all(maps, "dp", split_axis=0, concat_axis=0, tiled=True)
    scores = student_scores(
        qidx, passage_len, embeds, proj_weight, pieces, slices, count, tokens, group_queries
    )
    chunk = width // (CORES * chips * nt)
    sg, send, keep = student_backward(
        qidx, midx, passage_len, core.astype(jnp.int32).reshape(1), maps, scores, pieces, slices,
        embeds, turned, normed, inverse, gain2, bias2, proj_weight, proj_turned,
        count, tokens, group_queries, chunk,
    )

    ahead = ((chip + shifts) % chips).astype(jnp.int32)
    t_shifts = jnp.arange(nt, dtype=jnp.int32)
    t_ahead = ((mt + t_shifts) % nt).astype(jnp.int32)
    parts = split_sum([keep, swap_core(send)], ahead, "sum_cores")
    parts, sg = lax.optimization_barrier((parts, sg))
    grad_context = context_grad(sg, out_weight)
    parts = [parts[0]] + [shift_chip(parts[k], k) for k in range(1, chips)]
    parts, grad_context = lax.optimization_barrier((parts, grad_context))
    parts = split_sum(parts, t_ahead, "sum_plane")
    parts = [parts[0]] + [shift_t(parts[k], k) for k in range(1, nt)]
    total = plain_sum(parts, "sum_tensor")
    line = jnp.stack([total] + [shift_t(total, k) for k in range(1, nt)])
    plane = [line] + [shift_chip(line, k) for k in range(1, chips)]
    arrays = plane + [swap_core(a) for a in plane]
    base = jnp.concatenate([core * chips + behind, (1 - core) * chips + behind]) * nt
    index = (base[:, None] + ((mt - t_shifts) % nt)[None, :]).reshape(-1).astype(jnp.int32)
    grad_out, grad_proj, grad_gain, grad_bias, loss = unpack(
        arrays, index, width, emb, tokens, 1.0 / (count * dp * nt * tokens)
    )
    return (
        loss.reshape(()),
        grad_out.reshape(width, width),
        grad_proj.reshape(width, emb),
        grad_gain.reshape(width),
        grad_bias.reshape(width),
        grad_context.reshape(seq, count, width).transpose(1, 0, 2),
    )


def solution(mesh):
    return jax.shard_map(
        local,
        mesh=mesh,
        in_specs=(
            P(("dp", "tensor"), None, None),
            P(("dp", "tensor"), None, None),
            P(),
            P(),
            P(),
            P(),
            P("dp", None, None),
            P(("dp", "tensor")),
            P(("dp", "tensor")),
            P(("dp", "tensor"), None, None),
            P(None, "tensor"),
            P(None, "tensor"),
        ),
        out_specs=(P(), P(), P(), P(), P(), P(("dp", "tensor"), None, None)),
        check_vma=False,
    )
```

```python
import functools
import math

import jax
import jax.numpy as jnp
from jax import lax
from jax.experimental import pallas as pl
from jax.experimental.pallas import tpu as pltpu
from jax.sharding import PartitionSpec as P

sharpness = 0.05
softcap = 10.0
epsilon = 1e-06
CORES = 2
VMEM_LIMIT = 56 * 1024 * 1024
SMALL_LIMIT = 14 * 1024 * 1024

F32 = jnp.float32
BF16 = jnp.bfloat16
VMEM = pl.BlockSpec(memory_space=pltpu.VMEM)
SMEM = pl.BlockSpec(memory_space=pltpu.SMEM)
ANY = pl.BlockSpec(memory_space=pl.ANY)


def up(n, m):
    return -(-n // m) * m


def dot(a, b, ca, cb):
    return lax.dot_general(a, b, (((ca,), (cb,)), ((), ())), preferred_element_type=F32)


def split_rows(rows, most):
    return max(n for n in range(16, most + 1, 16) if rows % n == 0)


def one_row(ref):
    return jnp.concatenate([ref[v : v + 1] for v in range(ref.shape[0])], axis=1)


def params(**kw):
    return pltpu.CompilerParams(vmem_limit_bytes=VMEM_LIMIT, **kw)


def cost(flops, nbytes):
    return pl.CostEstimate(flops=int(flops), bytes_accessed=int(nbytes), transcendentals=0)


def forward_kernel(x_ref, str_ref, wo_ref, gain_ref, bias_ref, wp_ref, normed_ref, emb_ref, inv_ref, turned_ref, prod_s, hid_s):
    rows, width = x_ref.shape
    sub = rows
    gain, bias = one_row(gain_ref), one_row(bias_ref)
    for b in range(0, rows, sub):
        prod_s[b : b + sub] = dot(x_ref[b : b + sub], wo_ref[...], 1, 0)
        for c in range(b, b + sub, 16):
            summed = prod_s[c : c + 16] + str_ref[c : c + 16].astype(F32)
            centred = summed - jnp.mean(summed, axis=-1, keepdims=True)
            inverse = lax.rsqrt(jnp.mean(centred * centred, axis=-1, keepdims=True) + epsilon)
            normed = centred * inverse
            normed_ref[c : c + 16] = normed.astype(BF16)
            inv_ref[c : c + 16] = jnp.broadcast_to(inverse, (16, inv_ref.shape[1]))
            hid_s[c : c + 16] = (normed * gain + bias).astype(BF16)
        emb_ref[b : b + sub] = dot(hid_s[b : b + sub], wp_ref[...], 1, 0)
    turned_ref[0] = x_ref[...].T


def student_forward(x, stream, out_weight, gain, bias, proj_weight):
    total, width = x.shape
    emb = proj_weight.shape[1]
    rows = split_rows(total, 720)
    block = lambda last: pl.BlockSpec((rows, last), lambda s: (s, 0))
    whole = lambda a: pl.BlockSpec(a.shape, lambda s: (0,) * a.ndim)
    return pl.pallas_call(
        forward_kernel,
        grid=(total // rows,),
        in_specs=[block(width), block(width)] + [whole(a) for a in (out_weight, gain, bias, proj_weight)],
        out_specs=[block(width), block(emb), block(128), pl.BlockSpec((1, width, rows), lambda s: (s, 0, 0))],
        out_shape=[
            jax.ShapeDtypeStruct((total, width), BF16),
            jax.ShapeDtypeStruct((total, emb), F32),
            jax.ShapeDtypeStruct((total, 128), F32),
            jax.ShapeDtypeStruct((total // rows, width, rows), BF16),
        ],
        scratch_shapes=[pltpu.VMEM((rows, width), F32), pltpu.VMEM((rows, width), BF16)],
        compiler_params=params(),
        cost_estimate=cost(2 * total * width * (width + emb), 8 * total * width),
        name="student_forward",
    )(x, stream, out_weight, gain, bias, proj_weight)


def teacher_kernel(parts, count, tokens, order_ref, from_ref, rows_ref, states_ref, wq_ref, wk_ref, *rest):
    pieces, out_ref = rest[:parts], rest[parts]
    w_s, own_s, q_s, a_s, g_s, key_s, e_s, map_s, q_sem, key_sem, w_sem, own_sem = rest[parts + 1 :]
    depth = q_s.shape[1]
    slices = w_s.shape[0] // 2
    part_rows = pieces[0].shape[1]
    total = key_s.shape[0]
    seq = total // count
    blocks = key_sem.shape[0]
    rows = total // blocks
    first = count * tokens
    own = [
        pltpu.make_async_copy(wq_ref, own_s.at[0], own_sem.at[0]),
        pltpu.make_async_copy(wk_ref, own_s.at[1], own_sem.at[1]),
    ]
    queries = pltpu.make_async_copy(states_ref.at[pl.ds(0, first)], q_s, q_sem)
    gathered = [
        pltpu.make_async_copy(
            pieces[a].at[pl.ds(0, w_s.shape[0])],
            w_s.at[:, pl.ds(pl.multiple_of(rows_ref[a] * part_rows, part_rows), part_rows), :],
            w_sem.at[a],
        )
        for a in range(parts)
    ]
    keys = [
        pltpu.make_async_copy(
            states_ref.at[pl.ds(first + b * rows, rows)], key_s.at[pl.ds(b * rows, rows)], key_sem.at[b]
        )
        for b in range(blocks)
    ]
    queries.start()
    for copy in own + gathered:
        copy.start()
    queries.wait()
    for copy in own:
        copy.wait()
    for copy in keys:
        copy.start()
    q = q_s[...]
    heads = own_s.shape[2]
    a_s[:, slices * heads :] = dot(q, own_s[0], 1, 0).astype(BF16)
    for copy in gathered:
        copy.wait()
    for k in range(slices):
        a_s[:, k * heads : (k + 1) * heads] = dot(q, w_s[2 * k], 1, 0).astype(BF16)
    keys_weight = jnp.concatenate([w_s[2 * k + 1] for k in range(slices)] + [own_s[1]], axis=1)
    mixed = dot(a_s[...], keys_weight, 1, 1)
    for v in range(depth // 128):
        g_s[v] = mixed[:, v * 128 : (v + 1) * 128]
        for p in range(count):
            q_s[p * tokens : (p + 1) * tokens, v * 128 : (v + 1) * 128] = g_s[
                v, pl.ds(p, tokens, stride=count), :
            ].astype(BF16)
    mixed = q_s[...].T
    scale = 1.0 / (math.sqrt(depth) * softcap)
    side = 128 // tokens
    pair = lax.broadcasted_iota(jnp.int32, (rows, 128), 0) % count
    for b in range(blocks):
        keys[b].wait()
        raw = dot(key_s[b * rows : (b + 1) * rows], mixed, 1, 0)
        mine = raw[:, :128]
        for v in range(1, count // side):
            mine = jnp.where(pair >= v * side, raw[:, v * 128 : (v + 1) * 128], mine)
        e_s[b * rows : (b + 1) * rows] = jnp.exp(softcap * jnp.tanh(mine * scale))
    lane = lax.broadcasted_iota(jnp.int32, (seq, 128), 1) // tokens
    filler = jnp.zeros((up(seq, 128) - seq, 128), F32)
    for g in range(count // side):
        both = e_s[pl.ds(g * side, seq, stride=count), :]
        for v in range(1, side):
            both = jnp.where(lane == v, e_s[pl.ds(g * side + v, seq, stride=count), :], both)
        turned = jnp.concatenate([both, filler], axis=0).T
        for v in range(side):
            map_s[g * side + v] = turned[v * tokens : (v + 1) * tokens, :seq].astype(BF16)
    per = count // parts
    for n in range(count):
        out_ref[n] = map_s[order_ref[from_ref[n // per], n % per]]


def teacher_maps(order, source, rows, slices, states, wq, wk, pieces, count, tokens):
    total, depth = states.shape
    keys = total - count * tokens
    heads = wq.shape[1]
    parts = len(pieces)
    blocks = keys // split_rows(keys, 720)
    return pl.pallas_call(
        functools.partial(teacher_kernel, parts, count, tokens),
        in_specs=[SMEM] * 3 + [ANY] * (3 + parts),
        out_specs=VMEM,
        out_shape=jax.ShapeDtypeStruct((count, tokens, keys // count), BF16),
        scratch_shapes=[
            pltpu.VMEM((slices, depth, heads), BF16),
            pltpu.VMEM((2, depth, heads), BF16),
            pltpu.VMEM((count * tokens, depth), BF16),
            pltpu.VMEM((count * tokens, (slices // 2 + 1) * heads), BF16),
            pltpu.VMEM((depth // 128, count * tokens, 128), F32),
            pltpu.VMEM((keys, depth), BF16),
            pltpu.VMEM((keys, 128), F32),
            pltpu.VMEM((count, tokens, keys // count), BF16),
            pltpu.SemaphoreType.DMA,
            pltpu.SemaphoreType.DMA((blocks,)),
            pltpu.SemaphoreType.DMA((parts,)),
            pltpu.SemaphoreType.DMA((2,)),
        ],
        compiler_params=params(),
        cost_estimate=cost(8 * count * tokens * depth * depth, 2 * states.size + 4 * depth * depth),
        name="teacher_maps",
    )(order, source, rows, states, wq, wk, *pieces)


def rider_copies(pieces, slices, held, sem):
    part = pieces[0].shape[1]
    return [
        pltpu.make_async_copy(
            pieces[a].at[slices + x], held.at[a, pl.ds(x * part, part)], sem.at[a * (pieces[0].shape[0] - slices) + x]
        )
        for a in range(len(pieces))
        for x in range(pieces[0].shape[0] - slices)
    ]


def rider_states(held, a, each, width):
    heads = held.shape[2]
    return jnp.concatenate([held[a, n * each : (n + 1) * each] for n in range(width // heads)], axis=1)


def scores_kernel(tokens, count, group_queries, slices, parts, qidx_ref, len_ref, emb_ref, wp_ref, *rest):
    pieces = rest[:parts]
    (prob_ref, log_ref, units_ref, qunit_ref, qdir_ref, qlen_ref, qs_ref, dir_s, held_s, sem) = rest[parts:]
    copies = rider_copies(pieces, slices, held_s, sem)
    for copy in copies:
        copy.start()
    total, emb = emb_ref.shape
    seq = total // count
    sub = split_rows(total, 128)
    each = group_queries * tokens
    for b in range(0, total, sub):
        e = emb_ref[b : b + sub]
        dir_s[b : b + sub] = e / jnp.sqrt(jnp.sum(e * e, axis=-1, keepdims=True) + epsilon)
    for copy in copies:
        copy.wait()
    for a in range(parts):
        qs_ref[a * each : (a + 1) * each] = rider_states(held_s, a, each, qs_ref.shape[1])
    qe = dot(qs_ref[...], wp_ref[...], 1, 0)
    length = jnp.sqrt(jnp.sum(qe * qe, axis=-1, keepdims=True) + epsilon)
    qdir = qe / length
    qdir_ref[...] = qdir
    qlen_ref[...] = jnp.broadcast_to(length, qlen_ref.shape)
    qunit_ref[...] = qdir.astype(BF16).reshape(qunit_ref.shape)
    for r in range(count):
        units = dir_s[pl.ds(r, seq, stride=count), :].astype(BF16)
        units_ref[r] = units
        logits = dot(qunit_ref[qidx_ref[r]], units, 1, 1) / sharpness
        valid = lax.broadcasted_iota(jnp.int32, logits.shape, 1) < len_ref[r]
        student = jnp.where(valid, jnp.exp(logits), 0.0)
        student_total = jnp.sum(student, axis=-1, keepdims=True)
        prob_ref[r] = student / student_total
        log_ref[r] = logits - jnp.log(student_total)


def student_scores(qidx, lens, embeds, wp, pieces, slices, count, tokens, group_queries):
    total, emb = embeds.shape
    seq = total // count
    parts = len(pieces)
    queries = parts * group_queries
    riders, part, heads = pieces[0].shape
    riders -= slices
    return pl.pallas_call(
        functools.partial(scores_kernel, tokens, count, group_queries, slices, parts),
        in_specs=[SMEM, SMEM, VMEM, VMEM] + [ANY] * parts,
        out_specs=[VMEM] * 7,
        out_shape=[
            jax.ShapeDtypeStruct((count, tokens, seq), F32),
            jax.ShapeDtypeStruct((count, tokens, seq), F32),
            jax.ShapeDtypeStruct((count, seq, emb), BF16),
            jax.ShapeDtypeStruct((queries, tokens, emb), BF16),
            jax.ShapeDtypeStruct((queries * tokens, emb), F32),
            jax.ShapeDtypeStruct((queries * tokens, 128), F32),
            jax.ShapeDtypeStruct((queries * tokens, wp.shape[0]), BF16),
        ],
        scratch_shapes=[
            pltpu.VMEM((total, emb), F32),
            pltpu.VMEM((parts, riders * part, heads), BF16),
            pltpu.SemaphoreType.DMA((parts * riders,)),
        ],
        compiler_params=params(),
        cost_estimate=cost(1e9, 4 * total * emb),
        name="student_scores",
    )(qidx, lens, embeds, wp, *pieces)


def two_parts(a, b):
    high = a.astype(BF16)
    low = (a - high.astype(F32)).astype(BF16)
    return dot(high, b, 1, 0) + dot(low, b, 1, 0)


def backward_kernel(
    tokens, count, blocks,
    qidx_ref, midx_ref, len_ref, core_ref,
    maps_in, prob_in, log_in, units_in, qunit_in, emb_in, x_in, normed_in, inv_in, qs_in,
    qdir_ref, qlen_ref, gain_ref, bias_ref, wp_ref, wpt_ref,
    sg_out, send_ref, keep_ref,
    maps_s, prob_s, log_s, units_s, qunit_s, emb_s, x_s, normed_s, inv_s, qs_s,
    up_s, eg_s, mean_s, along_s, un_s, qg_s, hg_s, sg_s, wo_s, nt_s, right_s,
    first_sem, block_sem, out_sem, last_sem,
):
    total, width = normed_s.shape
    emb = emb_s.shape[1]
    seq = total // count
    rows = total // blocks
    sub = split_rows(rows, 256)
    thin = split_rows(total, 128)
    first = [
        pltpu.make_async_copy(src, dst, first_sem.at[n])
        for n, (src, dst) in enumerate(
            (
                (qunit_in, qunit_s), (maps_in, maps_s), (prob_in, prob_s), (log_in, log_s), (units_in, units_s),
                (emb_in, emb_s), (inv_in, inv_s),
            )
        )
    ]
    first, second = first[:5], first[5:]
    loads = [
        [
            pltpu.make_async_copy(
                normed_in.at[pl.ds(b * rows, rows)], normed_s.at[pl.ds(b * rows, rows)], block_sem.at[2 * b]
            ),
            pltpu.make_async_copy(x_in.at[b], x_s.at[b], block_sem.at[2 * b + 1]),
        ]
        for b in range(blocks)
    ]
    last = pltpu.make_async_copy(qs_in, qs_s, last_sem)
    for copy in first:
        copy.start()
    gain, bias = one_row(gain_ref), one_row(bias_ref)
    gain_w = two_parts(gain, wp_ref[...])
    bias_w = two_parts(bias, wp_ref[...])
    qg_s[...] = jnp.zeros_like(qg_s)
    for copy in first:
        copy.wait()
    for copy in second:
        copy.start()
    for pair in loads:
        for copy in pair:
            copy.start()
    last.start()

    spread = jnp.zeros((tokens, 1), F32)
    for r in range(count):
        teacher = maps_s[midx_ref[r]].astype(F32)
        valid = lax.broadcasted_iota(jnp.int32, teacher.shape, 1) < len_ref[r]
        teacher_log = jnp.log(teacher)
        teacher = jnp.where(valid, teacher, 0.0)
        teacher_total = jnp.sum(teacher, axis=-1, keepdims=True)
        teacher_prob = teacher / teacher_total
        gap = (teacher_log - jnp.log(teacher_total)) - log_s[r]
        spread += jnp.sum(jnp.where(valid, teacher_prob * gap, 0.0), axis=-1, keepdims=True)
        slope = ((prob_s[r] - teacher_prob) / (tokens * sharpness)).astype(BF16)
        up_s[pl.ds(r, seq, stride=count), :] = dot(slope, qunit_s[qidx_ref[r]], 0, 0).astype(BF16).astype(F32)
        un_s[r] = dot(slope, units_s[r], 1, 0)
    for r in range(count):
        qg_s[qidx_ref[r]] += un_s[r]
    total_eg = jnp.zeros((1, emb), F32)
    for copy in second:
        copy.wait()
    for b in range(0, total, thin):
        e = emb_s[b : b + thin]
        upstream = up_s[b : b + thin]
        length = jnp.sqrt(jnp.sum(e * e, axis=-1, keepdims=True) + epsilon)
        direction = e / length
        eg = (upstream - direction * jnp.sum(direction * upstream, axis=-1, keepdims=True)) / length
        eg = eg.astype(BF16)
        eg_s[b : b + thin] = eg
        eg = eg.astype(F32)
        total_eg += jnp.sum(eg, axis=0, keepdims=True)
        inverse = inv_s[b : b + thin]
        mean_s[b : b + thin] = inverse * (jnp.sum(eg * gain_w, axis=-1, keepdims=True) / width)
        along_s[b : b + thin] = inverse * (jnp.sum(eg * (e - bias_w), axis=-1, keepdims=True) / width)

    wo_s[...] = jnp.zeros_like(wo_s)
    nt_s[...] = jnp.zeros_like(nt_s)

    def wide(b, _):
        base = pl.multiple_of(b * rows, rows)
        part = pl.ds(base, rows)
        pltpu.make_async_copy(normed_in.at[part], normed_s.at[part], block_sem.at[2 * b]).wait()
        for n in range(0, rows, sub):
            hg_s[n : n + sub] = dot(eg_s[pl.ds(base + n, sub)], wpt_ref[...], 1, 0)
            for c in range(n, n + sub, 16):
                here = pl.ds(base + c, 16)
                inverse, mean, along = inv_s[here], mean_s[here], along_s[here]
                for v in range(0, width, 128):
                    scaled = hg_s[c : c + 16, v : v + 128] * gain[:, v : v + 128]
                    normed = normed_s[here, v : v + 128].astype(F32)
                    sg_s[here, v : v + 128] = (inverse * scaled - mean - normed * along).astype(BF16)
        pltpu.make_async_copy(sg_s.at[part], sg_out.at[part], out_sem.at[b]).start()
        pltpu.make_async_copy(x_in.at[b], x_s.at[b], block_sem.at[2 * b + 1]).wait()
        wo_s[...] += dot(x_s[b], sg_s[part], 1, 0)
        nt_s[...] += dot(eg_s[part], normed_s[part], 0, 0)
        return 0

    lax.fori_loop(0, blocks, wide, 0)

    last.wait()
    qg = qg_s[...].reshape(qdir_ref.shape)
    qdir = qdir_ref[...]
    qeg = (qg - qdir * jnp.sum(qdir * qg, axis=-1, keepdims=True)) / qlen_ref[:, :1]
    high = qeg.astype(BF16)
    low = (qeg - high.astype(F32)).astype(BF16)
    qs = qs_s[...]
    proj_query = dot(high, qs, 0, 0) + dot(low, qs, 0, 0)
    nt = nt_s[...]
    s = jnp.broadcast_to(total_eg, (emb, emb)).T[:, :1]
    wpt = wpt_ref[...].astype(F32)
    proj = nt * gain + s * bias + proj_query
    gain_row = jnp.sum(wpt * nt, axis=0, keepdims=True)
    bias_row = jnp.sum(wpt * s, axis=0, keepdims=True)
    index = lax.broadcasted_iota(jnp.int32, (tokens, width), 0)
    top = jnp.where(index == 0, gain_row, jnp.where(index == 1, bias_row, 0.0))
    rest_rows = jnp.zeros((128 - 2 * tokens, width), F32)
    right_s[...] = jnp.concatenate([proj, top, jnp.broadcast_to(spread, (tokens, width)), rest_rows], axis=0).T
    half = width // CORES
    chunk = send_ref.shape[1]
    for ref, which in ((send_ref, 1 - core_ref[0]), (keep_ref, core_ref[0])):
        start = pl.multiple_of(which * half, half)
        left = wo_s[pl.ds(start, half)].astype(BF16)
        right = right_s[pl.ds(start, half)].astype(BF16)
        for c in range(half // chunk):
            ref[c, :, :width] = left[c * chunk : (c + 1) * chunk]
            ref[c, :, width:] = right[c * chunk : (c + 1) * chunk]
    for b in range(blocks):
        part = pl.ds(b * rows, rows)
        pltpu.make_async_copy(sg_s.at[part], sg_out.at[part], out_sem.at[b]).wait()


def student_backward(
    qidx, midx, lens, core, maps, scores, embeds, x, normed, inverse, gain, bias, wp, wpt,
    count, tokens, group_queries, chunk,
):
    total, width = normed.shape
    emb = wp.shape[1]
    blocks = x.shape[0]
    chunks = width // CORES // chunk
    prob, log, units, qunit, qdir, qlen, qs = scores
    manual = [maps, prob, log, units, qunit, embeds, x, normed, inverse, qs]
    packed = jax.ShapeDtypeStruct((chunks, chunk, width + emb + 128), BF16)
    return pl.pallas_call(
        functools.partial(backward_kernel, tokens, count, blocks),
        in_specs=[SMEM] * 4 + [ANY] * len(manual) + [VMEM] * 6,
        out_specs=[ANY, VMEM, VMEM],
        scratch_shapes=[pltpu.VMEM(a.shape, a.dtype) for a in manual]
        + [
            pltpu.VMEM((total, emb), F32),
            pltpu.VMEM((total, emb), BF16),
            pltpu.VMEM((total, 128), F32),
            pltpu.VMEM((total, 128), F32),
            pltpu.VMEM((count, tokens, emb), F32),
            pltpu.VMEM(qunit.shape, F32),
            pltpu.VMEM((total // blocks, width), F32),
            pltpu.VMEM((total, width), BF16),
            pltpu.VMEM((width, width), F32),
            pltpu.VMEM((emb, width), F32),
            pltpu.VMEM((width, emb + 128), F32),
            pltpu.SemaphoreType.DMA((7,)),
            pltpu.SemaphoreType.DMA((2 * blocks,)),
            pltpu.SemaphoreType.DMA((blocks,)),
            pltpu.SemaphoreType.DMA,
        ],
        out_shape=[jax.ShapeDtypeStruct((total, width), BF16), packed, packed],
        compiler_params=params(),
        cost_estimate=cost(2 * total * width * (width + 2 * emb), 8 * total * width),
        name="student_backward",
    )(qidx, midx, lens, core, *manual, qdir, qlen, gain, bias, wp, wpt)


def context_kernel(sg_ref, wo_ref, out_ref):
    out_ref[...] = dot(sg_ref[...], wo_ref[...], 1, 1).astype(BF16)


def context_grad(sg, out_weight):
    total, width = sg.shape
    rows = split_rows(total, 720)
    block = pl.BlockSpec((rows, width), lambda s: (s, 0))
    return pl.pallas_call(
        context_kernel,
        grid=(total // rows,),
        in_specs=[block, pl.BlockSpec(out_weight.shape, lambda s: (0, 0))],
        out_specs=block,
        out_shape=jax.ShapeDtypeStruct(sg.shape, BF16),
        compiler_params=params(),
        cost_estimate=cost(2 * total * width * width, 4 * total * width),
        name="context_grad",
    )(sg, out_weight)


def split_sum_kernel(inputs, outputs, index_ref, *rest):
    ins, outs, total_s = rest[:inputs], rest[inputs : inputs + outputs], rest[-1]
    total = ins[0][...].astype(F32)
    for ref in ins[1:]:
        total = total + ref[...].astype(F32)
    total_s[...] = total.astype(BF16).reshape(total_s.shape)
    for k in range(outputs):
        outs[k][...] = total_s[index_ref[k]].reshape(outs[k].shape)


def split_sum(arrays, index, name):
    outputs = index.shape[0]
    shape = arrays[0].shape
    lead = shape[0] // outputs
    out = shape[1:] if lead == 1 else (lead,) + shape[1:]
    return pl.pallas_call(
        functools.partial(split_sum_kernel, len(arrays), outputs),
        in_specs=[SMEM] + [VMEM] * len(arrays),
        out_specs=[VMEM] * outputs,
        out_shape=[jax.ShapeDtypeStruct(out, BF16)] * outputs,
        scratch_shapes=[pltpu.VMEM((outputs, lead) + shape[1:], BF16)],
        compiler_params=pltpu.CompilerParams(vmem_limit_bytes=SMALL_LIMIT),
        name=name,
    )(index, *arrays)


def sum_kernel(*refs):
    total = refs[0][...].astype(F32)
    for ref in refs[1:-1]:
        total = total + ref[...].astype(F32)
    refs[-1][...] = total.astype(BF16)


def plain_sum(arrays, name):
    return pl.pallas_call(
        sum_kernel,
        in_specs=[VMEM] * len(arrays),
        out_specs=VMEM,
        out_shape=jax.ShapeDtypeStruct(arrays[0].shape, BF16),
        compiler_params=pltpu.CompilerParams(vmem_limit_bytes=SMALL_LIMIT),
        name=name,
    )(*arrays)


def unpack_kernel(parts, width, emb, tokens, scale, index_ref, *rest):
    ins = rest[:parts]
    wo_ref, proj_ref, gain_ref, bias_ref, loss_ref, small_s = rest[parts:]
    per = ins[0].shape[0]
    for a in range(parts):
        for k in range(per):
            c = index_ref[a * per + k]
            value = ins[a][k].astype(F32)
            wo_ref[c] = value[:, :width]
            proj_ref[c] = value[:, width : width + emb]
            small_s[c] = value[:, width + emb :]
    turned = small_s[...].reshape(width, 128).T
    for v in range(width // 128):
        gain_ref[v : v + 1] = turned[0:1, v * 128 : (v + 1) * 128]
        bias_ref[v : v + 1] = turned[1:2, v * 128 : (v + 1) * 128]
    loss_ref[0] = jnp.sum(turned[tokens : 2 * tokens, 0:1]) * scale


def unpack(arrays, index, width, emb, tokens, scale):
    parts = len(arrays)
    per, chunk, _ = arrays[0].shape
    chunks = parts * per
    return pl.pallas_call(
        functools.partial(unpack_kernel, parts, width, emb, tokens, scale),
        in_specs=[SMEM] + [VMEM] * parts,
        out_specs=[VMEM] * 4 + [SMEM],
        out_shape=[jax.ShapeDtypeStruct((chunks, chunk, n), F32) for n in (width, emb)]
        + [jax.ShapeDtypeStruct((width // 128, 128), F32)] * 2
        + [jax.ShapeDtypeStruct((1,), F32)],
        scratch_shapes=[pltpu.VMEM((chunks, chunk, 128), F32)],
        compiler_params=pltpu.CompilerParams(vmem_limit_bytes=SMALL_LIMIT),
        name="unpack",
    )(index, *arrays)


def local(
    context,
    stream,
    out_weight,
    gain,
    bias,
    proj_weight,
    query_states,
    passage_len,
    passage_dest,
    teacher_states,
    teacher_query,
    teacher_key,
):
    dp = lax.axis_size("dp")
    nt = lax.axis_size("tensor")
    chips = dp // CORES
    me = lax.axis_index("dp")
    chip, core = me // CORES, me % CORES
    mt = lax.axis_index("tensor")
    count, seq, width = context.shape
    emb = proj_weight.shape[1]
    group_queries, tokens, _ = query_states.shape
    depth, heads = teacher_query.shape
    per = count // dp
    per_query = count * nt // group_queries

    def flat(a):
        return a.transpose(1, 0, 2).reshape(-1, a.shape[2])

    def shift_chip(x, k):
        return lax.ppermute(
            x, "dp", [(c * CORES + o, (c + k) % chips * CORES + o) for c in range(chips) for o in range(CORES)]
        )

    def swap_core(x):
        return lax.ppermute(x, "dp", [(d, d ^ 1) for d in range(dp)])

    def shift_t(x, k):
        return lax.ppermute(x, "tensor", [(t, (t + k) % nt) for t in range(nt)])

    dest_group = passage_dest // (count * nt)
    rows = jnp.arange(count, dtype=jnp.int32)
    rank = jnp.sum(
        (dest_group[:, None] == dest_group[None, :]) & (rows[None, :] < rows[:, None]), axis=1, dtype=jnp.int32
    )
    place = dest_group * per + rank
    positions = jnp.sum(
        jnp.where(place[:, None] == rows[None, :], (passage_dest % count)[:, None], 0), axis=0
    )
    each = group_queries * tokens
    states = query_states.reshape(each, width)
    column_blocks = [states[:, n * heads : (n + 1) * heads] for n in range(width // heads)]
    extra = jnp.pad(positions.astype(BF16)[None, :], ((0, 15), (0, heads - count)))
    rider = jnp.concatenate(column_blocks + [extra], axis=0)

    part = depth // dp
    mine = jnp.stack(
        [lax.dynamic_slice_in_dim(w, me * part, part, 0) for w in (teacher_query, teacher_key)]
    )
    rider = jnp.pad(rider, ((0, -rider.shape[0] % part), (0, 0))).reshape(-1, part, heads)
    slices = 2 * (nt - 1)
    along = jnp.concatenate([shift_t(mine, k) for k in range(1, nt)] + [rider], axis=0)
    pieces = [along] + [shift_chip(along, k) for k in range(1, chips)]
    shifts = jnp.arange(chips, dtype=jnp.int32)
    behind = (chip - shifts) % chips
    piece_rows = jnp.concatenate([behind * CORES + core, behind * CORES + 1 - core]).astype(jnp.int32)
    midx = place.astype(jnp.int32)
    def piece_of(group):
        return (chip - group // CORES) % chips + jnp.where(group % CORES == core, 0, chips)

    qidx = passage_dest // per_query - dest_group * group_queries + piece_of(dest_group) * group_queries
    qidx = qidx.astype(jnp.int32)
    source = piece_of(jnp.arange(dp, dtype=jnp.int32)).astype(jnp.int32)

    gain2, bias2 = gain.reshape(-1, 128), bias.reshape(-1, 128)
    x = flat(context)
    normed, embeds, inverse, turned = student_forward(x, flat(stream), out_weight, gain2, bias2, proj_weight)
    pieces[1:], normed, embeds, inverse, turned, proj_turned = lax.optimization_barrier(
        (pieces[1:], normed, embeds, inverse, turned, proj_weight.T)
    )
    pieces = pieces + [swap_core(a) for a in pieces]
    told = [a[slices:].reshape(-1, heads)[width // heads * each, :count] for a in pieces]
    order = lax.dynamic_slice_in_dim(jnp.stack(told), me * per, per, 1).astype(jnp.int32)
    maps = teacher_maps(
        order, source, piece_rows, slices, flat(teacher_states), teacher_query, teacher_key, pieces, count, tokens
    )
    maps, embeds = lax.optimization_barrier((maps, embeds))
    maps = lax.all_to_all(maps, "dp", split_axis=0, concat_axis=0, tiled=True)
    scores = student_scores(
        qidx, passage_len, embeds, proj_weight, pieces, slices, count, tokens, group_queries
    )
    chunk = width // (CORES * chips * nt)
    sg, send, keep = student_backward(
        qidx, midx, passage_len, core.astype(jnp.int32).reshape(1), maps, scores,
        embeds, turned, normed, inverse, gain2, bias2, proj_weight, proj_turned,
        count, tokens, group_queries, chunk,
    )

    ahead = ((chip + shifts) % chips).astype(jnp.int32)
    t_shifts = jnp.arange(nt, dtype=jnp.int32)
    t_ahead = ((mt + t_shifts) % nt).astype(jnp.int32)
    parts = split_sum([keep, swap_core(send)], ahead, "sum_cores")
    parts, sg = lax.optimization_barrier((parts, sg))
    grad_context = context_grad(sg, out_weight)
    parts = [parts[0]] + [shift_chip(parts[k], k) for k in range(1, chips)]
    parts, grad_context = lax.optimization_barrier((parts, grad_context))
    parts = split_sum(parts, t_ahead, "sum_plane")
    parts = [parts[0]] + [shift_t(parts[k], k) for k in range(1, nt)]
    total = plain_sum(parts, "sum_tensor")
    line = jnp.stack([total] + [shift_t(total, k) for k in range(1, nt)])
    plane = [line] + [shift_chip(line, k) for k in range(1, chips)]
    arrays = plane + [swap_core(a) for a in plane]
    base = jnp.concatenate([core * chips + behind, (1 - core) * chips + behind]) * nt
    index = (base[:, None] + ((mt - t_shifts) % nt)[None, :]).reshape(-1).astype(jnp.int32)
    grad_out, grad_proj, grad_gain, grad_bias, loss = unpack(
        arrays, index, width, emb, tokens, 1.0 / (count * dp * nt * tokens)
    )
    return (
        loss.reshape(()),
        grad_out.reshape(width, width),
        grad_proj.reshape(width, emb),
        grad_gain.reshape(width),
        grad_bias.reshape(width),
        grad_context.reshape(seq, count, width).transpose(1, 0, 2),
    )


def solution(mesh):
    return jax.shard_map(
        local,
        mesh=mesh,
        in_specs=(
            P(("dp", "tensor"), None, None),
            P(("dp", "tensor"), None, None),
            P(),
            P(),
            P(),
            P(),
            P("dp", None, None),
            P(("dp", "tensor")),
            P(("dp", "tensor")),
            P(("dp", "tensor"), None, None),
            P(None, "tensor"),
            P(None, "tensor"),
        ),
        out_specs=(P(), P(), P(), P(), P(), P(("dp", "tensor"), None, None)),
        check_vma=False,
    )
```

```python
import functools
import math

import jax
import jax.numpy as jnp
from jax import lax
from jax.experimental import pallas as pl
from jax.experimental.pallas import tpu as pltpu
from jax.sharding import PartitionSpec as P

sharpness = 0.05
softcap = 10.0
epsilon = 1e-06
CORES = 2
VMEM_LIMIT = 56 * 1024 * 1024
SMALL_LIMIT = 14 * 1024 * 1024

F32 = jnp.float32
BF16 = jnp.bfloat16
VMEM = pl.BlockSpec(memory_space=pltpu.VMEM)
SMEM = pl.BlockSpec(memory_space=pltpu.SMEM)
ANY = pl.BlockSpec(memory_space=pl.ANY)


def up(n, m):
    return -(-n // m) * m


def dot(a, b, ca, cb):
    return lax.dot_general(a, b, (((ca,), (cb,)), ((), ())), preferred_element_type=F32)


def split_rows(rows, most):
    return max(n for n in range(16, most + 1, 16) if rows % n == 0)


def one_row(ref):
    return jnp.concatenate([ref[v : v + 1] for v in range(ref.shape[0])], axis=1)


def params(**kw):
    return pltpu.CompilerParams(vmem_limit_bytes=VMEM_LIMIT, **kw)


def cost(flops, nbytes):
    return pl.CostEstimate(flops=int(flops), bytes_accessed=int(nbytes), transcendentals=0)


def forward_kernel(x_ref, str_ref, wo_ref, gain_ref, bias_ref, wp_ref, *rest):
    normed_ref, emb_ref, inv_ref, turned_ref, prod_s, hid_s = rest[-6:]
    rows, width = x_ref.shape
    sub = rows
    gain, bias = one_row(gain_ref), one_row(bias_ref)
    for b in range(0, rows, sub):
        prod_s[b : b + sub] = dot(x_ref[b : b + sub], wo_ref[...], 1, 0)
        for c in range(b, b + sub, 16):
            summed = prod_s[c : c + 16] + str_ref[c : c + 16].astype(F32)
            centred = summed - jnp.mean(summed, axis=-1, keepdims=True)
            inverse = lax.rsqrt(jnp.mean(centred * centred, axis=-1, keepdims=True) + epsilon)
            normed = centred * inverse
            normed_ref[c : c + 16] = normed.astype(BF16)
            inv_ref[c : c + 16] = jnp.broadcast_to(inverse, (16, inv_ref.shape[1]))
            hid_s[c : c + 16] = (normed * gain + bias).astype(BF16)
        emb_ref[b : b + sub] = dot(hid_s[b : b + sub], wp_ref[...], 1, 0)
    turned_ref[0] = x_ref[...].T


def student_forward(x, stream, out_weight, gain, bias, proj_weight, first, last, before=()):
    total, width = x.shape
    emb = proj_weight.shape[1]
    rows = split_rows(total, 720)
    block = lambda n: pl.BlockSpec((rows, n), lambda s: (s + first, 0))
    whole = lambda a: pl.BlockSpec(a.shape, lambda s: (0,) * a.ndim)
    inputs = (x, stream, out_weight, gain, bias, proj_weight)
    return pl.pallas_call(
        forward_kernel,
        grid=(last - first,),
        in_specs=[block(width), block(width)] + [whole(a) for a in inputs[2:]] + [ANY] * len(before),
        out_specs=[block(width), block(emb), block(128), pl.BlockSpec((1, width, rows), lambda s: (s + first, 0, 0))],
        out_shape=[
            jax.ShapeDtypeStruct((total, width), BF16),
            jax.ShapeDtypeStruct((total, emb), F32),
            jax.ShapeDtypeStruct((total, 128), F32),
            jax.ShapeDtypeStruct((total // rows, width, rows), BF16),
        ],
        scratch_shapes=[pltpu.VMEM((rows, width), F32), pltpu.VMEM((rows, width), BF16)],
        input_output_aliases={len(inputs) + n: n for n in range(len(before))},
        compiler_params=params(),
        cost_estimate=cost(2 * (last - first) * rows * width * (width + emb), 8 * (last - first) * rows * width),
        name="student_forward",
    )(*inputs, *before)


def teacher_kernel(parts, count, tokens, order_ref, from_ref, rows_ref, states_ref, wq_ref, wk_ref, *rest):
    pieces, out_ref = rest[:parts], rest[parts]
    w_s, own_s, q_s, a_s, g_s, key_s, e_s, map_s, q_sem, key_sem, w_sem, own_sem = rest[parts + 1 :]
    depth = q_s.shape[1]
    slices = w_s.shape[0] // 2
    part_rows = pieces[0].shape[1]
    total = key_s.shape[0]
    seq = total // count
    blocks = key_sem.shape[0]
    rows = total // blocks
    first = count * tokens
    own = [
        pltpu.make_async_copy(wq_ref, own_s.at[0], own_sem.at[0]),
        pltpu.make_async_copy(wk_ref, own_s.at[1], own_sem.at[1]),
    ]
    queries = pltpu.make_async_copy(states_ref.at[pl.ds(0, first)], q_s, q_sem)
    gathered = [
        pltpu.make_async_copy(
            pieces[a].at[pl.ds(0, w_s.shape[0])],
            w_s.at[:, pl.ds(pl.multiple_of(rows_ref[a] * part_rows, part_rows), part_rows), :],
            w_sem.at[a],
        )
        for a in range(parts)
    ]
    keys = [
        pltpu.make_async_copy(
            states_ref.at[pl.ds(first + b * rows, rows)], key_s.at[pl.ds(b * rows, rows)], key_sem.at[b]
        )
        for b in range(blocks)
    ]
    queries.start()
    for copy in own + gathered:
        copy.start()
    queries.wait()
    for copy in own:
        copy.wait()
    for copy in keys:
        copy.start()
    q = q_s[...]
    heads = own_s.shape[2]
    a_s[:, slices * heads :] = dot(q, own_s[0], 1, 0).astype(BF16)
    for copy in gathered:
        copy.wait()
    for k in range(slices):
        a_s[:, k * heads : (k + 1) * heads] = dot(q, w_s[2 * k], 1, 0).astype(BF16)
    keys_weight = jnp.concatenate([w_s[2 * k + 1] for k in range(slices)] + [own_s[1]], axis=1)
    mixed = dot(a_s[...], keys_weight, 1, 1)
    for v in range(depth // 128):
        g_s[v] = mixed[:, v * 128 : (v + 1) * 128]
        for p in range(count):
            q_s[p * tokens : (p + 1) * tokens, v * 128 : (v + 1) * 128] = g_s[
                v, pl.ds(p, tokens, stride=count), :
            ].astype(BF16)
    mixed = q_s[...].T
    scale = 1.0 / (math.sqrt(depth) * softcap)
    side = 128 // tokens
    pair = lax.broadcasted_iota(jnp.int32, (rows, 128), 0) % count
    for b in range(blocks):
        keys[b].wait()
        raw = dot(key_s[b * rows : (b + 1) * rows], mixed, 1, 0)
        mine = raw[:, :128]
        for v in range(1, count // side):
            mine = jnp.where(pair >= v * side, raw[:, v * 128 : (v + 1) * 128], mine)
        e_s[b * rows : (b + 1) * rows] = jnp.exp(softcap * jnp.tanh(mine * scale))
    lane = lax.broadcasted_iota(jnp.int32, (seq, 128), 1) // tokens
    filler = jnp.zeros((up(seq, 128) - seq, 128), F32)
    for g in range(count // side):
        both = e_s[pl.ds(g * side, seq, stride=count), :]
        for v in range(1, side):
            both = jnp.where(lane == v, e_s[pl.ds(g * side + v, seq, stride=count), :], both)
        turned = jnp.concatenate([both, filler], axis=0).T
        for v in range(side):
            map_s[g * side + v] = turned[v * tokens : (v + 1) * tokens, :seq].astype(BF16)
    per = count // parts
    for n in range(count):
        out_ref[n] = map_s[order_ref[from_ref[n // per], n % per]]


def teacher_maps(order, source, rows, slices, states, wq, wk, pieces, count, tokens):
    total, depth = states.shape
    keys = total - count * tokens
    heads = wq.shape[1]
    parts = len(pieces)
    blocks = keys // split_rows(keys, 720)
    return pl.pallas_call(
        functools.partial(teacher_kernel, parts, count, tokens),
        in_specs=[SMEM] * 3 + [ANY] * (3 + parts),
        out_specs=VMEM,
        out_shape=jax.ShapeDtypeStruct((count, tokens, keys // count), BF16),
        scratch_shapes=[
            pltpu.VMEM((slices, depth, heads), BF16),
            pltpu.VMEM((2, depth, heads), BF16),
            pltpu.VMEM((count * tokens, depth), BF16),
            pltpu.VMEM((count * tokens, (slices // 2 + 1) * heads), BF16),
            pltpu.VMEM((depth // 128, count * tokens, 128), F32),
            pltpu.VMEM((keys, depth), BF16),
            pltpu.VMEM((keys, 128), F32),
            pltpu.VMEM((count, tokens, keys // count), BF16),
            pltpu.SemaphoreType.DMA,
            pltpu.SemaphoreType.DMA((blocks,)),
            pltpu.SemaphoreType.DMA((parts,)),
            pltpu.SemaphoreType.DMA((2,)),
        ],
        compiler_params=params(),
        cost_estimate=cost(8 * count * tokens * depth * depth, 2 * states.size + 4 * depth * depth),
        name="teacher_maps",
    )(order, source, rows, states, wq, wk, *pieces)


def rider_copies(pieces, slices, held, sem):
    part = pieces[0].shape[1]
    return [
        pltpu.make_async_copy(
            pieces[a].at[slices + x], held.at[a, pl.ds(x * part, part)], sem.at[a * (pieces[0].shape[0] - slices) + x]
        )
        for a in range(len(pieces))
        for x in range(pieces[0].shape[0] - slices)
    ]


def rider_states(held, a, each, width):
    heads = held.shape[2]
    return jnp.concatenate([held[a, n * each : (n + 1) * each] for n in range(width // heads)], axis=1)


def scores_kernel(tokens, count, group_queries, slices, parts, qidx_ref, len_ref, emb_ref, wp_ref, *rest):
    pieces = rest[:parts]
    (prob_ref, log_ref, units_ref, qunit_ref, qdir_ref, qlen_ref, qs_ref, dir_s, held_s, sem) = rest[parts:]
    copies = rider_copies(pieces, slices, held_s, sem)
    for copy in copies:
        copy.start()
    total, emb = emb_ref.shape
    seq = total // count
    sub = split_rows(total, 128)
    each = group_queries * tokens
    for b in range(0, total, sub):
        e = emb_ref[b : b + sub]
        dir_s[b : b + sub] = e / jnp.sqrt(jnp.sum(e * e, axis=-1, keepdims=True) + epsilon)
    for copy in copies:
        copy.wait()
    for a in range(parts):
        qs_ref[a * each : (a + 1) * each] = rider_states(held_s, a, each, qs_ref.shape[1])
    qe = dot(qs_ref[...], wp_ref[...], 1, 0)
    length = jnp.sqrt(jnp.sum(qe * qe, axis=-1, keepdims=True) + epsilon)
    qdir = qe / length
    qdir_ref[...] = qdir
    qlen_ref[...] = jnp.broadcast_to(length, qlen_ref.shape)
    qunit_ref[...] = qdir.astype(BF16).reshape(qunit_ref.shape)
    for r in range(count):
        units = dir_s[pl.ds(r, seq, stride=count), :].astype(BF16)
        units_ref[r] = units
        logits = dot(qunit_ref[qidx_ref[r]], units, 1, 1) / sharpness
        valid = lax.broadcasted_iota(jnp.int32, logits.shape, 1) < len_ref[r]
        student = jnp.where(valid, jnp.exp(logits), 0.0)
        student_total = jnp.sum(student, axis=-1, keepdims=True)
        prob_ref[r] = student / student_total
        log_ref[r] = logits - jnp.log(student_total)


def student_scores(qidx, lens, embeds, wp, pieces, slices, count, tokens, group_queries):
    total, emb = embeds.shape
    seq = total // count
    parts = len(pieces)
    queries = parts * group_queries
    riders, part, heads = pieces[0].shape
    riders -= slices
    return pl.pallas_call(
        functools.partial(scores_kernel, tokens, count, group_queries, slices, parts),
        in_specs=[SMEM, SMEM, VMEM, VMEM] + [ANY] * parts,
        out_specs=[VMEM] * 7,
        out_shape=[
            jax.ShapeDtypeStruct((count, tokens, seq), F32),
            jax.ShapeDtypeStruct((count, tokens, seq), F32),
            jax.ShapeDtypeStruct((count, seq, emb), BF16),
            jax.ShapeDtypeStruct((queries, tokens, emb), BF16),
            jax.ShapeDtypeStruct((queries * tokens, emb), F32),
            jax.ShapeDtypeStruct((queries * tokens, 128), F32),
            jax.ShapeDtypeStruct((queries * tokens, wp.shape[0]), BF16),
        ],
        scratch_shapes=[
            pltpu.VMEM((total, emb), F32),
            pltpu.VMEM((parts, riders * part, heads), BF16),
            pltpu.SemaphoreType.DMA((parts * riders,)),
        ],
        compiler_params=params(),
        cost_estimate=cost(1e9, 4 * total * emb),
        name="student_scores",
    )(qidx, lens, embeds, wp, *pieces)


def two_parts(a, b):
    high = a.astype(BF16)
    low = (a - high.astype(F32)).astype(BF16)
    return dot(high, b, 1, 0) + dot(low, b, 1, 0)


def backward_kernel(
    tokens, count, blocks,
    qidx_ref, midx_ref, len_ref, core_ref,
    maps_in, prob_in, log_in, units_in, qunit_in, emb_in, x_in, normed_in, inv_in, qs_in,
    qdir_ref, qlen_ref, gain_ref, bias_ref, wp_ref, wpt_ref,
    sg_out, send_ref, keep_ref,
    maps_s, prob_s, log_s, units_s, qunit_s, emb_s, x_s, normed_s, inv_s, qs_s,
    up_s, eg_s, mean_s, along_s, un_s, qg_s, hg_s, sg_s, wo_s, nt_s, right_s,
    first_sem, block_sem, out_sem, last_sem,
):
    total, width = normed_s.shape
    emb = emb_s.shape[1]
    seq = total // count
    rows = total // blocks
    sub = split_rows(rows, 256)
    thin = split_rows(total, 128)
    first = [
        pltpu.make_async_copy(src, dst, first_sem.at[n])
        for n, (src, dst) in enumerate(
            (
                (qunit_in, qunit_s), (maps_in, maps_s), (prob_in, prob_s), (log_in, log_s), (units_in, units_s),
                (emb_in, emb_s), (inv_in, inv_s),
            )
        )
    ]
    first, second = first[:5], first[5:]
    loads = [
        [
            pltpu.make_async_copy(
                normed_in.at[pl.ds(b * rows, rows)], normed_s.at[pl.ds(b * rows, rows)], block_sem.at[2 * b]
            ),
            pltpu.make_async_copy(x_in.at[b], x_s.at[b], block_sem.at[2 * b + 1]),
        ]
        for b in range(blocks)
    ]
    last = pltpu.make_async_copy(qs_in, qs_s, last_sem)
    for copy in first:
        copy.start()
    gain, bias = one_row(gain_ref), one_row(bias_ref)
    gain_w = two_parts(gain, wp_ref[...])
    bias_w = two_parts(bias, wp_ref[...])
    qg_s[...] = jnp.zeros_like(qg_s)
    for copy in first:
        copy.wait()
    for copy in second:
        copy.start()
    for pair in loads:
        for copy in pair:
            copy.start()
    last.start()

    spread = jnp.zeros((tokens, 1), F32)
    for r in range(count):
        teacher = maps_s[midx_ref[r]].astype(F32)
        valid = lax.broadcasted_iota(jnp.int32, teacher.shape, 1) < len_ref[r]
        teacher_log = jnp.log(teacher)
        teacher = jnp.where(valid, teacher, 0.0)
        teacher_total = jnp.sum(teacher, axis=-1, keepdims=True)
        teacher_prob = teacher / teacher_total
        gap = (teacher_log - jnp.log(teacher_total)) - log_s[r]
        spread += jnp.sum(jnp.where(valid, teacher_prob * gap, 0.0), axis=-1, keepdims=True)
        slope = ((prob_s[r] - teacher_prob) / (tokens * sharpness)).astype(BF16)
        up_s[pl.ds(r, seq, stride=count), :] = dot(slope, qunit_s[qidx_ref[r]], 0, 0).astype(BF16).astype(F32)
        un_s[r] = dot(slope, units_s[r], 1, 0)
    for r in range(count):
        qg_s[qidx_ref[r]] += un_s[r]
    total_eg = jnp.zeros((1, emb), F32)
    for copy in second:
        copy.wait()
    for b in range(0, total, thin):
        e = emb_s[b : b + thin]
        upstream = up_s[b : b + thin]
        length = jnp.sqrt(jnp.sum(e * e, axis=-1, keepdims=True) + epsilon)
        direction = e / length
        eg = (upstream - direction * jnp.sum(direction * upstream, axis=-1, keepdims=True)) / length
        eg = eg.astype(BF16)
        eg_s[b : b + thin] = eg
        eg = eg.astype(F32)
        total_eg += jnp.sum(eg, axis=0, keepdims=True)
        inverse = inv_s[b : b + thin]
        mean_s[b : b + thin] = inverse * (jnp.sum(eg * gain_w, axis=-1, keepdims=True) / width)
        along_s[b : b + thin] = inverse * (jnp.sum(eg * (e - bias_w), axis=-1, keepdims=True) / width)

    wo_s[...] = jnp.zeros_like(wo_s)
    nt_s[...] = jnp.zeros_like(nt_s)

    def wide(b, _):
        base = pl.multiple_of(b * rows, rows)
        part = pl.ds(base, rows)
        pltpu.make_async_copy(normed_in.at[part], normed_s.at[part], block_sem.at[2 * b]).wait()
        for n in range(0, rows, sub):
            hg_s[n : n + sub] = dot(eg_s[pl.ds(base + n, sub)], wpt_ref[...], 1, 0)
            for c in range(n, n + sub, 16):
                here = pl.ds(base + c, 16)
                inverse, mean, along = inv_s[here], mean_s[here], along_s[here]
                for v in range(0, width, 128):
                    scaled = hg_s[c : c + 16, v : v + 128] * gain[:, v : v + 128]
                    normed = normed_s[here, v : v + 128].astype(F32)
                    sg_s[here, v : v + 128] = (inverse * scaled - mean - normed * along).astype(BF16)
        pltpu.make_async_copy(sg_s.at[part], sg_out.at[part], out_sem.at[b]).start()
        pltpu.make_async_copy(x_in.at[b], x_s.at[b], block_sem.at[2 * b + 1]).wait()
        wo_s[...] += dot(x_s[b], sg_s[part], 1, 0)
        nt_s[...] += dot(eg_s[part], normed_s[part], 0, 0)
        return 0

    lax.fori_loop(0, blocks, wide, 0)

    last.wait()
    qg = qg_s[...].reshape(qdir_ref.shape)
    qdir = qdir_ref[...]
    qeg = (qg - qdir * jnp.sum(qdir * qg, axis=-1, keepdims=True)) / qlen_ref[:, :1]
    high = qeg.astype(BF16)
    low = (qeg - high.astype(F32)).astype(BF16)
    qs = qs_s[...]
    proj_query = dot(high, qs, 0, 0) + dot(low, qs, 0, 0)
    nt = nt_s[...]
    s = jnp.broadcast_to(total_eg, (emb, emb)).T[:, :1]
    wpt = wpt_ref[...].astype(F32)
    proj = nt * gain + s * bias + proj_query
    gain_row = jnp.sum(wpt * nt, axis=0, keepdims=True)
    bias_row = jnp.sum(wpt * s, axis=0, keepdims=True)
    index = lax.broadcasted_iota(jnp.int32, (tokens, width), 0)
    top = jnp.where(index == 0, gain_row, jnp.where(index == 1, bias_row, 0.0))
    rest_rows = jnp.zeros((128 - 2 * tokens, width), F32)
    right_s[...] = jnp.concatenate([proj, top, jnp.broadcast_to(spread, (tokens, width)), rest_rows], axis=0).T
    half = width // CORES
    chunk = send_ref.shape[1]
    for ref, which in ((send_ref, 1 - core_ref[0]), (keep_ref, core_ref[0])):
        start = pl.multiple_of(which * half, half)
        left, right = wo_s[pl.ds(start, half)], right_s[pl.ds(start, half)]
        for c in range(half // chunk):
            ref[c, :, :width] = left[c * chunk : (c + 1) * chunk].astype(BF16)
            ref[c, :, width:] = right[c * chunk : (c + 1) * chunk].astype(BF16)
    for b in range(blocks):
        part = pl.ds(b * rows, rows)
        pltpu.make_async_copy(sg_s.at[part], sg_out.at[part], out_sem.at[b]).wait()


def student_backward(
    qidx, midx, lens, core, maps, scores, embeds, x, normed, inverse, gain, bias, wp, wpt,
    count, tokens, group_queries, chunk,
):
    total, width = normed.shape
    emb = wp.shape[1]
    blocks = x.shape[0]
    chunks = width // CORES // chunk
    prob, log, units, qunit, qdir, qlen, qs = scores
    manual = [maps, prob, log, units, qunit, embeds, x, normed, inverse, qs]
    packed = jax.ShapeDtypeStruct((chunks, chunk, width + emb + 128), BF16)
    return pl.pallas_call(
        functools.partial(backward_kernel, tokens, count, blocks),
        in_specs=[SMEM] * 4 + [ANY] * len(manual) + [VMEM] * 6,
        out_specs=[ANY, VMEM, VMEM],
        scratch_shapes=[pltpu.VMEM(a.shape, a.dtype) for a in manual]
        + [
            pltpu.VMEM((total, emb), F32),
            pltpu.VMEM((total, emb), BF16),
            pltpu.VMEM((total, 128), F32),
            pltpu.VMEM((total, 128), F32),
            pltpu.VMEM((count, tokens, emb), F32),
            pltpu.VMEM(qunit.shape, F32),
            pltpu.VMEM((total // blocks, width), F32),
            pltpu.VMEM((total, width), BF16),
            pltpu.VMEM((width, width), F32),
            pltpu.VMEM((emb, width), F32),
            pltpu.VMEM((width, emb + 128), F32),
            pltpu.SemaphoreType.DMA((7,)),
            pltpu.SemaphoreType.DMA((2 * blocks,)),
            pltpu.SemaphoreType.DMA((blocks,)),
            pltpu.SemaphoreType.DMA,
        ],
        out_shape=[jax.ShapeDtypeStruct((total, width), BF16), packed, packed],
        compiler_params=params(),
        cost_estimate=cost(2 * total * width * (width + 2 * emb), 8 * total * width),
        name="student_backward",
    )(qidx, midx, lens, core, *manual, qdir, qlen, gain, bias, wp, wpt)


def context_kernel(sg_ref, wo_ref, *rest):
    out_ref = rest[-1]
    out_ref[...] = dot(sg_ref[...], wo_ref[...], 1, 1).astype(BF16)


def context_grad(sg, out_weight, first, last, before=()):
    total, width = sg.shape
    rows = split_rows(total, 720)
    block = pl.BlockSpec((rows, width), lambda s: (s + first, 0))
    return pl.pallas_call(
        context_kernel,
        grid=(last - first,),
        in_specs=[block, pl.BlockSpec(out_weight.shape, lambda s: (0, 0))] + [ANY] * len(before),
        out_specs=block,
        out_shape=jax.ShapeDtypeStruct(sg.shape, BF16),
        input_output_aliases={2: 0} if before else {},
        compiler_params=params(),
        cost_estimate=cost(2 * (last - first) * rows * width * width, 4 * (last - first) * rows * width),
        name="context_grad",
    )(sg, out_weight, *before)


def split_sum_kernel(inputs, outputs, index_ref, *rest):
    ins, outs, total_s = rest[:inputs], rest[inputs : inputs + outputs], rest[-1]
    total = ins[0][...].astype(F32)
    for ref in ins[1:]:
        total = total + ref[...].astype(F32)
    total_s[...] = total.astype(BF16).reshape(total_s.shape)
    for k in range(outputs):
        outs[k][...] = total_s[index_ref[k]].reshape(outs[k].shape)


def split_sum(arrays, index, name):
    outputs = index.shape[0]
    shape = arrays[0].shape
    lead = shape[0] // outputs
    out = shape[1:] if lead == 1 else (lead,) + shape[1:]
    return pl.pallas_call(
        functools.partial(split_sum_kernel, len(arrays), outputs),
        in_specs=[SMEM] + [VMEM] * len(arrays),
        out_specs=[VMEM] * outputs,
        out_shape=[jax.ShapeDtypeStruct(out, BF16)] * outputs,
        scratch_shapes=[pltpu.VMEM((outputs, lead) + shape[1:], BF16)],
        compiler_params=pltpu.CompilerParams(vmem_limit_bytes=SMALL_LIMIT),
        name=name,
    )(index, *arrays)


def sum_kernel(*refs):
    total = refs[0][...].astype(F32)
    for ref in refs[1:-1]:
        total = total + ref[...].astype(F32)
    refs[-1][...] = total.astype(BF16)


def plain_sum(arrays, name):
    return pl.pallas_call(
        sum_kernel,
        in_specs=[VMEM] * len(arrays),
        out_specs=VMEM,
        out_shape=jax.ShapeDtypeStruct(arrays[0].shape, BF16),
        compiler_params=pltpu.CompilerParams(vmem_limit_bytes=SMALL_LIMIT),
        name=name,
    )(*arrays)


def unpack_kernel(parts, width, emb, tokens, scale, index_ref, *rest):
    ins = rest[:parts]
    wo_ref, proj_ref, gain_ref, bias_ref, loss_ref, small_s = rest[parts:]
    per = ins[0].shape[0]
    for a in range(parts):
        for k in range(per):
            c = index_ref[a * per + k]
            value = ins[a][k].astype(F32)
            wo_ref[c] = value[:, :width]
            proj_ref[c] = value[:, width : width + emb]
            small_s[c] = value[:, width + emb :]
    turned = small_s[...].reshape(width, 128).T
    for v in range(width // 128):
        gain_ref[v : v + 1] = turned[0:1, v * 128 : (v + 1) * 128]
        bias_ref[v : v + 1] = turned[1:2, v * 128 : (v + 1) * 128]
    loss_ref[0] = jnp.sum(turned[tokens : 2 * tokens, 0:1]) * scale


def unpack(arrays, index, width, emb, tokens, scale):
    parts = len(arrays)
    per, chunk, _ = arrays[0].shape
    chunks = parts * per
    return pl.pallas_call(
        functools.partial(unpack_kernel, parts, width, emb, tokens, scale),
        in_specs=[SMEM] + [VMEM] * parts,
        out_specs=[VMEM] * 4 + [SMEM],
        out_shape=[jax.ShapeDtypeStruct((chunks, chunk, n), F32) for n in (width, emb)]
        + [jax.ShapeDtypeStruct((width // 128, 128), F32)] * 2
        + [jax.ShapeDtypeStruct((1,), F32)],
        scratch_shapes=[pltpu.VMEM((chunks, chunk, 128), F32)],
        compiler_params=pltpu.CompilerParams(vmem_limit_bytes=SMALL_LIMIT),
        name="unpack",
    )(index, *arrays)


def local(
    context,
    stream,
    out_weight,
    gain,
    bias,
    proj_weight,
    query_states,
    passage_len,
    passage_dest,
    teacher_states,
    teacher_query,
    teacher_key,
):
    dp = lax.axis_size("dp")
    nt = lax.axis_size("tensor")
    chips = dp // CORES
    me = lax.axis_index("dp")
    chip, core = me // CORES, me % CORES
    mt = lax.axis_index("tensor")
    count, seq, width = context.shape
    emb = proj_weight.shape[1]
    group_queries, tokens, _ = query_states.shape
    depth, heads = teacher_query.shape
    per = count // dp
    per_query = count * nt // group_queries

    def flat(a):
        return a.transpose(1, 0, 2).reshape(-1, a.shape[2])

    paired = chips & (chips - 1) == 0

    def partner(c, k):
        return c ^ k if paired else (c + k) % chips

    def shift_chip(x, k):
        return lax.ppermute(
            x, "dp", [(c * CORES + o, partner(c, k) * CORES + o) for c in range(chips) for o in range(CORES)]
        )

    def swap_core(x):
        return lax.ppermute(x, "dp", [(d, d ^ 1) for d in range(dp)])

    def shift_t(x, k):
        return lax.ppermute(x, "tensor", [(t, (t + k) % nt) for t in range(nt)])

    dest_group = passage_dest // (count * nt)
    rows = jnp.arange(count, dtype=jnp.int32)
    rank = jnp.sum(
        (dest_group[:, None] == dest_group[None, :]) & (rows[None, :] < rows[:, None]), axis=1, dtype=jnp.int32
    )
    place = dest_group * per + rank
    positions = jnp.sum(
        jnp.where(place[:, None] == rows[None, :], (passage_dest % count)[:, None], 0), axis=0
    )
    each = group_queries * tokens
    states = query_states.reshape(each, width)
    column_blocks = [states[:, n * heads : (n + 1) * heads] for n in range(width // heads)]
    extra = jnp.pad(positions.astype(BF16)[None, :], ((0, 15), (0, heads - count)))
    rider = jnp.concatenate(column_blocks + [extra], axis=0)

    part = depth // dp
    slices = 2 * (nt - 1)
    by_hops = sorted(range(1, chips), key=lambda k: (bin(k).count("1"), k))
    far = by_hops[len(by_hops) - chips // 4 :] if paired else []

    def slice_of(c):
        start = (c * CORES + core) * part
        return jnp.stack([lax.dynamic_slice_in_dim(w, start, part, 0) for w in (teacher_query, teacher_key)])

    mine, far_mine = slice_of(chip), [slice_of(partner(chip, k)) for k in far]
    rider = jnp.pad(rider, ((0, -rider.shape[0] % part), (0, 0))).reshape(-1, part, heads)
    along = jnp.concatenate([shift_t(mine, k) for k in range(1, nt)] + [rider], axis=0)
    gain2, bias2 = gain.reshape(-1, 128), bias.reshape(-1, 128)
    x = flat(context)
    blocks = x.shape[0] // split_rows(x.shape[0], 720)
    forward = functools.partial(student_forward, x, flat(stream), out_weight, gain2, bias2, proj_weight)
    begun = forward(0, 1)
    along, far_mine, begun = lax.optimization_barrier((along, far_mine, begun))
    pieces = [along] + [None] * (chips - 1)
    for k in range(1, chips):
        if k not in far:
            pieces[k] = shift_chip(along, k)
    for k, other in zip(far, far_mine):
        received = [shift_t(other, n) for n in range(1, nt)]
        pieces[k] = jnp.concatenate(received + [shift_chip(rider, k)], axis=0)
    shifts = jnp.arange(chips, dtype=jnp.int32)
    behind = chip ^ shifts if paired else (chip - shifts) % chips
    piece_rows = jnp.concatenate([behind * CORES + core, behind * CORES + 1 - core]).astype(jnp.int32)
    midx = place.astype(jnp.int32)
    def piece_of(group):
        apart = chip ^ (group // CORES) if paired else (chip - group // CORES) % chips
        return apart + jnp.where(group % CORES == core, 0, chips)

    qidx = passage_dest // per_query - dest_group * group_queries + piece_of(dest_group) * group_queries
    qidx = qidx.astype(jnp.int32)
    source = piece_of(jnp.arange(dp, dtype=jnp.int32)).astype(jnp.int32)

    normed, embeds, inverse, turned = forward(1, blocks, begun) if blocks > 1 else begun
    pieces[1:], normed, embeds, inverse, turned, proj_turned = lax.optimization_barrier(
        (pieces[1:], normed, embeds, inverse, turned, proj_weight.T)
    )
    pieces = pieces + [swap_core(a) for a in pieces]
    told = [a[slices:].reshape(-1, heads)[width // heads * each, :count] for a in pieces]
    order = lax.dynamic_slice_in_dim(jnp.stack(told), me * per, per, 1).astype(jnp.int32)
    maps = teacher_maps(
        order, source, piece_rows, slices, flat(teacher_states), teacher_query, teacher_key, pieces, count, tokens
    )
    maps, embeds = lax.optimization_barrier((maps, embeds))
    maps = lax.all_to_all(maps, "dp", split_axis=0, concat_axis=0, tiled=True)
    scores = student_scores(
        qidx, passage_len, embeds, proj_weight, pieces, slices, count, tokens, group_queries
    )
    chunk = width // (CORES * chips * nt)
    sg, send, keep = student_backward(
        qidx, midx, passage_len, core.astype(jnp.int32).reshape(1), maps, scores,
        embeds, turned, normed, inverse, gain2, bias2, proj_weight, proj_turned,
        count, tokens, group_queries, chunk,
    )

    ahead = partner(chip, shifts).astype(jnp.int32)
    t_shifts = jnp.arange(nt, dtype=jnp.int32)
    t_ahead = ((mt + t_shifts) % nt).astype(jnp.int32)
    parts = split_sum([keep, swap_core(send)], ahead, "sum_cores")
    parts, sg = lax.optimization_barrier((parts, sg))
    most = max(blocks - 1, 1)
    grad_context = context_grad(sg, out_weight, 0, most)
    parts = [parts[0]] + [shift_chip(parts[k], k) for k in range(1, chips)]
    parts, grad_context = lax.optimization_barrier((parts, grad_context))
    parts = split_sum(parts, t_ahead, "sum_plane")
    parts = [parts[0]] + [shift_t(parts[k], k) for k in range(1, nt)]
    total = plain_sum(parts, "sum_tensor")
    line = jnp.stack([total] + [shift_t(total, k) for k in range(1, nt)])
    if most < blocks:
        line, sg, grad_context = lax.optimization_barrier((line, sg, grad_context))
        grad_context = context_grad(sg, out_weight, most, blocks, (grad_context,))
    plane = [line] + [shift_chip(line, k) for k in range(1, chips)]
    arrays = plane + [swap_core(a) for a in plane]
    base = jnp.concatenate([core * chips + behind, (1 - core) * chips + behind]) * nt
    index = (base[:, None] + ((mt - t_shifts) % nt)[None, :]).reshape(-1).astype(jnp.int32)
    grad_out, grad_proj, grad_gain, grad_bias, loss = unpack(
        arrays, index, width, emb, tokens, 1.0 / (count * dp * nt * tokens)
    )
    return (
        loss.reshape(()),
        grad_out.reshape(width, width),
        grad_proj.reshape(width, emb),
        grad_gain.reshape(width),
        grad_bias.reshape(width),
        grad_context.reshape(seq, count, width).transpose(1, 0, 2),
    )


def solution(mesh):
    return jax.shard_map(
        local,
        mesh=mesh,
        in_specs=(
            P(("dp", "tensor"), None, None),
            P(("dp", "tensor"), None, None),
            P(),
            P(),
            P(),
            P(),
            P("dp", None, None),
            P(("dp", "tensor")),
            P(("dp", "tensor")),
            P(("dp", "tensor"), None, None),
            P(None, "tensor"),
            P(None, "tensor"),
        ),
        out_specs=(P(), P(), P(), P(), P(), P(("dp", "tensor"), None, None)),
        check_vma=False,
    )
```

```python
import functools
import math

import jax
import jax.numpy as jnp
from jax import lax
from jax.experimental import pallas as pl
from jax.experimental.pallas import tpu as pltpu
from jax.sharding import PartitionSpec as P

sharpness = 0.05
softcap = 10.0
epsilon = 1e-06
CORES = 2
VMEM_LIMIT = 56 * 1024 * 1024
SMALL_LIMIT = 14 * 1024 * 1024

F32 = jnp.float32
BF16 = jnp.bfloat16
VMEM = pl.BlockSpec(memory_space=pltpu.VMEM)
SMEM = pl.BlockSpec(memory_space=pltpu.SMEM)
ANY = pl.BlockSpec(memory_space=pl.ANY)


def up(n, m):
    return -(-n // m) * m


def dot(a, b, ca, cb):
    return lax.dot_general(a, b, (((ca,), (cb,)), ((), ())), preferred_element_type=F32)


def split_rows(rows, most):
    return max(n for n in range(16, most + 1, 16) if rows % n == 0)


def one_row(ref):
    return jnp.concatenate([ref[v : v + 1] for v in range(ref.shape[0])], axis=1)


def params(**kw):
    return pltpu.CompilerParams(vmem_limit_bytes=VMEM_LIMIT, **kw)


def cost(flops, nbytes):
    return pl.CostEstimate(flops=int(flops), bytes_accessed=int(nbytes), transcendentals=0)


def forward_kernel(x_ref, str_ref, wo_ref, gain_ref, bias_ref, wp_ref,
                   normed_ref, emb_ref, inv_ref, turned_ref, prod_s, hid_s):
    rows, width = x_ref.shape
    sub = rows
    gain, bias = one_row(gain_ref), one_row(bias_ref)
    for b in range(0, rows, sub):
        prod_s[b : b + sub] = dot(x_ref[b : b + sub], wo_ref[...], 1, 0)
        for c in range(b, b + sub, 16):
            summed = prod_s[c : c + 16] + str_ref[c : c + 16].astype(F32)
            centred = summed - jnp.mean(summed, axis=-1, keepdims=True)
            inverse = lax.rsqrt(jnp.mean(centred * centred, axis=-1, keepdims=True) + epsilon)
            normed = centred * inverse
            normed_ref[c : c + 16] = normed.astype(BF16)
            inv_ref[c : c + 16] = jnp.broadcast_to(inverse, (16, inv_ref.shape[1]))
            hid_s[c : c + 16] = (normed * gain + bias).astype(BF16)
        emb_ref[b : b + sub] = dot(hid_s[b : b + sub], wp_ref[...], 1, 0)
    turned_ref[0] = x_ref[...].T


def student_forward(x, stream, out_weight, gain, bias, proj_weight):
    total, width = x.shape
    emb = proj_weight.shape[1]
    rows = split_rows(total, 720)
    block = lambda n: pl.BlockSpec((rows, n), lambda s: (s, 0))
    whole = lambda a: pl.BlockSpec(a.shape, lambda s: (0,) * a.ndim)
    inputs = (x, stream, out_weight, gain, bias, proj_weight)
    return pl.pallas_call(
        forward_kernel,
        grid=(total // rows,),
        in_specs=[block(width), block(width)] + [whole(a) for a in inputs[2:]],
        out_specs=[block(width), block(emb), block(128), pl.BlockSpec((1, width, rows), lambda s: (s, 0, 0))],
        out_shape=[
            jax.ShapeDtypeStruct((total, width), BF16),
            jax.ShapeDtypeStruct((total, emb), F32),
            jax.ShapeDtypeStruct((total, 128), F32),
            jax.ShapeDtypeStruct((total // rows, width, rows), BF16),
        ],
        scratch_shapes=[pltpu.VMEM((rows, width), F32), pltpu.VMEM((rows, width), BF16)],
        compiler_params=params(),
        cost_estimate=cost(2 * total * width * (width + emb), 8 * total * width),
        name="student_forward",
    )(*inputs)


def teacher_kernel(parts, count, tokens, order_ref, from_ref, rows_ref, states_ref, wq_ref, wk_ref, *rest):
    pieces, out_ref = rest[:parts], rest[parts]
    w_s, own_s, q_s, a_s, g_s, key_s, e_s, map_s, q_sem, key_sem, w_sem, own_sem = rest[parts + 1 :]
    depth = q_s.shape[1]
    slices = w_s.shape[0] // 2
    part_rows = pieces[0].shape[1]
    total = key_s.shape[0]
    seq = total // count
    blocks = key_sem.shape[0]
    rows = total // blocks
    first = count * tokens
    own = [
        pltpu.make_async_copy(wq_ref, own_s.at[0], own_sem.at[0]),
        pltpu.make_async_copy(wk_ref, own_s.at[1], own_sem.at[1]),
    ]
    queries = pltpu.make_async_copy(states_ref.at[pl.ds(0, first)], q_s, q_sem)
    gathered = [
        pltpu.make_async_copy(
            pieces[a].at[pl.ds(0, w_s.shape[0])],
            w_s.at[:, pl.ds(pl.multiple_of(rows_ref[a] * part_rows, part_rows), part_rows), :],
            w_sem.at[a],
        )
        for a in range(parts)
    ]
    keys = [
        pltpu.make_async_copy(
            states_ref.at[pl.ds(first + b * rows, rows)], key_s.at[pl.ds(b * rows, rows)], key_sem.at[b]
        )
        for b in range(blocks)
    ]
    queries.start()
    for copy in own + gathered:
        copy.start()
    queries.wait()
    for copy in own:
        copy.wait()
    for copy in keys:
        copy.start()
    q = q_s[...]
    heads = own_s.shape[2]
    a_s[:, slices * heads :] = dot(q, own_s[0], 1, 0).astype(BF16)
    for copy in gathered:
        copy.wait()
    for k in range(slices):
        a_s[:, k * heads : (k + 1) * heads] = dot(q, w_s[2 * k], 1, 0).astype(BF16)
    keys_weight = jnp.concatenate([w_s[2 * k + 1] for k in range(slices)] + [own_s[1]], axis=1)
    mixed = dot(a_s[...], keys_weight, 1, 1)
    for v in range(depth // 128):
        g_s[v] = mixed[:, v * 128 : (v + 1) * 128]
        for p in range(count):
            q_s[p * tokens : (p + 1) * tokens, v * 128 : (v + 1) * 128] = g_s[
                v, pl.ds(p, tokens, stride=count), :
            ].astype(BF16)
    mixed = q_s[...].T
    scale = 1.0 / (math.sqrt(depth) * softcap)
    side = 128 // tokens
    pair = lax.broadcasted_iota(jnp.int32, (rows, 128), 0) % count
    for b in range(blocks):
        keys[b].wait()
        raw = dot(key_s[b * rows : (b + 1) * rows], mixed, 1, 0)
        mine = raw[:, :128]
        for v in range(1, count // side):
            mine = jnp.where(pair >= v * side, raw[:, v * 128 : (v + 1) * 128], mine)
        e_s[b * rows : (b + 1) * rows] = jnp.exp(softcap * jnp.tanh(mine * scale))
    lane = lax.broadcasted_iota(jnp.int32, (seq, 128), 1) // tokens
    filler = jnp.zeros((up(seq, 128) - seq, 128), F32)
    for g in range(count // side):
        both = e_s[pl.ds(g * side, seq, stride=count), :]
        for v in range(1, side):
            both = jnp.where(lane == v, e_s[pl.ds(g * side + v, seq, stride=count), :], both)
        turned = jnp.concatenate([both, filler], axis=0).T
        for v in range(side):
            map_s[g * side + v] = turned[v * tokens : (v + 1) * tokens, :seq].astype(BF16)
    per = count // parts
    for n in range(count):
        out_ref[n] = map_s[order_ref[from_ref[n // per], n % per]]


def teacher_maps(order, source, rows, slices, states, wq, wk, pieces, count, tokens):
    total, depth = states.shape
    keys = total - count * tokens
    heads = wq.shape[1]
    parts = len(pieces)
    blocks = keys // split_rows(keys, 720)
    return pl.pallas_call(
        functools.partial(teacher_kernel, parts, count, tokens),
        in_specs=[SMEM] * 3 + [ANY] * (3 + parts),
        out_specs=VMEM,
        out_shape=jax.ShapeDtypeStruct((count, tokens, keys // count), BF16),
        scratch_shapes=[
            pltpu.VMEM((slices, depth, heads), BF16),
            pltpu.VMEM((2, depth, heads), BF16),
            pltpu.VMEM((count * tokens, depth), BF16),
            pltpu.VMEM((count * tokens, (slices // 2 + 1) * heads), BF16),
            pltpu.VMEM((depth // 128, count * tokens, 128), F32),
            pltpu.VMEM((keys, depth), BF16),
            pltpu.VMEM((keys, 128), F32),
            pltpu.VMEM((count, tokens, keys // count), BF16),
            pltpu.SemaphoreType.DMA,
            pltpu.SemaphoreType.DMA((blocks,)),
            pltpu.SemaphoreType.DMA((parts,)),
            pltpu.SemaphoreType.DMA((2,)),
        ],
        compiler_params=params(),
        cost_estimate=cost(8 * count * tokens * depth * depth, 2 * states.size + 4 * depth * depth),
        name="teacher_maps",
    )(order, source, rows, states, wq, wk, *pieces)


def rider_copies(pieces, slices, held, sem):
    part = pieces[0].shape[1]
    return [
        pltpu.make_async_copy(
            pieces[a].at[slices + x], held.at[a, pl.ds(x * part, part)], sem.at[a * (pieces[0].shape[0] - slices) + x]
        )
        for a in range(len(pieces))
        for x in range(pieces[0].shape[0] - slices)
    ]


def rider_states(held, a, each, width):
    heads = held.shape[2]
    return jnp.concatenate([held[a, n * each : (n + 1) * each] for n in range(width // heads)], axis=1)


def scores_kernel(tokens, count, group_queries, slices, parts, qidx_ref, len_ref, emb_ref, wp_ref, *rest):
    pieces = rest[:parts]
    (prob_ref, log_ref, units_ref, qunit_ref, qdir_ref, qlen_ref, qs_ref, dir_s, held_s, sem) = rest[parts:]
    copies = rider_copies(pieces, slices, held_s, sem)
    for copy in copies:
        copy.start()
    total, emb = emb_ref.shape
    seq = total // count
    sub = split_rows(total, 128)
    each = group_queries * tokens
    for b in range(0, total, sub):
        e = emb_ref[b : b + sub]
        dir_s[b : b + sub] = e / jnp.sqrt(jnp.sum(e * e, axis=-1, keepdims=True) + epsilon)
    for copy in copies:
        copy.wait()
    for a in range(parts):
        qs_ref[a * each : (a + 1) * each] = rider_states(held_s, a, each, qs_ref.shape[1])
    qe = dot(qs_ref[...], wp_ref[...], 1, 0)
    length = jnp.sqrt(jnp.sum(qe * qe, axis=-1, keepdims=True) + epsilon)
    qdir = qe / length
    qdir_ref[...] = qdir
    qlen_ref[...] = jnp.broadcast_to(length, qlen_ref.shape)
    qunit_ref[...] = qdir.astype(BF16).reshape(qunit_ref.shape)
    for r in range(count):
        units = dir_s[pl.ds(r, seq, stride=count), :].astype(BF16)
        units_ref[r] = units
        logits = dot(qunit_ref[qidx_ref[r]], units, 1, 1) / sharpness
        valid = lax.broadcasted_iota(jnp.int32, logits.shape, 1) < len_ref[r]
        student = jnp.where(valid, jnp.exp(logits), 0.0)
        student_total = jnp.sum(student, axis=-1, keepdims=True)
        prob_ref[r] = student / student_total
        log_ref[r] = logits - jnp.log(student_total)


def student_scores(qidx, lens, embeds, wp, pieces, slices, count, tokens, group_queries):
    total, emb = embeds.shape
    seq = total // count
    parts = len(pieces)
    queries = parts * group_queries
    riders, part, heads = pieces[0].shape
    riders -= slices
    return pl.pallas_call(
        functools.partial(scores_kernel, tokens, count, group_queries, slices, parts),
        in_specs=[SMEM, SMEM, VMEM, VMEM] + [ANY] * parts,
        out_specs=[VMEM] * 7,
        out_shape=[
            jax.ShapeDtypeStruct((count, tokens, seq), F32),
            jax.ShapeDtypeStruct((count, tokens, seq), F32),
            jax.ShapeDtypeStruct((count, seq, emb), BF16),
            jax.ShapeDtypeStruct((queries, tokens, emb), BF16),
            jax.ShapeDtypeStruct((queries * tokens, emb), F32),
            jax.ShapeDtypeStruct((queries * tokens, 128), F32),
            jax.ShapeDtypeStruct((queries * tokens, wp.shape[0]), BF16),
        ],
        scratch_shapes=[
            pltpu.VMEM((total, emb), F32),
            pltpu.VMEM((parts, riders * part, heads), BF16),
            pltpu.SemaphoreType.DMA((parts * riders,)),
        ],
        compiler_params=params(),
        cost_estimate=cost(1e9, 4 * total * emb),
        name="student_scores",
    )(qidx, lens, embeds, wp, *pieces)


def two_parts(a, b):
    high = a.astype(BF16)
    low = (a - high.astype(F32)).astype(BF16)
    return dot(high, b, 1, 0) + dot(low, b, 1, 0)


def backward_kernel(
    tokens, count, blocks,
    qidx_ref, midx_ref, len_ref, core_ref,
    maps_in, prob_in, log_in, units_in, qunit_in, emb_in, x_in, normed_in, inv_in, qs_in,
    qdir_ref, qlen_ref, gain_ref, bias_ref, wp_ref, wpt_ref,
    sg_out, send_ref, keep_ref,
    maps_s, prob_s, log_s, units_s, qunit_s, emb_s, x_s, normed_s, inv_s, qs_s,
    up_s, eg_s, mean_s, along_s, un_s, qg_s, hg_s, sg_s, wo_s, nt_s, right_s,
    first_sem, block_sem, out_sem, last_sem,
):
    total, width = normed_s.shape
    emb = emb_s.shape[1]
    seq = total // count
    rows = total // blocks
    sub = split_rows(rows, 256)
    thin = split_rows(total, 128)
    first = [
        pltpu.make_async_copy(src, dst, first_sem.at[n])
        for n, (src, dst) in enumerate(
            (
                (qunit_in, qunit_s), (maps_in, maps_s), (prob_in, prob_s), (log_in, log_s), (units_in, units_s),
                (emb_in, emb_s), (inv_in, inv_s),
            )
        )
    ]
    first, second = first[:5], first[5:]
    loads = [
        [
            pltpu.make_async_copy(
                normed_in.at[pl.ds(b * rows, rows)], normed_s.at[pl.ds(b * rows, rows)], block_sem.at[2 * b]
            ),
            pltpu.make_async_copy(x_in.at[b], x_s.at[b], block_sem.at[2 * b + 1]),
        ]
        for b in range(blocks)
    ]
    last = pltpu.make_async_copy(qs_in, qs_s, last_sem)
    for copy in first:
        copy.start()
    gain, bias = one_row(gain_ref), one_row(bias_ref)
    gain_w = two_parts(gain, wp_ref[...])
    bias_w = two_parts(bias, wp_ref[...])
    qg_s[...] = jnp.zeros_like(qg_s)
    for copy in first:
        copy.wait()
    for copy in second:
        copy.start()
    for pair in loads:
        for copy in pair:
            copy.start()
    last.start()

    spread = jnp.zeros((tokens, 1), F32)
    for r in range(count):
        teacher = maps_s[midx_ref[r]].astype(F32)
        valid = lax.broadcasted_iota(jnp.int32, teacher.shape, 1) < len_ref[r]
        teacher_log = jnp.log(teacher)
        teacher = jnp.where(valid, teacher, 0.0)
        teacher_total = jnp.sum(teacher, axis=-1, keepdims=True)
        teacher_prob = teacher / teacher_total
        gap = (teacher_log - jnp.log(teacher_total)) - log_s[r]
        spread += jnp.sum(jnp.where(valid, teacher_prob * gap, 0.0), axis=-1, keepdims=True)
        slope = ((prob_s[r] - teacher_prob) / (tokens * sharpness)).astype(BF16)
        up_s[pl.ds(r, seq, stride=count), :] = dot(slope, qunit_s[qidx_ref[r]], 0, 0).astype(BF16).astype(F32)
        un_s[r] = dot(slope, units_s[r], 1, 0)
    for r in range(count):
        qg_s[qidx_ref[r]] += un_s[r]
    total_eg = jnp.zeros((1, emb), F32)
    for copy in second:
        copy.wait()
    for b in range(0, total, thin):
        e = emb_s[b : b + thin]
        upstream = up_s[b : b + thin]
        length = jnp.sqrt(jnp.sum(e * e, axis=-1, keepdims=True) + epsilon)
        direction = e / length
        eg = (upstream - direction * jnp.sum(direction * upstream, axis=-1, keepdims=True)) / length
        eg = eg.astype(BF16)
        eg_s[b : b + thin] = eg
        eg = eg.astype(F32)
        total_eg += jnp.sum(eg, axis=0, keepdims=True)
        inverse = inv_s[b : b + thin]
        mean_s[b : b + thin] = inverse * (jnp.sum(eg * gain_w, axis=-1, keepdims=True) / width)
        along_s[b : b + thin] = inverse * (jnp.sum(eg * (e - bias_w), axis=-1, keepdims=True) / width)

    wo_s[...] = jnp.zeros_like(wo_s)
    nt_s[...] = jnp.zeros_like(nt_s)

    def wide(b, _):
        base = pl.multiple_of(b * rows, rows)
        part = pl.ds(base, rows)
        pltpu.make_async_copy(normed_in.at[part], normed_s.at[part], block_sem.at[2 * b]).wait()
        for n in range(0, rows, sub):
            hg_s[n : n + sub] = dot(eg_s[pl.ds(base + n, sub)], wpt_ref[...], 1, 0)
            for c in range(n, n + sub, 16):
                here = pl.ds(base + c, 16)
                inverse, mean, along = inv_s[here], mean_s[here], along_s[here]
                for v in range(0, width, 128):
                    scaled = hg_s[c : c + 16, v : v + 128] * gain[:, v : v + 128]
                    normed = normed_s[here, v : v + 128].astype(F32)
                    sg_s[here, v : v + 128] = (inverse * scaled - mean - normed * along).astype(BF16)
        pltpu.make_async_copy(sg_s.at[part], sg_out.at[part], out_sem.at[b]).start()
        pltpu.make_async_copy(x_in.at[b], x_s.at[b], block_sem.at[2 * b + 1]).wait()
        wo_s[...] += dot(x_s[b], sg_s[part], 1, 0)
        nt_s[...] += dot(eg_s[part], normed_s[part], 0, 0)
        return 0

    lax.fori_loop(0, blocks, wide, 0)

    last.wait()
    qg = qg_s[...].reshape(qdir_ref.shape)
    qdir = qdir_ref[...]
    qeg = (qg - qdir * jnp.sum(qdir * qg, axis=-1, keepdims=True)) / qlen_ref[:, :1]
    high = qeg.astype(BF16)
    low = (qeg - high.astype(F32)).astype(BF16)
    qs = qs_s[...]
    proj_query = dot(high, qs, 0, 0) + dot(low, qs, 0, 0)
    nt = nt_s[...]
    s = jnp.broadcast_to(total_eg, (emb, emb)).T[:, :1]
    wpt = wpt_ref[...].astype(F32)
    proj = nt * gain + s * bias + proj_query
    gain_row = jnp.sum(wpt * nt, axis=0, keepdims=True)
    bias_row = jnp.sum(wpt * s, axis=0, keepdims=True)
    index = lax.broadcasted_iota(jnp.int32, (tokens, width), 0)
    top = jnp.where(index == 0, gain_row, jnp.where(index == 1, bias_row, 0.0))
    rest_rows = jnp.zeros((128 - 2 * tokens, width), F32)
    right_s[...] = jnp.concatenate([proj, top, jnp.broadcast_to(spread, (tokens, width)), rest_rows], axis=0).T
    half = width // CORES
    chunk = send_ref.shape[1]
    for ref, which in ((send_ref, 1 - core_ref[0]), (keep_ref, core_ref[0])):
        start = pl.multiple_of(which * half, half)
        left, right = wo_s[pl.ds(start, half)], right_s[pl.ds(start, half)]
        for c in range(half // chunk):
            ref[c, :, :width] = left[c * chunk : (c + 1) * chunk].astype(BF16)
            ref[c, :, width:] = right[c * chunk : (c + 1) * chunk].astype(BF16)
    for b in range(blocks):
        part = pl.ds(b * rows, rows)
        pltpu.make_async_copy(sg_s.at[part], sg_out.at[part], out_sem.at[b]).wait()


def student_backward(
    qidx, midx, lens, core, maps, scores, embeds, x, normed, inverse, gain, bias, wp, wpt,
    count, tokens, group_queries, chunk,
):
    total, width = normed.shape
    emb = wp.shape[1]
    blocks = x.shape[0]
    chunks = width // CORES // chunk
    prob, log, units, qunit, qdir, qlen, qs = scores
    manual = [maps, prob, log, units, qunit, embeds, x, normed, inverse, qs]
    packed = jax.ShapeDtypeStruct((chunks, chunk, width + emb + 128), BF16)
    return pl.pallas_call(
        functools.partial(backward_kernel, tokens, count, blocks),
        in_specs=[SMEM] * 4 + [ANY] * len(manual) + [VMEM] * 6,
        out_specs=[ANY, VMEM, VMEM],
        scratch_shapes=[pltpu.VMEM(a.shape, a.dtype) for a in manual]
        + [
            pltpu.VMEM((total, emb), F32),
            pltpu.VMEM((total, emb), BF16),
            pltpu.VMEM((total, 128), F32),
            pltpu.VMEM((total, 128), F32),
            pltpu.VMEM((count, tokens, emb), F32),
            pltpu.VMEM(qunit.shape, F32),
            pltpu.VMEM((total // blocks, width), F32),
            pltpu.VMEM((total, width), BF16),
            pltpu.VMEM((width, width), F32),
            pltpu.VMEM((emb, width), F32),
            pltpu.VMEM((width, emb + 128), F32),
            pltpu.SemaphoreType.DMA((7,)),
            pltpu.SemaphoreType.DMA((2 * blocks,)),
            pltpu.SemaphoreType.DMA((blocks,)),
            pltpu.SemaphoreType.DMA,
        ],
        out_shape=[jax.ShapeDtypeStruct((total, width), BF16), packed, packed],
        compiler_params=params(),
        cost_estimate=cost(2 * total * width * (width + 2 * emb), 8 * total * width),
        name="student_backward",
    )(qidx, midx, lens, core, *manual, qdir, qlen, gain, bias, wp, wpt)


def context_kernel(sg_ref, wo_ref, out_ref):
    out_ref[...] = dot(sg_ref[...], wo_ref[...], 1, 1).astype(BF16)


def context_grad(sg, out_weight):
    total, width = sg.shape
    rows = split_rows(total, 720)
    block = pl.BlockSpec((rows, width), lambda s: (s, 0))
    return pl.pallas_call(
        context_kernel,
        grid=(total // rows,),
        in_specs=[block, pl.BlockSpec(out_weight.shape, lambda s: (0, 0))],
        out_specs=block,
        out_shape=jax.ShapeDtypeStruct(sg.shape, BF16),
        compiler_params=params(),
        cost_estimate=cost(2 * total * width * width, 4 * total * width),
        name="context_grad",
    )(sg, out_weight)


def split_sum_kernel(inputs, outputs, index_ref, *rest):
    ins, outs, total_s = rest[:inputs], rest[inputs : inputs + outputs], rest[-1]
    total = ins[0][...].astype(F32)
    for ref in ins[1:]:
        total = total + ref[...].astype(F32)
    total_s[...] = total.astype(BF16).reshape(total_s.shape)
    for k in range(outputs):
        outs[k][...] = total_s[index_ref[k]].reshape(outs[k].shape)


def split_sum(arrays, index, name):
    outputs = index.shape[0]
    shape = arrays[0].shape
    lead = shape[0] // outputs
    out = shape[1:] if lead == 1 else (lead,) + shape[1:]
    return pl.pallas_call(
        functools.partial(split_sum_kernel, len(arrays), outputs),
        in_specs=[SMEM] + [VMEM] * len(arrays),
        out_specs=[VMEM] * outputs,
        out_shape=[jax.ShapeDtypeStruct(out, BF16)] * outputs,
        scratch_shapes=[pltpu.VMEM((outputs, lead) + shape[1:], BF16)],
        compiler_params=pltpu.CompilerParams(vmem_limit_bytes=SMALL_LIMIT),
        name=name,
    )(index, *arrays)


def sum_kernel(*refs):
    total = refs[0][...].astype(F32)
    for ref in refs[1:-1]:
        total = total + ref[...].astype(F32)
    refs[-1][...] = total.astype(BF16)


def plain_sum(arrays, name):
    return pl.pallas_call(
        sum_kernel,
        in_specs=[VMEM] * len(arrays),
        out_specs=VMEM,
        out_shape=jax.ShapeDtypeStruct(arrays[0].shape, BF16),
        compiler_params=pltpu.CompilerParams(vmem_limit_bytes=SMALL_LIMIT),
        name=name,
    )(*arrays)


def unpack_kernel(parts, width, emb, tokens, scale, index_ref, *rest):
    ins = rest[:parts]
    wo_ref, proj_ref, gain_ref, bias_ref, loss_ref, small_s = rest[parts:]
    per = ins[0].shape[0]
    for a in range(parts):
        for k in range(per):
            c = index_ref[a * per + k]
            value = ins[a][k].astype(F32)
            wo_ref[c] = value[:, :width]
            proj_ref[c] = value[:, width : width + emb]
            small_s[c] = value[:, width + emb :]
    turned = small_s[...].reshape(width, 128).T
    for v in range(width // 128):
        gain_ref[v : v + 1] = turned[0:1, v * 128 : (v + 1) * 128]
        bias_ref[v : v + 1] = turned[1:2, v * 128 : (v + 1) * 128]
    loss_ref[0] = jnp.sum(turned[tokens : 2 * tokens, 0:1]) * scale


def unpack(arrays, index, width, emb, tokens, scale):
    parts = len(arrays)
    per, chunk, _ = arrays[0].shape
    chunks = parts * per
    return pl.pallas_call(
        functools.partial(unpack_kernel, parts, width, emb, tokens, scale),
        in_specs=[SMEM] + [VMEM] * parts,
        out_specs=[VMEM] * 4 + [SMEM],
        out_shape=[jax.ShapeDtypeStruct((chunks, chunk, n), F32) for n in (width, emb)]
        + [jax.ShapeDtypeStruct((width // 128, 128), F32)] * 2
        + [jax.ShapeDtypeStruct((1,), F32)],
        scratch_shapes=[pltpu.VMEM((chunks, chunk, 128), F32)],
        compiler_params=pltpu.CompilerParams(vmem_limit_bytes=SMALL_LIMIT),
        name="unpack",
    )(index, *arrays)


def local(
    context,
    stream,
    out_weight,
    gain,
    bias,
    proj_weight,
    query_states,
    passage_len,
    passage_dest,
    teacher_states,
    teacher_query,
    teacher_key,
):
    dp = lax.axis_size("dp")
    nt = lax.axis_size("tensor")
    chips = dp // CORES
    me = lax.axis_index("dp")
    chip, core = me // CORES, me % CORES
    mt = lax.axis_index("tensor")
    count, seq, width = context.shape
    emb = proj_weight.shape[1]
    group_queries, tokens, _ = query_states.shape
    depth, heads = teacher_query.shape
    per = count // dp
    per_query = count * nt // group_queries

    def flat(a):
        return a.transpose(1, 0, 2).reshape(-1, a.shape[2])

    paired = chips & (chips - 1) == 0

    def partner(c, k):
        return c ^ k if paired else (c + k) % chips

    def shift_chip(x, k):
        return lax.ppermute(
            x, "dp", [(c * CORES + o, partner(c, k) * CORES + o) for c in range(chips) for o in range(CORES)]
        )

    def swap_core(x):
        return lax.ppermute(x, "dp", [(d, d ^ 1) for d in range(dp)])

    def shift_t(x, k):
        return lax.ppermute(x, "tensor", [(t, (t + k) % nt) for t in range(nt)])

    dest_group = passage_dest // (count * nt)
    rows = jnp.arange(count, dtype=jnp.int32)
    rank = jnp.sum(
        (dest_group[:, None] == dest_group[None, :]) & (rows[None, :] < rows[:, None]), axis=1, dtype=jnp.int32
    )
    place = dest_group * per + rank
    positions = jnp.sum(
        jnp.where(place[:, None] == rows[None, :], (passage_dest % count)[:, None], 0), axis=0
    )
    each = group_queries * tokens
    states = query_states.reshape(each, width)
    column_blocks = [states[:, n * heads : (n + 1) * heads] for n in range(width // heads)]
    extra = jnp.pad(positions.astype(BF16)[None, :], ((0, 15), (0, heads - count)))
    rider = jnp.concatenate(column_blocks + [extra], axis=0)

    part = depth // dp
    slices = 2 * (nt - 1)
    by_hops = sorted(range(1, chips), key=lambda k: (bin(k).count("1"), k))
    far = by_hops[len(by_hops) - chips // 4 :] if paired else []

    def slice_of(c):
        start = (c * CORES + core) * part
        return jnp.stack([lax.dynamic_slice_in_dim(w, start, part, 0) for w in (teacher_query, teacher_key)])

    mine, far_mine = slice_of(chip), [slice_of(partner(chip, k)) for k in far]
    rider = jnp.pad(rider, ((0, -rider.shape[0] % part), (0, 0))).reshape(-1, part, heads)
    along = jnp.concatenate([shift_t(mine, k) for k in range(1, nt)] + [rider], axis=0)
    gain2, bias2 = gain.reshape(-1, 128), bias.reshape(-1, 128)
    x = flat(context)
    far_riders = [shift_chip(rider, k) for k in far]
    along, far_mine, far_riders, forward_gain = lax.optimization_barrier((along, far_mine, far_riders, gain2))
    pieces = [along] + [None] * (chips - 1)
    for k in range(1, chips):
        if k not in far:
            pieces[k] = shift_chip(along, k)
    for k, other, far_rider in zip(far, far_mine, far_riders):
        pieces[k] = jnp.concatenate([shift_t(other, n) for n in range(1, nt)] + [far_rider], axis=0)
    shifts = jnp.arange(chips, dtype=jnp.int32)
    behind = chip ^ shifts if paired else (chip - shifts) % chips
    piece_rows = jnp.concatenate([behind * CORES + core, behind * CORES + 1 - core]).astype(jnp.int32)
    midx = place.astype(jnp.int32)
    def piece_of(group):
        apart = chip ^ (group // CORES) if paired else (chip - group // CORES) % chips
        return apart + jnp.where(group % CORES == core, 0, chips)

    qidx = passage_dest // per_query - dest_group * group_queries + piece_of(dest_group) * group_queries
    qidx = qidx.astype(jnp.int32)
    source = piece_of(jnp.arange(dp, dtype=jnp.int32)).astype(jnp.int32)

    normed, embeds, inverse, turned = student_forward(
        x, flat(stream), out_weight, forward_gain, bias2, proj_weight
    )
    pieces[1:], normed, embeds, inverse, turned, proj_turned = lax.optimization_barrier(
        (pieces[1:], normed, embeds, inverse, turned, proj_weight.T)
    )
    pieces = pieces + [swap_core(a) for a in pieces]
    told = [a[slices:].reshape(-1, heads)[width // heads * each, :count] for a in pieces]
    order = lax.dynamic_slice_in_dim(jnp.stack(told), me * per, per, 1).astype(jnp.int32)
    maps = teacher_maps(
        order, source, piece_rows, slices, flat(teacher_states), teacher_query, teacher_key, pieces, count, tokens
    )
    maps, embeds = lax.optimization_barrier((maps, embeds))
    maps = lax.all_to_all(maps, "dp", split_axis=0, concat_axis=0, tiled=True)
    scores = student_scores(
        qidx, passage_len, embeds, proj_weight, pieces, slices, count, tokens, group_queries
    )
    chunk = width // (CORES * chips * nt)
    sg, send, keep = student_backward(
        qidx, midx, passage_len, core.astype(jnp.int32).reshape(1), maps, scores,
        embeds, turned, normed, inverse, gain2, bias2, proj_weight, proj_turned,
        count, tokens, group_queries, chunk,
    )

    ahead = partner(chip, shifts).astype(jnp.int32)
    t_shifts = jnp.arange(nt, dtype=jnp.int32)
    t_ahead = ((mt + t_shifts) % nt).astype(jnp.int32)
    parts = split_sum([keep, swap_core(send)], ahead, "sum_cores")
    parts, sg = lax.optimization_barrier((parts, sg))
    grad_context = context_grad(sg, out_weight)
    parts = [parts[0]] + [shift_chip(parts[k], k) for k in range(1, chips)]
    parts, grad_context = lax.optimization_barrier((parts, grad_context))
    parts = split_sum(parts, t_ahead, "sum_plane")
    parts = [parts[0]] + [shift_t(parts[k], k) for k in range(1, nt)]
    total = plain_sum(parts, "sum_tensor")
    line = jnp.stack([total] + [shift_t(total, k) for k in range(1, nt)])
    plane = [line] + [shift_chip(line, k) for k in range(1, chips)]
    arrays = plane + [swap_core(a) for a in plane]
    base = jnp.concatenate([core * chips + behind, (1 - core) * chips + behind]) * nt
    index = (base[:, None] + ((mt - t_shifts) % nt)[None, :]).reshape(-1).astype(jnp.int32)
    grad_out, grad_proj, grad_gain, grad_bias, loss = unpack(
        arrays, index, width, emb, tokens, 1.0 / (count * dp * nt * tokens)
    )
    return (
        loss.reshape(()),
        grad_out.reshape(width, width),
        grad_proj.reshape(width, emb),
        grad_gain.reshape(width),
        grad_bias.reshape(width),
        grad_context.reshape(seq, count, width).transpose(1, 0, 2),
    )


def solution(mesh):
    return jax.shard_map(
        local,
        mesh=mesh,
        in_specs=(
            P(("dp", "tensor"), None, None),
            P(("dp", "tensor"), None, None),
            P(),
            P(),
            P(),
            P(),
            P("dp", None, None),
            P(("dp", "tensor")),
            P(("dp", "tensor")),
            P(("dp", "tensor"), None, None),
            P(None, "tensor"),
            P(None, "tensor"),
        ),
        out_specs=(P(), P(), P(), P(), P(), P(("dp", "tensor"), None, None)),
        check_vma=False,
    )
```

```python
import functools
import math

import jax
import jax.numpy as jnp
from jax import lax
from jax.experimental import pallas as pl
from jax.experimental.pallas import tpu as pltpu
from jax.sharding import PartitionSpec as P

sharpness = 0.05
softcap = 10.0
epsilon = 1e-06
CORES = 2
VMEM_LIMIT = 56 * 1024 * 1024
SMALL_LIMIT = 14 * 1024 * 1024

F32 = jnp.float32
BF16 = jnp.bfloat16
VMEM = pl.BlockSpec(memory_space=pltpu.VMEM)
SMEM = pl.BlockSpec(memory_space=pltpu.SMEM)
ANY = pl.BlockSpec(memory_space=pl.ANY)


def up(n, m):
    return -(-n // m) * m


def dot(a, b, ca, cb):
    return lax.dot_general(a, b, (((ca,), (cb,)), ((), ())), preferred_element_type=F32)


def split_rows(rows, most):
    return max(n for n in range(16, most + 1, 16) if rows % n == 0)


def one_row(ref):
    return jnp.concatenate([ref[v : v + 1] for v in range(ref.shape[0])], axis=1)


def params(**kw):
    return pltpu.CompilerParams(vmem_limit_bytes=VMEM_LIMIT, **kw)


def cost(flops, nbytes):
    return pl.CostEstimate(flops=int(flops), bytes_accessed=int(nbytes), transcendentals=0)


def forward_kernel(x_ref, str_ref, wo_ref, gain_ref, bias_ref, wp_ref,
                   normed_ref, emb_ref, inv_ref, turned_ref, prod_s, hid_s):
    rows, width = x_ref.shape
    sub = rows
    gain, bias = one_row(gain_ref), one_row(bias_ref)
    for b in range(0, rows, sub):
        prod_s[b : b + sub] = dot(x_ref[b : b + sub], wo_ref[...], 1, 0)
        for c in range(b, b + sub, 16):
            summed = prod_s[c : c + 16] + str_ref[c : c + 16].astype(F32)
            centred = summed - jnp.mean(summed, axis=-1, keepdims=True)
            inverse = lax.rsqrt(jnp.mean(centred * centred, axis=-1, keepdims=True) + epsilon)
            normed = centred * inverse
            normed_ref[c : c + 16] = normed.astype(BF16)
            inv_ref[c : c + 16] = jnp.broadcast_to(inverse, (16, inv_ref.shape[1]))
            hid_s[c : c + 16] = (normed * gain + bias).astype(BF16)
        emb_ref[b : b + sub] = dot(hid_s[b : b + sub], wp_ref[...], 1, 0)
    turned_ref[0] = x_ref[...].T


def student_forward(x, stream, out_weight, gain, bias, proj_weight):
    total, width = x.shape
    emb = proj_weight.shape[1]
    rows = split_rows(total, 720)
    block = lambda n: pl.BlockSpec((rows, n), lambda s: (s, 0))
    whole = lambda a: pl.BlockSpec(a.shape, lambda s: (0,) * a.ndim)
    inputs = (x, stream, out_weight, gain, bias, proj_weight)
    return pl.pallas_call(
        forward_kernel,
        grid=(total // rows,),
        in_specs=[block(width), block(width)] + [whole(a) for a in inputs[2:]],
        out_specs=[block(width), block(emb), block(128), pl.BlockSpec((1, width, rows), lambda s: (s, 0, 0))],
        out_shape=[
            jax.ShapeDtypeStruct((total, width), BF16),
            jax.ShapeDtypeStruct((total, emb), F32),
            jax.ShapeDtypeStruct((total, 128), F32),
            jax.ShapeDtypeStruct((total // rows, width, rows), BF16),
        ],
        scratch_shapes=[pltpu.VMEM((rows, width), F32), pltpu.VMEM((rows, width), BF16)],
        compiler_params=params(),
        cost_estimate=cost(2 * total * width * (width + emb), 8 * total * width),
        name="student_forward",
    )(*inputs)


def teacher_kernel(parts, count, tokens, order_ref, from_ref, rows_ref, states_ref, wq_ref, wk_ref, *rest):
    pieces, out_ref = rest[:parts], rest[parts]
    w_s, own_s, q_s, a_s, g_s, key_s, e_s, map_s, q_sem, key_sem, w_sem, own_sem = rest[parts + 1 :]
    depth = q_s.shape[1]
    slices = w_s.shape[0] // 2
    part_rows = pieces[0].shape[1]
    total = key_s.shape[0]
    seq = total // count
    blocks = key_sem.shape[0]
    rows = total // blocks
    first = count * tokens
    own = [
        pltpu.make_async_copy(wq_ref, own_s.at[0], own_sem.at[0]),
        pltpu.make_async_copy(wk_ref, own_s.at[1], own_sem.at[1]),
    ]
    queries = pltpu.make_async_copy(states_ref.at[pl.ds(0, first)], q_s, q_sem)
    gathered = [
        pltpu.make_async_copy(
            pieces[a].at[pl.ds(0, w_s.shape[0])],
            w_s.at[:, pl.ds(pl.multiple_of(rows_ref[a] * part_rows, part_rows), part_rows), :],
            w_sem.at[a],
        )
        for a in range(parts)
    ]
    keys = [
        pltpu.make_async_copy(
            states_ref.at[pl.ds(first + b * rows, rows)], key_s.at[pl.ds(b * rows, rows)], key_sem.at[b]
        )
        for b in range(blocks)
    ]
    queries.start()
    for copy in own + gathered:
        copy.start()
    queries.wait()
    for copy in own:
        copy.wait()
    q = q_s[...]
    heads = own_s.shape[2]
    a_s[:, slices * heads :] = dot(q, own_s[0], 1, 0).astype(BF16)
    for copy in gathered:
        copy.wait()
    for copy in keys:
        copy.start()
    for k in range(slices):
        a_s[:, k * heads : (k + 1) * heads] = dot(q, w_s[2 * k], 1, 0).astype(BF16)
    keys_weight = jnp.concatenate([w_s[2 * k + 1] for k in range(slices)] + [own_s[1]], axis=1)
    mixed = dot(a_s[...], keys_weight, 1, 1)
    for v in range(depth // 128):
        g_s[v] = mixed[:, v * 128 : (v + 1) * 128]
        for p in range(count):
            q_s[p * tokens : (p + 1) * tokens, v * 128 : (v + 1) * 128] = g_s[
                v, pl.ds(p, tokens, stride=count), :
            ].astype(BF16)
    mixed = q_s[...].T
    scale = 1.0 / (math.sqrt(depth) * softcap)
    side = 128 // tokens
    pair = lax.broadcasted_iota(jnp.int32, (rows, 128), 0) % count
    for b in range(blocks):
        keys[b].wait()
        raw = dot(key_s[b * rows : (b + 1) * rows], mixed, 1, 0)
        mine = raw[:, :128]
        for v in range(1, count // side):
            mine = jnp.where(pair >= v * side, raw[:, v * 128 : (v + 1) * 128], mine)
        e_s[b * rows : (b + 1) * rows] = jnp.exp(softcap * jnp.tanh(mine * scale))
    lane = lax.broadcasted_iota(jnp.int32, (seq, 128), 1) // tokens
    filler = jnp.zeros((up(seq, 128) - seq, 128), F32)
    for g in range(count // side):
        both = e_s[pl.ds(g * side, seq, stride=count), :]
        for v in range(1, side):
            both = jnp.where(lane == v, e_s[pl.ds(g * side + v, seq, stride=count), :], both)
        turned = jnp.concatenate([both, filler], axis=0).T
        for v in range(side):
            map_s[g * side + v] = turned[v * tokens : (v + 1) * tokens, :seq].astype(BF16)
    per = count // parts
    for n in range(count):
        out_ref[n] = map_s[order_ref[from_ref[n // per], n % per]]


def teacher_maps(order, source, rows, slices, states, wq, wk, pieces, count, tokens):
    total, depth = states.shape
    keys = total - count * tokens
    heads = wq.shape[1]
    parts = len(pieces)
    blocks = keys // split_rows(keys, 720)
    return pl.pallas_call(
        functools.partial(teacher_kernel, parts, count, tokens),
        in_specs=[SMEM] * 3 + [ANY] * (3 + parts),
        out_specs=VMEM,
        out_shape=jax.ShapeDtypeStruct((count, tokens, keys // count), BF16),
        scratch_shapes=[
            pltpu.VMEM((slices, depth, heads), BF16),
            pltpu.VMEM((2, depth, heads), BF16),
            pltpu.VMEM((count * tokens, depth), BF16),
            pltpu.VMEM((count * tokens, (slices // 2 + 1) * heads), BF16),
            pltpu.VMEM((depth // 128, count * tokens, 128), F32),
            pltpu.VMEM((keys, depth), BF16),
            pltpu.VMEM((keys, 128), F32),
            pltpu.VMEM((count, tokens, keys // count), BF16),
            pltpu.SemaphoreType.DMA,
            pltpu.SemaphoreType.DMA((blocks,)),
            pltpu.SemaphoreType.DMA((parts,)),
            pltpu.SemaphoreType.DMA((2,)),
        ],
        compiler_params=params(),
        cost_estimate=cost(8 * count * tokens * depth * depth, 2 * states.size + 4 * depth * depth),
        name="teacher_maps",
    )(order, source, rows, states, wq, wk, *pieces)


def rider_copies(pieces, slices, held, sem):
    part = pieces[0].shape[1]
    return [
        pltpu.make_async_copy(
            pieces[a].at[slices + x], held.at[a, pl.ds(x * part, part)], sem.at[a * (pieces[0].shape[0] - slices) + x]
        )
        for a in range(len(pieces))
        for x in range(pieces[0].shape[0] - slices)
    ]


def rider_states(held, a, each, width):
    heads = held.shape[2]
    return jnp.concatenate([held[a, n * each : (n + 1) * each] for n in range(width // heads)], axis=1)


def scores_kernel(tokens, count, group_queries, slices, parts, qidx_ref, len_ref, emb_ref, wp_ref, *rest):
    pieces = rest[:parts]
    (prob_ref, log_ref, units_ref, qunit_ref, qdir_ref, qlen_ref, qs_ref, dir_s, held_s, sem) = rest[parts:]
    copies = rider_copies(pieces, slices, held_s, sem)
    for copy in copies:
        copy.start()
    total, emb = emb_ref.shape
    seq = total // count
    sub = split_rows(total, 128)
    each = group_queries * tokens
    for b in range(0, total, sub):
        e = emb_ref[b : b + sub]
        dir_s[b : b + sub] = e / jnp.sqrt(jnp.sum(e * e, axis=-1, keepdims=True) + epsilon)
    for copy in copies:
        copy.wait()
    for a in range(parts):
        qs_ref[a * each : (a + 1) * each] = rider_states(held_s, a, each, qs_ref.shape[1])
    qe = dot(qs_ref[...], wp_ref[...], 1, 0)
    length = jnp.sqrt(jnp.sum(qe * qe, axis=-1, keepdims=True) + epsilon)
    qdir = qe / length
    qdir_ref[...] = qdir
    qlen_ref[...] = jnp.broadcast_to(length, qlen_ref.shape)
    qunit_ref[...] = qdir.astype(BF16).reshape(qunit_ref.shape)
    for r in range(count):
        units = dir_s[pl.ds(r, seq, stride=count), :].astype(BF16)
        units_ref[r] = units
        logits = dot(qunit_ref[qidx_ref[r]], units, 1, 1) / sharpness
        valid = lax.broadcasted_iota(jnp.int32, logits.shape, 1) < len_ref[r]
        student = jnp.where(valid, jnp.exp(logits), 0.0)
        student_total = jnp.sum(student, axis=-1, keepdims=True)
        prob_ref[r] = student / student_total
        log_ref[r] = logits - jnp.log(student_total)


def student_scores(qidx, lens, embeds, wp, pieces, slices, count, tokens, group_queries):
    total, emb = embeds.shape
    seq = total // count
    parts = len(pieces)
    queries = parts * group_queries
    riders, part, heads = pieces[0].shape
    riders -= slices
    return pl.pallas_call(
        functools.partial(scores_kernel, tokens, count, group_queries, slices, parts),
        in_specs=[SMEM, SMEM, VMEM, VMEM] + [ANY] * parts,
        out_specs=[VMEM] * 7,
        out_shape=[
            jax.ShapeDtypeStruct((count, tokens, seq), F32),
            jax.ShapeDtypeStruct((count, tokens, seq), F32),
            jax.ShapeDtypeStruct((count, seq, emb), BF16),
            jax.ShapeDtypeStruct((queries, tokens, emb), BF16),
            jax.ShapeDtypeStruct((queries * tokens, emb), F32),
            jax.ShapeDtypeStruct((queries * tokens, 128), F32),
            jax.ShapeDtypeStruct((queries * tokens, wp.shape[0]), BF16),
        ],
        scratch_shapes=[
            pltpu.VMEM((total, emb), F32),
            pltpu.VMEM((parts, riders * part, heads), BF16),
            pltpu.SemaphoreType.DMA((parts * riders,)),
        ],
        compiler_params=params(),
        cost_estimate=cost(1e9, 4 * total * emb),
        name="student_scores",
    )(qidx, lens, embeds, wp, *pieces)


def two_parts(a, b):
    high = a.astype(BF16)
    low = (a - high.astype(F32)).astype(BF16)
    return dot(high, b, 1, 0) + dot(low, b, 1, 0)


def backward_kernel(
    tokens, count, blocks,
    qidx_ref, midx_ref, len_ref, core_ref,
    maps_in, prob_in, log_in, units_in, qunit_in, emb_in, x_in, normed_in, inv_in, qs_in,
    qdir_ref, qlen_ref, gain_ref, bias_ref, wp_ref, wpt_ref,
    sg_out, send_ref, keep_ref,
    maps_s, prob_s, log_s, units_s, qunit_s, emb_s, x_s, normed_s, inv_s, qs_s,
    up_s, eg_s, mean_s, along_s, un_s, qg_s, hg_s, sg_s, wo_s, nt_s, right_s,
    first_sem, block_sem, out_sem, last_sem,
):
    total, width = normed_s.shape
    emb = emb_s.shape[1]
    seq = total // count
    rows = total // blocks
    sub = split_rows(rows, 256)
    thin = split_rows(total, 128)
    first = [
        pltpu.make_async_copy(src, dst, first_sem.at[n])
        for n, (src, dst) in enumerate(
            (
                (qunit_in, qunit_s), (maps_in, maps_s), (prob_in, prob_s), (log_in, log_s), (units_in, units_s),
                (emb_in, emb_s), (inv_in, inv_s),
            )
        )
    ]
    first, second = first[:5], first[5:]

    def loads(b):
        part = pl.ds(pl.multiple_of(b * rows, rows), rows)
        return (
            pltpu.make_async_copy(normed_in.at[part], normed_s.at[part], block_sem.at[2 * b]),
            pltpu.make_async_copy(x_in.at[b], x_s.at[b], block_sem.at[2 * b + 1]),
        )

    last = pltpu.make_async_copy(qs_in, qs_s, last_sem)
    for copy in first:
        copy.start()
    gain, bias = one_row(gain_ref), one_row(bias_ref)
    gain_w = two_parts(gain, wp_ref[...])
    bias_w = two_parts(bias, wp_ref[...])
    qg_s[...] = jnp.zeros_like(qg_s)
    for copy in first:
        copy.wait()
    for copy in second:
        copy.start()
    loads(0)[0].start()

    spread = jnp.zeros((tokens, 1), F32)
    for r in range(count):
        teacher = maps_s[midx_ref[r]].astype(F32)
        valid = lax.broadcasted_iota(jnp.int32, teacher.shape, 1) < len_ref[r]
        teacher_log = jnp.log(teacher)
        teacher = jnp.where(valid, teacher, 0.0)
        teacher_total = jnp.sum(teacher, axis=-1, keepdims=True)
        teacher_prob = teacher / teacher_total
        gap = (teacher_log - jnp.log(teacher_total)) - log_s[r]
        spread += jnp.sum(jnp.where(valid, teacher_prob * gap, 0.0), axis=-1, keepdims=True)
        slope = ((prob_s[r] - teacher_prob) / (tokens * sharpness)).astype(BF16)
        up_s[pl.ds(r, seq, stride=count), :] = dot(slope, qunit_s[qidx_ref[r]], 0, 0).astype(BF16).astype(F32)
        un_s[r] = dot(slope, units_s[r], 1, 0)
    for r in range(count):
        qg_s[qidx_ref[r]] += un_s[r]
    total_eg = jnp.zeros((1, emb), F32)
    for copy in second:
        copy.wait()
    loads(0)[1].start()
    if blocks > 1:
        for copy in loads(1):
            copy.start()
    for b in range(0, total, thin):
        e = emb_s[b : b + thin]
        upstream = up_s[b : b + thin]
        length = jnp.sqrt(jnp.sum(e * e, axis=-1, keepdims=True) + epsilon)
        direction = e / length
        eg = (upstream - direction * jnp.sum(direction * upstream, axis=-1, keepdims=True)) / length
        eg = eg.astype(BF16)
        eg_s[b : b + thin] = eg
        eg = eg.astype(F32)
        total_eg += jnp.sum(eg, axis=0, keepdims=True)
        inverse = inv_s[b : b + thin]
        mean_s[b : b + thin] = inverse * (jnp.sum(eg * gain_w, axis=-1, keepdims=True) / width)
        along_s[b : b + thin] = inverse * (jnp.sum(eg * (e - bias_w), axis=-1, keepdims=True) / width)

    wo_s[...] = jnp.zeros_like(wo_s)
    nt_s[...] = jnp.zeros_like(nt_s)

    def wide(b, _):
        base = pl.multiple_of(b * rows, rows)
        part = pl.ds(base, rows)
        loads(b)[0].wait()

        @pl.when(b + 2 < blocks)
        def _():
            for copy in loads(b + 2):
                copy.start()

        @pl.when(b == blocks - 1)
        def _():
            last.start()

        for n in range(0, rows, sub):
            hg_s[n : n + sub] = dot(eg_s[pl.ds(base + n, sub)], wpt_ref[...], 1, 0)
            for c in range(n, n + sub, 16):
                here = pl.ds(base + c, 16)
                inverse, mean, along = inv_s[here], mean_s[here], along_s[here]
                for v in range(0, width, 128):
                    scaled = hg_s[c : c + 16, v : v + 128] * gain[:, v : v + 128]
                    normed = normed_s[here, v : v + 128].astype(F32)
                    sg_s[here, v : v + 128] = (inverse * scaled - mean - normed * along).astype(BF16)
        pltpu.make_async_copy(sg_s.at[part], sg_out.at[part], out_sem.at[b]).start()
        loads(b)[1].wait()
        wo_s[...] += dot(x_s[b], sg_s[part], 1, 0)
        nt_s[...] += dot(eg_s[part], normed_s[part], 0, 0)
        return 0

    lax.fori_loop(0, blocks, wide, 0)

    last.wait()
    qg = qg_s[...].reshape(qdir_ref.shape)
    qdir = qdir_ref[...]
    qeg = (qg - qdir * jnp.sum(qdir * qg, axis=-1, keepdims=True)) / qlen_ref[:, :1]
    high = qeg.astype(BF16)
    low = (qeg - high.astype(F32)).astype(BF16)
    qs = qs_s[...]
    proj_query = dot(high, qs, 0, 0) + dot(low, qs, 0, 0)
    nt = nt_s[...]
    s = jnp.broadcast_to(total_eg, (emb, emb)).T[:, :1]
    wpt = wpt_ref[...].astype(F32)
    proj = nt * gain + s * bias + proj_query
    gain_row = jnp.sum(wpt * nt, axis=0, keepdims=True)
    bias_row = jnp.sum(wpt * s, axis=0, keepdims=True)
    index = lax.broadcasted_iota(jnp.int32, (tokens, width), 0)
    top = jnp.where(index == 0, gain_row, jnp.where(index == 1, bias_row, 0.0))
    rest_rows = jnp.zeros((128 - 2 * tokens, width), F32)
    right_s[...] = jnp.concatenate([proj, top, jnp.broadcast_to(spread, (tokens, width)), rest_rows], axis=0).T
    half = width // CORES
    chunk = send_ref.shape[1]
    for ref, which in ((send_ref, 1 - core_ref[0]), (keep_ref, core_ref[0])):
        start = pl.multiple_of(which * half, half)
        left, right = wo_s[pl.ds(start, half)], right_s[pl.ds(start, half)]
        for c in range(half // chunk):
            ref[c, :, :width] = left[c * chunk : (c + 1) * chunk].astype(BF16)
            ref[c, :, width:] = right[c * chunk : (c + 1) * chunk].astype(BF16)
    for b in range(blocks):
        part = pl.ds(b * rows, rows)
        pltpu.make_async_copy(sg_s.at[part], sg_out.at[part], out_sem.at[b]).wait()


def student_backward(
    qidx, midx, lens, core, maps, scores, embeds, x, normed, inverse, gain, bias, wp, wpt,
    count, tokens, group_queries, chunk,
):
    total, width = normed.shape
    emb = wp.shape[1]
    blocks = x.shape[0]
    chunks = width // CORES // chunk
    prob, log, units, qunit, qdir, qlen, qs = scores
    manual = [maps, prob, log, units, qunit, embeds, x, normed, inverse, qs]
    packed = jax.ShapeDtypeStruct((chunks, chunk, width + emb + 128), BF16)
    return pl.pallas_call(
        functools.partial(backward_kernel, tokens, count, blocks),
        in_specs=[SMEM] * 4 + [ANY] * len(manual) + [VMEM] * 6,
        out_specs=[ANY, VMEM, VMEM],
        scratch_shapes=[pltpu.VMEM(a.shape, a.dtype) for a in manual]
        + [
            pltpu.VMEM((total, emb), F32),
            pltpu.VMEM((total, emb), BF16),
            pltpu.VMEM((total, 128), F32),
            pltpu.VMEM((total, 128), F32),
            pltpu.VMEM((count, tokens, emb), F32),
            pltpu.VMEM(qunit.shape, F32),
            pltpu.VMEM((total // blocks, width), F32),
            pltpu.VMEM((total, width), BF16),
            pltpu.VMEM((width, width), F32),
            pltpu.VMEM((emb, width), F32),
            pltpu.VMEM((width, emb + 128), F32),
            pltpu.SemaphoreType.DMA((7,)),
            pltpu.SemaphoreType.DMA((2 * blocks,)),
            pltpu.SemaphoreType.DMA((blocks,)),
            pltpu.SemaphoreType.DMA,
        ],
        out_shape=[jax.ShapeDtypeStruct((total, width), BF16), packed, packed],
        compiler_params=params(),
        cost_estimate=cost(2 * total * width * (width + 2 * emb), 8 * total * width),
        name="student_backward",
    )(qidx, midx, lens, core, *manual, qdir, qlen, gain, bias, wp, wpt)


def context_kernel(sg_ref, wo_ref, out_ref):
    out_ref[...] = dot(sg_ref[...], wo_ref[...], 1, 1).astype(BF16)


def context_grad(sg, out_weight):
    total, width = sg.shape
    rows = split_rows(total, 720)
    block = pl.BlockSpec((rows, width), lambda s: (s, 0))
    return pl.pallas_call(
        context_kernel,
        grid=(total // rows,),
        in_specs=[block, pl.BlockSpec(out_weight.shape, lambda s: (0, 0))],
        out_specs=block,
        out_shape=jax.ShapeDtypeStruct(sg.shape, BF16),
        compiler_params=params(),
        cost_estimate=cost(2 * total * width * width, 4 * total * width),
        name="context_grad",
    )(sg, out_weight)


def split_sum_kernel(inputs, outputs, index_ref, *rest):
    ins, outs, total_s = rest[:inputs], rest[inputs : inputs + outputs], rest[-1]
    total = ins[0][...].astype(F32)
    for ref in ins[1:]:
        total = total + ref[...].astype(F32)
    total_s[...] = total.astype(BF16).reshape(total_s.shape)
    for k in range(outputs):
        outs[k][...] = total_s[index_ref[k]].reshape(outs[k].shape)


def split_sum(arrays, index, name):
    outputs = index.shape[0]
    shape = arrays[0].shape
    lead = shape[0] // outputs
    out = shape[1:] if lead == 1 else (lead,) + shape[1:]
    return pl.pallas_call(
        functools.partial(split_sum_kernel, len(arrays), outputs),
        in_specs=[SMEM] + [VMEM] * len(arrays),
        out_specs=[VMEM] * outputs,
        out_shape=[jax.ShapeDtypeStruct(out, BF16)] * outputs,
        scratch_shapes=[pltpu.VMEM((outputs, lead) + shape[1:], BF16)],
        compiler_params=pltpu.CompilerParams(vmem_limit_bytes=SMALL_LIMIT),
        name=name,
    )(index, *arrays)


def sum_kernel(*refs):
    total = refs[0][...].astype(F32)
    for ref in refs[1:-1]:
        total = total + ref[...].astype(F32)
    refs[-1][...] = total.astype(BF16)


def plain_sum(arrays, name):
    return pl.pallas_call(
        sum_kernel,
        in_specs=[VMEM] * len(arrays),
        out_specs=VMEM,
        out_shape=jax.ShapeDtypeStruct(arrays[0].shape, BF16),
        compiler_params=pltpu.CompilerParams(vmem_limit_bytes=SMALL_LIMIT),
        name=name,
    )(*arrays)


def unpack_kernel(parts, width, emb, tokens, scale, index_ref, *rest):
    ins = rest[:parts]
    wo_ref, proj_ref, gain_ref, bias_ref, loss_ref, small_s = rest[parts:]
    per = ins[0].shape[0]
    for a in range(parts):
        for k in range(per):
            c = index_ref[a * per + k]
            value = ins[a][k].astype(F32)
            wo_ref[c] = value[:, :width]
            proj_ref[c] = value[:, width : width + emb]
            small_s[c] = value[:, width + emb :]
    turned = small_s[...].reshape(width, 128).T
    for v in range(width // 128):
        gain_ref[v : v + 1] = turned[0:1, v * 128 : (v + 1) * 128]
        bias_ref[v : v + 1] = turned[1:2, v * 128 : (v + 1) * 128]
    loss_ref[0] = jnp.sum(turned[tokens : 2 * tokens, 0:1]) * scale


def unpack(arrays, index, width, emb, tokens, scale):
    parts = len(arrays)
    per, chunk, _ = arrays[0].shape
    chunks = parts * per
    return pl.pallas_call(
        functools.partial(unpack_kernel, parts, width, emb, tokens, scale),
        in_specs=[SMEM] + [VMEM] * parts,
        out_specs=[VMEM] * 4 + [SMEM],
        out_shape=[jax.ShapeDtypeStruct((chunks, chunk, n), F32) for n in (width, emb)]
        + [jax.ShapeDtypeStruct((width // 128, 128), F32)] * 2
        + [jax.ShapeDtypeStruct((1,), F32)],
        scratch_shapes=[pltpu.VMEM((chunks, chunk, 128), F32)],
        compiler_params=pltpu.CompilerParams(vmem_limit_bytes=SMALL_LIMIT),
        name="unpack",
    )(index, *arrays)


def local(
    context,
    stream,
    out_weight,
    gain,
    bias,
    proj_weight,
    query_states,
    passage_len,
    passage_dest,
    teacher_states,
    teacher_query,
    teacher_key,
):
    dp = lax.axis_size("dp")
    nt = lax.axis_size("tensor")
    chips = dp // CORES
    me = lax.axis_index("dp")
    chip, core = me // CORES, me % CORES
    mt = lax.axis_index("tensor")
    count, seq, width = context.shape
    emb = proj_weight.shape[1]
    group_queries, tokens, _ = query_states.shape
    depth, heads = teacher_query.shape
    per = count // dp
    per_query = count * nt // group_queries

    def flat(a):
        return a.transpose(1, 0, 2).reshape(-1, a.shape[2])

    paired = chips & (chips - 1) == 0

    def partner(c, k):
        return c ^ k if paired else (c + k) % chips

    def shift_chip(x, k):
        return lax.ppermute(
            x, "dp", [(c * CORES + o, partner(c, k) * CORES + o) for c in range(chips) for o in range(CORES)]
        )

    def swap_core(x):
        return lax.ppermute(x, "dp", [(d, d ^ 1) for d in range(dp)])

    def shift_t(x, k):
        return lax.ppermute(x, "tensor", [(t, (t + k) % nt) for t in range(nt)])

    dest_group = passage_dest // (count * nt)
    rows = jnp.arange(count, dtype=jnp.int32)
    rank = jnp.sum(
        (dest_group[:, None] == dest_group[None, :]) & (rows[None, :] < rows[:, None]), axis=1, dtype=jnp.int32
    )
    place = dest_group * per + rank
    positions = jnp.sum(
        jnp.where(place[:, None] == rows[None, :], (passage_dest % count)[:, None], 0), axis=0
    )
    each = group_queries * tokens
    states = query_states.reshape(each, width)
    column_blocks = [states[:, n * heads : (n + 1) * heads] for n in range(width // heads)]
    extra = jnp.pad(positions.astype(BF16)[None, :], ((0, 15), (0, heads - count)))
    rider = jnp.concatenate(column_blocks + [extra], axis=0)

    part = depth // dp
    slices = 2 * (nt - 1)
    by_hops = sorted(range(1, chips), key=lambda k: (bin(k).count("1"), k))
    far = by_hops[len(by_hops) - chips // 4 :] if paired else []

    def slice_of(c):
        start = (c * CORES + core) * part
        return jnp.stack([lax.dynamic_slice_in_dim(w, start, part, 0) for w in (teacher_query, teacher_key)])

    mine, far_mine = slice_of(chip), [slice_of(partner(chip, k)) for k in far]
    rider = jnp.pad(rider, ((0, -rider.shape[0] % part), (0, 0))).reshape(-1, part, heads)
    along = jnp.concatenate([shift_t(mine, k) for k in range(1, nt)] + [rider], axis=0)
    gain2, bias2 = gain.reshape(-1, 128), bias.reshape(-1, 128)
    x = flat(context)
    far_riders = [shift_chip(rider, k) for k in far]
    along, far_mine, far_riders, forward_gain = lax.optimization_barrier((along, far_mine, far_riders, gain2))
    pieces = [along] + [None] * (chips - 1)
    for k in range(1, chips):
        if k not in far:
            pieces[k] = shift_chip(along, k)
    for k, other, far_rider in zip(far, far_mine, far_riders):
        pieces[k] = jnp.concatenate([shift_t(other, n) for n in range(1, nt)] + [far_rider], axis=0)
    shifts = jnp.arange(chips, dtype=jnp.int32)
    behind = chip ^ shifts if paired else (chip - shifts) % chips
    piece_rows = jnp.concatenate([behind * CORES + core, behind * CORES + 1 - core]).astype(jnp.int32)
    midx = place.astype(jnp.int32)
    def piece_of(group):
        apart = chip ^ (group // CORES) if paired else (chip - group // CORES) % chips
        return apart + jnp.where(group % CORES == core, 0, chips)

    qidx = passage_dest // per_query - dest_group * group_queries + piece_of(dest_group) * group_queries
    qidx = qidx.astype(jnp.int32)
    source = piece_of(jnp.arange(dp, dtype=jnp.int32)).astype(jnp.int32)

    normed, embeds, inverse, turned = student_forward(
        x, flat(stream), out_weight, forward_gain, bias2, proj_weight
    )
    pieces[1:], normed, embeds, inverse, turned, proj_turned = lax.optimization_barrier(
        (pieces[1:], normed, embeds, inverse, turned, proj_weight.T)
    )
    pieces = pieces + [swap_core(a) for a in pieces]
    told = [a[slices:].reshape(-1, heads)[width // heads * each, :count] for a in pieces]
    order = lax.dynamic_slice_in_dim(jnp.stack(told), me * per, per, 1).astype(jnp.int32)
    maps = teacher_maps(
        order, source, piece_rows, slices, flat(teacher_states), teacher_query, teacher_key, pieces, count, tokens
    )
    maps, embeds = lax.optimization_barrier((maps, embeds))
    maps = lax.all_to_all(maps, "dp", split_axis=0, concat_axis=0, tiled=True)
    scores = student_scores(
        qidx, passage_len, embeds, proj_weight, pieces, slices, count, tokens, group_queries
    )
    chunk = width // (CORES * chips * nt)
    sg, send, keep = student_backward(
        qidx, midx, passage_len, core.astype(jnp.int32).reshape(1), maps, scores,
        embeds, turned, normed, inverse, gain2, bias2, proj_weight, proj_turned,
        count, tokens, group_queries, chunk,
    )

    ahead = partner(chip, shifts).astype(jnp.int32)
    t_shifts = jnp.arange(nt, dtype=jnp.int32)
    t_ahead = ((mt + t_shifts) % nt).astype(jnp.int32)
    parts = split_sum([keep, swap_core(send)], ahead, "sum_cores")
    parts, sg = lax.optimization_barrier((parts, sg))
    grad_context = context_grad(sg, out_weight)
    parts = [parts[0]] + [shift_chip(parts[k], k) for k in range(1, chips)]
    parts, grad_context = lax.optimization_barrier((parts, grad_context))
    parts = split_sum(parts, t_ahead, "sum_plane")
    parts = [parts[0]] + [shift_t(parts[k], k) for k in range(1, nt)]
    total = plain_sum(parts, "sum_tensor")
    line = jnp.stack([total] + [shift_t(total, k) for k in range(1, nt)])
    plane = [line] + [shift_chip(line, k) for k in range(1, chips)]
    arrays = plane + [swap_core(a) for a in plane]
    base = jnp.concatenate([core * chips + behind, (1 - core) * chips + behind]) * nt
    index = (base[:, None] + ((mt - t_shifts) % nt)[None, :]).reshape(-1).astype(jnp.int32)
    grad_out, grad_proj, grad_gain, grad_bias, loss = unpack(
        arrays, index, width, emb, tokens, 1.0 / (count * dp * nt * tokens)
    )
    return (
        loss.reshape(()),
        grad_out.reshape(width, width),
        grad_proj.reshape(width, emb),
        grad_gain.reshape(width),
        grad_bias.reshape(width),
        grad_context.reshape(seq, count, width).transpose(1, 0, 2),
    )


def solution(mesh):
    return jax.shard_map(
        local,
        mesh=mesh,
        in_specs=(
            P(("dp", "tensor"), None, None),
            P(("dp", "tensor"), None, None),
            P(),
            P(),
            P(),
            P(),
            P("dp", None, None),
            P(("dp", "tensor")),
            P(("dp", "tensor")),
            P(("dp", "tensor"), None, None),
            P(None, "tensor"),
            P(None, "tensor"),
        ),
        out_specs=(P(), P(), P(), P(), P(), P(("dp", "tensor"), None, None)),
        check_vma=False,
    )
```

```python
import functools
import math

import jax
import jax.numpy as jnp
from jax import lax
from jax.experimental import pallas as pl
from jax.experimental.pallas import tpu as pltpu
from jax.sharding import PartitionSpec as P

sharpness = 0.05
softcap = 10.0
epsilon = 1e-06
CORES = 2
VMEM_LIMIT = 56 * 1024 * 1024
SMALL_LIMIT = 14 * 1024 * 1024
TEACHER_LIMIT = 50 * 1024 * 1024

F32 = jnp.float32
BF16 = jnp.bfloat16
VMEM = pl.BlockSpec(memory_space=pltpu.VMEM)
SMEM = pl.BlockSpec(memory_space=pltpu.SMEM)
ANY = pl.BlockSpec(memory_space=pl.ANY)


def up(n, m):
    return -(-n // m) * m


def dot(a, b, ca, cb):
    return lax.dot_general(a, b, (((ca,), (cb,)), ((), ())), preferred_element_type=F32)


def split_rows(rows, most):
    return max(n for n in range(16, most + 1, 16) if rows % n == 0)


def one_row(ref):
    return jnp.concatenate([ref[v : v + 1] for v in range(ref.shape[0])], axis=1)


def params(**kw):
    return pltpu.CompilerParams(vmem_limit_bytes=VMEM_LIMIT, **kw)


def cost(flops, nbytes):
    return pl.CostEstimate(flops=int(flops), bytes_accessed=int(nbytes), transcendentals=0)


def forward_kernel(x_ref, str_ref, wo_ref, gain_ref, bias_ref, wp_ref,
                   normed_ref, emb_ref, inv_ref, turned_ref, prod_s, hid_s):
    rows, width = x_ref.shape
    sub = rows
    gain, bias = one_row(gain_ref), one_row(bias_ref)
    for b in range(0, rows, sub):
        prod_s[b : b + sub] = dot(x_ref[b : b + sub], wo_ref[...], 1, 0)
        for c in range(b, b + sub, 16):
            summed = prod_s[c : c + 16] + str_ref[c : c + 16].astype(F32)
            centred = summed - jnp.mean(summed, axis=-1, keepdims=True)
            inverse = lax.rsqrt(jnp.mean(centred * centred, axis=-1, keepdims=True) + epsilon)
            normed = centred * inverse
            normed_ref[c : c + 16] = normed.astype(BF16)
            inv_ref[c : c + 16] = jnp.broadcast_to(inverse, (16, inv_ref.shape[1]))
            hid_s[c : c + 16] = (normed * gain + bias).astype(BF16)
        emb_ref[b : b + sub] = dot(hid_s[b : b + sub], wp_ref[...], 1, 0)
    turned_ref[0] = x_ref[...].T


def student_forward(x, stream, out_weight, gain, bias, proj_weight):
    total, width = x.shape
    emb = proj_weight.shape[1]
    rows = split_rows(total, 720)
    block = lambda n: pl.BlockSpec((rows, n), lambda s: (s, 0))
    whole = lambda a: pl.BlockSpec(a.shape, lambda s: (0,) * a.ndim)
    inputs = (x, stream, out_weight, gain, bias, proj_weight)
    return pl.pallas_call(
        forward_kernel,
        grid=(total // rows,),
        in_specs=[block(width), block(width)] + [whole(a) for a in inputs[2:]],
        out_specs=[block(width), block(emb), block(128), pl.BlockSpec((1, width, rows), lambda s: (s, 0, 0))],
        out_shape=[
            jax.ShapeDtypeStruct((total, width), BF16),
            jax.ShapeDtypeStruct((total, emb), F32),
            jax.ShapeDtypeStruct((total, 128), F32),
            jax.ShapeDtypeStruct((total // rows, width, rows), BF16),
        ],
        scratch_shapes=[pltpu.VMEM((rows, width), F32), pltpu.VMEM((rows, width), BF16)],
        compiler_params=params(),
        cost_estimate=cost(2 * total * width * (width + emb), 8 * total * width),
        name="student_forward",
    )(*inputs)


def teacher_kernel(parts, count, tokens, order_ref, from_ref, rows_ref, states_ref, wq_ref, wk_ref, *rest):
    pieces, out_ref = rest[:parts], rest[parts]
    w_s, own_s, q_s, a_s, g_s, key_s, e_s, map_s, q_sem, key_sem, w_sem, own_sem = rest[parts + 1 :]
    depth = q_s.shape[1]
    slices = w_s.shape[0] // 2
    part_rows = pieces[0].shape[1]
    total = key_s.shape[0]
    seq = total // count
    blocks = key_sem.shape[0]
    rows = total // blocks
    first = count * tokens
    own = [
        pltpu.make_async_copy(wq_ref, own_s.at[0], own_sem.at[0]),
        pltpu.make_async_copy(wk_ref, own_s.at[1], own_sem.at[1]),
    ]
    queries = pltpu.make_async_copy(states_ref.at[pl.ds(0, first)], q_s, q_sem)
    gathered = [
        pltpu.make_async_copy(
            pieces[a].at[pl.ds(0, w_s.shape[0])],
            w_s.at[:, pl.ds(pl.multiple_of(rows_ref[a] * part_rows, part_rows), part_rows), :],
            w_sem.at[a],
        )
        for a in range(parts)
    ]
    keys = [
        pltpu.make_async_copy(
            states_ref.at[pl.ds(first + b * rows, rows)], key_s.at[pl.ds(b * rows, rows)], key_sem.at[b]
        )
        for b in range(blocks)
    ]
    queries.start()
    for copy in own + gathered:
        copy.start()
    queries.wait()
    for copy in own:
        copy.wait()
    q = q_s[...]
    heads = own_s.shape[2]
    a_s[:, slices * heads :] = dot(q, own_s[0], 1, 0).astype(BF16)
    for copy in gathered:
        copy.wait()
    for copy in keys:
        copy.start()
    for k in range(slices):
        a_s[:, k * heads : (k + 1) * heads] = dot(q, w_s[2 * k], 1, 0).astype(BF16)
    keys_weight = jnp.concatenate([w_s[2 * k + 1] for k in range(slices)] + [own_s[1]], axis=1)
    mixed = dot(a_s[...], keys_weight, 1, 1)
    for v in range(depth // 128):
        g_s[v] = mixed[:, v * 128 : (v + 1) * 128]
        for p in range(count):
            q_s[p * tokens : (p + 1) * tokens, v * 128 : (v + 1) * 128] = g_s[
                v, pl.ds(p, tokens, stride=count), :
            ].astype(BF16)
    mixed = q_s[...].T
    scale = 1.0 / (math.sqrt(depth) * softcap)
    side = 128 // tokens
    pair = lax.broadcasted_iota(jnp.int32, (rows, 128), 0) % count
    for b in range(blocks):
        keys[b].wait()
        raw = dot(key_s[b * rows : (b + 1) * rows], mixed, 1, 0)
        mine = raw[:, :128]
        for v in range(1, count // side):
            mine = jnp.where(pair >= v * side, raw[:, v * 128 : (v + 1) * 128], mine)
        e_s[b * rows : (b + 1) * rows] = jnp.exp(softcap * jnp.tanh(mine * scale))
    lane = lax.broadcasted_iota(jnp.int32, (seq, 128), 1) // tokens
    filler = jnp.zeros((up(seq, 128) - seq, 128), F32)
    for g in range(count // side):
        both = e_s[pl.ds(g * side, seq, stride=count), :]
        for v in range(1, side):
            both = jnp.where(lane == v, e_s[pl.ds(g * side + v, seq, stride=count), :], both)
        turned = jnp.concatenate([both, filler], axis=0).T
        for v in range(side):
            map_s[g * side + v] = turned[v * tokens : (v + 1) * tokens, :seq].astype(BF16)
    per = count // parts
    for n in range(count):
        out_ref[n] = map_s[order_ref[from_ref[n // per], n % per]]


def teacher_maps(order, source, rows, slices, states, wq, wk, pieces, count, tokens):
    total, depth = states.shape
    keys = total - count * tokens
    heads = wq.shape[1]
    parts = len(pieces)
    blocks = keys // split_rows(keys, 720)
    return pl.pallas_call(
        functools.partial(teacher_kernel, parts, count, tokens),
        in_specs=[SMEM] * 3 + [ANY] * (3 + parts),
        out_specs=VMEM,
        out_shape=jax.ShapeDtypeStruct((count, tokens, keys // count), BF16),
        scratch_shapes=[
            pltpu.VMEM((slices, depth, heads), BF16),
            pltpu.VMEM((2, depth, heads), BF16),
            pltpu.VMEM((count * tokens, depth), BF16),
            pltpu.VMEM((count * tokens, (slices // 2 + 1) * heads), BF16),
            pltpu.VMEM((depth // 128, count * tokens, 128), F32),
            pltpu.VMEM((keys, depth), BF16),
            pltpu.VMEM((keys, 128), F32),
            pltpu.VMEM((count, tokens, keys // count), BF16),
            pltpu.SemaphoreType.DMA,
            pltpu.SemaphoreType.DMA((blocks,)),
            pltpu.SemaphoreType.DMA((parts,)),
            pltpu.SemaphoreType.DMA((2,)),
        ],
        compiler_params=pltpu.CompilerParams(vmem_limit_bytes=TEACHER_LIMIT),
        cost_estimate=cost(8 * count * tokens * depth * depth, 2 * states.size + 4 * depth * depth),
        name="teacher_maps",
    )(order, source, rows, states, wq, wk, *pieces)


def rider_copies(pieces, slices, held, sem):
    part = pieces[0].shape[1]
    return [
        pltpu.make_async_copy(
            pieces[a].at[slices + x], held.at[a, pl.ds(x * part, part)], sem.at[a * (pieces[0].shape[0] - slices) + x]
        )
        for a in range(len(pieces))
        for x in range(pieces[0].shape[0] - slices)
    ]


def rider_states(held, a, each, width):
    heads = held.shape[2]
    return jnp.concatenate([held[a, n * each : (n + 1) * each] for n in range(width // heads)], axis=1)


def scores_kernel(tokens, count, group_queries, slices, parts, qidx_ref, len_ref, emb_ref, wp_ref, *rest):
    pieces = rest[:parts]
    (prob_ref, log_ref, units_ref, qunit_ref, qdir_ref, qlen_ref, qs_ref, dir_s, held_s, sem) = rest[parts:]
    copies = rider_copies(pieces, slices, held_s, sem)
    for copy in copies:
        copy.start()
    total, emb = emb_ref.shape
    seq = total // count
    sub = split_rows(total, 128)
    each = group_queries * tokens
    for b in range(0, total, sub):
        e = emb_ref[b : b + sub]
        dir_s[b : b + sub] = e / jnp.sqrt(jnp.sum(e * e, axis=-1, keepdims=True) + epsilon)
    for copy in copies:
        copy.wait()
    for a in range(parts):
        qs_ref[a * each : (a + 1) * each] = rider_states(held_s, a, each, qs_ref.shape[1])
    qe = dot(qs_ref[...], wp_ref[...], 1, 0)
    length = jnp.sqrt(jnp.sum(qe * qe, axis=-1, keepdims=True) + epsilon)
    qdir = qe / length
    qdir_ref[...] = qdir
    qlen_ref[...] = jnp.broadcast_to(length, qlen_ref.shape)
    qunit_ref[...] = qdir.astype(BF16).reshape(qunit_ref.shape)
    for r in range(count):
        units = dir_s[pl.ds(r, seq, stride=count), :].astype(BF16)
        units_ref[r] = units
        logits = dot(qunit_ref[qidx_ref[r]], units, 1, 1) / sharpness
        valid = lax.broadcasted_iota(jnp.int32, logits.shape, 1) < len_ref[r]
        student = jnp.where(valid, jnp.exp(logits), 0.0)
        student_total = jnp.sum(student, axis=-1, keepdims=True)
        prob_ref[r] = student / student_total
        log_ref[r] = logits - jnp.log(student_total)


def student_scores(qidx, lens, embeds, wp, pieces, slices, count, tokens, group_queries):
    total, emb = embeds.shape
    seq = total // count
    parts = len(pieces)
    queries = parts * group_queries
    riders, part, heads = pieces[0].shape
    riders -= slices
    return pl.pallas_call(
        functools.partial(scores_kernel, tokens, count, group_queries, slices, parts),
        in_specs=[SMEM, SMEM, VMEM, VMEM] + [ANY] * parts,
        out_specs=[VMEM] * 7,
        out_shape=[
            jax.ShapeDtypeStruct((count, tokens, seq), F32),
            jax.ShapeDtypeStruct((count, tokens, seq), F32),
            jax.ShapeDtypeStruct((count, seq, emb), BF16),
            jax.ShapeDtypeStruct((queries, tokens, emb), BF16),
            jax.ShapeDtypeStruct((queries * tokens, emb), F32),
            jax.ShapeDtypeStruct((queries * tokens, 128), F32),
            jax.ShapeDtypeStruct((queries * tokens, wp.shape[0]), BF16),
        ],
        scratch_shapes=[
            pltpu.VMEM((total, emb), F32),
            pltpu.VMEM((parts, riders * part, heads), BF16),
            pltpu.SemaphoreType.DMA((parts * riders,)),
        ],
        compiler_params=params(),
        cost_estimate=cost(1e9, 4 * total * emb),
        name="student_scores",
    )(qidx, lens, embeds, wp, *pieces)


def two_parts(a, b):
    high = a.astype(BF16)
    low = (a - high.astype(F32)).astype(BF16)
    return dot(high, b, 1, 0) + dot(low, b, 1, 0)


def backward_kernel(
    tokens, count, blocks,
    qidx_ref, midx_ref, len_ref, core_ref,
    maps_in, prob_in, log_in, units_in, qunit_in, emb_in, x_in, normed_in, inv_in, qs_in,
    qdir_ref, qlen_ref, gain_ref, bias_ref, wp_ref, wpt_ref,
    sg_out, send_ref, keep_ref,
    maps_s, prob_s, log_s, units_s, qunit_s, emb_s, x_s, normed_s, inv_s, qs_s,
    up_s, eg_s, mean_s, along_s, un_s, qg_s, hg_s, sg_s, wo_s, nt_s, right_s,
    first_sem, block_sem, out_sem, last_sem,
):
    total, width = normed_s.shape
    emb = emb_s.shape[1]
    seq = total // count
    rows = total // blocks
    sub = split_rows(rows, 256)
    thin = split_rows(total, 128)
    first = [
        pltpu.make_async_copy(src, dst, first_sem.at[n])
        for n, (src, dst) in enumerate(
            (
                (qunit_in, qunit_s), (maps_in, maps_s), (prob_in, prob_s), (log_in, log_s), (units_in, units_s),
                (emb_in, emb_s), (inv_in, inv_s),
            )
        )
    ]
    first, second = first[:5], first[5:]

    def loads(b):
        part = pl.ds(pl.multiple_of(b * rows, rows), rows)
        return (
            pltpu.make_async_copy(normed_in.at[part], normed_s.at[part], block_sem.at[2 * b]),
            pltpu.make_async_copy(x_in.at[b], x_s.at[b], block_sem.at[2 * b + 1]),
        )

    last = pltpu.make_async_copy(qs_in, qs_s, last_sem)
    for copy in first:
        copy.start()
    gain, bias = one_row(gain_ref), one_row(bias_ref)
    gain_w = two_parts(gain, wp_ref[...])
    bias_w = two_parts(bias, wp_ref[...])
    qg_s[...] = jnp.zeros_like(qg_s)
    for copy in first:
        copy.wait()
    for copy in second:
        copy.start()
    loads(0)[0].start()

    spread = jnp.zeros((tokens, 1), F32)
    for r in range(count):
        teacher = maps_s[midx_ref[r]].astype(F32)
        valid = lax.broadcasted_iota(jnp.int32, teacher.shape, 1) < len_ref[r]
        teacher_log = jnp.log(teacher)
        teacher = jnp.where(valid, teacher, 0.0)
        teacher_total = jnp.sum(teacher, axis=-1, keepdims=True)
        teacher_prob = teacher / teacher_total
        gap = (teacher_log - jnp.log(teacher_total)) - log_s[r]
        spread += jnp.sum(jnp.where(valid, teacher_prob * gap, 0.0), axis=-1, keepdims=True)
        slope = ((prob_s[r] - teacher_prob) / (tokens * sharpness)).astype(BF16)
        up_s[pl.ds(r, seq, stride=count), :] = dot(slope, qunit_s[qidx_ref[r]], 0, 0).astype(BF16).astype(F32)
        un_s[r] = dot(slope, units_s[r], 1, 0)
    for r in range(count):
        qg_s[qidx_ref[r]] += un_s[r]
    total_eg = jnp.zeros((1, emb), F32)
    for copy in second:
        copy.wait()
    loads(0)[1].start()
    if blocks > 1:
        for copy in loads(1):
            copy.start()
    for b in range(0, total, thin):
        e = emb_s[b : b + thin]
        upstream = up_s[b : b + thin]
        length = jnp.sqrt(jnp.sum(e * e, axis=-1, keepdims=True) + epsilon)
        direction = e / length
        eg = (upstream - direction * jnp.sum(direction * upstream, axis=-1, keepdims=True)) / length
        eg = eg.astype(BF16)
        eg_s[b : b + thin] = eg
        eg = eg.astype(F32)
        total_eg += jnp.sum(eg, axis=0, keepdims=True)
        inverse = inv_s[b : b + thin]
        mean_s[b : b + thin] = inverse * (jnp.sum(eg * gain_w, axis=-1, keepdims=True) / width)
        along_s[b : b + thin] = inverse * (jnp.sum(eg * (e - bias_w), axis=-1, keepdims=True) / width)

    wo_s[...] = jnp.zeros_like(wo_s)
    nt_s[...] = jnp.zeros_like(nt_s)

    def wide(b, _):
        base = pl.multiple_of(b * rows, rows)
        part = pl.ds(base, rows)
        loads(b)[0].wait()

        @pl.when(b + 2 < blocks)
        def _():
            for copy in loads(b + 2):
                copy.start()

        @pl.when(b == blocks - 1)
        def _():
            last.start()

        for n in range(0, rows, sub):
            hg_s[n : n + sub] = dot(eg_s[pl.ds(base + n, sub)], wpt_ref[...], 1, 0)
            for c in range(n, n + sub, 16):
                here = pl.ds(base + c, 16)
                inverse, mean, along = inv_s[here], mean_s[here], along_s[here]
                for v in range(0, width, 128):
                    scaled = hg_s[c : c + 16, v : v + 128] * gain[:, v : v + 128]
                    normed = normed_s[here, v : v + 128].astype(F32)
                    sg_s[here, v : v + 128] = (inverse * scaled - mean - normed * along).astype(BF16)
        pltpu.make_async_copy(sg_s.at[part], sg_out.at[part], out_sem.at[b]).start()
        loads(b)[1].wait()
        wo_s[...] += dot(x_s[b], sg_s[part], 1, 0)
        nt_s[...] += dot(eg_s[part], normed_s[part], 0, 0)
        return 0

    lax.fori_loop(0, blocks, wide, 0)

    last.wait()
    qg = qg_s[...].reshape(qdir_ref.shape)
    qdir = qdir_ref[...]
    qeg = (qg - qdir * jnp.sum(qdir * qg, axis=-1, keepdims=True)) / qlen_ref[:, :1]
    high = qeg.astype(BF16)
    low = (qeg - high.astype(F32)).astype(BF16)
    qs = qs_s[...]
    proj_query = dot(high, qs, 0, 0) + dot(low, qs, 0, 0)
    nt = nt_s[...]
    s = jnp.broadcast_to(total_eg, (emb, emb)).T[:, :1]
    wpt = wpt_ref[...].astype(F32)
    proj = nt * gain + s * bias + proj_query
    gain_row = jnp.sum(wpt * nt, axis=0, keepdims=True)
    bias_row = jnp.sum(wpt * s, axis=0, keepdims=True)
    index = lax.broadcasted_iota(jnp.int32, (tokens, width), 0)
    top = jnp.where(index == 0, gain_row, jnp.where(index == 1, bias_row, 0.0))
    rest_rows = jnp.zeros((128 - 2 * tokens, width), F32)
    right_s[...] = jnp.concatenate([proj, top, jnp.broadcast_to(spread, (tokens, width)), rest_rows], axis=0).T
    half = width // CORES
    chunk = send_ref.shape[1]
    for ref, which in ((send_ref, 1 - core_ref[0]), (keep_ref, core_ref[0])):
        start = pl.multiple_of(which * half, half)
        left, right = wo_s[pl.ds(start, half)], right_s[pl.ds(start, half)]
        for c in range(half // chunk):
            ref[c, :, :width] = left[c * chunk : (c + 1) * chunk].astype(BF16)
            ref[c, :, width:] = right[c * chunk : (c + 1) * chunk].astype(BF16)
    for b in range(blocks):
        part = pl.ds(b * rows, rows)
        pltpu.make_async_copy(sg_s.at[part], sg_out.at[part], out_sem.at[b]).wait()


def student_backward(
    qidx, midx, lens, core, maps, scores, embeds, x, normed, inverse, gain, bias, wp, wpt,
    count, tokens, group_queries, chunk,
):
    total, width = normed.shape
    emb = wp.shape[1]
    blocks = x.shape[0]
    chunks = width // CORES // chunk
    prob, log, units, qunit, qdir, qlen, qs = scores
    manual = [maps, prob, log, units, qunit, embeds, x, normed, inverse, qs]
    packed = jax.ShapeDtypeStruct((chunks, chunk, width + emb + 128), BF16)
    return pl.pallas_call(
        functools.partial(backward_kernel, tokens, count, blocks),
        in_specs=[SMEM] * 4 + [ANY] * len(manual) + [VMEM] * 6,
        out_specs=[ANY, VMEM, VMEM],
        scratch_shapes=[pltpu.VMEM(a.shape, a.dtype) for a in manual]
        + [
            pltpu.VMEM((total, emb), F32),
            pltpu.VMEM((total, emb), BF16),
            pltpu.VMEM((total, 128), F32),
            pltpu.VMEM((total, 128), F32),
            pltpu.VMEM((count, tokens, emb), F32),
            pltpu.VMEM(qunit.shape, F32),
            pltpu.VMEM((total // blocks, width), F32),
            pltpu.VMEM((total, width), BF16),
            pltpu.VMEM((width, width), F32),
            pltpu.VMEM((emb, width), F32),
            pltpu.VMEM((width, emb + 128), F32),
            pltpu.SemaphoreType.DMA((7,)),
            pltpu.SemaphoreType.DMA((2 * blocks,)),
            pltpu.SemaphoreType.DMA((blocks,)),
            pltpu.SemaphoreType.DMA,
        ],
        out_shape=[jax.ShapeDtypeStruct((total, width), BF16), packed, packed],
        compiler_params=params(),
        cost_estimate=cost(2 * total * width * (width + 2 * emb), 8 * total * width),
        name="student_backward",
    )(qidx, midx, lens, core, *manual, qdir, qlen, gain, bias, wp, wpt)


def context_kernel(sg_ref, wo_ref, out_ref):
    out_ref[...] = dot(sg_ref[...], wo_ref[...], 1, 1).astype(BF16)


def context_grad(sg, out_weight):
    total, width = sg.shape
    rows = split_rows(total, 720)
    block = pl.BlockSpec((rows, width), lambda s: (s, 0))
    return pl.pallas_call(
        context_kernel,
        grid=(total // rows,),
        in_specs=[block, pl.BlockSpec(out_weight.shape, lambda s: (0, 0))],
        out_specs=block,
        out_shape=jax.ShapeDtypeStruct(sg.shape, BF16),
        compiler_params=params(),
        cost_estimate=cost(2 * total * width * width, 4 * total * width),
        name="context_grad",
    )(sg, out_weight)


def split_sum_kernel(inputs, outputs, index_ref, *rest):
    ins, outs, total_s = rest[:inputs], rest[inputs : inputs + outputs], rest[-1]
    total = ins[0][...].astype(F32)
    for ref in ins[1:]:
        total = total + ref[...].astype(F32)
    total_s[...] = total.astype(BF16).reshape(total_s.shape)
    for k in range(outputs):
        outs[k][...] = total_s[index_ref[k]].reshape(outs[k].shape)


def split_sum(arrays, index, name):
    outputs = index.shape[0]
    shape = arrays[0].shape
    lead = shape[0] // outputs
    out = shape[1:] if lead == 1 else (lead,) + shape[1:]
    return pl.pallas_call(
        functools.partial(split_sum_kernel, len(arrays), outputs),
        in_specs=[SMEM] + [VMEM] * len(arrays),
        out_specs=[VMEM] * outputs,
        out_shape=[jax.ShapeDtypeStruct(out, BF16)] * outputs,
        scratch_shapes=[pltpu.VMEM((outputs, lead) + shape[1:], BF16)],
        compiler_params=pltpu.CompilerParams(vmem_limit_bytes=SMALL_LIMIT),
        name=name,
    )(index, *arrays)


def sum_kernel(*refs):
    total = refs[0][...].astype(F32)
    for ref in refs[1:-1]:
        total = total + ref[...].astype(F32)
    refs[-1][...] = total.astype(BF16)


def plain_sum(arrays, name):
    return pl.pallas_call(
        sum_kernel,
        in_specs=[VMEM] * len(arrays),
        out_specs=VMEM,
        out_shape=jax.ShapeDtypeStruct(arrays[0].shape, BF16),
        compiler_params=pltpu.CompilerParams(vmem_limit_bytes=SMALL_LIMIT),
        name=name,
    )(*arrays)


def unpack_kernel(parts, width, emb, tokens, scale, index_ref, *rest):
    ins = rest[:parts]
    wo_ref, proj_ref, gain_ref, bias_ref, loss_ref, small_s = rest[parts:]
    per = ins[0].shape[0]
    for a in range(parts):
        for k in range(per):
            c = index_ref[a * per + k]
            value = ins[a][k].astype(F32)
            wo_ref[c] = value[:, :width]
            proj_ref[c] = value[:, width : width + emb]
            small_s[c] = value[:, width + emb :]
    turned = small_s[...].reshape(width, 128).T
    for v in range(width // 128):
        gain_ref[v : v + 1] = turned[0:1, v * 128 : (v + 1) * 128]
        bias_ref[v : v + 1] = turned[1:2, v * 128 : (v + 1) * 128]
    loss_ref[0] = jnp.sum(turned[tokens : 2 * tokens, 0:1]) * scale


def unpack(arrays, index, width, emb, tokens, scale):
    parts = len(arrays)
    per, chunk, _ = arrays[0].shape
    chunks = parts * per
    return pl.pallas_call(
        functools.partial(unpack_kernel, parts, width, emb, tokens, scale),
        in_specs=[SMEM] + [VMEM] * parts,
        out_specs=[VMEM] * 4 + [SMEM],
        out_shape=[jax.ShapeDtypeStruct((chunks, chunk, n), F32) for n in (width, emb)]
        + [jax.ShapeDtypeStruct((width // 128, 128), F32)] * 2
        + [jax.ShapeDtypeStruct((1,), F32)],
        scratch_shapes=[pltpu.VMEM((chunks, chunk, 128), F32)],
        compiler_params=pltpu.CompilerParams(vmem_limit_bytes=SMALL_LIMIT),
        name="unpack",
    )(index, *arrays)


def local(
    context,
    stream,
    out_weight,
    gain,
    bias,
    proj_weight,
    query_states,
    passage_len,
    passage_dest,
    teacher_states,
    teacher_query,
    teacher_key,
):
    dp = lax.axis_size("dp")
    nt = lax.axis_size("tensor")
    chips = dp // CORES
    me = lax.axis_index("dp")
    chip, core = me // CORES, me % CORES
    mt = lax.axis_index("tensor")
    count, seq, width = context.shape
    emb = proj_weight.shape[1]
    group_queries, tokens, _ = query_states.shape
    depth, heads = teacher_query.shape
    per = count // dp
    per_query = count * nt // group_queries

    def flat(a):
        return a.transpose(1, 0, 2).reshape(-1, a.shape[2])

    paired = chips & (chips - 1) == 0

    def partner(c, k):
        return c ^ k if paired else (c + k) % chips

    def shift_chip(x, k):
        return lax.ppermute(
            x, "dp", [(c * CORES + o, partner(c, k) * CORES + o) for c in range(chips) for o in range(CORES)]
        )

    def swap_core(x):
        return lax.ppermute(x, "dp", [(d, d ^ 1) for d in range(dp)])

    def shift_t(x, k):
        return lax.ppermute(x, "tensor", [(t, (t + k) % nt) for t in range(nt)])

    dest_group = passage_dest // (count * nt)
    rows = jnp.arange(count, dtype=jnp.int32)
    rank = jnp.sum(
        (dest_group[:, None] == dest_group[None, :]) & (rows[None, :] < rows[:, None]), axis=1, dtype=jnp.int32
    )
    place = dest_group * per + rank
    positions = jnp.sum(
        jnp.where(place[:, None] == rows[None, :], (passage_dest % count)[:, None], 0), axis=0
    )
    each = group_queries * tokens
    states = query_states.reshape(each, width)
    column_blocks = [states[:, n * heads : (n + 1) * heads] for n in range(width // heads)]
    extra = jnp.pad(positions.astype(BF16)[None, :], ((0, 15), (0, heads - count)))
    rider = jnp.concatenate(column_blocks + [extra], axis=0)

    part = depth // dp
    slices = 2 * (nt - 1)
    by_hops = sorted(range(1, chips), key=lambda k: (bin(k).count("1"), k))
    far = by_hops[len(by_hops) - chips // 4 :] if paired else []

    def slice_of(c):
        start = (c * CORES + core) * part
        return jnp.stack([lax.dynamic_slice_in_dim(w, start, part, 0) for w in (teacher_query, teacher_key)])

    mine, far_mine = slice_of(chip), [slice_of(partner(chip, k)) for k in far]
    rider = jnp.pad(rider, ((0, -rider.shape[0] % part), (0, 0))).reshape(-1, part, heads)
    along = jnp.concatenate([shift_t(mine, k) for k in range(1, nt)] + [rider], axis=0)
    gain2, bias2 = gain.reshape(-1, 128), bias.reshape(-1, 128)
    x = flat(context)
    far_riders = [shift_chip(rider, k) for k in far]
    along, far_mine, far_riders, forward_gain = lax.optimization_barrier((along, far_mine, far_riders, gain2))
    pieces = [along] + [None] * (chips - 1)
    for k in range(1, chips):
        if k not in far:
            pieces[k] = shift_chip(along, k)
    for k, other, far_rider in zip(far, far_mine, far_riders):
        pieces[k] = jnp.concatenate([shift_t(other, n) for n in range(1, nt)] + [far_rider], axis=0)
    shifts = jnp.arange(chips, dtype=jnp.int32)
    behind = chip ^ shifts if paired else (chip - shifts) % chips
    piece_rows = jnp.concatenate([behind * CORES + core, behind * CORES + 1 - core]).astype(jnp.int32)
    midx = place.astype(jnp.int32)
    def piece_of(group):
        apart = chip ^ (group // CORES) if paired else (chip - group // CORES) % chips
        return apart + jnp.where(group % CORES == core, 0, chips)

    qidx = passage_dest // per_query - dest_group * group_queries + piece_of(dest_group) * group_queries
    qidx = qidx.astype(jnp.int32)
    source = piece_of(jnp.arange(dp, dtype=jnp.int32)).astype(jnp.int32)

    normed, embeds, inverse, turned = student_forward(
        x, flat(stream), out_weight, forward_gain, bias2, proj_weight
    )
    pieces[1:], normed, embeds, inverse, turned, proj_turned = lax.optimization_barrier(
        (pieces[1:], normed, embeds, inverse, turned, proj_weight.T)
    )
    pieces = pieces + [swap_core(a) for a in pieces]
    told = [a[slices:].reshape(-1, heads)[width // heads * each, :count] for a in pieces]
    order = lax.dynamic_slice_in_dim(jnp.stack(told), me * per, per, 1).astype(jnp.int32)
    maps = teacher_maps(
        order, source, piece_rows, slices, flat(teacher_states), teacher_query, teacher_key, pieces, count, tokens
    )
    maps, embeds = lax.optimization_barrier((maps, embeds))
    maps = lax.all_to_all(maps, "dp", split_axis=0, concat_axis=0, tiled=True)
    scores = student_scores(
        qidx, passage_len, embeds, proj_weight, pieces, slices, count, tokens, group_queries
    )
    chunk = width // (CORES * chips * nt)
    sg, send, keep = student_backward(
        qidx, midx, passage_len, core.astype(jnp.int32).reshape(1), maps, scores,
        embeds, turned, normed, inverse, gain2, bias2, proj_weight, proj_turned,
        count, tokens, group_queries, chunk,
    )

    ahead = partner(chip, shifts).astype(jnp.int32)
    t_shifts = jnp.arange(nt, dtype=jnp.int32)
    t_ahead = ((mt + t_shifts) % nt).astype(jnp.int32)
    parts = split_sum([keep, swap_core(send)], ahead, "sum_cores")
    parts, sg = lax.optimization_barrier((parts, sg))
    grad_context = context_grad(sg, out_weight)
    parts = [parts[0]] + [shift_chip(parts[k], k) for k in range(1, chips)]
    parts, grad_context = lax.optimization_barrier((parts, grad_context))
    parts = split_sum(parts, t_ahead, "sum_plane")
    parts = [parts[0]] + [shift_t(parts[k], k) for k in range(1, nt)]
    total = plain_sum(parts, "sum_tensor")
    line = jnp.stack([total] + [shift_t(total, k) for k in range(1, nt)])
    plane = [line] + [shift_chip(line, k) for k in range(1, chips)]
    arrays = plane + [swap_core(a) for a in plane]
    base = jnp.concatenate([core * chips + behind, (1 - core) * chips + behind]) * nt
    index = (base[:, None] + ((mt - t_shifts) % nt)[None, :]).reshape(-1).astype(jnp.int32)
    grad_out, grad_proj, grad_gain, grad_bias, loss = unpack(
        arrays, index, width, emb, tokens, 1.0 / (count * dp * nt * tokens)
    )
    return (
        loss.reshape(()),
        grad_out.reshape(width, width),
        grad_proj.reshape(width, emb),
        grad_gain.reshape(width),
        grad_bias.reshape(width),
        grad_context.reshape(seq, count, width).transpose(1, 0, 2),
    )


def solution(mesh):
    return jax.shard_map(
        local,
        mesh=mesh,
        in_specs=(
            P(("dp", "tensor"), None, None),
            P(("dp", "tensor"), None, None),
            P(),
            P(),
            P(),
            P(),
            P("dp", None, None),
            P(("dp", "tensor")),
            P(("dp", "tensor")),
            P(("dp", "tensor"), None, None),
            P(None, "tensor"),
            P(None, "tensor"),
        ),
        out_specs=(P(), P(), P(), P(), P(), P(("dp", "tensor"), None, None)),
        check_vma=False,
    )
```
